32 devices in a mesh: rep: 8 (over z, y), blk: 4 (over x, core).
Axes of the slice: x: 2, y: 2, z: 4, core: 2. Of those that a mesh axis runs over, the one named last changes fastest.
Arguments:
- encoded: bfloat16 [128, 512, 512], P(('rep', 'blk')), may hold values from -6 to 6
- queries: bfloat16 [1024, 512], P('blk'), may hold values from -0.25 to 0.25
- classifiers: bfloat16 [1024, 512], P('blk'), may hold values from -1 to 1
- lengths: int32 [128], P(('rep', 'blk')), may hold values from 1 to 512, 49152 in all
- beam: int32 [128, 1024], P(('rep', 'blk')), may hold values 0 or 1
- logit_grad: float32 [128, 1024], P(('rep', 'blk')), may hold values from -6 to 6
Outputs:
- logits: float32 [128, 1024], P(('rep', 'blk'))
- encoded_grad: bfloat16 [128, 512, 512], P(('rep', 'blk'))
- label_grad: float32 [1024, 1024], P('blk')
The draws below stay inside these ranges and needn't reach their ends.
Inputs may be any that keep to these rules, and one draw needn't show every extreme that they name: `lengths`: every document has at least one real token, and some document has exactly 512.
All inputs are finite; a program needn't handle non-finite values. No bound on the sum of `lengths` or of `beam` on one device may be relied on, other than what follows from the above.
Results may differ from the reference program's by a relative error of at most 0.0058.
Values may be sent and summed in bfloat16 or wider, within the bound.
No kernel may reach another device: no remote copies, remote signals or barrier semaphores. Data moves between devices by JAX's collectives and lax.ppermute only.
A program may use at most 64 MiB of HBM per device.

```python
import math
import jax
import jax.numpy as jnp
import numpy as np
from jax import lax

E = 512
LABELS = 1024
L = 512
DOCS = 128


def touch_ends(entries, stream_key, low, top_value):
    index_at = [jax.random.randint(jax.random.fold_in(stream_key, axis), (), 0, length) for axis, length in enumerate(entries.shape)]
    main_axis = entries.shape.index(max(entries.shape))
    next_to = index_at[:main_axis] + [(index_at[main_axis] + 1) % entries.shape[main_axis]] + index_at[main_axis + 1:]
    return entries.at[tuple(index_at)].set(low).at[tuple(next_to)].set(top_value)


def strengthened(result, rng, source, target, parts, factor):
    owner, partner = [(jnp.arange(result.shape[dim]) // (result.shape[dim] // parts)).reshape([-1 if axis == dim else 1 for axis in range(result.ndim)]) for dim in (source, target)]
    chosen = jax.random.permutation(rng, parts)[partner]
    strong = (owner == chosen) | (owner == (partner + parts // 2) % parts)
    return jnp.where(strong, factor * result, result)


def steps_of(key, extent, split, least, high):
    def one(axis_at, shards_of):
        draws = jax.random.uniform(jax.random.fold_in(jax.random.fold_in(key, 6), axis_at), (shards_of,), jnp.float32, least / len(split), high / len(split))
        return jnp.repeat(jnp.exp(draws), extent[axis_at] // shards_of).reshape((-1,) + (1,) * (len(extent) - axis_at - 1))

    level = one(*split[0])
    for cut in split[1:]:
        level = level * one(*cut)
    return level


def split_up(count, total, most, skew):
    weights = [(1 << 20) // math.isqrt(standing ** skew) + 1 for standing in range(2, count + 1)]
    surplus, counts = total - most - (count - 1), [1] * (count - 1)
    while surplus > 0:
        movable = [i for i in range(count - 1) if counts[i] < most]
        pool, budget = sum([weights[i] for i in movable]), surplus
        for i in movable:
            more = min(most - counts[i], max(1, budget * weights[i] // pool), surplus)
            counts[i] = counts[i] + more
            surplus = surplus - more
    return np.array([most] + counts)


def ragged_sizes(own_key, count, total, bound, slope):
    if count == 2:
        one = jax.random.randint(own_key, (), max(1, total - bound), min(bound, total - 1) + 1)
        return jnp.stack([one, total - one])
    sizes = jnp.asarray(split_up(count, total, bound, slope), jnp.int32)
    pairs = (count - 1) // 2
    source_of, receiver = sizes[1:1 + 2 * pairs:2], sizes[2:2 + 2 * pairs:2]
    room = jnp.minimum(source_of - 1, bound - receiver)
    moved = jax.random.randint(jax.random.fold_in(own_key, 1), (pairs,), 0, 1 << 20) % (room + 1)
    sizes = sizes.at[1:1 + 2 * pairs:2].set(source_of - moved).at[2:2 + 2 * pairs:2].set(receiver + moved)
    return sizes[jax.random.permutation(jax.random.fold_in(own_key, 2), count)]


def centred(own_key, shape, scale, limit, split=(), dtype=jnp.bfloat16):
    loudness = steps_of(own_key, shape, split, -0.22, 0.18) if split else 1.0
    array = jax.random.normal(own_key, shape, jnp.float32) * scale * loudness
    return jnp.minimum(jnp.maximum(array, -limit), limit).astype(dtype)


def heavy_noise(own_key, dims, deviation, most, cuts, heavy, dtype=jnp.bfloat16):
    entries = deviation * jax.random.normal(own_key, dims, jnp.float32)
    if cuts:
        entries = entries * steps_of(own_key, dims, cuts, -0.22, 0.18)
    return jnp.clip(strengthened(entries, jax.random.fold_in(own_key, 3), *heavy), -most, most).astype(dtype)


def setup_inputs(seed: int = 0) -> dict:
    splits = jax.random.split(jax.random.key(seed), 7)
    return {
        "encoded": centred(splits[0], (DOCS, L, E), 1.0, 6.0, ((0, 32),)),
        "queries": centred(splits[1], (LABELS, E), E ** -0.5, 0.25, ((0, 4),)),
        "classifiers": centred(splits[2], (LABELS, E), (E // 16) ** -0.5, 1.0, ((0, 4),)),
        "lengths": ragged_sizes(splits[3], DOCS, DOCS * L * 3 // 4, L, 1).astype(jnp.int32),
        "beam": touch_ends((jax.random.randint(splits[4], (DOCS, LABELS), 0, 4) < 1).astype(jnp.int32), jax.random.fold_in(splits[4], 1), 0, 1),
        "logit_grad": heavy_noise(splits[5], (DOCS, LABELS), 1.0, 6.0, ((0, 32),), (0, 1, 32, 2.75), jnp.float32),
    }


def one_document(states, length, beam_row, grad_row, queries, classifiers):
    scores = jnp.dot(queries, states.T, preferred_element_type=jnp.float32)
    valid = jnp.arange(states.shape[0]) < length
    expo = jnp.where(valid[None, :], jnp.exp(scores), 0.0)
    attn = expo / jnp.sum(expo, axis=1, keepdims=True)
    attn_b = attn.astype(jnp.bfloat16)
    context = jnp.dot(attn_b, states, preferred_element_type=jnp.float32)
    cls_f = classifiers.astype(jnp.float32)
    logit = jnp.sum(context * cls_f, axis=1)
    g_row = grad_row * beam_row.astype(jnp.float32)
    ctx_grad = (g_row[:, None] * cls_f).astype(jnp.bfloat16)
    attn_grad = jnp.dot(ctx_grad, states.T, preferred_element_type=jnp.float32)
    score_grad = (attn * (attn_grad - jnp.sum(attn * attn_grad, axis=1, keepdims=True))).astype(jnp.bfloat16)
    query_grad = jnp.dot(score_grad, states, preferred_element_type=jnp.float32)
    class_grad = g_row[:, None] * context
    state_grad = jnp.dot(attn_b.T, ctx_grad, preferred_element_type=jnp.float32) + jnp.dot(score_grad.T, queries, preferred_element_type=jnp.float32)
    return logit, query_grad, class_grad, state_grad.astype(jnp.bfloat16)


def reference(encoded, queries, classifiers, lengths, beam, logit_grad):
    def step(carry, items):
        states, length, beam_row, grad_row = items
        logit, query_grad, class_grad, state_grad = one_document(states, length, beam_row, grad_row, queries, classifiers)
        return (carry[0] + query_grad, carry[1] + class_grad), (logit, state_grad)

    zeros = jnp.zeros((LABELS, E), jnp.float32)
    sums, outs = lax.scan(step, (zeros, zeros), (encoded, lengths, beam, logit_grad))
    label_grad = jnp.concatenate([sums[0], sums[1]], axis=1)
    return outs[0], outs[1], label_grad
```

```python
import functools

import jax
import jax.numpy as jnp
from jax import lax
from jax.experimental import pallas as pl
from jax.experimental.pallas import tpu as pltpu
from jax.sharding import PartitionSpec as P

F32 = jnp.float32
BF16 = jnp.bfloat16
PARAMS = pltpu.CompilerParams(vmem_limit_bytes=40 * 1024 * 1024)


def mm(a, b):
    return jnp.dot(a, b, preferred_element_type=F32)


def swap(x, axis, size, mask):
    return lax.ppermute(x, axis, [(i, i ^ mask) for i in range(size)])


def label_kernel(first, lens_ref, at_ref, enc_ref, *refs):
    if first:
        q_ref, c_ref, beam_ref, grad_ref, attn_ref, score_ref, logit_ref, out_ref, enct_ref = refs[:9]
    else:
        enct_ref, q_ref, c_ref, beam_ref, grad_ref, attn_ref, score_ref, logit_ref, out_ref = refs[:9]
    qt_ref, ct_ref, qacc_ref, cacc_ref = refs[9:]
    doc = pl.program_id(0)
    width = enc_ref.shape[2]

    @pl.when(doc == 0)
    def _():
        qt_ref[...] = q_ref[...].astype(F32).T.astype(BF16)
        ct_ref[...] = c_ref[...].astype(F32).T
        qacc_ref[...] = jnp.zeros_like(qacc_ref)
        cacc_ref[...] = jnp.zeros_like(cacc_ref)

    enc = enc_ref[0]
    if first:
        enct_ref[0] = enc.astype(F32).T.astype(BF16)
    enct = enct_ref[0]
    ct = ct_ref[...]
    g = grad_ref[pl.ds(doc, 1), :] * beam_ref[pl.ds(doc, 1), :].astype(F32)
    scores = mm(enc, qt_ref[...])
    attn_grad = mm(enc, (ct * g).astype(BF16))
    token = lax.broadcasted_iota(jnp.int32, scores.shape, 0)
    expo = jnp.where(token < lens_ref[doc], jnp.exp(scores), 0.0)
    attn = expo * (1.0 / jnp.sum(expo, axis=0, keepdims=True))
    attn_b = attn.astype(BF16)
    attn_ref[0] = attn_b
    context = mm(enct, attn_b)
    logit_ref[pl.ds(doc, 1), :] = jnp.sum(context * ct, axis=0, keepdims=True)
    cacc_ref[...] += context * g
    inner = jnp.sum(attn * attn_grad, axis=0, keepdims=True)
    score_grad = (attn * (attn_grad - inner)).astype(BF16)
    score_ref[0] = score_grad
    qacc_ref[...] += mm(enct, score_grad)

    @pl.when(doc == pl.num_programs(0) - 1)
    def _():
        out_ref[:, :width] = qacc_ref[...].T.astype(BF16)
        out_ref[:, width:] = cacc_ref[...].T.astype(BF16)


def label_chunk(lens, at, enc, enct, q, c, beam, grad):
    docs, tokens, width = enc.shape
    labels = q.shape[0]
    first = enct is None
    whole = pl.BlockSpec((1, tokens, width), lambda d, lens, at: (d, 0, 0))
    turned = pl.BlockSpec((1, width, tokens), lambda d, lens, at: (d, 0, 0))
    chunk = pl.BlockSpec((1, tokens, labels), lambda d, lens, at: (d, 0, 0))
    label = pl.BlockSpec((labels, width), lambda d, lens, at: (0, 0))
    row = pl.BlockSpec((docs, labels), lambda d, lens, at: (0, at[0]))
    out_shape = [
        jax.ShapeDtypeStruct((docs, tokens, labels), BF16),
        jax.ShapeDtypeStruct((docs, tokens, labels), BF16),
        jax.ShapeDtypeStruct((docs, labels), F32),
        jax.ShapeDtypeStruct((labels, 2 * width), BF16),
    ]
    out_specs = [
        chunk,
        chunk,
        pl.BlockSpec((docs, labels), lambda d, lens, at: (0, 0)),
        pl.BlockSpec((labels, 2 * width), lambda d, lens, at: (0, 0)),
    ]
    if first:
        out_shape.append(jax.ShapeDtypeStruct((docs, width, tokens), BF16))
        out_specs.append(turned)
    outs = pl.pallas_call(
        functools.partial(label_kernel, first),
        out_shape=out_shape,
        grid_spec=pltpu.PrefetchScalarGridSpec(
            num_scalar_prefetch=2,
            grid=(docs,),
            in_specs=[whole] + ([] if first else [turned]) + [label, label, row, row],
            out_specs=out_specs,
            scratch_shapes=[
                pltpu.VMEM((width, labels), BF16),
                pltpu.VMEM((width, labels), F32),
                pltpu.VMEM((width, labels), F32),
                pltpu.VMEM((width, labels), F32),
            ],
        ),
        compiler_params=PARAMS,
        name="label_chunk",
    )(lens, at, enc, *([] if first else [enct]), q, c, beam, grad)
    return outs


def state_kernel(count, has_acc, ats_ref, *refs):
    ins, out_ref = refs[:-1], refs[-1]
    doc = pl.program_id(0)
    total = ins[-1][0] if has_acc else None
    for k in range(count):
        attn_ref, score_ref, q_ref, c_ref, beam_ref, grad_ref = ins[6 * k : 6 * k + 6]
        g = grad_ref[...] * beam_ref[...].astype(F32)
        rows = lax.broadcasted_iota(jnp.int32, g.shape, 0)
        g = jnp.sum(jnp.where(rows == doc, g, 0.0), axis=0, keepdims=True)
        column = jnp.broadcast_to(g, (128, g.shape[1])).T[:, :1]
        ctx_grad = (c_ref[...].astype(F32) * column).astype(BF16)
        part = mm(attn_ref[0], ctx_grad) + mm(score_ref[0], q_ref[...])
        total = part if total is None else total + part
    out_ref[0] = total.astype(out_ref.dtype)


def state_chunks(ats, parts, acc, beam, grad, out_dtype):
    docs, tokens, labels = parts[0][0].shape
    width = parts[0][2].shape[1]
    chunk = pl.BlockSpec((1, tokens, labels), lambda d, ats: (d, 0, 0))
    label = pl.BlockSpec((labels, width), lambda d, ats: (0, 0))
    whole = pl.BlockSpec((1, tokens, width), lambda d, ats: (d, 0, 0))
    specs, args = [], []
    for k, (attn, score, q, c) in enumerate(parts):
        row = pl.BlockSpec((docs, labels), lambda d, ats, k=k: (0, ats[k]))
        specs += [chunk, chunk, label, label, row, row]
        args += [attn, score, q, c, beam, grad]
    if acc is not None:
        specs.append(whole)
        args.append(acc)
    return pl.pallas_call(
        functools.partial(state_kernel, len(parts), acc is not None),
        out_shape=jax.ShapeDtypeStruct((docs, tokens, width), out_dtype),
        grid_spec=pltpu.PrefetchScalarGridSpec(
            num_scalar_prefetch=1, grid=(docs,), in_specs=specs, out_specs=whole
        ),
        compiler_params=PARAMS,
        name="state_grad",
    )(ats, *args)


def split_kernel(count, place_ref, *refs):
    ins, outs = refs[:count], refs[count:]
    size = outs[0].shape[0]
    for j, out_ref in enumerate(outs):
        at = pl.ds(pl.multiple_of((place_ref[0] ^ j) * size, size), size)
        total = ins[0][at, :].astype(F32)
        for ref in ins[1:]:
            total = total + ref[at, :].astype(F32)
        out_ref[...] = total.astype(out_ref.dtype)


def split_sum(place, arrays, group):
    rows, cols = arrays[0].shape
    size = rows // group
    vmem = pl.BlockSpec(memory_space=pltpu.VMEM)
    return pl.pallas_call(
        functools.partial(split_kernel, len(arrays)),
        out_shape=[jax.ShapeDtypeStruct((size, cols), F32)]
        + [jax.ShapeDtypeStruct((size, cols), BF16)] * (group - 1),
        in_specs=[pl.BlockSpec(memory_space=pltpu.SMEM)] + [vmem] * len(arrays),
        out_specs=[vmem] * group,
        compiler_params=PARAMS,
        name="split_sum",
    )(place, *arrays)


def join_kernel(place_ref, *refs):
    ins, out_ref = refs[:-1], refs[-1]
    size = ins[0].shape[0]
    for j, ref in enumerate(ins):
        at = pl.ds(pl.multiple_of((place_ref[0] ^ j) * size, size), size)
        out_ref[at, :] = ref[...].astype(F32)


def join(place, pieces):
    size, cols = pieces[0].shape
    vmem = pl.BlockSpec(memory_space=pltpu.VMEM)
    return pl.pallas_call(
        join_kernel,
        out_shape=jax.ShapeDtypeStruct((size * len(pieces), cols), F32),
        in_specs=[pl.BlockSpec(memory_space=pltpu.SMEM)] + [vmem] * len(pieces),
        out_specs=vmem,
        compiler_params=PARAMS,
        name="join",
    )(place, *pieces)


def per_device(reps, blks, encoded, queries, classifiers, lengths, beam, logit_grad):
    labels = queries.shape[0]
    mine = lax.axis_index("blk")
    rep = lax.axis_index("rep")

    qs, cs = {0: queries}, {0: classifiers}
    for k in range(1, blks):
        low = k & -k
        qs[k] = swap(qs[k ^ low], "blk", blks, low)
        cs[k] = swap(cs[k ^ low], "blk", blks, low)

    ats = [(mine ^ k).reshape(1).astype(jnp.int32) for k in range(blks)]
    enct = None
    attns, scores, logits, grads = {}, {}, {}, {}
    for k in range(blks):
        outs = label_chunk(lengths, ats[k], encoded, enct, qs[k], cs[k], beam, logit_grad)
        attns[k], scores[k], logits[k], grads[k] = outs[:4]
        if k == 0:
            enct = outs[4]

    summed = {k: [grads[k]] for k in range(blks)}
    bit = 1
    while bit < blks:
        for k in [k for k in summed if k & bit]:
            arrays = summed.pop(k)
            whole = arrays[0]
            if len(arrays) > 1:
                whole = sum(a.astype(F32) for a in arrays).astype(BF16)
            summed[k ^ bit].append(swap(whole, "blk", blks, bit))
        bit *= 2

    group = min(reps, 8)
    place = (rep % group).reshape(1).astype(jnp.int32)
    pieces = split_sum(place, summed[0], group)
    total = pieces[0]
    for j in range(1, group):
        total = total + swap(pieces[j], "rep", reps, j).astype(F32)
    if group < reps:
        members = [[i * group + j for i in range(reps // group)] for j in range(group)]
        total = lax.psum(total, "rep", axis_index_groups=members)
    total = total.astype(BF16)
    label_grad = join(place, [total] + [swap(total, "rep", reps, j) for j in range(1, group)])

    half = blks // 2
    order = jnp.concatenate(ats)
    state = state_chunks(
        order[:half],
        [(attns[k], scores[k], qs[k], cs[k]) for k in range(half)],
        None, beam, logit_grad, F32,
    )
    state = state_chunks(
        order[half:],
        [(attns[k], scores[k], qs[k], cs[k]) for k in range(half, blks)],
        state, beam, logit_grad, BF16,
    )
    stacked = jnp.stack([logits[k] for k in range(blks)], axis=1)
    logit = jnp.take(stacked, order, axis=1).reshape(encoded.shape[0], blks * labels)
    return logit, state, label_grad


def solution(mesh):
    reps, blks = mesh.shape["rep"], mesh.shape["blk"]
    in_specs = (
        P(("rep", "blk"), None, None),
        P("blk", None),
        P("blk", None),
        P(("rep", "blk")),
        P(("rep", "blk"), None),
        P(("rep", "blk"), None),
    )
    out_specs = (P(("rep", "blk"), None), P(("rep", "blk"), None, None), P("blk", None))
    return jax.shard_map(
        functools.partial(per_device, reps, blks),
        mesh=mesh, in_specs=in_specs, out_specs=out_specs, check_vma=False,
    )
```

```python
import functools

import jax
import jax.numpy as jnp
from jax import lax
from jax.experimental import pallas as pl
from jax.experimental.pallas import tpu as pltpu
from jax.sharding import PartitionSpec as P

F32 = jnp.float32
BF16 = jnp.bfloat16
VMEM = pl.BlockSpec(memory_space=pltpu.VMEM)
SMEM = pl.BlockSpec(memory_space=pltpu.SMEM)
PARAMS = pltpu.CompilerParams(vmem_limit_bytes=24 * 1024 * 1024)
GROUP = 8


def shape(dims, dtype):
    return jax.ShapeDtypeStruct(dims, dtype)


def mm(a, b):
    return jnp.dot(a, b, preferred_element_type=F32)


def cost(products, docs, tokens, width, labels):
    return pl.CostEstimate(
        flops=2 * products * docs * tokens * width * labels,
        transcendentals=docs * tokens * labels,
        bytes_accessed=4 * docs * tokens * width,
    )


def call(kernel, out_shape, ins, name, scratch=(), estimate=None):
    single = not isinstance(out_shape, (list, tuple))
    return pl.pallas_call(
        kernel,
        out_shape=out_shape,
        in_specs=[SMEM if x.ndim == 1 else VMEM for x in ins],
        out_specs=VMEM if single else [VMEM] * len(out_shape),
        scratch_shapes=scratch,
        compiler_params=PARAMS,
        cost_estimate=estimate,
        name=name,
    )(*ins)


def label_kernel(ks, first, info_ref, lens_ref, enc_ref, *refs):
    if not first:
        enct_ref, refs = refs[0], refs[1:]
    qc_refs, refs = refs[: 2 * len(ks)], refs[2 * len(ks) :]
    beam_ref, grad_ref, refs = refs[0], refs[1], refs[2:]
    if first:
        enct_ref, refs = refs[0], refs[1:]
    out_refs = refs
    docs, tokens, width = enc_ref.shape
    labels = qc_refs[0].shape[0]
    if first:
        for d in range(docs):
            enct_ref[d] = enc_ref[d].T
    for n, k in enumerate(ks):
        q_ref, c_ref = qc_refs[2 * n : 2 * n + 2]
        attn_ref, score_ref, logit_ref, out_ref = out_refs[4 * n : 4 * n + 4]
        lanes = pl.ds(pl.multiple_of((info_ref[0] ^ k) * labels, labels), labels)
        gate = grad_ref[:, lanes] * beam_ref[:, lanes].astype(F32)
        qt = q_ref[...].T
        ct = c_ref[...].T.astype(F32)
        token = lax.broadcasted_iota(jnp.int32, (tokens, labels), 0)

        def products(d):
            enc = enc_ref[d]
            return mm(enc, qt), mm(enc, (ct * gate[d : d + 1, :]).astype(BF16))

        def soften(d, scores, attn_grad):
            expo = jnp.where(token < lens_ref[d], jnp.exp(scores), 0.0)
            attn = expo * (1.0 / jnp.sum(expo, axis=0, keepdims=True))
            attn_b = attn.astype(BF16)
            attn_ref[d] = attn_b
            inner = jnp.sum(attn * attn_grad, axis=0, keepdims=True)
            score_grad = (attn * (attn_grad - inner)).astype(BF16)
            score_ref[d] = score_grad
            return attn_b, score_grad

        query_grad, class_grad = None, None
        ahead = products(0)
        for d in range(docs):
            now = ahead
            if d + 1 < docs:
                ahead = products(d + 1)
            attn_b, score_grad = soften(d, *now)
            enct = enct_ref[d]
            context = mm(enct, attn_b)
            logit_ref[d : d + 1, :] = jnp.sum(context * ct, axis=0, keepdims=True)
            part = context * gate[d : d + 1, :]
            class_grad = part if class_grad is None else class_grad + part
            part = mm(enct, score_grad)
            query_grad = part if query_grad is None else query_grad + part
        query_grad = query_grad.astype(BF16).T
        class_grad = class_grad.astype(BF16).T
        size = labels // GROUP
        for i in range(GROUP):
            rows = pl.ds(pl.multiple_of((info_ref[1] ^ i) * size, size), size)
            out_ref[rows, :width] = query_grad[i * size : (i + 1) * size, :]
            out_ref[rows, width:] = class_grad[i * size : (i + 1) * size, :]


def label_chunks(ks, info, lens, enc, enct, qs, cs, beam, grad):
    docs, tokens, width = enc.shape
    labels = qs[0].shape[0]
    first = enct is None
    out_shape = [shape((docs, width, tokens), BF16)] if first else []
    for _ in ks:
        out_shape += [
            shape((docs, tokens, labels), BF16),
            shape((docs, tokens, labels), BF16),
            shape((docs, labels), F32),
            shape((labels, 2 * width), BF16),
        ]
    ins = [info, lens, enc] + ([] if first else [enct])
    for k in ks:
        ins += [qs[k], cs[k]]
    outs = call(
        functools.partial(label_kernel, ks, first), out_shape, ins + [beam, grad], "label_chunk",
        estimate=cost(4 * len(ks), docs, tokens, width, labels),
    )
    if first:
        enct, outs = outs[0], outs[1:]
    return enct, {k: tuple(outs[4 * n : 4 * n + 4]) for n, k in enumerate(ks)}


def state_kernel(ks, has_acc, info_ref, *refs):
    beam_ref, grad_ref, refs = refs[0], refs[1], refs[2:]
    ins, out_ref = refs[:-1], refs[-1]
    docs = out_ref.shape[0]
    labels = ins[2].shape[0]
    ctx_grads = [[] for _ in range(docs)]
    for n, k in enumerate(ks):
        lanes = pl.ds(pl.multiple_of((info_ref[0] ^ k) * labels, labels), labels)
        gate = grad_ref[:, lanes] * beam_ref[:, lanes].astype(F32)
        gate = jnp.concatenate([gate, jnp.zeros((128 - docs, labels), F32)], axis=0).T
        c = ins[4 * n + 3][...].astype(F32)
        for d in range(docs):
            ctx_grads[d].append((c * gate[:, d : d + 1]).astype(BF16))
    for d in range(docs):
        total = ins[-1][d] if has_acc else None
        for n in range(len(ks)):
            attn_ref, score_ref, q_ref = ins[4 * n : 4 * n + 3]
            part = mm(attn_ref[d], ctx_grads[d][n]) + mm(score_ref[d], q_ref[...])
            total = part if total is None else total + part
        out_ref[d] = total.astype(out_ref.dtype)


def state_chunks(ks, info, parts, qs, cs, acc, beam, grad, out_dtype):
    docs, tokens, labels = parts[ks[0]][0].shape
    width = qs[0].shape[1]
    ins = [info, beam, grad]
    for k in ks:
        ins += [parts[k][0], parts[k][1], qs[k], cs[k]]
    if acc is not None:
        ins.append(acc)
    return call(
        functools.partial(state_kernel, ks, acc is not None),
        shape((docs, tokens, width), out_dtype), ins, "state_grad",
        estimate=cost(2 * len(ks), docs, tokens, width, labels),
    )


def core_kernel(info_ref, own_ref, own_in_ref, far_ref, far_in_ref, keep_ref, send_ref):
    half = own_ref.shape[0] // 2
    size = half // 4

    def total(a_ref, b_ref, rows):
        return a_ref[rows, :].astype(F32) + b_ref[rows, :].astype(F32)

    @pl.when(info_ref[2] == 0)
    def _():
        rows = pl.ds(0, 2 * half)
        keep_ref[...] = total(own_ref, own_in_ref, rows)
        send_ref[...] = total(far_ref, far_in_ref, rows).astype(BF16)

    @pl.when(info_ref[2] == 1)
    def _():
        for z in range(2):
            for x, (a_ref, b_ref) in enumerate(((own_ref, own_in_ref), (far_ref, far_in_ref))):
                to = pl.ds((2 * z + x) * 2 * size, 2 * size)
                keep_ref[to, :] = total(a_ref, b_ref, pl.ds(2 * z * size, 2 * size))
                send_ref[to, :] = total(a_ref, b_ref, pl.ds(half + 2 * z * size, 2 * size)).astype(BF16)


def add_kernel(keep_ref, in_ref, *out_refs):
    total = keep_ref[...] + in_ref[...].astype(F32)
    if len(out_refs) == 1:
        out_refs[0][...] = total.astype(BF16)
    else:
        half = total.shape[0] // 2
        out_refs[0][...] = total[:half]
        out_refs[1][...] = total[half:].astype(BF16)


def add_split(keep, received):
    rows, cols = keep.shape
    out = [shape((rows // 2, cols), F32), shape((rows // 2, cols), BF16)]
    return call(add_kernel, out, [keep, received], "add_split")


def add_last(keep, received):
    return call(add_kernel, shape(keep.shape, BF16), [keep, received], "add_last")


def join_kernel(chunks, info_ref, own_ref, z_ref, two_ref, four_ref, *refs):
    logit_refs, (out_ref, logit_ref) = refs[:chunks], refs[chunks:]
    size = own_ref.shape[0]

    def put(ref, at, block):
        rows = pl.ds(pl.multiple_of((info_ref[1] ^ block) * size, size), size)
        out_ref[rows, :] = ref[at * size : (at + 1) * size, :].astype(F32)

    put(own_ref, 0, 0)
    put(z_ref, 0, 1)
    for core, (early, late) in enumerate(((2, 4), (4, 2))):
        @pl.when(info_ref[2] == core)
        def _():
            for z in range(2):
                put(two_ref, z, early + z)
                for e in range(2):
                    put(four_ref, 2 * e + z, late + e * early + z)

    labels = logit_refs[0].shape[1]
    for k in range(chunks):
        lanes = pl.ds(pl.multiple_of((info_ref[0] ^ k) * labels, labels), labels)
        logit_ref[:, lanes] = logit_refs[k][...]


def per_device(reps, blks, encoded, queries, classifiers, lengths, beam, logit_grad):
    labels, width = queries.shape
    docs = encoded.shape[0]
    total = reps * blks
    blk, rep = lax.axis_index("blk"), lax.axis_index("rep")
    turn = (rep & 1) * 4 + (rep & 2) + ((rep >> 2) & 1)
    info = jnp.stack([blk, turn, blk & 1]).astype(jnp.int32)

    def swap(x, mask, odd_mask=None):
        masks = (mask, mask if odd_mask is None else odd_mask)
        return lax.ppermute(x, ("rep", "blk"), [(i, i ^ masks[i & 1]) for i in range(total)])

    core, ax = 1, 2
    ay, az, azz = blks, 2 * blks, 4 * blks

    qs, cs = {0: queries}, {0: classifiers}
    qs[2], cs[2] = swap(queries, ax), swap(classifiers, ax)
    qs[1], cs[1] = swap(queries, core), swap(classifiers, core)

    enct, parts = label_chunks((0, 1), info, lengths, encoded, None, qs, cs, beam, logit_grad)
    enct, qs[2], cs[2] = lax.optimization_barrier((enct, qs[2], cs[2]))
    qs[3], cs[3] = swap(qs[2], core), swap(cs[2], core)
    for k in (2, 3):
        _, more = label_chunks((k,), info, lengths, encoded, enct, qs, cs, beam, logit_grad)
        parts.update(more)

    grads = {k: parts[k][3] for k in parts}
    own_in, far_in = swap(grads[1], core), swap(grads[3], core)
    keep, send = call(
        core_kernel,
        [shape((labels, 2 * width), F32), shape((labels, 2 * width), BF16)],
        [info, grads[0], own_in, grads[2], far_in],
        "core_sum",
    )
    parts[0], parts[1], send = lax.optimization_barrier((parts[0], parts[1], send))
    state = state_chunks((0, 1), info, parts, qs, cs, None, beam, logit_grad, F32)
    received, state = lax.optimization_barrier((swap(send, ax, ay), state))
    keep, send = add_split(keep, received)
    keep, send = add_split(keep, swap(send, ay, az))
    keep, send = add_split(keep, swap(send, az, ax))
    own = add_last(keep, swap(send, azz))
    if reps > GROUP:
        members = [[i * GROUP + j for i in range(reps // GROUP)] for j in range(GROUP)]
        own = lax.psum(own.astype(F32), "rep", axis_index_groups=members).astype(BF16)

    one = swap(own, azz)
    pair = jnp.concatenate([own, one])
    two = swap(pair, az, ay)
    four = swap(jnp.concatenate([pair, two]), ay, az)

    state = state_chunks((2, 3), info, parts, qs, cs, state, beam, logit_grad, BF16)
    label_grad, logits = call(
        functools.partial(join_kernel, blks),
        [shape((labels, 2 * width), F32), shape((docs, blks * labels), F32)],
        [info, own, one, two, four] + [parts[k][2] for k in range(blks)],
        "join",
    )
    return logits, state, label_grad


def solution(mesh):
    reps, blks = mesh.shape["rep"], mesh.shape["blk"]
    assert blks == 4 and reps >= GROUP and reps & (reps - 1) == 0
    in_specs = (
        P(("rep", "blk"), None, None),
        P("blk", None),
        P("blk", None),
        P(("rep", "blk")),
        P(("rep", "blk"), None),
        P(("rep", "blk"), None),
    )
    out_specs = (P(("rep", "blk"), None), P(("rep", "blk"), None, None), P("blk", None))
    return jax.shard_map(
        functools.partial(per_device, reps, blks),
        mesh=mesh, in_specs=in_specs, out_specs=out_specs, check_vma=False,
    )
```

```python
import functools

import jax
import jax.numpy as jnp
from jax import lax
from jax.experimental import pallas as pl
from jax.experimental.pallas import tpu as pltpu
from jax.sharding import PartitionSpec as P

F32 = jnp.float32
BF16 = jnp.bfloat16
VMEM = pl.BlockSpec(memory_space=pltpu.VMEM)
SMEM = pl.BlockSpec(memory_space=pltpu.SMEM)
HBM = pl.BlockSpec(memory_space=pltpu.HBM)
PARAMS = pltpu.CompilerParams(vmem_limit_bytes=24 * 1024 * 1024)
GROUP = 8


def shape(dims, dtype):
    return jax.ShapeDtypeStruct(dims, dtype)


def mm(a, b):
    return jnp.dot(a, b, preferred_element_type=F32)


def cost(products, docs, tokens, width, labels):
    return pl.CostEstimate(
        flops=2 * products * docs * tokens * width * labels,
        transcendentals=docs * tokens * labels,
        bytes_accessed=4 * docs * tokens * width,
    )


def call(kernel, out_shape, ins, name, scratch=(), estimate=None, in_hbm=()):
    single = not isinstance(out_shape, (list, tuple))
    return pl.pallas_call(
        kernel,
        out_shape=out_shape,
        in_specs=[
            SMEM if x.ndim == 1 else HBM if i in in_hbm else VMEM for i, x in enumerate(ins)
        ],
        out_specs=VMEM if single else [VMEM] * len(out_shape),
        scratch_shapes=scratch,
        compiler_params=PARAMS,
        cost_estimate=estimate,
        name=name,
    )(*ins)


def in_hbm(x):
    return pltpu.with_memory_space_constraint(x, pltpu.HBM)


def label_kernel(ks, first, info_ref, lens_ref, *refs):
    if first:
        sources, qc_refs, refs = refs[:5], refs[5 : 3 + 2 * len(ks)], refs[3 + 2 * len(ks) :]
        targets, enct_ref, out_refs, sem = refs[:5], refs[5], refs[6:-1], refs[-1]
        enc_ref, q_ref, c_ref, beam_ref, grad_ref = targets
        qc_refs = (q_ref, c_ref) + tuple(qc_refs)
        docs = enc_ref.shape[0]
        copies = [
            pltpu.make_async_copy(sources[i], targets[i], sem.at[docs + i]) for i in range(1, 5)
        ]
        loads = [
            pltpu.make_async_copy(sources[0].at[d], enc_ref.at[d], sem.at[d]) for d in range(docs)
        ]
        for copy in copies[:2] + loads[:1] + copies[2:] + loads[1:]:
            copy.start()
        for copy in copies:
            copy.wait()
    else:
        enc_ref, enct_ref, refs = refs[0], refs[1], refs[2:]
        qc_refs, refs = refs[: 2 * len(ks)], refs[2 * len(ks) :]
        beam_ref, grad_ref, out_refs = refs[0], refs[1], refs[2:]
    docs, tokens, width = enc_ref.shape
    labels = qc_refs[0].shape[0]
    for n, k in enumerate(ks):
        q_ref, c_ref = qc_refs[2 * n : 2 * n + 2]
        attn_ref, score_ref, logit_ref, out_ref = out_refs[4 * n : 4 * n + 4]
        lanes = pl.ds(pl.multiple_of((info_ref[0] ^ k) * labels, labels), labels)
        gate = grad_ref[:, lanes] * beam_ref[:, lanes].astype(F32)
        qt = q_ref[...].T
        ct = c_ref[...].T.astype(F32)
        token = lax.broadcasted_iota(jnp.int32, (tokens, labels), 0)

        def products(d):
            if first and n == 0:
                loads[d].wait()
                enct_ref[d] = enc_ref[d].T
            enc = enc_ref[d]
            return mm(enc, qt), mm(enc, (ct * gate[d : d + 1, :]).astype(BF16))

        def soften(d, scores, attn_grad):
            expo = jnp.where(token < lens_ref[d], jnp.exp(scores), 0.0)
            attn = expo * (1.0 / jnp.sum(expo, axis=0, keepdims=True))
            attn_b = attn.astype(BF16)
            attn_ref[d] = attn_b
            inner = jnp.sum(attn * attn_grad, axis=0, keepdims=True)
            score_grad = (attn * (attn_grad - inner)).astype(BF16)
            score_ref[d] = score_grad
            return attn_b, score_grad

        query_grad, class_grad = None, None
        ahead = products(0)
        for d in range(docs):
            now = ahead
            if d + 1 < docs:
                ahead = products(d + 1)
            attn_b, score_grad = soften(d, *now)
            enct = enct_ref[d]
            context = mm(enct, attn_b)
            logit_ref[d : d + 1, :] = jnp.sum(context * ct, axis=0, keepdims=True)
            part = context * gate[d : d + 1, :]
            class_grad = part if class_grad is None else class_grad + part
            part = mm(enct, score_grad)
            query_grad = part if query_grad is None else query_grad + part
        query_grad = query_grad.astype(BF16).T
        class_grad = class_grad.astype(BF16).T
        size = labels // GROUP
        for i in range(GROUP):
            rows = pl.ds(pl.multiple_of((info_ref[1] ^ i) * size, size), size)
            out_ref[rows, :width] = query_grad[i * size : (i + 1) * size, :]
            out_ref[rows, width:] = class_grad[i * size : (i + 1) * size, :]


def label_outs(ks, docs, tokens, width, labels):
    return [
        shape((docs, tokens, labels), BF16),
        shape((docs, tokens, labels), BF16),
        shape((docs, labels), F32),
        shape((labels, 2 * width), BF16),
    ] * len(ks)


def label_chunks(ks, info, lens, enc, enct, qs, cs, beam, grad):
    docs, tokens, width = enc.shape
    labels = qs[0].shape[0]
    out_shape = label_outs(ks, docs, tokens, width, labels)
    estimate = cost(4 * len(ks), docs, tokens, width, labels)
    if enct is None:
        ins = [info, lens] + [in_hbm(x) for x in (enc, qs[0], cs[0], beam, grad)]
        own = [shape(x.shape, x.dtype) for x in ins[2:]] + [shape((docs, width, tokens), BF16)]
        for k in ks[1:]:
            ins += [qs[k], cs[k]]
        outs = call(
            functools.partial(label_kernel, ks, True), own + out_shape, ins, "first_labels",
            [pltpu.SemaphoreType.DMA((docs + 5,))], estimate, range(2, 7),
        )
        own, outs = outs[:6], outs[6:]
    else:
        ins = [info, lens, enc, enct]
        for k in ks:
            ins += [qs[k], cs[k]]
        own, outs = None, call(
            functools.partial(label_kernel, ks, False), out_shape, ins + [beam, grad], "labels",
            estimate=estimate,
        )
    return own, {k: tuple(outs[4 * n : 4 * n + 4]) for n, k in enumerate(ks)}


def state_kernel(ks, has_acc, info_ref, *refs):
    beam_ref, grad_ref, refs = refs[0], refs[1], refs[2:]
    ins, out_ref = refs[:-1], refs[-1]
    docs = out_ref.shape[0]
    labels = ins[2].shape[0]
    ctx_grads = [[] for _ in range(docs)]
    for n, k in enumerate(ks):
        lanes = pl.ds(pl.multiple_of((info_ref[0] ^ k) * labels, labels), labels)
        gate = grad_ref[:, lanes] * beam_ref[:, lanes].astype(F32)
        gate = jnp.concatenate([gate, jnp.zeros((128 - docs, labels), F32)], axis=0).T
        c = ins[4 * n + 3][...].astype(F32)
        for d in range(docs):
            ctx_grads[d].append((c * gate[:, d : d + 1]).astype(BF16))
    for d in range(docs):
        total = ins[-1][d] if has_acc else None
        for n in range(len(ks)):
            attn_ref, score_ref, q_ref = ins[4 * n : 4 * n + 3]
            part = mm(attn_ref[d], ctx_grads[d][n]) + mm(score_ref[d], q_ref[...])
            total = part if total is None else total + part
        out_ref[d] = total.astype(out_ref.dtype)


def state_chunks(ks, info, parts, qs, cs, acc, beam, grad, out_dtype):
    docs, tokens, labels = parts[ks[0]][0].shape
    width = qs[0].shape[1]
    ins = [info, beam, grad]
    for k in ks:
        ins += [parts[k][0], parts[k][1], qs[k], cs[k]]
    if acc is not None:
        ins.append(acc)
    return call(
        functools.partial(state_kernel, ks, acc is not None),
        shape((docs, tokens, width), out_dtype), ins, "state_grad",
        estimate=cost(2 * len(ks), docs, tokens, width, labels),
    )


def core_kernel(info_ref, own_ref, own_in_ref, far_ref, far_in_ref, keep_ref, send_ref):
    half = own_ref.shape[0] // 2
    size = half // 4

    def total(a_ref, b_ref, rows):
        return a_ref[rows, :].astype(F32) + b_ref[rows, :].astype(F32)

    @pl.when(info_ref[2] == 0)
    def _():
        rows = pl.ds(0, 2 * half)
        keep_ref[...] = total(own_ref, own_in_ref, rows)
        send_ref[...] = total(far_ref, far_in_ref, rows).astype(BF16)

    @pl.when(info_ref[2] == 1)
    def _():
        for z in range(2):
            for x, (a_ref, b_ref) in enumerate(((own_ref, own_in_ref), (far_ref, far_in_ref))):
                to = pl.ds((2 * z + x) * 2 * size, 2 * size)
                keep_ref[to, :] = total(a_ref, b_ref, pl.ds(2 * z * size, 2 * size))
                send_ref[to, :] = total(a_ref, b_ref, pl.ds(half + 2 * z * size, 2 * size)).astype(BF16)


def add_kernel(keep_ref, in_ref, *out_refs):
    total = keep_ref[...] + in_ref[...].astype(F32)
    if len(out_refs) == 1:
        out_refs[0][...] = total.astype(BF16)
    else:
        half = total.shape[0] // 2
        out_refs[0][...] = total[:half]
        out_refs[1][...] = total[half:].astype(BF16)


def add_split(keep, received):
    rows, cols = keep.shape
    out = [shape((rows // 2, cols), F32), shape((rows // 2, cols), BF16)]
    return call(add_kernel, out, [keep, received], "add_split")


def add_last(keep, received):
    return call(add_kernel, shape(keep.shape, BF16), [keep, received], "add_last")


def join_kernel(chunks, info_ref, pieces_ref, *refs):
    logit_refs, (out_ref, logit_ref) = refs[:chunks], refs[chunks:]
    size = pieces_ref.shape[0] // GROUP
    for r in range(GROUP):
        at = turned(r) * size
        out_ref[at : at + size, :] = pieces_ref[r * size : (r + 1) * size, :].astype(F32)
    labels = logit_refs[0].shape[1]
    for k in range(chunks):
        lanes = pl.ds(pl.multiple_of((info_ref[0] ^ k) * labels, labels), labels)
        logit_ref[:, lanes] = logit_refs[k][...]


def turned(rep):
    return (rep & 1) * 4 + (rep & 2) + ((rep >> 2) & 1)


def per_device(reps, blks, encoded, queries, classifiers, lengths, beam, logit_grad):
    labels, width = queries.shape
    docs = encoded.shape[0]
    total = reps * blks
    blk, rep = lax.axis_index("blk"), lax.axis_index("rep")
    lengths = in_hbm(lengths)
    info = jnp.stack([blk, turned(rep), blk & 1]).astype(jnp.int32)

    def swap(x, mask, odd_mask=None):
        masks = (mask, mask if odd_mask is None else odd_mask)
        return lax.ppermute(x, ("rep", "blk"), [(i, i ^ masks[i & 1]) for i in range(total)])

    core, ax = 1, 2
    ay, az, azz = blks, 2 * blks, 4 * blks

    qs, cs = {0: queries}, {0: classifiers}
    qs[2], cs[2] = swap(queries, ax), swap(classifiers, ax)
    qs[1], cs[1] = swap(queries, core), swap(classifiers, core)

    own, parts = label_chunks((0, 1), info, lengths, encoded, None, qs, cs, beam, logit_grad)
    encoded, qs[0], cs[0], beam, logit_grad, enct = own
    state = state_chunks((0, 1), info, parts, qs, cs, None, beam, logit_grad, F32)
    state, qs[2], cs[2] = lax.optimization_barrier((state, qs[2], cs[2]))
    qs[3], cs[3] = swap(qs[2], core), swap(cs[2], core)
    for k in (3, 2):
        _, more = label_chunks((k,), info, lengths, encoded, enct, qs, cs, beam, logit_grad)
        parts.update(more)

    grads = {k: parts[k][3] for k in parts}
    own_in, far_in = swap(grads[1], core), swap(grads[3], core)
    keep, send = call(
        core_kernel,
        [shape((labels, 2 * width), F32), shape((labels, 2 * width), BF16)],
        [info, grads[0], own_in, grads[2], far_in],
        "core_sum",
    )
    parts[2], parts[3], send = lax.optimization_barrier((parts[2], parts[3], send))
    state = state_chunks((2, 3), info, parts, qs, cs, state, beam, logit_grad, BF16)
    received, state = lax.optimization_barrier((swap(send, ax, ay), state))
    keep, send = add_split(keep, received)
    keep, send = add_split(keep, swap(send, ay, az))
    keep, send = add_split(keep, swap(send, az, ax))
    own = add_last(keep, swap(send, azz))
    groups = None
    if reps > GROUP:
        members = [[i * GROUP + j for i in range(reps // GROUP)] for j in range(GROUP)]
        own = lax.psum(own.astype(F32), "rep", axis_index_groups=members).astype(BF16)
        groups = [[i * GROUP + j for j in range(GROUP)] for i in range(reps // GROUP)]
    pieces = lax.all_gather(own, "rep", axis_index_groups=groups, tiled=True)
    label_grad, logits = call(
        functools.partial(join_kernel, blks),
        [shape((labels, 2 * width), F32), shape((docs, blks * labels), F32)],
        [info, pieces] + [parts[k][2] for k in range(blks)],
        "join",
    )
    return logits, state, label_grad


def solution(mesh):
    reps, blks = mesh.shape["rep"], mesh.shape["blk"]
    assert blks == 4 and reps >= GROUP and reps & (reps - 1) == 0
    in_specs = (
        P(("rep", "blk"), None, None),
        P("blk", None),
        P("blk", None),
        P(("rep", "blk")),
        P(("rep", "blk"), None),
        P(("rep", "blk"), None),
    )
    out_specs = (P(("rep", "blk"), None), P(("rep", "blk"), None, None), P("blk", None))
    return jax.shard_map(
        functools.partial(per_device, reps, blks),
        mesh=mesh, in_specs=in_specs, out_specs=out_specs, check_vma=False,
    )
```

```python
import functools

import jax
import jax.numpy as jnp
from jax import lax
from jax.experimental import pallas as pl
from jax.experimental.pallas import tpu as pltpu
from jax.sharding import PartitionSpec as P

F32 = jnp.float32
BF16 = jnp.bfloat16
VMEM = pl.BlockSpec(memory_space=pltpu.VMEM)
SMEM = pl.BlockSpec(memory_space=pltpu.SMEM)
HBM = pl.BlockSpec(memory_space=pltpu.HBM)
PARAMS = pltpu.CompilerParams(vmem_limit_bytes=20 * 1024 * 1024)
GROUP = 4


def shape(dims, dtype):
    return jax.ShapeDtypeStruct(dims, dtype)


def mm(a, b):
    return jnp.dot(a, b, preferred_element_type=F32)


def cost(products, docs, tokens, width, labels):
    return pl.CostEstimate(
        flops=2 * products * docs * tokens * width * labels,
        transcendentals=docs * tokens * labels,
        bytes_accessed=4 * docs * tokens * width,
    )


def call(kernel, out_shape, ins, name, scratch=(), estimate=None, hbm=0):
    single = not isinstance(out_shape, (list, tuple))
    ins = [pltpu.with_memory_space_constraint(x, pltpu.HBM) for x in ins[:hbm]] + list(ins[hbm:])
    return pl.pallas_call(
        kernel,
        out_shape=out_shape,
        in_specs=[
            HBM if i < hbm else SMEM if x.ndim == 1 else VMEM for i, x in enumerate(ins)
        ],
        out_specs=VMEM if single else [VMEM] * len(out_shape),
        scratch_shapes=scratch,
        compiler_params=PARAMS,
        cost_estimate=estimate,
        name=name,
    )(*ins)


def lanes_of(info_ref, k, labels):
    return pl.ds(pl.multiple_of((info_ref[0] ^ k) * labels, labels), labels)


def label_chunk(docs, q, c, lanes, sums):
    qt = q.T
    ct = c.T.astype(F32)
    labels = q.shape[0]

    def products(doc):
        load, enc_ref, enct_ref, gate_ref = doc[:4]
        load()
        enc = enc_ref[...]
        g = gate_ref[:, lanes]
        return g, mm(enc, qt), mm(enc, (ct * g).astype(BF16))

    query_grad, class_grad = sums
    ahead = products(docs[0])
    for i, (_, _, enct_ref, gate_ref, attn_ref, score_ref, logit_ref) in enumerate(docs):
        g, scores, attn_grad = ahead
        if i + 1 < len(docs):
            ahead = products(docs[i + 1])
        length = gate_ref[:, gate_ref.shape[1] - 128 :][:, :1]
        token = lax.broadcasted_iota(jnp.int32, scores.shape, 0).astype(F32)
        expo = jnp.where(token < length, jnp.exp(scores), 0.0)
        attn = expo * (1.0 / jnp.sum(expo, axis=0, keepdims=True))
        attn_b = attn.astype(BF16)
        attn_ref[...] = attn_b
        inner = jnp.sum(attn * attn_grad, axis=0, keepdims=True)
        score_grad = (attn * (attn_grad - inner)).astype(BF16)
        score_ref[...] = score_grad
        enct = enct_ref[...]
        context = mm(enct, attn_b)
        logit_ref[...] = jnp.sum(context * ct, axis=0, keepdims=True)
        part = context * g
        class_grad = part if class_grad is None else class_grad + part
        part = mm(enct, score_grad)
        query_grad = part if query_grad is None else query_grad + part
    return query_grad, class_grad


def doc_list(loads, enc_ref, enct_ref, gate_ref, attn_ref, score_ref, logit_ref):
    return [
        (loads[d], enc_ref.at[d], enct_ref.at[d], gate_ref.at[d : d + 1], attn_ref.at[d],
         score_ref.at[d], logit_ref.at[d : d + 1])
        for d in range(enc_ref.shape[0])
    ]


def turn_around(enc_ref, enct_ref, copies=None):
    def load(d):
        if copies is not None:
            copies[d].wait()
        enct_ref[d] = enc_ref[d].T

    return [functools.partial(load, d) for d in range(enc_ref.shape[0])]


def own_kernel(enc_in, q_in, c_in, info_ref, gate_ref, enc_ref, q_ref, c_ref, enct_ref,
               attn_ref, score_ref, logit_ref, qsum_ref, csum_ref, sem):
    docs = enc_ref.shape[0]
    label_copies = [
        pltpu.make_async_copy(q_in, q_ref, sem.at[docs]),
        pltpu.make_async_copy(c_in, c_ref, sem.at[docs + 1]),
    ]
    copies = [
        pltpu.make_async_copy(enc_in.at[d], enc_ref.at[d], sem.at[d]) for d in range(docs)
    ]
    for copy in label_copies + copies:
        copy.start()
    for copy in label_copies:
        copy.wait()
    loads = turn_around(enc_ref, enct_ref, copies)
    qsum_ref[...], csum_ref[...] = label_chunk(
        doc_list(loads, enc_ref, enct_ref, gate_ref, attn_ref, score_ref, logit_ref),
        q_ref[...], c_ref[...], lanes_of(info_ref, 0, q_ref.shape[0]), (None, None),
    )


def other_kernel(info_ref, gate_ref, enc_ref, q_ref, c_ref, qsum_ref, csum_ref, enct_ref,
                 attn_ref, score_ref, logit_ref, out_ref):
    width = enc_ref.shape[2]
    query_grad, class_grad = label_chunk(
        doc_list(turn_around(enc_ref, enct_ref), enc_ref, enct_ref, gate_ref, attn_ref,
                 score_ref, logit_ref),
        q_ref[...], c_ref[...], lanes_of(info_ref, 0, q_ref.shape[0]),
        (qsum_ref[...], csum_ref[...]),
    )
    query_grad, class_grad = query_grad.T, class_grad.T
    size = out_ref.shape[0] // GROUP
    for i in range(GROUP):
        to = pl.ds(pl.multiple_of((info_ref[1] ^ i) * size, size), size)
        out_ref[to, :width] = query_grad[i * size : (i + 1) * size, :]
        out_ref[to, width:] = class_grad[i * size : (i + 1) * size, :]


def far_kernel(info_ref, gate_ref, gate2_ref, enc_ref, enc2_ref, enct_ref, enct2_ref, q_ref, c_ref,
               own_ref, attn_ref, score_ref, logit_ref, attn2_ref, score2_ref, logit2_ref,
               keep_ref, send_ref, far_ref):
    docs, _, width = enc_ref.shape
    loads = [lambda: None] * docs
    query_grad, class_grad = label_chunk(
        doc_list(loads, enc_ref, enct_ref, gate_ref, attn_ref, score_ref, logit_ref)
        + doc_list(loads, enc2_ref, enct2_ref, gate2_ref, attn2_ref, score2_ref, logit2_ref),
        q_ref[...], c_ref[...], lanes_of(info_ref, 2, q_ref.shape[0]), (None, None),
    )
    query_grad, class_grad = query_grad.T, class_grad.T
    size = far_ref.shape[0] // GROUP
    for i in range(GROUP):
        to = pl.ds(pl.multiple_of((info_ref[1] ^ i) * size, size), size)
        far_ref[to, :width] = query_grad[i * size : (i + 1) * size, :]
        far_ref[to, width:] = class_grad[i * size : (i + 1) * size, :]

    @pl.when(info_ref[2] == 0)
    def _():
        keep_ref[...] = own_ref[...]
        send_ref[...] = far_ref[...].astype(BF16)

    @pl.when(info_ref[2] == 1)
    def _():
        for z in range(2):
            for x, ref in enumerate((own_ref, far_ref)):
                to = slice((2 * z + x) * size, (2 * z + x + 1) * size)
                keep_ref[to, :] = ref[z * size : (z + 1) * size, :]
                send_ref[to, :] = ref[(2 + z) * size : (3 + z) * size, :].astype(BF16)


def state_kernel(k, info_ref, gate_ref, attn_ref, score_ref, q_ref, c_ref, *refs):
    more, out_ref = refs[:-1], refs[-1]
    docs, labels = out_ref.shape[0], q_ref.shape[0]
    gate = gate_ref[:, lanes_of(info_ref, k, labels)]
    gate = jnp.concatenate([gate, jnp.zeros((128 - docs, labels), F32)], axis=0).T
    c, q = c_ref[...].astype(F32), q_ref[...]
    for d in range(docs):
        ctx_grad = (c * gate[:, d : d + 1]).astype(BF16)
        total = mm(attn_ref[d], ctx_grad) + mm(score_ref[d], q)
        for ref in more:
            total = total + ref[d].astype(F32)
        out_ref[d] = total.astype(out_ref.dtype)


def state_grad(k, info, gate, attn, score, q, c, more, dtype):
    docs, tokens, labels = attn.shape
    width = q.shape[1]
    return call(
        functools.partial(state_kernel, k), shape((docs, tokens, width), dtype),
        [info, gate, attn, score, q, c, *more], "state_grad",
        estimate=cost(2, docs, tokens, width, labels),
    )


def add_kernel(keep_ref, in_ref, *out_refs):
    total = keep_ref[...].astype(F32) + in_ref[...].astype(F32)
    if len(out_refs) == 1:
        out_refs[0][...] = total.astype(BF16)
    else:
        half = total.shape[0] // 2
        out_refs[0][...] = total[:half]
        out_refs[1][...] = total[half:].astype(BF16)


def add_split(keep, received):
    rows, cols = keep.shape
    out = [shape((rows // 2, cols), F32), shape((rows // 2, cols), BF16)]
    return call(add_kernel, out, [keep, received], "add_split")


def add(keep, received):
    return call(add_kernel, shape(keep.shape, BF16), [keep, received], "add")


def join_kernel(info_ref, one_ref, two_ref, four_ref, *refs):
    logit_refs, (out_ref, logit_ref) = refs[:-2], refs[-2:]
    size = one_ref.shape[0]

    def put(ref, at, block):
        rows = pl.ds(pl.multiple_of((info_ref[1] ^ block) * size, size), size)
        out_ref[rows, :] = ref[at * size : (at + 1) * size, :].astype(F32)

    put(one_ref, 0, 0)
    for core, (early, late) in enumerate(((1, 2), (2, 1))):
        @pl.when(info_ref[2] == core)
        def _():
            put(two_ref, 0, early)
            put(four_ref, 0, late)
            put(four_ref, 1, late + early)

    for k, ref in enumerate(logit_refs):
        labels = ref.shape[1]
        logit_ref[:, lanes_of(info_ref, k, labels)] = ref[...]


def per_device(reps, blks, encoded, queries, classifiers, lengths, beam, logit_grad):
    labels, width = queries.shape
    docs, tokens, _ = encoded.shape
    total = reps * blks
    blk, rep = lax.axis_index("blk"), lax.axis_index("rep")
    info = jnp.stack([blk, (rep & 1) * 2 + ((rep >> 1) & 1), blk & 1]).astype(jnp.int32)

    def swap(x, mask, odd_mask=None):
        masks = (mask, mask if odd_mask is None else odd_mask)
        return lax.ppermute(x, ("rep", "blk"), [(i, i ^ masks[i & 1]) for i in range(total)])

    core, ax = 1, 2
    ay, az, azz = blks, 2 * blks, 4 * blks

    far_q, far_c = swap(queries, ax), swap(classifiers, ax)
    gate = jnp.concatenate(
        [
            logit_grad * beam.astype(F32),
            jnp.broadcast_to(lengths.astype(F32)[:, None], (docs, 128)),
        ],
        axis=1,
    )
    gate2, encoded2 = swap(gate, core), swap(encoded, core)

    per_chunk = [
        shape((docs, tokens, labels), BF16),
        shape((docs, tokens, labels), BF16),
        shape((docs, labels), F32),
    ]
    turned = shape((docs, width, tokens), BF16)
    flat = shape((labels, 2 * width), F32)
    sums = [shape((width, labels), F32)] * 2
    estimate = functools.partial(cost, tokens=tokens, width=width, labels=labels)

    enc, q, c, enct, attn, score, logit, *acc = call(
        own_kernel,
        [shape(encoded.shape, BF16)] + [shape(queries.shape, BF16)] * 2 + [turned] + per_chunk + sums,
        [encoded, queries, classifiers, info, gate], "own_labels",
        [pltpu.SemaphoreType.DMA((docs + 2,))], estimate(4, docs), hbm=3,
    )
    state = state_grad(0, info, gate, attn, score, q, c, [], F32)
    state, encoded2 = lax.optimization_barrier((state, encoded2))
    enct2, attn, score, logit_away, near = call(
        other_kernel, [turned] + per_chunk + [flat], [info, gate2, encoded2, q, c, *acc],
        "own_labels_other_docs", estimate=estimate(4, docs),
    )
    state2 = state_grad(0, info, gate2, attn, score, q, c, [], F32)
    state2, far_q, far_c = lax.optimization_barrier((state2, far_q, far_c))
    attn, score, far_logit, attn2, score2, far_logit_away, keep, send = call(
        far_kernel, per_chunk + per_chunk + [flat, shape(flat.shape, BF16)],
        [info, gate, gate2, enc, encoded2, enct, enct2, far_q, far_c, near], "far_labels",
        [pltpu.VMEM(flat.shape, F32)], estimate(4, 2 * docs),
    )

    state2 = state_grad(2, info, gate2, attn2, score2, far_q, far_c, [state2], BF16)
    received, state2 = lax.optimization_barrier((swap(send, ax, ay), state2))
    state_in = swap(state2, core)
    logits_in = swap(jnp.concatenate([logit_away, far_logit_away], axis=1), core)
    keep, send = add_split(keep, received)
    keep, send = add_split(keep, swap(send, ay, az))
    own = add(keep, swap(send, az, ax))
    own = add(own, swap(own, azz))
    if reps > 8:
        members = [[i * 8 + j for i in range(reps // 8)] for j in range(8)]
        own = lax.psum(own.astype(F32), "rep", axis_index_groups=members).astype(BF16)

    two = swap(own, az, ay)
    pair = jnp.concatenate([own, two])
    attn, score, pair = lax.optimization_barrier((attn, score, pair))
    state = state_grad(2, info, gate, attn, score, far_q, far_c, [state, state_in], BF16)
    four, state = lax.optimization_barrier((swap(pair, ay, az), state))
    label_grad, logits = call(
        join_kernel,
        [flat, shape((docs, blks * labels), F32)],
        [info, own, two, four, logit, logits_in[:, :labels], far_logit, logits_in[:, labels:]],
        "join",
    )
    return logits, state, label_grad


def solution(mesh):
    reps, blks = mesh.shape["rep"], mesh.shape["blk"]
    assert blks == 4 and reps >= 8 and reps & (reps - 1) == 0
    in_specs = (
        P(("rep", "blk"), None, None),
        P("blk", None),
        P("blk", None),
        P(("rep", "blk")),
        P(("rep", "blk"), None),
        P(("rep", "blk"), None),
    )
    out_specs = (P(("rep", "blk"), None), P(("rep", "blk"), None, None), P("blk", None))
    return jax.shard_map(
        functools.partial(per_device, reps, blks),
        mesh=mesh, in_specs=in_specs, out_specs=out_specs, check_vma=False,
    )
```

```python
import functools

import jax
import jax.numpy as jnp
from jax import lax
from jax.experimental import pallas as pl
from jax.experimental.pallas import tpu as pltpu
from jax.sharding import PartitionSpec as P

F32 = jnp.float32
BF16 = jnp.bfloat16
VMEM = pl.BlockSpec(memory_space=pltpu.VMEM)
SMEM = pl.BlockSpec(memory_space=pltpu.SMEM)
HBM = pl.BlockSpec(memory_space=pltpu.HBM)
PARAMS = pltpu.CompilerParams(vmem_limit_bytes=20 * 1024 * 1024)
GROUP = 4


def shape(dims, dtype):
    return jax.ShapeDtypeStruct(dims, dtype)


def mm(a, b):
    return jnp.dot(a, b, preferred_element_type=F32)


def cost(products, docs, tokens, width, labels):
    return pl.CostEstimate(
        flops=2 * products * docs * tokens * width * labels,
        transcendentals=docs * tokens * labels,
        bytes_accessed=4 * docs * tokens * width,
    )


def call(kernel, out_shape, ins, name, scratch=(), estimate=None, hbm=0):
    single = not isinstance(out_shape, (list, tuple))
    ins = [pltpu.with_memory_space_constraint(x, pltpu.HBM) for x in ins[:hbm]] + list(ins[hbm:])
    return pl.pallas_call(
        kernel,
        out_shape=out_shape,
        in_specs=[
            HBM if i < hbm else SMEM if x.ndim == 1 else VMEM for i, x in enumerate(ins)
        ],
        out_specs=VMEM if single else [VMEM] * len(out_shape),
        scratch_shapes=scratch,
        compiler_params=PARAMS,
        cost_estimate=estimate,
        name=name,
    )(*ins)


def lanes_of(info_ref, k, labels):
    return pl.ds(pl.multiple_of((info_ref[0] ^ k) * labels, labels), labels)


def label_chunk(docs, q, c, lanes, sums):
    qt = q.T
    ct = c.T.astype(F32)
    labels = q.shape[0]

    def products(doc):
        load, enc_ref, enct_ref, gate_ref = doc[:4]
        load()
        enc = enc_ref[...]
        g = gate_ref[:, lanes]
        return g, mm(enc, qt), mm(enc, (ct * g).astype(BF16))

    query_grad, class_grad = sums
    ahead = products(docs[0])
    for i, (_, _, enct_ref, _, length, attn_ref, score_ref, logit_ref) in enumerate(docs):
        g, scores, attn_grad = ahead
        if i + 1 < len(docs):
            ahead = products(docs[i + 1])
        token = lax.broadcasted_iota(jnp.int32, scores.shape, 0)
        expo = jnp.where(token < length, jnp.exp(scores), 0.0)
        attn = expo * (1.0 / jnp.sum(expo, axis=0, keepdims=True))
        attn_b = attn.astype(BF16)
        attn_ref[...] = attn_b
        inner = jnp.sum(attn * attn_grad, axis=0, keepdims=True)
        score_grad = (attn * (attn_grad - inner)).astype(BF16)
        score_ref[...] = score_grad
        enct = enct_ref[...]
        context = mm(enct, attn_b)
        logit_ref[...] = jnp.sum(context * ct, axis=0, keepdims=True)
        part = context * g
        class_grad = part if class_grad is None else class_grad + part
        part = mm(enct, score_grad)
        query_grad = part if query_grad is None else query_grad + part
    return query_grad, class_grad


def doc_list(loads, enc_ref, enct_ref, gate_ref, lens_ref, attn_ref, score_ref, logit_ref):
    return [
        (loads[d], enc_ref.at[d], enct_ref.at[d], gate_ref.at[d : d + 1], lens_ref[d],
         attn_ref.at[d], score_ref.at[d], logit_ref.at[d : d + 1])
        for d in range(enc_ref.shape[0])
    ]


def turn_around(enc_ref, enct_ref, copies=None):
    def load(d):
        if copies is not None:
            copies[d].wait()
        enct_ref[d] = enc_ref[d].T

    return [functools.partial(load, d) for d in range(enc_ref.shape[0])]


def own_kernel(enc_in, q_in, c_in, beam_in, grad_in, info_ref, lens_ref, enc_ref, q_ref, c_ref,
               gate_ref, enct_ref, attn_ref, score_ref, logit_ref, qsum_ref, csum_ref, beam_ref,
               sem):
    docs = enc_ref.shape[0]
    small = [(q_in, q_ref), (c_in, c_ref), (beam_in, beam_ref), (grad_in, gate_ref)]
    small = [pltpu.make_async_copy(x, y, sem.at[docs + i]) for i, (x, y) in enumerate(small)]
    copies = [
        pltpu.make_async_copy(enc_in.at[d], enc_ref.at[d], sem.at[d]) for d in range(docs)
    ]
    for copy in small + copies:
        copy.start()
    for copy in small:
        copy.wait()
    gate_ref[...] = gate_ref[...] * beam_ref[...].astype(F32)
    loads = turn_around(enc_ref, enct_ref, copies)
    qsum_ref[...], csum_ref[...] = label_chunk(
        doc_list(loads, enc_ref, enct_ref, gate_ref, lens_ref, attn_ref, score_ref, logit_ref),
        q_ref[...], c_ref[...], lanes_of(info_ref, 0, q_ref.shape[0]), (None, None),
    )


def other_kernel(info_ref, lens_ref, beam_ref, grad_ref, enc_ref, q_ref, c_ref, qsum_ref, csum_ref,
                 gate_ref, enct_ref, attn_ref, score_ref, logit_ref, out_ref):
    width = enc_ref.shape[2]
    gate_ref[...] = grad_ref[...] * beam_ref[...].astype(F32)
    query_grad, class_grad = label_chunk(
        doc_list(turn_around(enc_ref, enct_ref), enc_ref, enct_ref, gate_ref, lens_ref,
                 attn_ref, score_ref, logit_ref),
        q_ref[...], c_ref[...], lanes_of(info_ref, 0, q_ref.shape[0]),
        (qsum_ref[...], csum_ref[...]),
    )
    query_grad, class_grad = query_grad.T, class_grad.T
    size = out_ref.shape[0] // GROUP
    for i in range(GROUP):
        to = pl.ds(pl.multiple_of((info_ref[1] ^ i) * size, size), size)
        out_ref[to, :width] = query_grad[i * size : (i + 1) * size, :]
        out_ref[to, width:] = class_grad[i * size : (i + 1) * size, :]


def far_kernel(info_ref, lens_ref, lens2_ref, gate_ref, gate2_ref, enc_ref, enc2_ref, enct_ref, enct2_ref, q_ref, c_ref,
               own_ref, attn_ref, score_ref, logit_ref, attn2_ref, score2_ref, logit2_ref,
               keep_ref, send_ref, far_ref):
    docs, _, width = enc_ref.shape
    loads = [lambda: None] * docs
    query_grad, class_grad = label_chunk(
        doc_list(loads, enc_ref, enct_ref, gate_ref, lens_ref, attn_ref, score_ref, logit_ref)
        + doc_list(loads, enc2_ref, enct2_ref, gate2_ref, lens2_ref, attn2_ref, score2_ref,
                   logit2_ref),
        q_ref[...], c_ref[...], lanes_of(info_ref, 2, q_ref.shape[0]), (None, None),
    )
    query_grad, class_grad = query_grad.T, class_grad.T
    size = far_ref.shape[0] // GROUP
    for i in range(GROUP):
        to = pl.ds(pl.multiple_of((info_ref[1] ^ i) * size, size), size)
        far_ref[to, :width] = query_grad[i * size : (i + 1) * size, :]
        far_ref[to, width:] = class_grad[i * size : (i + 1) * size, :]

    @pl.when(info_ref[2] == 0)
    def _():
        keep_ref[...] = own_ref[...]
        send_ref[...] = far_ref[...].astype(BF16)

    @pl.when(info_ref[2] == 1)
    def _():
        for z in range(2):
            for x, ref in enumerate((own_ref, far_ref)):
                to = slice((2 * z + x) * size, (2 * z + x + 1) * size)
                keep_ref[to, :] = ref[z * size : (z + 1) * size, :]
                send_ref[to, :] = ref[(2 + z) * size : (3 + z) * size, :].astype(BF16)


def state_kernel(ks, info_ref, gate_ref, *refs):
    chunks, more, out_ref = refs[: 4 * len(ks)], refs[4 * len(ks) : -1], refs[-1]
    docs = out_ref.shape[0]
    ctx_grads = []
    for n, k in enumerate(ks):
        c_ref = chunks[4 * n + 3]
        labels = c_ref.shape[0]
        gate = gate_ref[:, lanes_of(info_ref, k, labels)]
        gate = jnp.concatenate([gate, jnp.zeros((128 - docs, labels), F32)], axis=0).T
        c = c_ref[...].astype(F32)
        ctx_grads.append([(c * gate[:, d : d + 1]).astype(BF16) for d in range(docs)])
    for d in range(docs):
        total = None
        for n in range(len(ks)):
            attn_ref, score_ref, q_ref = chunks[4 * n : 4 * n + 3]
            part = mm(attn_ref[d], ctx_grads[n][d]) + mm(score_ref[d], q_ref[...])
            total = part if total is None else total + part
        for ref in more:
            total = total + ref[d].astype(F32)
        out_ref[d] = total.astype(out_ref.dtype)


def state_grad(info, gate, parts, more):
    docs, tokens, labels = parts[0][0].shape
    width = parts[0][2].shape[1]
    return call(
        functools.partial(state_kernel, (0, 2)), shape((docs, tokens, width), BF16),
        [info, gate, *parts[0], *parts[1], *more], "state_grad",
        estimate=cost(4, docs, tokens, width, labels),
    )


def add_kernel(keep_ref, in_ref, *out_refs):
    total = keep_ref[...].astype(F32) + in_ref[...].astype(F32)
    if len(out_refs) == 1:
        out_refs[0][...] = total.astype(BF16)
    else:
        half = total.shape[0] // 2
        out_refs[0][...] = total[:half]
        out_refs[1][...] = total[half:].astype(BF16)


def add_split(keep, received):
    rows, cols = keep.shape
    out = [shape((rows // 2, cols), F32), shape((rows // 2, cols), BF16)]
    return call(add_kernel, out, [keep, received], "add_split")


def add(keep, received):
    return call(add_kernel, shape(keep.shape, BF16), [keep, received], "add")


def put(info_ref, out_ref, ref, at, block):
    size = out_ref.shape[0] // GROUP
    rows = pl.ds(pl.multiple_of((info_ref[1] ^ block) * size, size), size)
    out_ref[rows, :] = ref[at * size : (at + 1) * size, :].astype(F32)


def early_kernel(info_ref, one_ref, two_ref, *refs):
    logit_refs, (out_ref, logit_ref) = refs[:-2], refs[-2:]
    put(info_ref, out_ref, one_ref, 0, 0)
    for core, near in enumerate((1, 2)):
        @pl.when(info_ref[2] == core)
        def _():
            put(info_ref, out_ref, two_ref, 0, near)

    for k, ref in enumerate(logit_refs):
        labels = ref.shape[1]
        logit_ref[:, lanes_of(info_ref, k, labels)] = ref[...]


def late_kernel(info_ref, four_ref, early_ref, out_ref, rows_ref, sem):
    del early_ref
    size = four_ref.shape[0] // 2
    rows_ref[...] = four_ref[...].astype(F32)
    far = 2 - info_ref[2]
    copies = []
    for at, block in enumerate((far, 3)):
        to = pl.ds(pl.multiple_of((info_ref[1] ^ block) * size, size), size)
        copies.append(
            pltpu.make_async_copy(rows_ref.at[pl.ds(at * size, size)], out_ref.at[to], sem.at[at])
        )
    for copy in copies:
        copy.start()
    for copy in copies:
        copy.wait()


def late_rows(info, four, early):
    return pl.pallas_call(
        late_kernel,
        out_shape=shape(early.shape, early.dtype),
        in_specs=[SMEM, VMEM, pl.BlockSpec(memory_space=pl.ANY)],
        out_specs=pl.BlockSpec(memory_space=pl.ANY),
        scratch_shapes=[pltpu.VMEM(four.shape, F32), pltpu.SemaphoreType.DMA((2,))],
        input_output_aliases={2: 0},
        compiler_params=PARAMS,
        name="late_rows",
    )(info, four, early)


def per_device(reps, blks, encoded, queries, classifiers, lengths, beam, logit_grad):
    labels, width = queries.shape
    docs, tokens, _ = encoded.shape
    total = reps * blks
    blk, rep = lax.axis_index("blk"), lax.axis_index("rep")
    info = jnp.stack([blk, (rep & 1) * 2 + ((rep >> 1) & 1), blk & 1]).astype(jnp.int32)

    def swap(x, mask, odd_mask=None):
        masks = (mask, mask if odd_mask is None else odd_mask)
        return lax.ppermute(x, ("rep", "blk"), [(i, i ^ masks[i & 1]) for i in range(total)])

    core, ax = 1, 2
    ay, az, azz = blks, 2 * blks, 4 * blks

    far_q, far_c = swap(queries, ax), swap(classifiers, ax)
    encoded2, beam2, grad2 = swap(encoded, core), swap(beam, core), swap(logit_grad, core)
    lengths2 = swap(lengths, core)
    lengths = pltpu.with_memory_space_constraint(lengths, pltpu.HBM)

    per_chunk = [
        shape((docs, tokens, labels), BF16),
        shape((docs, tokens, labels), BF16),
        shape((docs, labels), F32),
    ]
    gates = shape(beam.shape, F32)
    turned = shape((docs, width, tokens), BF16)
    flat = shape((labels, 2 * width), F32)
    sums = [shape((width, labels), F32)] * 2
    estimate = functools.partial(cost, tokens=tokens, width=width, labels=labels)

    enc, q, c, gate, enct, attn, score, logit, *acc = call(
        own_kernel,
        [shape(encoded.shape, BF16)] + [shape(queries.shape, BF16)] * 2 + [gates, turned]
        + per_chunk + sums,
        [encoded, queries, classifiers, beam, logit_grad, info, lengths], "own_labels",
        [pltpu.VMEM(beam.shape, jnp.int32), pltpu.SemaphoreType.DMA((docs + 4,))],
        estimate(4, docs), hbm=5,
    )
    gate2, enct2, attn2, score2, logit_away, near = call(
        other_kernel, [gates, turned] + per_chunk + [flat],
        [info, lengths2, beam2, grad2, encoded2, q, c, *acc], "own_labels_other_docs",
        estimate=estimate(4, docs),
    )
    near, far_q, far_c = lax.optimization_barrier((near, far_q, far_c))
    far_attn, far_score, far_logit, far_attn2, far_score2, far_logit_away, keep, send = call(
        far_kernel, per_chunk + per_chunk + [flat, shape(flat.shape, BF16)],
        [info, lengths, lengths2, gate, gate2, enc, encoded2, enct, enct2, far_q, far_c, near],
        "far_labels", [pltpu.VMEM(flat.shape, F32)], estimate(4, 2 * docs),
    )

    state2 = state_grad(
        info, gate2, [(attn2, score2, q, c), (far_attn2, far_score2, far_q, far_c)], []
    )
    received, state2 = lax.optimization_barrier((swap(send, ax, ay), state2))
    state_in = swap(state2, core)
    logits_in = swap(jnp.concatenate([logit_away, far_logit_away], axis=1), core)
    keep, send = add_split(keep, received)
    keep, send = add_split(keep, swap(send, ay, az))
    own = add(keep, swap(send, az, ax))
    far_attn, far_score, own, logits_in = lax.optimization_barrier(
        (far_attn, far_score, own, logits_in)
    )
    state = state_grad(
        info, gate, [(attn, score, q, c), (far_attn, far_score, far_q, far_c)], [state_in]
    )
    received, state = lax.optimization_barrier((swap(own, azz), state))
    own = add(own, received)
    if reps > 8:
        members = [[i * 8 + j for i in range(reps // 8)] for j in range(8)]
        own = lax.psum(own.astype(F32), "rep", axis_index_groups=members).astype(BF16)

    two = swap(own, az, ay)
    pair = jnp.concatenate([own, two])
    own, pair = lax.optimization_barrier((own, pair))
    early, logits = call(
        early_kernel,
        [flat, shape((docs, blks * labels), F32)],
        [info, own, two, logit, logits_in[:, :labels], far_logit, logits_in[:, labels:]],
        "early_rows",
    )
    four, early = lax.optimization_barrier((swap(pair, ay, az), early))
    label_grad = late_rows(info, four, early)
    return logits, state, label_grad


def solution(mesh):
    reps, blks = mesh.shape["rep"], mesh.shape["blk"]
    assert blks == 4 and reps >= 8 and reps & (reps - 1) == 0
    in_specs = (
        P(("rep", "blk"), None, None),
        P("blk", None),
        P("blk", None),
        P(("rep", "blk")),
        P(("rep", "blk"), None),
        P(("rep", "blk"), None),
    )
    out_specs = (P(("rep", "blk"), None), P(("rep", "blk"), None, None), P("blk", None))
    return jax.shard_map(
        functools.partial(per_device, reps, blks),
        mesh=mesh, in_specs=in_specs, out_specs=out_specs, check_vma=False,
    )
```

```python
import functools

import jax
import jax.numpy as jnp
from jax import lax
from jax.experimental import pallas as pl
from jax.experimental.pallas import tpu as pltpu
from jax.sharding import PartitionSpec as P

F32 = jnp.float32
BF16 = jnp.bfloat16
VMEM = pl.BlockSpec(memory_space=pltpu.VMEM)
SMEM = pl.BlockSpec(memory_space=pltpu.SMEM)
HBM = pl.BlockSpec(memory_space=pltpu.HBM)
PARAMS = pltpu.CompilerParams(vmem_limit_bytes=20 * 1024 * 1024)
GROUP = 4


def shape(dims, dtype):
    return jax.ShapeDtypeStruct(dims, dtype)


def mm(a, b):
    return jnp.dot(a, b, preferred_element_type=F32)


def cost(products, docs, tokens, width, labels):
    return pl.CostEstimate(
        flops=2 * products * docs * tokens * width * labels,
        transcendentals=docs * tokens * labels,
        bytes_accessed=4 * docs * tokens * width,
    )


def call(kernel, out_shape, ins, name, scratch=(), estimate=None, hbm=0):
    single = not isinstance(out_shape, (list, tuple))
    ins = [pltpu.with_memory_space_constraint(x, pltpu.HBM) for x in ins[:hbm]] + list(ins[hbm:])
    return pl.pallas_call(
        kernel,
        out_shape=out_shape,
        in_specs=[
            HBM if i < hbm else SMEM if x.ndim == 1 else VMEM for i, x in enumerate(ins)
        ],
        out_specs=VMEM if single else [VMEM] * len(out_shape),
        scratch_shapes=scratch,
        compiler_params=PARAMS,
        cost_estimate=estimate,
        name=name,
    )(*ins)


def lanes_of(info_ref, k, labels):
    return pl.ds(pl.multiple_of((info_ref[0] ^ k) * labels, labels), labels)


def label_chunk(docs, q, c, lanes, sums):
    qt = q.T
    ct = c.T.astype(F32)
    labels = q.shape[0]

    def products(doc):
        load, enc_ref, enct_ref, gate_ref = doc[:4]
        load()
        enc = enc_ref[...]
        g = gate_ref[:, lanes]
        return g, mm(enc, qt), mm(enc, (ct * g).astype(BF16))

    query_grad, class_grad = sums
    ahead = products(docs[0])
    for i, (_, _, enct_ref, _, length, attn_ref, score_ref, logit_ref) in enumerate(docs):
        g, scores, attn_grad = ahead
        if i + 1 < len(docs):
            ahead = products(docs[i + 1])
        token = lax.broadcasted_iota(jnp.int32, scores.shape, 0)
        expo = jnp.where(token < length, jnp.exp(scores), 0.0)
        attn = expo * (1.0 / jnp.sum(expo, axis=0, keepdims=True))
        attn_b = attn.astype(BF16)
        attn_ref[...] = attn_b
        inner = jnp.sum(attn * attn_grad, axis=0, keepdims=True)
        score_grad = (attn * (attn_grad - inner)).astype(BF16)
        score_ref[...] = score_grad
        enct = enct_ref[...]
        context = mm(enct, attn_b)
        logit_ref[...] = jnp.sum(context * ct, axis=0, keepdims=True)
        part = context * g
        class_grad = part if class_grad is None else class_grad + part
        part = mm(enct, score_grad)
        query_grad = part if query_grad is None else query_grad + part
    return query_grad, class_grad


def doc_list(loads, enc_ref, enct_ref, gate_ref, lens_ref, attn_ref, score_ref, logit_ref):
    return [
        (loads[d], enc_ref.at[d], enct_ref.at[d], gate_ref.at[d : d + 1], lens_ref[d],
         attn_ref.at[d], score_ref.at[d], logit_ref.at[d : d + 1])
        for d in range(enc_ref.shape[0])
    ]


def turn_around(enc_ref, enct_ref, copies=None):
    def load(d):
        if copies is not None:
            copies[d].wait()
        enct_ref[d] = enc_ref[d].T

    return [functools.partial(load, d) for d in range(enc_ref.shape[0])]


def pack_kernel(q_in, c_in, qc_ref, sem):
    copies = [pltpu.make_async_copy(x, qc_ref.at[i], sem.at[i]) for i, x in enumerate((q_in, c_in))]
    for copy in copies:
        copy.start()
    for copy in copies:
        copy.wait()


def own_kernel(enc_in, beam_in, grad_in, info_ref, lens_ref, qc_ref, enc_ref, gate_ref, enct_ref,
               attn_ref, score_ref, logit_ref, qsum_ref, csum_ref, beam_ref, sem):
    docs = enc_ref.shape[0]
    small = [(beam_in, beam_ref), (grad_in, gate_ref)]
    small = [pltpu.make_async_copy(x, y, sem.at[docs + i]) for i, (x, y) in enumerate(small)]
    copies = [
        pltpu.make_async_copy(enc_in.at[d], enc_ref.at[d], sem.at[d]) for d in range(docs)
    ]
    for copy in small + copies:
        copy.start()
    for copy in small:
        copy.wait()
    gate_ref[...] = gate_ref[...] * beam_ref[...].astype(F32)
    loads = turn_around(enc_ref, enct_ref, copies)
    qsum_ref[...], csum_ref[...] = label_chunk(
        doc_list(loads, enc_ref, enct_ref, gate_ref, lens_ref, attn_ref, score_ref, logit_ref),
        qc_ref[0], qc_ref[1], lanes_of(info_ref, 0, qc_ref.shape[1]), (None, None),
    )


def other_kernel(info_ref, lens_ref, beam_ref, grad_ref, enc_ref, qc_ref, qsum_ref, csum_ref,
                 gate_ref, enct_ref, attn_ref, score_ref, logit_ref, out_ref):
    width = enc_ref.shape[2]
    gate_ref[...] = grad_ref[...] * beam_ref[...].astype(F32)
    query_grad, class_grad = label_chunk(
        doc_list(turn_around(enc_ref, enct_ref), enc_ref, enct_ref, gate_ref, lens_ref,
                 attn_ref, score_ref, logit_ref),
        qc_ref[0], qc_ref[1], lanes_of(info_ref, 0, qc_ref.shape[1]),
        (qsum_ref[...], csum_ref[...]),
    )
    query_grad, class_grad = query_grad.T, class_grad.T
    size = out_ref.shape[0] // GROUP
    for i in range(GROUP):
        to = pl.ds(pl.multiple_of((info_ref[1] ^ i) * size, size), size)
        out_ref[to, :width] = query_grad[i * size : (i + 1) * size, :]
        out_ref[to, width:] = class_grad[i * size : (i + 1) * size, :]


def far_kernel(info_ref, lens_ref, lens2_ref, gate_ref, gate2_ref, enc_ref, enc2_ref, enct_ref, enct2_ref, qc_ref,
               own_ref, attn_ref, score_ref, logit_ref, attn2_ref, score2_ref, logit2_ref,
               keep_ref, send_ref, far_ref):
    docs, _, width = enc_ref.shape
    loads = [lambda: None] * docs
    query_grad, class_grad = label_chunk(
        doc_list(loads, enc_ref, enct_ref, gate_ref, lens_ref, attn_ref, score_ref, logit_ref)
        + doc_list(loads, enc2_ref, enct2_ref, gate2_ref, lens2_ref, attn2_ref, score2_ref,
                   logit2_ref),
        qc_ref[0], qc_ref[1], lanes_of(info_ref, 2, qc_ref.shape[1]), (None, None),
    )
    query_grad, class_grad = query_grad.T, class_grad.T
    size = far_ref.shape[0] // GROUP
    for i in range(GROUP):
        to = pl.ds(pl.multiple_of((info_ref[1] ^ i) * size, size), size)
        far_ref[to, :width] = query_grad[i * size : (i + 1) * size, :]
        far_ref[to, width:] = class_grad[i * size : (i + 1) * size, :]

    @pl.when(info_ref[2] == 0)
    def _():
        keep_ref[...] = own_ref[...]
        send_ref[...] = far_ref[...].astype(BF16)

    @pl.when(info_ref[2] == 1)
    def _():
        for z in range(2):
            for x, ref in enumerate((own_ref, far_ref)):
                to = slice((2 * z + x) * size, (2 * z + x + 1) * size)
                keep_ref[to, :] = ref[z * size : (z + 1) * size, :]
                send_ref[to, :] = ref[(2 + z) * size : (3 + z) * size, :].astype(BF16)


def state_kernel(ks, info_ref, gate_ref, *refs):
    chunks, more, out_ref = refs[: 3 * len(ks)], refs[3 * len(ks) : -1], refs[-1]
    docs = out_ref.shape[0]
    ctx_grads = []
    for n, k in enumerate(ks):
        qc_ref = chunks[3 * n + 2]
        labels = qc_ref.shape[1]
        gate = gate_ref[:, lanes_of(info_ref, k, labels)]
        gate = jnp.concatenate([gate, jnp.zeros((128 - docs, labels), F32)], axis=0).T
        c = qc_ref[1].astype(F32)
        ctx_grads.append([(c * gate[:, d : d + 1]).astype(BF16) for d in range(docs)])
    for d in range(docs):
        total = None
        for n in range(len(ks)):
            attn_ref, score_ref, qc_ref = chunks[3 * n : 3 * n + 3]
            part = mm(attn_ref[d], ctx_grads[n][d]) + mm(score_ref[d], qc_ref[0])
            total = part if total is None else total + part
        for ref in more:
            total = total + ref[d].astype(F32)
        out_ref[d] = total.astype(out_ref.dtype)


def state_grad(info, gate, parts, more):
    docs, tokens, labels = parts[0][0].shape
    width = parts[0][2].shape[2]
    return call(
        functools.partial(state_kernel, (0, 2)), shape((docs, tokens, width), BF16),
        [info, gate, *parts[0], *parts[1], *more], "state_grad",
        estimate=cost(4, docs, tokens, width, labels),
    )


def split_kernel(keep_ref, in_ref, *out_refs):
    total = keep_ref[...] + in_ref[...].astype(F32)
    size = out_refs[0].shape[0]
    for i, ref in enumerate(out_refs):
        ref[...] = total[i * size : (i + 1) * size].astype(ref.dtype)


def add_kernel(*refs):
    total = refs[0][...].astype(F32)
    for ref in refs[1:-1]:
        total = total + ref[...].astype(F32)
    refs[-1][...] = total.astype(BF16)


def add_split(keep, received):
    rows, cols = keep.shape
    out = [shape((rows // 4, cols), F32)] + [shape((rows // 4, cols), BF16)] * 3
    return call(split_kernel, out, [keep, received], "add_split")


def add(*arrays):
    return call(add_kernel, shape(arrays[0].shape, BF16), arrays, "add")


def early_kernel(info_ref, own_ref, first_ref, *refs):
    logit_refs, (out_ref, logit_ref) = refs[:-2], refs[-2:]
    size = own_ref.shape[0]
    for block, ref in enumerate((own_ref, first_ref)):
        rows = pl.ds(pl.multiple_of((info_ref[1] ^ block) * size, size), size)
        out_ref[rows, :] = ref[...].astype(F32)
    for k, ref in enumerate(logit_refs):
        labels = ref.shape[1]
        logit_ref[:, lanes_of(info_ref, k, labels)] = ref[...]


def late_kernel(info_ref, two_ref, three_ref, early_ref, out_ref, rows_ref, sem):
    del early_ref
    size = two_ref.shape[0]
    copies = []
    for i, ref in enumerate((two_ref, three_ref)):
        rows_ref[i] = ref[...].astype(F32)
        to = pl.ds(pl.multiple_of((info_ref[1] ^ (2 + i)) * size, size), size)
        copies.append(pltpu.make_async_copy(rows_ref.at[i], out_ref.at[to], sem.at[i]))
        copies[-1].start()
    for copy in copies:
        copy.wait()


def late_rows(info, two, three, early):
    return pl.pallas_call(
        late_kernel,
        out_shape=shape(early.shape, early.dtype),
        in_specs=[SMEM, VMEM, VMEM, pl.BlockSpec(memory_space=pl.ANY)],
        out_specs=pl.BlockSpec(memory_space=pl.ANY),
        scratch_shapes=[pltpu.VMEM((2, *two.shape), F32), pltpu.SemaphoreType.DMA((2,))],
        input_output_aliases={3: 0},
        compiler_params=PARAMS,
        name="late_rows",
    )(info, two, three, early)


def per_device(reps, blks, encoded, queries, classifiers, lengths, beam, logit_grad):
    labels, width = queries.shape
    docs, tokens, _ = encoded.shape
    total = reps * blks
    blk, rep = lax.axis_index("blk"), lax.axis_index("rep")
    info = jnp.stack([blk, (rep & 1) * 2 + ((rep >> 1) & 1), blk & 1]).astype(jnp.int32)

    def swap(x, mask, odd_mask=None):
        masks = (mask, mask if odd_mask is None else odd_mask)
        return lax.ppermute(x, ("rep", "blk"), [(i, i ^ masks[i & 1]) for i in range(total)])

    core, ax = 1, 2
    ay, az, azz = blks, 2 * blks, 4 * blks

    qc = call(
        pack_kernel, shape((2, labels, width), BF16), [queries, classifiers], "pack",
        [pltpu.SemaphoreType.DMA((2,))], hbm=2,
    )
    far_qc = swap(qc, ax)
    encoded2, beam2, grad2 = swap(encoded, core), swap(beam, core), swap(logit_grad, core)
    lengths2 = swap(lengths, core)
    lengths = pltpu.with_memory_space_constraint(lengths, pltpu.HBM)

    per_chunk = [
        shape((docs, tokens, labels), BF16),
        shape((docs, tokens, labels), BF16),
        shape((docs, labels), F32),
    ]
    gates = shape(beam.shape, F32)
    turned = shape((docs, width, tokens), BF16)
    flat = shape((labels, 2 * width), F32)
    sums = [shape((width, labels), F32)] * 2
    estimate = functools.partial(cost, tokens=tokens, width=width, labels=labels)

    enc, gate, enct, attn, score, logit, *acc = call(
        own_kernel,
        [shape(encoded.shape, BF16), gates, turned] + per_chunk + sums,
        [encoded, beam, logit_grad, info, lengths, qc], "own_labels",
        [pltpu.VMEM(beam.shape, jnp.int32), pltpu.SemaphoreType.DMA((docs + 2,))],
        estimate(4, docs), hbm=3,
    )
    gate2, enct2, attn2, score2, logit_away, near = call(
        other_kernel, [gates, turned] + per_chunk + [flat],
        [info, lengths2, beam2, grad2, encoded2, qc, *acc], "own_labels_other_docs",
        estimate=estimate(4, docs),
    )
    near, far_qc = lax.optimization_barrier((near, far_qc))
    far_attn, far_score, far_logit, far_attn2, far_score2, far_logit_away, keep, send = call(
        far_kernel, per_chunk + per_chunk + [flat, shape(flat.shape, BF16)],
        [info, lengths, lengths2, gate, gate2, enc, encoded2, enct, enct2, far_qc, near],
        "far_labels", [pltpu.VMEM(flat.shape, F32)], estimate(4, 2 * docs),
    )

    state2 = state_grad(
        info, gate2, [(attn2, score2, qc), (far_attn2, far_score2, far_qc)], []
    )
    received, state2 = lax.optimization_barrier((swap(send, ax, ay), state2))
    state_in = swap(state2, core)
    logits_in = swap(jnp.concatenate([logit_away, far_logit_away], axis=1), core)
    keep, one, two, three = add_split(keep, received)
    own = add(keep, swap(two, ay, az), swap(three, ay | az, az | ax), swap(one, az, ax))
    far_attn, far_score, own, logits_in = lax.optimization_barrier(
        (far_attn, far_score, own, logits_in)
    )
    state = state_grad(
        info, gate, [(attn, score, qc), (far_attn, far_score, far_qc)], [state_in]
    )
    received, state = lax.optimization_barrier((swap(own, azz), state))
    own = add(own, received)
    if reps > 8:
        members = [[i * 8 + j for i in range(reps // 8)] for j in range(8)]
        own = lax.psum(own.astype(F32), "rep", axis_index_groups=members).astype(BF16)

    one, three, two = swap(own, az), swap(own, ay | az), swap(own, ay)
    early, logits = call(
        early_kernel,
        [flat, shape((docs, blks * labels), F32)],
        [info, own, one, logit, logits_in[:, :labels], far_logit, logits_in[:, labels:]],
        "early_rows",
    )
    early, two, three = lax.optimization_barrier((early, two, three))
    label_grad = late_rows(info, two, three, early)
    return logits, state, label_grad


def solution(mesh):
    reps, blks = mesh.shape["rep"], mesh.shape["blk"]
    assert blks == 4 and reps >= 8 and reps & (reps - 1) == 0
    in_specs = (
        P(("rep", "blk"), None, None),
        P("blk", None),
        P("blk", None),
        P(("rep", "blk")),
        P(("rep", "blk"), None),
        P(("rep", "blk"), None),
    )
    out_specs = (P(("rep", "blk"), None), P(("rep", "blk"), None, None), P("blk", None))
    return jax.shard_map(
        functools.partial(per_device, reps, blks),
        mesh=mesh, in_specs=in_specs, out_specs=out_specs, check_vma=False,
    )
```

```python
import functools

import jax
import jax.numpy as jnp
from jax import lax
from jax.experimental import pallas as pl
from jax.experimental.pallas import tpu as pltpu
from jax.sharding import PartitionSpec as P

F32 = jnp.float32
BF16 = jnp.bfloat16
VMEM = pl.BlockSpec(memory_space=pltpu.VMEM)
SMEM = pl.BlockSpec(memory_space=pltpu.SMEM)
HBM = pl.BlockSpec(memory_space=pltpu.HBM)
PARAMS = pltpu.CompilerParams(vmem_limit_bytes=20 * 1024 * 1024)
GROUP = 4


def shape(dims, dtype):
    return jax.ShapeDtypeStruct(dims, dtype)


def mm(a, b):
    return jnp.dot(a, b, preferred_element_type=F32)


def cost(products, docs, tokens, width, labels):
    return pl.CostEstimate(
        flops=2 * products * docs * tokens * width * labels,
        transcendentals=docs * tokens * labels,
        bytes_accessed=4 * docs * tokens * width,
    )


def call(kernel, out_shape, ins, name, scratch=(), estimate=None, hbm=0):
    single = not isinstance(out_shape, (list, tuple))
    ins = [pltpu.with_memory_space_constraint(x, pltpu.HBM) for x in ins[:hbm]] + list(ins[hbm:])
    return pl.pallas_call(
        kernel,
        out_shape=out_shape,
        in_specs=[
            HBM if i < hbm else SMEM if x.ndim == 1 else VMEM for i, x in enumerate(ins)
        ],
        out_specs=VMEM if single else [VMEM] * len(out_shape),
        scratch_shapes=scratch,
        compiler_params=PARAMS,
        cost_estimate=estimate,
        name=name,
    )(*ins)


def lanes_of(info_ref, k, labels):
    return pl.ds(pl.multiple_of((info_ref[0] ^ k) * labels, labels), labels)


def label_chunk(docs, q, c, lanes, sums):
    qt = q.T
    ct = c.T.astype(F32)
    labels = q.shape[0]

    def products(doc):
        load, enc_ref, enct_ref, gate_ref = doc[:4]
        load()
        enc = enc_ref[...]
        g = gate_ref[:, lanes]
        return g, mm(enc, qt), mm(enc, (ct * g).astype(BF16))

    query_grad, class_grad = sums
    ahead = products(docs[0])
    for i, (_, _, enct_ref, _, length, attn_ref, score_ref, logit_ref) in enumerate(docs):
        g, scores, attn_grad = ahead
        if i + 1 < len(docs):
            ahead = products(docs[i + 1])
        token = lax.broadcasted_iota(jnp.int32, scores.shape, 0)
        expo = jnp.where(token < length, jnp.exp(scores), 0.0)
        attn = expo * (1.0 / jnp.sum(expo, axis=0, keepdims=True))
        attn_b = attn.astype(BF16)
        attn_ref[...] = attn_b
        inner = jnp.sum(attn * attn_grad, axis=0, keepdims=True)
        score_grad = (attn * (attn_grad - inner)).astype(BF16)
        score_ref[...] = score_grad
        enct = enct_ref[...]
        context = mm(enct, attn_b)
        logit_ref[...] = jnp.sum(context * ct, axis=0, keepdims=True)
        part = context * g
        class_grad = part if class_grad is None else class_grad + part
        part = mm(enct, score_grad)
        query_grad = part if query_grad is None else query_grad + part
    return query_grad, class_grad


def doc_list(loads, enc_ref, enct_ref, gate_ref, lens_ref, attn_ref, score_ref, logit_ref):
    return [
        (loads[d], enc_ref.at[d], enct_ref.at[d], gate_ref.at[d : d + 1], lens_ref[d],
         attn_ref.at[d], score_ref.at[d], logit_ref.at[d : d + 1])
        for d in range(enc_ref.shape[0])
    ]


def turn_around(enc_ref, enct_ref, copies=None):
    def load(d):
        if copies is not None:
            copies[d].wait()
        enct_ref[d] = enc_ref[d].T

    return [functools.partial(load, d) for d in range(enc_ref.shape[0])]


def pack_kernel(q_in, c_in, qc_ref, sem):
    copies = [pltpu.make_async_copy(x, qc_ref.at[i], sem.at[i]) for i, x in enumerate((q_in, c_in))]
    for copy in copies:
        copy.start()
    for copy in copies:
        copy.wait()


def own_kernel(enc_in, beam_in, grad_in, info_ref, lens_ref, qc_ref, enc_ref, gate_ref, enct_ref,
               attn_ref, score_ref, logit_ref, qsum_ref, csum_ref, beam_ref, sem):
    docs = enc_ref.shape[0]
    small = [(beam_in, beam_ref), (grad_in, gate_ref)]
    small = [pltpu.make_async_copy(x, y, sem.at[docs + i]) for i, (x, y) in enumerate(small)]
    copies = [
        pltpu.make_async_copy(enc_in.at[d], enc_ref.at[d], sem.at[d]) for d in range(docs)
    ]
    for copy in copies[:1] + small + copies[1:]:
        copy.start()
    loads = turn_around(enc_ref, enct_ref, copies)

    def first_load():
        load()
        for copy in small:
            copy.wait()
        gate_ref[...] = gate_ref[...] * beam_ref[...].astype(F32)

    load, loads[0] = loads[0], first_load
    qsum_ref[...], csum_ref[...] = label_chunk(
        doc_list(loads, enc_ref, enct_ref, gate_ref, lens_ref, attn_ref, score_ref, logit_ref),
        qc_ref[0], qc_ref[1], lanes_of(info_ref, 0, qc_ref.shape[1]), (None, None),
    )


def to_blocks(info_ref, sums, rows_ref, out_refs):
    query_grad, class_grad = sums
    width = query_grad.shape[0]
    rows_ref[:, :width] = query_grad.T
    rows_ref[:, width:] = class_grad.T
    size = out_refs[0].shape[0]
    for i, ref in enumerate(out_refs):
        block = rows_ref[pl.ds(pl.multiple_of((info_ref[1] ^ i) * size, size), size), :]
        ref[...] = block.astype(ref.dtype)


def other_kernel(info_ref, lens_ref, beam_ref, grad_ref, enc_ref, qc_ref, qsum_ref, csum_ref,
                 gate_ref, enct_ref, attn_ref, score_ref, logit_ref, *refs):
    gate_ref[...] = grad_ref[...] * beam_ref[...].astype(F32)
    sums = label_chunk(
        doc_list(turn_around(enc_ref, enct_ref), enc_ref, enct_ref, gate_ref, lens_ref,
                 attn_ref, score_ref, logit_ref),
        qc_ref[0], qc_ref[1], lanes_of(info_ref, 0, qc_ref.shape[1]),
        (qsum_ref[...], csum_ref[...]),
    )
    to_blocks(info_ref, sums, refs[-1], refs[:-1])


def far_kernel(info_ref, lens_ref, lens2_ref, gate_ref, gate2_ref, enc_ref, enc2_ref, enct_ref,
               enct2_ref, qc_ref, attn_ref, score_ref, logit_ref, attn2_ref, score2_ref,
               logit2_ref, *refs):
    loads = [lambda: None] * enc_ref.shape[0]
    sums = label_chunk(
        doc_list(loads, enc_ref, enct_ref, gate_ref, lens_ref, attn_ref, score_ref, logit_ref)
        + doc_list(loads, enc2_ref, enct2_ref, gate2_ref, lens2_ref, attn2_ref, score2_ref,
                   logit2_ref),
        qc_ref[0], qc_ref[1], lanes_of(info_ref, 2, qc_ref.shape[1]), (None, None),
    )
    to_blocks(info_ref, sums, refs[-1], refs[:-1])


def state_kernel(ks, info_ref, gate_ref, *refs):
    chunks, more, out_ref = refs[: 3 * len(ks)], refs[3 * len(ks) : -1], refs[-1]
    docs = out_ref.shape[0]
    ctx_grads = []
    for n, k in enumerate(ks):
        qc_ref = chunks[3 * n + 2]
        labels = qc_ref.shape[1]
        gate = gate_ref[:, lanes_of(info_ref, k, labels)]
        gate = jnp.concatenate([gate, jnp.zeros((128 - docs, labels), F32)], axis=0).T
        c = qc_ref[1].astype(F32)
        ctx_grads.append([(c * gate[:, d : d + 1]).astype(BF16) for d in range(docs)])
    for d in range(docs):
        total = None
        for n in range(len(ks)):
            attn_ref, score_ref, qc_ref = chunks[3 * n : 3 * n + 3]
            part = mm(attn_ref[d], ctx_grads[n][d]) + mm(score_ref[d], qc_ref[0])
            total = part if total is None else total + part
        for ref in more:
            total = total + ref[d].astype(F32)
        out_ref[d] = total.astype(out_ref.dtype)


def state_grad(info, gate, parts, more):
    docs, tokens, labels = parts[0][0].shape
    width = parts[0][2].shape[2]
    return call(
        functools.partial(state_kernel, (0, 2)), shape((docs, tokens, width), BF16),
        [info, gate, *parts[0], *parts[1], *more], "state_grad",
        estimate=cost(4, docs, tokens, width, labels),
    )


def add_kernel(*refs):
    total = refs[0][...].astype(F32)
    for ref in refs[1:-1]:
        total = total + ref[...].astype(F32)
    refs[-1][...] = total.astype(BF16)


def add(*arrays):
    return call(add_kernel, shape(arrays[0].shape, BF16), arrays, "add")


def early_kernel(info_ref, own_ref, *refs):
    logit_refs, (out_ref, logit_ref) = refs[:-2], refs[-2:]
    size = own_ref.shape[0]
    out_ref[pl.ds(pl.multiple_of(info_ref[1] * size, size), size), :] = own_ref[...].astype(F32)
    for k, ref in enumerate(logit_refs):
        labels = ref.shape[1]
        logit_ref[:, lanes_of(info_ref, k, labels)] = ref[...]


def late_kernel(info_ref, *refs):
    block_refs, (_, out_ref, rows_ref, sem) = refs[:-4], refs[-4:]
    size = block_refs[0].shape[0]
    copies = []
    for i, ref in enumerate(block_refs):
        rows_ref[i] = ref[...].astype(F32)
        to = pl.ds(pl.multiple_of((info_ref[1] ^ (1 + i)) * size, size), size)
        copies.append(pltpu.make_async_copy(rows_ref.at[i], out_ref.at[to], sem.at[i]))
        copies[-1].start()
    for copy in copies:
        copy.wait()


def late_rows(info, blocks, early):
    count = len(blocks)
    return pl.pallas_call(
        late_kernel,
        out_shape=shape(early.shape, early.dtype),
        in_specs=[SMEM] + [VMEM] * count + [pl.BlockSpec(memory_space=pl.ANY)],
        out_specs=pl.BlockSpec(memory_space=pl.ANY),
        scratch_shapes=[
            pltpu.VMEM((count, *blocks[0].shape), F32), pltpu.SemaphoreType.DMA((count,))
        ],
        input_output_aliases={1 + count: 0},
        compiler_params=PARAMS,
        name="late_rows",
    )(info, *blocks, early)


def per_device(reps, blks, encoded, queries, classifiers, lengths, beam, logit_grad):
    labels, width = queries.shape
    docs, tokens, _ = encoded.shape
    total = reps * blks
    blk, rep = lax.axis_index("blk"), lax.axis_index("rep")
    info = jnp.stack([blk, (rep & 1) * 2 + ((rep >> 1) & 1)]).astype(jnp.int32)

    def swap(x, mask):
        return lax.ppermute(x, ("rep", "blk"), [(i, i ^ mask) for i in range(total)])

    core, ax = 1, 2
    ay, az, azz = blks, 2 * blks, 4 * blks
    turns = [0, az, ay, ay | az]

    qc = call(
        pack_kernel, shape((2, labels, width), BF16), [queries, classifiers], "pack",
        [pltpu.SemaphoreType.DMA((2,))], hbm=2,
    )
    far_qc = swap(qc, ax)
    encoded2, beam2, grad2 = swap(encoded, core), swap(beam, core), swap(logit_grad, core)
    lengths2 = swap(lengths, core)
    lengths = pltpu.with_memory_space_constraint(lengths, pltpu.HBM)

    per_chunk = [
        shape((docs, tokens, labels), BF16),
        shape((docs, tokens, labels), BF16),
        shape((docs, labels), F32),
    ]
    gates = shape(beam.shape, F32)
    turned = shape((docs, width, tokens), BF16)
    flat = shape((labels, 2 * width), F32)
    blocks = [shape((labels // GROUP, 2 * width), BF16)] * GROUP
    rows = [pltpu.VMEM(flat.shape, F32)]
    sums = [shape((width, labels), F32)] * 2
    estimate = functools.partial(cost, tokens=tokens, width=width, labels=labels)

    enc, gate, enct, attn, score, logit, *acc = call(
        own_kernel,
        [shape(encoded.shape, BF16), gates, turned] + per_chunk + sums,
        [encoded, beam, logit_grad, info, lengths, qc], "own_labels",
        [pltpu.VMEM(beam.shape, jnp.int32), pltpu.SemaphoreType.DMA((docs + 2,))],
        estimate(4, docs), hbm=3,
    )
    gate2, enct2, attn2, score2, logit_away, keep, *near = call(
        other_kernel,
        [gates, turned] + per_chunk + [shape(blocks[0].shape, F32)] + blocks[1:],
        [info, lengths2, beam2, grad2, encoded2, qc, *acc], "own_labels_other_docs",
        rows, estimate(4, docs),
    )
    keep, far_qc = lax.optimization_barrier((keep, far_qc))
    far_attn, far_score, far_logit, far_attn2, far_score2, far_logit_away, *far = call(
        far_kernel, per_chunk + per_chunk + blocks,
        [info, lengths, lengths2, gate, gate2, enc, encoded2, enct, enct2, far_qc],
        "far_labels", rows, estimate(4, 2 * docs),
    )

    received = [swap(x, ax | mask) for x, mask in zip(far, turns)]
    received += [swap(x, mask) for x, mask in zip(near, turns[1:])]
    state2 = state_grad(
        info, gate2, [(attn2, score2, qc), (far_attn2, far_score2, far_qc)], []
    )
    received, state2 = lax.optimization_barrier((received, state2))
    state_in = swap(state2, core)
    logits_in = swap(jnp.concatenate([logit_away, far_logit_away], axis=1), core)
    own = add(keep, *received)
    own = add(own, swap(own, azz))
    if reps > 8:
        members = [[i * 8 + j for i in range(reps // 8)] for j in range(8)]
        own = lax.psum(own.astype(F32), "rep", axis_index_groups=members).astype(BF16)

    far_attn, far_score, own = lax.optimization_barrier((far_attn, far_score, own))
    others = [swap(own, mask) for mask in turns[1:]]
    early, logits = call(
        early_kernel,
        [flat, shape((docs, blks * labels), F32)],
        [info, own, logit, logits_in[:, :labels], far_logit, logits_in[:, labels:]],
        "early_rows",
    )
    state = state_grad(
        info, gate, [(attn, score, qc), (far_attn, far_score, far_qc)], [state_in]
    )
    early, state, others = lax.optimization_barrier((early, state, others))
    label_grad = late_rows(info, others, early)
    return logits, state, label_grad


def solution(mesh):
    reps, blks = mesh.shape["rep"], mesh.shape["blk"]
    assert blks == 4 and reps >= 8 and reps & (reps - 1) == 0
    in_specs = (
        P(("rep", "blk"), None, None),
        P("blk", None),
        P("blk", None),
        P(("rep", "blk")),
        P(("rep", "blk"), None),
        P(("rep", "blk"), None),
    )
    out_specs = (P(("rep", "blk"), None), P(("rep", "blk"), None, None), P("blk", None))
    return jax.shard_map(
        functools.partial(per_device, reps, blks),
        mesh=mesh, in_specs=in_specs, out_specs=out_specs, check_vma=False,
    )
```

```python
import functools

import jax
import jax.numpy as jnp
from jax import lax
from jax.experimental import pallas as pl
from jax.experimental.pallas import tpu as pltpu
from jax.sharding import PartitionSpec as P

F32 = jnp.float32
BF16 = jnp.bfloat16
VMEM = pl.BlockSpec(memory_space=pltpu.VMEM)
SMEM = pl.BlockSpec(memory_space=pltpu.SMEM)
HBM = pl.BlockSpec(memory_space=pltpu.HBM)
PARAMS = pltpu.CompilerParams(vmem_limit_bytes=20 * 1024 * 1024)
GROUP = 4
EXTRA = 16


def shape(dims, dtype):
    return jax.ShapeDtypeStruct(dims, dtype)


def mm(a, b):
    return jnp.dot(a, b, preferred_element_type=F32)


def cost(products, docs, tokens, width, labels):
    return pl.CostEstimate(
        flops=2 * products * docs * tokens * width * labels,
        transcendentals=docs * tokens * labels,
        bytes_accessed=4 * docs * tokens * width,
    )


def call(kernel, out_shape, ins, name, scratch=(), estimate=None, hbm=0):
    single = not isinstance(out_shape, (list, tuple))
    ins = [pltpu.with_memory_space_constraint(x, pltpu.HBM) for x in ins[:hbm]] + list(ins[hbm:])
    return pl.pallas_call(
        kernel,
        out_shape=out_shape,
        in_specs=[
            HBM if i < hbm else SMEM if x.ndim == 1 else VMEM for i, x in enumerate(ins)
        ],
        out_specs=VMEM if single else [VMEM] * len(out_shape),
        scratch_shapes=scratch,
        compiler_params=PARAMS,
        cost_estimate=estimate,
        name=name,
    )(*ins)


def lanes_of(info_ref, k, labels):
    return pl.ds(pl.multiple_of((info_ref[0] ^ k) * labels, labels), labels)


def label_chunk(docs, q, c, lanes, sums):
    qt = q.T
    ct = c.T.astype(F32)
    labels = q.shape[0]

    def products(doc):
        load, enc_ref, enct_ref, gate_ref = doc[:4]
        load()
        enc = enc_ref[...]
        g = gate_ref[:, lanes]
        return g, mm(enc, qt), mm(enc, (ct * g).astype(BF16))

    query_grad, class_grad = sums
    ahead = products(docs[0])
    for i, (_, _, enct_ref, _, length, attn_ref, score_ref, logit_ref) in enumerate(docs):
        g, scores, attn_grad = ahead
        if i + 1 < len(docs):
            ahead = products(docs[i + 1])
        token = lax.broadcasted_iota(jnp.int32, scores.shape, 0)
        expo = jnp.where(token < length, jnp.exp(scores), 0.0)
        attn = expo * (1.0 / jnp.sum(expo, axis=0, keepdims=True))
        attn_b = attn.astype(BF16)
        attn_ref[...] = attn_b
        inner = jnp.sum(attn * attn_grad, axis=0, keepdims=True)
        score_grad = (attn * (attn_grad - inner)).astype(BF16)
        score_ref[...] = score_grad
        enct = enct_ref[...]
        context = mm(enct, attn_b)
        logit_ref[...] = jnp.sum(context * ct, axis=0, keepdims=True)
        part = context * g
        class_grad = part if class_grad is None else class_grad + part
        part = mm(enct, score_grad)
        query_grad = part if query_grad is None else query_grad + part
    return query_grad, class_grad


def doc_list(loads, enc_ref, enct_ref, gate_ref, lens_ref, attn_ref, score_ref, logit_ref):
    return [
        (loads[d], enc_ref.at[d], enct_ref.at[d], gate_ref.at[d : d + 1], lens_ref[d],
         attn_ref.at[d], score_ref.at[d], logit_ref.at[d : d + 1])
        for d in range(enc_ref.shape[0])
    ]


def turn_around(enc_ref, enct_ref, copies=None):
    def load(d):
        if copies is not None:
            copies[d].wait()
        enct_ref[d] = enc_ref[d].T

    return [functools.partial(load, d) for d in range(enc_ref.shape[0])]


def pack_kernel(q_in, c_in, qc_ref, sem):
    copies = [pltpu.make_async_copy(x, qc_ref.at[i], sem.at[i]) for i, x in enumerate((q_in, c_in))]
    for copy in copies:
        copy.start()
    for copy in copies:
        copy.wait()


def own_kernel(enc_in, beam_in, grad_in, info_ref, lens_ref, qc_ref, enc_ref, gate_ref, enct_ref,
               attn_ref, score_ref, logit_ref, qsum_ref, csum_ref, beam_ref, sem):
    docs = enc_ref.shape[0]
    small = [(beam_in, beam_ref), (grad_in, gate_ref)]
    small = [pltpu.make_async_copy(x, y, sem.at[docs + i]) for i, (x, y) in enumerate(small)]
    copies = [
        pltpu.make_async_copy(enc_in.at[d], enc_ref.at[d], sem.at[d]) for d in range(docs)
    ]
    for copy in copies[:1] + small + copies[1:]:
        copy.start()
    loads = turn_around(enc_ref, enct_ref, copies)

    def first_load():
        load()
        for copy in small:
            copy.wait()
        gate_ref[...] = gate_ref[...] * beam_ref[...].astype(F32)

    load, loads[0] = loads[0], first_load
    qsum_ref[...], csum_ref[...] = label_chunk(
        doc_list(loads, enc_ref, enct_ref, gate_ref, lens_ref, attn_ref, score_ref, logit_ref),
        qc_ref[0], qc_ref[1], lanes_of(info_ref, 0, qc_ref.shape[1]), (None, None),
    )


def to_blocks(info_ref, sums, rows_ref, out_refs):
    query_grad, class_grad = sums
    width = query_grad.shape[0]
    rows_ref[:, :width] = query_grad.T
    rows_ref[:, width:] = class_grad.T
    size = rows_ref.shape[0] // GROUP
    count = GROUP // len(out_refs)
    for i in range(GROUP):
        ref = out_refs[i // count]
        block = rows_ref[pl.ds(pl.multiple_of((info_ref[1] ^ i) * size, size), size), :]
        ref[(i % count) * size : (i % count + 1) * size, :] = block.astype(ref.dtype)


def other_kernel(info_ref, lens_ref, beam_ref, grad_ref, enc_ref, qc_ref, qsum_ref, csum_ref,
                 gate_ref, enct_ref, attn_ref, score_ref, logit_ref, *refs):
    gate_ref[...] = grad_ref[...] * beam_ref[...].astype(F32)
    sums = label_chunk(
        doc_list(turn_around(enc_ref, enct_ref), enc_ref, enct_ref, gate_ref, lens_ref,
                 attn_ref, score_ref, logit_ref),
        qc_ref[0], qc_ref[1], lanes_of(info_ref, 0, qc_ref.shape[1]),
        (qsum_ref[...], csum_ref[...]),
    )
    to_blocks(info_ref, sums, refs[-1], refs[:-1])


def far_kernel(info_ref, lens_ref, lens2_ref, gate_ref, gate2_ref, enc_ref, enc2_ref, enct_ref,
               enct2_ref, qc_ref, attn_ref, score_ref, logit_ref, attn2_ref, score2_ref,
               logit2_ref, *refs):
    loads = [lambda: None] * enc_ref.shape[0]
    sums = label_chunk(
        doc_list(loads, enc_ref, enct_ref, gate_ref, lens_ref, attn_ref, score_ref, logit_ref)
        + doc_list(loads, enc2_ref, enct2_ref, gate2_ref, lens2_ref, attn2_ref, score2_ref,
                   logit2_ref),
        qc_ref[0], qc_ref[1], lanes_of(info_ref, 2, qc_ref.shape[1]), (None, None),
    )
    to_blocks(info_ref, sums, refs[-1], refs[:-1])


def state_kernel(ks, info_ref, gate_ref, *refs):
    chunks, refs = refs[: 4 * len(ks)], refs[4 * len(ks) :]
    docs, labels = gate_ref.shape[0], chunks[2].shape[1]
    in_ref = refs[0] if len(refs) == 3 else None
    out_ref = refs[0] if in_ref is None else refs[1]
    tokens, width = chunks[0].shape[1], chunks[2].shape[2]
    ctx_grads = []
    for n, k in enumerate(ks):
        gate = gate_ref[:, lanes_of(info_ref, k, labels)]
        gate = jnp.concatenate([gate, jnp.zeros((128 - docs, labels), F32)], axis=0).T
        c = chunks[4 * n + 2][1].astype(F32)
        ctx_grads.append([(c * gate[:, d : d + 1]).astype(BF16) for d in range(docs)])
    for d in range(docs):
        total = None
        for n in range(len(ks)):
            attn_ref, score_ref, qc_ref = chunks[4 * n : 4 * n + 3]
            part = mm(attn_ref[d], ctx_grads[n][d]) + mm(score_ref[d], qc_ref[0])
            total = part if total is None else total + part
        if in_ref is not None:
            total = total + in_ref[d, :tokens].astype(F32)
        out_ref[d, :tokens] = total.astype(out_ref.dtype)
        for n in range(len(ks)):
            own = chunks[4 * n + 3][d : d + 1, :]
            if in_ref is None:
                high = own.astype(BF16)
                low = (own - high.astype(F32)).astype(BF16)
                pair = jnp.concatenate([high.astype(F32), low.astype(F32)], axis=0)
                pad = jnp.zeros((EXTRA - 2, labels), F32)
                pair = jnp.concatenate([pair, pad], axis=0).astype(BF16)
                out_ref[d, tokens:, n * labels : (n + 1) * labels] = pair
                continue
            logit_ref = refs[2]
            pair = in_ref[d, tokens:, n * labels : (n + 1) * labels].astype(F32)
            logit_ref[d : d + 1, lanes_of(info_ref, ks[n], labels)] = own
            logit_ref[d : d + 1, lanes_of(info_ref, ks[n] ^ 1, labels)] = pair[0:1] + pair[1:2]


def state_grad(info, gate, parts, more):
    docs, tokens, labels = parts[0][0].shape
    width = parts[0][2].shape[2]
    if more:
        out = [shape((docs, tokens, width), BF16), shape(gate.shape, F32)]
    else:
        out = shape((docs, tokens + EXTRA, width), BF16)
    return call(
        functools.partial(state_kernel, (0, 2)), out, [info, gate, *parts[0], *parts[1], *more],
        "state_grad", estimate=cost(4, docs, tokens, width, labels),
    )


def add_kernel(count, *refs):
    total = refs[0][...].astype(F32)
    for ref in refs[1:count]:
        total = total + ref[...].astype(F32)
    size = refs[count].shape[0]
    for i, ref in enumerate(refs[count:]):
        ref[...] = total[i * size : (i + 1) * size].astype(ref.dtype)


def add(arrays, dtypes):
    rows, cols = arrays[0].shape
    out = [shape((rows // len(dtypes), cols), dtype) for dtype in dtypes]
    return call(functools.partial(add_kernel, len(arrays)), out, arrays, "add")


def rows_kernel(info_ref, *refs):
    block_refs, (out_ref, rows_ref, sem) = refs[:-3], refs[-3:]
    size = block_refs[0].shape[0]
    copies = []
    for i, ref in enumerate(block_refs):
        rows_ref[i] = ref[...].astype(F32)
        to = pl.ds(pl.multiple_of((info_ref[1] ^ i) * size, size), size)
        copies.append(pltpu.make_async_copy(rows_ref.at[i], out_ref.at[to], sem.at[i]))
        copies[-1].start()
    for copy in copies:
        copy.wait()


def to_rows(info, blocks):
    count = len(blocks)
    rows, cols = blocks[0].shape
    return pl.pallas_call(
        rows_kernel,
        out_shape=shape((count * rows, cols), F32),
        in_specs=[SMEM] + [VMEM] * count,
        out_specs=pl.BlockSpec(memory_space=pl.ANY),
        scratch_shapes=[pltpu.VMEM((count, rows, cols), F32), pltpu.SemaphoreType.DMA((count,))],
        compiler_params=PARAMS,
        name="to_rows",
    )(info, *blocks)


def per_device(reps, blks, encoded, queries, classifiers, lengths, beam, logit_grad):
    labels, width = queries.shape
    docs, tokens, _ = encoded.shape
    total = reps * blks
    blk, rep = lax.axis_index("blk"), lax.axis_index("rep")
    info = jnp.stack([blk, (rep & 1) * 2 + ((rep >> 1) & 1)]).astype(jnp.int32)

    def swap(x, mask):
        return lax.ppermute(x, ("rep", "blk"), [(i, i ^ mask) for i in range(total)])

    core, ax = 1, 2
    ay, az, azz = blks, 2 * blks, 4 * blks
    turns = [0, az, ay, ay | az]

    qc = call(
        pack_kernel, shape((2, labels, width), BF16), [queries, classifiers], "pack",
        [pltpu.SemaphoreType.DMA((2,))], hbm=2,
    )
    far_qc = swap(qc, ax)
    encoded2, beam2, grad2 = swap(encoded, core), swap(beam, core), swap(logit_grad, core)
    lengths2 = swap(lengths, core)
    lengths = pltpu.with_memory_space_constraint(lengths, pltpu.HBM)

    per_chunk = [
        shape((docs, tokens, labels), BF16),
        shape((docs, tokens, labels), BF16),
        shape((docs, labels), F32),
    ]
    gates = shape(beam.shape, F32)
    turned = shape((docs, width, tokens), BF16)
    block = shape((labels // GROUP, 2 * width), BF16)
    halves = [shape((labels // 2, 2 * width), dtype) for dtype in (F32, BF16)]
    rows = [pltpu.VMEM((labels, 2 * width), F32)]
    sums = [shape((width, labels), F32)] * 2
    estimate = functools.partial(cost, tokens=tokens, width=width, labels=labels)

    enc, gate, enct, attn, score, logit, *acc = call(
        own_kernel,
        [shape(encoded.shape, BF16), gates, turned] + per_chunk + sums,
        [encoded, beam, logit_grad, info, lengths, qc], "own_labels",
        [pltpu.VMEM(beam.shape, jnp.int32), pltpu.SemaphoreType.DMA((docs + 2,))],
        estimate(4, docs), hbm=3,
    )
    gate2, enct2, attn2, score2, logit2, keep, send = call(
        other_kernel, [gates, turned] + per_chunk + halves,
        [info, lengths2, beam2, grad2, encoded2, qc, *acc], "own_labels_other_docs",
        rows, estimate(4, docs),
    )
    received = swap(send, ay)
    keep, far_qc = lax.optimization_barrier((keep, far_qc))
    far_attn, far_score, far_logit, far_attn2, far_score2, far_logit2, *far = call(
        far_kernel, per_chunk + per_chunk + [block] * GROUP,
        [info, lengths, lengths2, gate, gate2, enc, encoded2, enct, enct2, far_qc],
        "far_labels", rows, estimate(4, 2 * docs),
    )

    far, keep, received = lax.optimization_barrier((far, keep, received))
    keep, send = add([keep, received], [F32, BF16])
    far, send = lax.optimization_barrier((far, send))
    received = [swap(x, ax | mask) for x, mask in zip(far, turns)]
    near = swap(send, az)
    state2 = state_grad(
        info, gate2,
        [(attn2, score2, qc, logit2), (far_attn2, far_score2, far_qc, far_logit2)], [],
    )
    near, received, state2 = lax.optimization_barrier((near, received, state2))
    state_in = swap(state2, core)
    (own,) = add([keep, near, *received], [BF16])
    far_attn, far_score, own = lax.optimization_barrier((far_attn, far_score, own))
    state, logits = state_grad(
        info, gate, [(attn, score, qc, logit), (far_attn, far_score, far_qc, far_logit)],
        [state_in],
    )
    received, state = lax.optimization_barrier((swap(own, azz), state))
    (own,) = add([own, received], [BF16])
    if reps > 8:
        members = [[i * 8 + j for i in range(reps // 8)] for j in range(8)]
        own = lax.psum(own.astype(F32), "rep", axis_index_groups=members).astype(BF16)

    label_grad = to_rows(info, [own] + [swap(own, mask) for mask in turns[1:]])
    return logits, state, label_grad


def solution(mesh):
    reps, blks = mesh.shape["rep"], mesh.shape["blk"]
    assert blks == 4 and reps >= 8 and reps & (reps - 1) == 0
    in_specs = (
        P(("rep", "blk"), None, None),
        P("blk", None),
        P("blk", None),
        P(("rep", "blk")),
        P(("rep", "blk"), None),
        P(("rep", "blk"), None),
    )
    out_specs = (P(("rep", "blk"), None), P(("rep", "blk"), None, None), P("blk", None))
    return jax.shard_map(
        functools.partial(per_device, reps, blks),
        mesh=mesh, in_specs=in_specs, out_specs=out_specs, check_vma=False,
    )
```

```python
import functools

import jax
import jax.numpy as jnp
from jax import lax
from jax.experimental import pallas as pl
from jax.experimental.pallas import tpu as pltpu
from jax.sharding import PartitionSpec as P

F32 = jnp.float32
BF16 = jnp.bfloat16
VMEM = pl.BlockSpec(memory_space=pltpu.VMEM)
SMEM = pl.BlockSpec(memory_space=pltpu.SMEM)
HBM = pl.BlockSpec(memory_space=pltpu.HBM)
PARAMS = pltpu.CompilerParams(vmem_limit_bytes=20 * 1024 * 1024)
GROUP = 4
LANES = 128
EXTRA = 16


def shape(dims, dtype):
    return jax.ShapeDtypeStruct(dims, dtype)


def mm(a, b):
    return jnp.dot(a, b, preferred_element_type=F32)


def cost(products, docs, tokens, width, labels):
    return pl.CostEstimate(
        flops=2 * products * docs * tokens * width * labels,
        transcendentals=docs * tokens * labels,
        bytes_accessed=4 * docs * tokens * width,
    )


def call(kernel, out_shape, ins, name, scratch=(), estimate=None, hbm=0):
    single = not isinstance(out_shape, (list, tuple))
    ins = [pltpu.with_memory_space_constraint(x, pltpu.HBM) for x in ins[:hbm]] + list(ins[hbm:])
    return pl.pallas_call(
        kernel,
        out_shape=out_shape,
        in_specs=[
            HBM if i < hbm else SMEM if x.ndim == 1 else VMEM for i, x in enumerate(ins)
        ],
        out_specs=VMEM if single else [VMEM] * len(out_shape),
        scratch_shapes=scratch,
        compiler_params=PARAMS,
        cost_estimate=estimate,
        name=name,
    )(*ins)


def lanes_of(info_ref, k, labels):
    return pl.ds(pl.multiple_of((info_ref[0] ^ k) * labels, labels), labels)


def label_chunk(docs, q, c, lanes, sums):
    qt = q.T
    ct = c.T.astype(F32)
    labels = q.shape[0]

    def products(doc):
        load, enc_ref, enct_ref, gate_ref = doc[:4]
        load()
        enc = enc_ref[...]
        g = gate_ref[:, lanes]
        return g, mm(enc, qt), mm(enc, (ct * g).astype(BF16))

    query_grad, class_grad = sums
    ahead = products(docs[0])
    for i, (_, _, enct_ref, gate_ref, attn_ref, score_ref, logit_ref) in enumerate(docs):
        g, scores, attn_grad = ahead
        if i + 1 < len(docs):
            ahead = products(docs[i + 1])
        length = gate_ref[:, gate_ref.shape[1] - LANES :][:, :1]
        token = lax.broadcasted_iota(jnp.int32, scores.shape, 0).astype(F32)
        expo = jnp.where(token < length, jnp.exp(scores), 0.0)
        attn = expo * (1.0 / jnp.sum(expo, axis=0, keepdims=True))
        attn_b = attn.astype(BF16)
        attn_ref[...] = attn_b
        inner = jnp.sum(attn * attn_grad, axis=0, keepdims=True)
        score_grad = (attn * (attn_grad - inner)).astype(BF16)
        score_ref[...] = score_grad
        enct = enct_ref[...]
        context = mm(enct, attn_b)
        logit_ref[...] = jnp.sum(context * ct, axis=0, keepdims=True)
        part = context * g
        class_grad = part if class_grad is None else class_grad + part
        part = mm(enct, score_grad)
        query_grad = part if query_grad is None else query_grad + part
    return query_grad, class_grad


def doc_list(loads, enc_ref, enct_ref, gate_ref, attn_ref, score_ref, logit_ref):
    return [
        (loads[d], enc_ref.at[d], enct_ref.at[d], gate_ref.at[d : d + 1], attn_ref.at[d],
         score_ref.at[d], logit_ref.at[d : d + 1])
        for d in range(enc_ref.shape[0])
    ]


def turn_around(enc_ref, enct_ref, copies=None):
    def load(d):
        if copies is not None:
            copies[d].wait()
        enct_ref[d] = enc_ref[d].T

    return [functools.partial(load, d) for d in range(enc_ref.shape[0])]


def pack_kernel(q_in, c_in, beam_in, grad_in, info_ref, lens_ref, qc_ref, half_ref, gate_ref,
                beam_ref, grad_ref, sem):
    size = half_ref.shape[1]
    part = pl.ds(pl.multiple_of(info_ref[2] * size, size), size)
    pairs = [(beam_in, beam_ref), (grad_in, grad_ref)]
    for i, ref in enumerate((q_in, c_in)):
        pairs += [(ref, qc_ref.at[i]), (ref.at[part], half_ref.at[i])]
    copies = [pltpu.make_async_copy(x, y, sem.at[i]) for i, (x, y) in enumerate(pairs)]
    for copy in copies:
        copy.start()
    for copy in copies:
        copy.wait()
    docs, labels = beam_ref.shape
    gate_ref[:, :labels] = grad_ref[...] * beam_ref[...].astype(F32)
    for d in range(docs):
        gate_ref[d : d + 1, labels:] = jnp.full((1, LANES), lens_ref[d], jnp.int32).astype(F32)


def own_kernel(enc_in, info_ref, gate_ref, qc_ref, enc_ref, enct_ref, attn_ref, score_ref,
               logit_ref, qsum_ref, csum_ref, sem):
    copies = [
        pltpu.make_async_copy(enc_in.at[d], enc_ref.at[d], sem.at[d])
        for d in range(enc_ref.shape[0])
    ]
    for copy in copies:
        copy.start()
    qsum_ref[...], csum_ref[...] = label_chunk(
        doc_list(turn_around(enc_ref, enct_ref, copies), enc_ref, enct_ref, gate_ref, attn_ref,
                 score_ref, logit_ref),
        qc_ref[0], qc_ref[1], lanes_of(info_ref, 0, qc_ref.shape[1]), (None, None),
    )


def to_rows_of(info_ref, sums, rows_ref, out_refs):
    query_grad, class_grad = sums
    width = query_grad.shape[0]
    rows_ref[:, :width] = query_grad.T
    rows_ref[:, width:] = class_grad.T
    size = rows_ref.shape[0] // GROUP
    for ref, blocks in out_refs:
        for i, block in enumerate(blocks):
            at = pl.ds(pl.multiple_of((info_ref[1] ^ block) * size, size), size)
            ref[i * size : (i + 1) * size, :] = rows_ref[at, :].astype(ref.dtype)


def other_kernel(info_ref, gate_ref, enc_ref, qc_ref, qsum_ref, csum_ref, enct_ref, attn_ref,
                 score_ref, logit_ref, keep_ref, send_ref, rows_ref):
    sums = label_chunk(
        doc_list(turn_around(enc_ref, enct_ref), enc_ref, enct_ref, gate_ref, attn_ref, score_ref,
                 logit_ref),
        qc_ref[0], qc_ref[1], lanes_of(info_ref, 0, qc_ref.shape[1]),
        (qsum_ref[...], csum_ref[...]),
    )
    to_rows_of(info_ref, sums, rows_ref, [(keep_ref, (0, 1)), (send_ref, (2, 3))])


def far_kernel(info_ref, gate_ref, gate2_ref, enc_ref, enc2_ref, enct_ref, enct2_ref, full_ref,
               half_ref, rest_ref, qc_ref, attn_ref, score_ref, logit_ref, attn2_ref, score2_ref,
               logit2_ref, keep_ref, send_ref, third_ref, fourth_ref, rows_ref):
    size = half_ref.shape[1]

    @pl.when(info_ref[0] & 1 == 0)
    def _():
        qc_ref[...] = full_ref[...]

    @pl.when(info_ref[0] & 1 == 1)
    def _():
        for ref, at in ((half_ref, info_ref[2]), (rest_ref, 1 - info_ref[2])):
            qc_ref[:, pl.ds(pl.multiple_of(at * size, size), size), :] = ref[...]

    loads = [lambda: None] * enc_ref.shape[0]
    sums = label_chunk(
        doc_list(loads, enc_ref, enct_ref, gate_ref, attn_ref, score_ref, logit_ref)
        + doc_list(loads, enc2_ref, enct2_ref, gate2_ref, attn2_ref, score2_ref, logit2_ref),
        qc_ref[0], qc_ref[1], lanes_of(info_ref, 2, qc_ref.shape[1]), (None, None),
    )
    outs = [(keep_ref, (0, 1)), (send_ref, (2, 3)), (third_ref, (2,)), (fourth_ref, (3,))]
    to_rows_of(info_ref, sums, rows_ref, outs)


def state_kernel(ks, info_ref, gate_ref, *refs):
    chunks, refs = refs[: 4 * len(ks)], refs[4 * len(ks) :]
    docs, labels = gate_ref.shape[0], chunks[2].shape[1]
    in_ref = refs[0] if len(refs) == 3 else None
    out_ref = refs[0] if in_ref is None else refs[1]
    tokens, width = chunks[0].shape[1], chunks[2].shape[2]
    ctx_grads = []
    for n, k in enumerate(ks):
        gate = gate_ref[:, lanes_of(info_ref, k, labels)]
        gate = jnp.concatenate([gate, jnp.zeros((128 - docs, labels), F32)], axis=0).T
        c = chunks[4 * n + 2][1].astype(F32)
        ctx_grads.append([(c * gate[:, d : d + 1]).astype(BF16) for d in range(docs)])
    for d in range(docs):
        total = None
        for n in range(len(ks)):
            attn_ref, score_ref, qc_ref = chunks[4 * n : 4 * n + 3]
            part = mm(attn_ref[d], ctx_grads[n][d]) + mm(score_ref[d], qc_ref[0])
            total = part if total is None else total + part
        if in_ref is not None:
            total = total + in_ref[d, :tokens].astype(F32)
        out_ref[d, :tokens] = total.astype(out_ref.dtype)
        for n in range(len(ks)):
            own = chunks[4 * n + 3][d : d + 1, :]
            if in_ref is None:
                high = own.astype(BF16)
                low = (own - high.astype(F32)).astype(BF16)
                pair = jnp.concatenate([high.astype(F32), low.astype(F32)], axis=0)
                pad = jnp.zeros((EXTRA - 2, labels), F32)
                pair = jnp.concatenate([pair, pad], axis=0).astype(BF16)
                out_ref[d, tokens:, n * labels : (n + 1) * labels] = pair
                continue
            logit_ref = refs[2]
            pair = in_ref[d, tokens:, n * labels : (n + 1) * labels].astype(F32)
            logit_ref[d : d + 1, lanes_of(info_ref, ks[n], labels)] = own
            logit_ref[d : d + 1, lanes_of(info_ref, ks[n] ^ 1, labels)] = pair[0:1] + pair[1:2]


def state_grad(info, gate, parts, more):
    all_labels = gate.shape[1] - LANES
    docs, tokens, labels = parts[0][0].shape
    width = parts[0][2].shape[2]
    if more:
        out = [shape((docs, tokens, width), BF16), shape((docs, all_labels), F32)]
    else:
        out = shape((docs, tokens + EXTRA, width), BF16)
    return call(
        functools.partial(state_kernel, (0, 2)), out, [info, gate, *parts[0], *parts[1], *more],
        "state_grad", estimate=cost(4, docs, tokens, width, labels),
    )


def add_kernel(count, *refs):
    total = refs[0][...].astype(F32)
    for ref in refs[1:count]:
        total = total + ref[...].astype(F32)
    size = refs[count].shape[0]
    for i, ref in enumerate(refs[count:]):
        ref[...] = total[i * size : (i + 1) * size].astype(ref.dtype)


def add(arrays, dtypes):
    rows, cols = arrays[0].shape
    out = [shape((rows // len(dtypes), cols), dtype) for dtype in dtypes]
    return call(functools.partial(add_kernel, len(arrays)), out, arrays, "add")


def rows_kernel(info_ref, *refs):
    block_refs, (out_ref, rows_ref, sem) = refs[:-3], refs[-3:]
    size = block_refs[0].shape[0]
    copies = []
    for i, ref in enumerate(block_refs):
        rows_ref[i] = ref[...].astype(F32)
        to = pl.ds(pl.multiple_of((info_ref[1] ^ i) * size, size), size)
        copies.append(pltpu.make_async_copy(rows_ref.at[i], out_ref.at[to], sem.at[i]))
        copies[-1].start()
    for copy in copies:
        copy.wait()


def to_rows(info, blocks):
    count = len(blocks)
    rows, cols = blocks[0].shape
    return pl.pallas_call(
        rows_kernel,
        out_shape=shape((count * rows, cols), F32),
        in_specs=[SMEM] + [VMEM] * count,
        out_specs=pl.BlockSpec(memory_space=pl.ANY),
        scratch_shapes=[pltpu.VMEM((count, rows, cols), F32), pltpu.SemaphoreType.DMA((count,))],
        compiler_params=PARAMS,
        name="to_rows",
    )(info, *blocks)


def per_device(reps, blks, encoded, queries, classifiers, lengths, beam, logit_grad):
    labels, width = queries.shape
    docs, tokens, _ = encoded.shape
    total = reps * blks
    blk, rep = lax.axis_index("blk"), lax.axis_index("rep")
    turn = (rep & 1) * 2 + ((rep >> 1) & 1)
    info = jnp.stack([blk, turn, rep & 1]).astype(jnp.int32)

    def swap(x, *masks):
        masks = masks * (3 - len(masks))
        pairs = [(i, masks[i & 1]) for i in range(total) if masks[i & 1] is not None]
        return lax.ppermute(x, ("rep", "blk"), [(i, i ^ mask) for i, mask in pairs])

    core, ax = 1, 2
    ay, az, azz = blks, 2 * blks, 4 * blks
    turns = [0, az, ay, ay | az]

    qc, half, gate = call(
        pack_kernel,
        [
            shape((2, labels, width), BF16),
            shape((2, labels // 2, width), BF16),
            shape((docs, blks * labels + LANES), F32),
        ],
        [queries, classifiers, beam, logit_grad, info,
         pltpu.with_memory_space_constraint(lengths, pltpu.HBM)],
        "pack",
        [pltpu.VMEM(beam.shape, jnp.int32), pltpu.VMEM(beam.shape, F32),
         pltpu.SemaphoreType.DMA((6,))],
        hbm=4,
    )
    far_full, far_half = swap(qc, ax, None), swap(half, None, ax)
    encoded2, gate2 = swap(encoded, core), swap(gate, core)

    per_chunk = [
        shape((docs, tokens, labels), BF16),
        shape((docs, tokens, labels), BF16),
        shape((docs, labels), F32),
    ]
    turned = shape((docs, width, tokens), BF16)
    block = shape((labels // GROUP, 2 * width), BF16)
    halves = [shape((labels // 2, 2 * width), dtype) for dtype in (F32, BF16)]
    rows = [pltpu.VMEM((labels, 2 * width), F32)]
    sums = [shape((width, labels), F32)] * 2
    estimate = functools.partial(cost, tokens=tokens, width=width, labels=labels)

    enc, enct, attn, score, logit, *acc = call(
        own_kernel, [shape(encoded.shape, BF16), turned] + per_chunk + sums,
        [encoded, info, gate, qc], "own_labels", [pltpu.SemaphoreType.DMA((docs,))],
        estimate(4, docs), hbm=1,
    )
    acc, far_half, gate2 = lax.optimization_barrier((acc, far_half, gate2))
    far_rest = swap(far_half, None, ay)
    enct2, attn2, score2, logit2, keep, send = call(
        other_kernel, [turned] + per_chunk + halves, [info, gate2, encoded2, qc, *acc],
        "own_labels_other_docs", rows, estimate(4, docs),
    )
    received = swap(send, ay)
    far_qc, far_attn, far_score, far_logit, far_attn2, far_score2, far_logit2, *far = call(
        far_kernel, [shape(qc.shape, BF16)] + per_chunk + per_chunk + halves + [block] * 2,
        [info, gate, gate2, enc, encoded2, enct, enct2, far_full, far_half, far_rest],
        "far_labels", rows, estimate(4, 2 * docs),
    )

    far, received = lax.optimization_barrier((far, received))
    far_keep, far_send, third, fourth = far
    blocks = [swap(third, ax | ay, None), swap(fourth, ax | ay | az, None)]
    far_in = swap(far_send, None, ay)
    keep, send = add([keep, received], [F32, BF16])
    near = swap(send, az)
    first, second = add([far_keep, far_in], [BF16, BF16])
    first, second, far_attn2 = lax.optimization_barrier((first, second, far_attn2))
    blocks += [swap(first, ax), swap(second, ax | az)]
    state2 = state_grad(
        info, gate2,
        [(attn2, score2, qc, logit2), (far_attn2, far_score2, far_qc, far_logit2)], [],
    )
    near, blocks, state2 = lax.optimization_barrier((near, blocks, state2))
    state_in = swap(state2, core)
    (own,) = add([keep, near, *blocks], [BF16])
    (own,) = add([own, swap(own, azz)], [BF16])
    if reps > 8:
        members = [[i * 8 + j for i in range(reps // 8)] for j in range(8)]
        own = lax.psum(own.astype(F32), "rep", axis_index_groups=members).astype(BF16)

    far_attn, far_score, own = lax.optimization_barrier((far_attn, far_score, own))
    others = [swap(own, mask) for mask in turns[1:]]
    state, logits = state_grad(
        info, gate, [(attn, score, qc, logit), (far_attn, far_score, far_qc, far_logit)],
        [state_in],
    )
    state, others = lax.optimization_barrier((state, others))
    label_grad = to_rows(info, [own, *others])
    return logits, state, label_grad


def solution(mesh):
    reps, blks = mesh.shape["rep"], mesh.shape["blk"]
    assert blks == 4 and reps >= 8 and reps & (reps - 1) == 0
    in_specs = (
        P(("rep", "blk"), None, None),
        P("blk", None),
        P("blk", None),
        P(("rep", "blk")),
        P(("rep", "blk"), None),
        P(("rep", "blk"), None),
    )
    out_specs = (P(("rep", "blk"), None), P(("rep", "blk"), None, None), P("blk", None))
    return jax.shard_map(
        functools.partial(per_device, reps, blks),
        mesh=mesh, in_specs=in_specs, out_specs=out_specs, check_vma=False,
    )
```

```python
import functools

import jax
import jax.numpy as jnp
from jax import lax
from jax.experimental import pallas as pl
from jax.experimental.pallas import tpu as pltpu
from jax.sharding import PartitionSpec as P

F32 = jnp.float32
BF16 = jnp.bfloat16
VMEM = pl.BlockSpec(memory_space=pltpu.VMEM)
SMEM = pl.BlockSpec(memory_space=pltpu.SMEM)
HBM = pl.BlockSpec(memory_space=pltpu.HBM)
PARAMS = pltpu.CompilerParams(vmem_limit_bytes=20 * 1024 * 1024)
GROUP = 4
TILE = 128
EXTRA = 16


def shape(dims, dtype):
    return jax.ShapeDtypeStruct(dims, dtype)


def mm(a, b):
    return jnp.dot(a, b, preferred_element_type=F32)


def cost(products, docs, tokens, width, labels):
    return pl.CostEstimate(
        flops=2 * products * docs * tokens * width * labels,
        transcendentals=docs * tokens * labels,
        bytes_accessed=4 * docs * tokens * width,
    )


def call(kernel, out_shape, ins, name, scratch=(), estimate=None, hbm=0):
    single = not isinstance(out_shape, (list, tuple))
    ins = [pltpu.with_memory_space_constraint(x, pltpu.HBM) for x in ins[:hbm]] + list(ins[hbm:])
    return pl.pallas_call(
        kernel,
        out_shape=out_shape,
        in_specs=[
            HBM if i < hbm else SMEM if x.ndim == 1 else VMEM for i, x in enumerate(ins)
        ],
        out_specs=VMEM if single else [VMEM] * len(out_shape),
        scratch_shapes=scratch,
        compiler_params=PARAMS,
        cost_estimate=estimate,
        name=name,
    )(*ins)


def lanes_of(info_ref, k, labels):
    return pl.ds(pl.multiple_of((info_ref[0] ^ k) * labels, labels), labels)


def label_chunk(docs, q, c, lanes, sums, expo_refs):
    qt = q.T
    ct = c.T.astype(F32)
    labels = q.shape[0]

    def products(doc):
        load, enc_ref, enct_ref, gate_ref = doc[:4]
        load()
        enc = enc_ref[...]
        g = gate_ref[:, lanes]
        return g, mm(enc, qt), mm(enc, (ct * g).astype(BF16))

    query_grad, class_grad = sums
    ahead = products(docs[0])
    for i, (_, _, enct_ref, _, length, attn_ref, score_ref, logit_ref) in enumerate(docs):
        g, scores, attn_grad = ahead
        if i + 1 < len(docs):
            ahead = products(docs[i + 1])
        expo_ref = expo_refs.at[i % 2]
        tokens = scores.shape[0]
        tiles = [slice(at, at + TILE) for at in range(0, tokens, TILE)]
        token = lax.broadcasted_iota(jnp.int32, (TILE, labels), 0)
        total = jnp.zeros((1, labels), F32)
        for rows in tiles:
            expo = jnp.where(token < length - rows.start, jnp.exp(scores[rows]), 0.0)
            expo_ref[rows, :] = expo
            total = total + jnp.sum(expo, axis=0, keepdims=True)
        scale = 1.0 / total
        inner = jnp.zeros((1, labels), F32)
        for rows in tiles:
            attn = expo_ref[rows, :] * scale
            attn_ref[rows, :] = attn.astype(BF16)
            inner = inner + jnp.sum(attn * attn_grad[rows], axis=0, keepdims=True)
        for rows in tiles:
            attn = expo_ref[rows, :] * scale
            score_ref[rows, :] = (attn * (attn_grad[rows] - inner)).astype(BF16)
        attn_b, score_grad = attn_ref[...], score_ref[...]
        enct = enct_ref[...]
        context = mm(enct, attn_b)
        logit_ref[...] = jnp.sum(context * ct, axis=0, keepdims=True)
        part = context * g
        class_grad = part if class_grad is None else class_grad + part
        part = mm(enct, score_grad)
        query_grad = part if query_grad is None else query_grad + part
    return query_grad, class_grad


def doc_list(loads, enc_ref, enct_ref, gate_ref, lens_ref, attn_ref, score_ref, logit_ref):
    return [
        (loads[d], enc_ref.at[d], enct_ref.at[d], gate_ref.at[d : d + 1], lens_ref[d],
         attn_ref.at[d], score_ref.at[d], logit_ref.at[d : d + 1])
        for d in range(enc_ref.shape[0])
    ]


def turn_around(enc_ref, enct_ref, copies=None):
    def load(d):
        if copies is not None:
            copies[d].wait()
        enct_ref[d] = enc_ref[d].T

    return [functools.partial(load, d) for d in range(enc_ref.shape[0])]


def pack_kernel(q_in, c_in, qc_ref, sem):
    copies = [pltpu.make_async_copy(x, qc_ref.at[i], sem.at[i]) for i, x in enumerate((q_in, c_in))]
    for copy in copies:
        copy.start()
    for copy in copies:
        copy.wait()


def own_kernel(enc_in, beam_in, grad_in, info_ref, lens_ref, qc_ref, enc_ref, gate_ref, enct_ref,
               attn_ref, score_ref, logit_ref, qsum_ref, csum_ref, expo_refs, beam_ref, sem):
    docs = enc_ref.shape[0]
    small = [(beam_in, beam_ref), (grad_in, gate_ref)]
    small = [pltpu.make_async_copy(x, y, sem.at[docs + i]) for i, (x, y) in enumerate(small)]
    copies = [
        pltpu.make_async_copy(enc_in.at[d], enc_ref.at[d], sem.at[d]) for d in range(docs)
    ]
    for copy in copies[:1] + small + copies[1:]:
        copy.start()
    loads = turn_around(enc_ref, enct_ref, copies)

    def first_load():
        load()
        for copy in small:
            copy.wait()
        gate_ref[...] = gate_ref[...] * beam_ref[...].astype(F32)

    load, loads[0] = loads[0], first_load
    qsum_ref[...], csum_ref[...] = label_chunk(
        doc_list(loads, enc_ref, enct_ref, gate_ref, lens_ref, attn_ref, score_ref, logit_ref),
        qc_ref[0], qc_ref[1], lanes_of(info_ref, 0, qc_ref.shape[1]), (None, None), expo_refs,
    )


def to_blocks(info_ref, sums, rows_ref, out_refs):
    query_grad, class_grad = sums
    width = query_grad.shape[0]
    rows_ref[:, :width] = query_grad.T
    rows_ref[:, width:] = class_grad.T
    size = rows_ref.shape[0] // GROUP
    count = GROUP // len(out_refs)
    for i in range(GROUP):
        ref = out_refs[i // count]
        block = rows_ref[pl.ds(pl.multiple_of((info_ref[1] ^ i) * size, size), size), :]
        ref[(i % count) * size : (i % count + 1) * size, :] = block.astype(ref.dtype)


def other_kernel(info_ref, lens_ref, beam_ref, grad_ref, enc_ref, qc_ref, qsum_ref, csum_ref,
                 gate_ref, enct_ref, attn_ref, score_ref, logit_ref, *refs):
    expo_refs, refs = refs[-1], refs[:-1]
    gate_ref[...] = grad_ref[...] * beam_ref[...].astype(F32)
    sums = label_chunk(
        doc_list(turn_around(enc_ref, enct_ref), enc_ref, enct_ref, gate_ref, lens_ref,
                 attn_ref, score_ref, logit_ref),
        qc_ref[0], qc_ref[1], lanes_of(info_ref, 0, qc_ref.shape[1]),
        (qsum_ref[...], csum_ref[...]), expo_refs,
    )
    to_blocks(info_ref, sums, refs[-1], refs[:-1])


def far_kernel(info_ref, lens_ref, lens2_ref, gate_ref, gate2_ref, enc_ref, enc2_ref, enct_ref,
               enct2_ref, qc_ref, attn_ref, score_ref, logit_ref, attn2_ref, score2_ref,
               logit2_ref, *refs):
    expo_refs, refs = refs[-1], refs[:-1]
    loads = [lambda: None] * enc_ref.shape[0]
    sums = label_chunk(
        doc_list(loads, enc_ref, enct_ref, gate_ref, lens_ref, attn_ref, score_ref, logit_ref)
        + doc_list(loads, enc2_ref, enct2_ref, gate2_ref, lens2_ref, attn2_ref, score2_ref,
                   logit2_ref),
        qc_ref[0], qc_ref[1], lanes_of(info_ref, 2, qc_ref.shape[1]), (None, None), expo_refs,
    )
    to_blocks(info_ref, sums, refs[-1], refs[:-1])


def state_kernel(ks, info_ref, gate_ref, *refs):
    chunks, refs = refs[: 4 * len(ks)], refs[4 * len(ks) :]
    docs, labels = gate_ref.shape[0], chunks[2].shape[1]
    in_ref = refs[0] if len(refs) == 3 else None
    out_ref = refs[0] if in_ref is None else refs[1]
    tokens, width = chunks[0].shape[1], chunks[2].shape[2]
    ctx_grads = []
    for n, k in enumerate(ks):
        gate = gate_ref[:, lanes_of(info_ref, k, labels)]
        gate = jnp.concatenate([gate, jnp.zeros((128 - docs, labels), F32)], axis=0).T
        c = chunks[4 * n + 2][1].astype(F32)
        ctx_grads.append([(c * gate[:, d : d + 1]).astype(BF16) for d in range(docs)])
    for d in range(docs):
        total = None
        for n in range(len(ks)):
            attn_ref, score_ref, qc_ref = chunks[4 * n : 4 * n + 3]
            part = mm(attn_ref[d], ctx_grads[n][d]) + mm(score_ref[d], qc_ref[0])
            total = part if total is None else total + part
        if in_ref is not None:
            total = total + in_ref[d, :tokens].astype(F32)
        out_ref[d, :tokens] = total.astype(out_ref.dtype)
        for n in range(len(ks)):
            own = chunks[4 * n + 3][d : d + 1, :]
            if in_ref is None:
                high = own.astype(BF16)
                low = (own - high.astype(F32)).astype(BF16)
                pair = jnp.concatenate([high.astype(F32), low.astype(F32)], axis=0)
                pad = jnp.zeros((EXTRA - 2, labels), F32)
                pair = jnp.concatenate([pair, pad], axis=0).astype(BF16)
                out_ref[d, tokens:, n * labels : (n + 1) * labels] = pair
                continue
            logit_ref = refs[2]
            pair = in_ref[d, tokens:, n * labels : (n + 1) * labels].astype(F32)
            logit_ref[d : d + 1, lanes_of(info_ref, ks[n], labels)] = own
            logit_ref[d : d + 1, lanes_of(info_ref, ks[n] ^ 1, labels)] = pair[0:1] + pair[1:2]


def state_grad(info, gate, parts, more):
    docs, tokens, labels = parts[0][0].shape
    width = parts[0][2].shape[2]
    if more:
        out = [shape((docs, tokens, width), BF16), shape(gate.shape, F32)]
    else:
        out = shape((docs, tokens + EXTRA, width), BF16)
    return call(
        functools.partial(state_kernel, (0, 2)), out, [info, gate, *parts[0], *parts[1], *more],
        "state_grad", estimate=cost(4, docs, tokens, width, labels),
    )


def add_kernel(count, *refs):
    total = refs[0][...].astype(F32)
    for ref in refs[1:count]:
        total = total + ref[...].astype(F32)
    size = refs[count].shape[0]
    for i, ref in enumerate(refs[count:]):
        ref[...] = total[i * size : (i + 1) * size].astype(ref.dtype)


def add(arrays, dtypes):
    rows, cols = arrays[0].shape
    out = [shape((rows // len(dtypes), cols), dtype) for dtype in dtypes]
    return call(functools.partial(add_kernel, len(arrays)), out, arrays, "add")


def rows_kernel(info_ref, *refs):
    block_refs, (out_ref, rows_ref, sem) = refs[:-3], refs[-3:]
    size = block_refs[0].shape[0]
    copies = []
    for i, ref in enumerate(block_refs):
        rows_ref[i] = ref[...].astype(F32)
        to = pl.ds(pl.multiple_of((info_ref[1] ^ i) * size, size), size)
        copies.append(pltpu.make_async_copy(rows_ref.at[i], out_ref.at[to], sem.at[i]))
        copies[-1].start()
    for copy in copies:
        copy.wait()


def to_rows(info, blocks):
    count = len(blocks)
    rows, cols = blocks[0].shape
    return pl.pallas_call(
        rows_kernel,
        out_shape=shape((count * rows, cols), F32),
        in_specs=[SMEM] + [VMEM] * count,
        out_specs=pl.BlockSpec(memory_space=pl.ANY),
        scratch_shapes=[pltpu.VMEM((count, rows, cols), F32), pltpu.SemaphoreType.DMA((count,))],
        compiler_params=PARAMS,
        name="to_rows",
    )(info, *blocks)


def per_device(reps, blks, encoded, queries, classifiers, lengths, beam, logit_grad):
    labels, width = queries.shape
    docs, tokens, _ = encoded.shape
    total = reps * blks
    blk, rep = lax.axis_index("blk"), lax.axis_index("rep")
    info = jnp.stack([blk, (rep & 1) * 2 + ((rep >> 1) & 1)]).astype(jnp.int32)

    def swap(x, mask):
        return lax.ppermute(x, ("rep", "blk"), [(i, i ^ mask) for i in range(total)])

    core, ax = 1, 2
    ay, az, azz = blks, 2 * blks, 4 * blks
    turns = [0, az, ay, ay | az]

    qc = call(
        pack_kernel, shape((2, labels, width), BF16), [queries, classifiers], "pack",
        [pltpu.SemaphoreType.DMA((2,))], hbm=2,
    )
    encoded2, qc = lax.optimization_barrier((encoded, qc))
    far_qc = swap(qc, ax)
    encoded2, beam2, grad2 = swap(encoded2, core), swap(beam, core), swap(logit_grad, core)
    lengths2 = swap(lengths, core)
    lengths = pltpu.with_memory_space_constraint(lengths, pltpu.HBM)

    per_chunk = [
        shape((docs, tokens, labels), BF16),
        shape((docs, tokens, labels), BF16),
        shape((docs, labels), F32),
    ]
    gates = shape(beam.shape, F32)
    turned = shape((docs, width, tokens), BF16)
    block = shape((labels // GROUP, 2 * width), BF16)
    halves = [shape((labels // 2, 2 * width), dtype) for dtype in (F32, BF16)]
    expos = pltpu.VMEM((2, tokens, labels), F32)
    rows = [pltpu.VMEM((labels, 2 * width), F32), expos]
    sums = [shape((width, labels), F32)] * 2
    estimate = functools.partial(cost, tokens=tokens, width=width, labels=labels)

    enc, gate, enct, attn, score, logit, *acc = call(
        own_kernel,
        [shape(encoded.shape, BF16), gates, turned] + per_chunk + sums,
        [encoded, beam, logit_grad, info, lengths, qc], "own_labels",
        [expos, pltpu.VMEM(beam.shape, jnp.int32), pltpu.SemaphoreType.DMA((docs + 2,))],
        estimate(4, docs), hbm=3,
    )
    gate2, enct2, attn2, score2, logit2, keep, send = call(
        other_kernel, [gates, turned] + per_chunk + halves,
        [info, lengths2, beam2, grad2, encoded2, qc, *acc], "own_labels_other_docs",
        rows, estimate(4, docs),
    )
    received = swap(send, ay)
    far_attn, far_score, far_logit, far_attn2, far_score2, far_logit2, *far = call(
        far_kernel, per_chunk + per_chunk + [block] * GROUP,
        [info, lengths, lengths2, gate, gate2, enc, encoded2, enct, enct2, far_qc],
        "far_labels", rows, estimate(4, 2 * docs),
    )

    far, keep, received = lax.optimization_barrier((far, keep, received))
    keep, send = add([keep, received], [F32, BF16])
    far, send = lax.optimization_barrier((far, send))
    received = [swap(x, ax | mask) for x, mask in zip(far, turns)]
    near = swap(send, az)
    state2 = state_grad(
        info, gate2,
        [(attn2, score2, qc, logit2), (far_attn2, far_score2, far_qc, far_logit2)], [],
    )
    received, state2, near = lax.optimization_barrier((received, state2, near))
    state_in = swap(state2, core)
    (own,) = add([keep, near, *received], [BF16])
    far_attn, far_score, own = lax.optimization_barrier((far_attn, far_score, own))
    state, logits = state_grad(
        info, gate, [(attn, score, qc, logit), (far_attn, far_score, far_qc, far_logit)],
        [state_in],
    )
    received, state = lax.optimization_barrier((swap(own, azz), state))
    (own,) = add([own, received], [BF16])
    if reps > 8:
        members = [[i * 8 + j for i in range(reps // 8)] for j in range(8)]
        own = lax.psum(own.astype(F32), "rep", axis_index_groups=members).astype(BF16)

    label_grad = to_rows(info, [own] + [swap(own, mask) for mask in turns[1:]])
    return logits, state, label_grad


def solution(mesh):
    reps, blks = mesh.shape["rep"], mesh.shape["blk"]
    assert blks == 4 and reps >= 8 and reps & (reps - 1) == 0
    in_specs = (
        P(("rep", "blk"), None, None),
        P("blk", None),
        P("blk", None),
        P(("rep", "blk")),
        P(("rep", "blk"), None),
        P(("rep", "blk"), None),
    )
    out_specs = (P(("rep", "blk"), None), P(("rep", "blk"), None, None), P("blk", None))
    return jax.shard_map(
        functools.partial(per_device, reps, blks),
        mesh=mesh, in_specs=in_specs, out_specs=out_specs, check_vma=False,
    )
```

```python
import functools

import jax
import jax.numpy as jnp
from jax import lax
from jax.experimental import pallas as pl
from jax.experimental.pallas import tpu as pltpu
from jax.sharding import PartitionSpec as P

F32 = jnp.float32
BF16 = jnp.bfloat16
VMEM = pl.BlockSpec(memory_space=pltpu.VMEM)
SMEM = pl.BlockSpec(memory_space=pltpu.SMEM)
HBM = pl.BlockSpec(memory_space=pltpu.HBM)
PARAMS = pltpu.CompilerParams(vmem_limit_bytes=20 * 1024 * 1024)
GROUP = 4
EXTRA = 16


def shape(dims, dtype):
    return jax.ShapeDtypeStruct(dims, dtype)


def mm(a, b):
    return jnp.dot(a, b, preferred_element_type=F32)


def cost(products, docs, tokens, width, labels):
    return pl.CostEstimate(
        flops=2 * products * docs * tokens * width * labels,
        transcendentals=docs * tokens * labels,
        bytes_accessed=4 * docs * tokens * width,
    )


def call(kernel, out_shape, ins, name, scratch=(), estimate=None, hbm=0):
    single = not isinstance(out_shape, (list, tuple))
    ins = [pltpu.with_memory_space_constraint(x, pltpu.HBM) for x in ins[:hbm]] + list(ins[hbm:])
    return pl.pallas_call(
        kernel,
        out_shape=out_shape,
        in_specs=[
            HBM if i < hbm else SMEM if x.ndim == 1 else VMEM for i, x in enumerate(ins)
        ],
        out_specs=VMEM if single else [VMEM] * len(out_shape),
        scratch_shapes=scratch,
        compiler_params=PARAMS,
        cost_estimate=estimate,
        name=name,
    )(*ins)


def lanes_of(info_ref, k, labels):
    return pl.ds(pl.multiple_of((info_ref[0] ^ k) * labels, labels), labels)


def label_chunk(docs, q, c, lanes, sums):
    qt = q.T
    ct = c.T.astype(F32)
    labels = q.shape[0]

    def products(doc):
        load, enc_ref, enct_ref, gate_ref = doc[:4]
        load()
        enc = enc_ref[...]
        g = gate_ref[:, lanes]
        return g, mm(enc, qt), mm(enc, (ct * g).astype(BF16))

    query_grad, class_grad = sums
    ahead = products(docs[0])
    for i, (_, _, enct_ref, _, length, attn_ref, score_ref, logit_ref) in enumerate(docs):
        g, scores, attn_grad = ahead
        if i + 1 < len(docs):
            ahead = products(docs[i + 1])
        token = lax.broadcasted_iota(jnp.int32, scores.shape, 0)
        expo = jnp.where(token < length, jnp.exp(scores), 0.0)
        attn = expo * (1.0 / jnp.sum(expo, axis=0, keepdims=True))
        attn_b = attn.astype(BF16)
        attn_ref[...] = attn_b
        inner = jnp.sum(attn * attn_grad, axis=0, keepdims=True)
        score_grad = (attn * (attn_grad - inner)).astype(BF16)
        score_ref[...] = score_grad
        enct = enct_ref[...]
        context = mm(enct, attn_b)
        logit_ref[...] = jnp.sum(context * ct, axis=0, keepdims=True)
        part = context * g
        class_grad = part if class_grad is None else class_grad + part
        part = mm(enct, score_grad)
        query_grad = part if query_grad is None else query_grad + part
    return query_grad, class_grad


def doc_list(loads, enc_ref, enct_ref, gate_ref, lens_ref, attn_ref, score_ref, logit_ref):
    return [
        (loads[d], enc_ref.at[d], enct_ref.at[d], gate_ref.at[d : d + 1], lens_ref[d],
         attn_ref.at[d], score_ref.at[d], logit_ref.at[d : d + 1])
        for d in range(enc_ref.shape[0])
    ]


def turn_around(enc_ref, enct_ref, copies=None):
    def load(d):
        if copies is not None:
            copies[d].wait()
        enct_ref[d] = enc_ref[d].T

    return [functools.partial(load, d) for d in range(enc_ref.shape[0])]


def pack_kernel(q_in, c_in, qc_ref, sem):
    copies = [pltpu.make_async_copy(x, qc_ref.at[i], sem.at[i]) for i, x in enumerate((q_in, c_in))]
    for copy in copies:
        copy.start()
    for copy in copies:
        copy.wait()


def own_kernel(enc_in, beam_in, grad_in, info_ref, lens_ref, qc_ref, enc_ref, gate_ref, enct_ref,
               attn_ref, score_ref, logit_ref, qsum_ref, csum_ref, beam_ref, sem):
    docs = enc_ref.shape[0]
    small = [(beam_in, beam_ref), (grad_in, gate_ref)]
    small = [pltpu.make_async_copy(x, y, sem.at[docs + i]) for i, (x, y) in enumerate(small)]
    copies = [
        pltpu.make_async_copy(enc_in.at[d], enc_ref.at[d], sem.at[d]) for d in range(docs)
    ]
    for copy in copies[:1] + small + copies[1:]:
        copy.start()
    loads = turn_around(enc_ref, enct_ref, copies)

    def first_load():
        load()
        for copy in small:
            copy.wait()
        gate_ref[...] = gate_ref[...] * beam_ref[...].astype(F32)

    load, loads[0] = loads[0], first_load
    qsum_ref[...], csum_ref[...] = label_chunk(
        doc_list(loads, enc_ref, enct_ref, gate_ref, lens_ref, attn_ref, score_ref, logit_ref),
        qc_ref[0], qc_ref[1], lanes_of(info_ref, 0, qc_ref.shape[1]), (None, None),
    )


def to_blocks(info_ref, sums, rows_ref, out_refs):
    query_grad, class_grad = sums
    width = query_grad.shape[0]
    rows_ref[:, :width] = query_grad.T
    rows_ref[:, width:] = class_grad.T
    size = rows_ref.shape[0] // GROUP
    count = GROUP // len(out_refs)
    for i in range(GROUP):
        ref = out_refs[i // count]
        block = rows_ref[pl.ds(pl.multiple_of((info_ref[1] ^ i) * size, size), size), :]
        ref[(i % count) * size : (i % count + 1) * size, :] = block.astype(ref.dtype)


def other_kernel(info_ref, lens_ref, beam_ref, grad_ref, enc_ref, qc_ref, qsum_ref, csum_ref,
                 gate_ref, enct_ref, attn_ref, score_ref, logit_ref, *refs):
    gate_ref[...] = grad_ref[...] * beam_ref[...].astype(F32)
    sums = label_chunk(
        doc_list(turn_around(enc_ref, enct_ref), enc_ref, enct_ref, gate_ref, lens_ref,
                 attn_ref, score_ref, logit_ref),
        qc_ref[0], qc_ref[1], lanes_of(info_ref, 0, qc_ref.shape[1]),
        (qsum_ref[...], csum_ref[...]),
    )
    to_blocks(info_ref, sums, refs[-1], refs[:-1])


def far_kernel(info_ref, lens_ref, lens2_ref, gate_ref, gate2_ref, enc_ref, enc2_ref, enct_ref,
               enct2_ref, qc_ref, attn_ref, score_ref, logit_ref, attn2_ref, score2_ref,
               logit2_ref, *refs):
    loads = [lambda: None] * enc_ref.shape[0]
    sums = label_chunk(
        doc_list(loads, enc_ref, enct_ref, gate_ref, lens_ref, attn_ref, score_ref, logit_ref)
        + doc_list(loads, enc2_ref, enct2_ref, gate2_ref, lens2_ref, attn2_ref, score2_ref,
                   logit2_ref),
        qc_ref[0], qc_ref[1], lanes_of(info_ref, 2, qc_ref.shape[1]), (None, None),
    )
    to_blocks(info_ref, sums, refs[-1], refs[:-1])


def state_parts(ks, info_ref, gate_ref, chunks):
    docs, labels = gate_ref.shape[0], chunks[2].shape[1]
    ctx_grads = []
    for n, k in enumerate(ks):
        gate = gate_ref[:, lanes_of(info_ref, k, labels)]
        gate = jnp.concatenate([gate, jnp.zeros((128 - docs, labels), F32)], axis=0).T
        c = chunks[4 * n + 2][1].astype(F32)
        ctx_grads.append([(c * gate[:, d : d + 1]).astype(BF16) for d in range(docs)])
    for d in range(docs):
        total = None
        for n in range(len(ks)):
            attn_ref, score_ref, qc_ref = chunks[4 * n : 4 * n + 3]
            part = mm(attn_ref[d], ctx_grads[n][d]) + mm(score_ref[d], qc_ref[0])
            total = part if total is None else total + part
        yield d, total


def away_kernel(ks, info_ref, gate_ref, *refs):
    chunks, out_ref = refs[:-1], refs[-1]
    tokens, labels = chunks[0].shape[1:]
    for d, total in state_parts(ks, info_ref, gate_ref, chunks):
        out_ref[d, :tokens] = total.astype(BF16)
        for n in range(len(ks)):
            logit = chunks[4 * n + 3][d : d + 1, :]
            high = logit.astype(BF16).astype(F32)
            pad = jnp.zeros((EXTRA - 2, labels), F32)
            pair = jnp.concatenate([high, logit - high, pad], axis=0)
            out_ref[d, tokens:, n * labels : (n + 1) * labels] = pair.astype(BF16)


def home_kernel(ks, info_ref, gate_ref, *refs):
    chunks, (in_ref, out_ref, logit_ref, done_ref, sem) = refs[:-5], refs[-5:]
    tokens, labels = chunks[0].shape[1:]
    copies = []
    for d, total in state_parts(ks, info_ref, gate_ref, chunks):
        done_ref[d] = (total + in_ref[d, :tokens].astype(F32)).astype(BF16)
        copies.append(pltpu.make_async_copy(done_ref.at[d], out_ref.at[d], sem.at[d]))
        copies[-1].start()
        for n, k in enumerate(ks):
            pair = in_ref[d, tokens:, n * labels : (n + 1) * labels].astype(F32)
            logit_ref[d : d + 1, lanes_of(info_ref, k, labels)] = chunks[4 * n + 3][d : d + 1, :]
            logit_ref[d : d + 1, lanes_of(info_ref, k ^ 1, labels)] = pair[0:1] + pair[1:2]
    for copy in copies:
        copy.wait()


def state_grad(info, gate, parts, more):
    docs, tokens, labels = parts[0][0].shape
    width = parts[0][2].shape[2]
    ins = [info, gate, *parts[0], *parts[1], *more]
    estimate = cost(4, docs, tokens, width, labels)
    if not more:
        out = shape((docs, tokens + EXTRA, width), BF16)
        return call(functools.partial(away_kernel, (0, 2)), out, ins, "state_away", (), estimate)
    out = shape((docs, tokens, width), BF16)
    return pl.pallas_call(
        functools.partial(home_kernel, (0, 2)),
        out_shape=[out, shape(gate.shape, F32)],
        in_specs=[SMEM] + [VMEM] * (len(ins) - 1),
        out_specs=[pl.BlockSpec(memory_space=pl.ANY), VMEM],
        scratch_shapes=[pltpu.VMEM(out.shape, BF16), pltpu.SemaphoreType.DMA((docs,))],
        compiler_params=PARAMS,
        cost_estimate=estimate,
        name="state_home",
    )(*ins)


def add_kernel(count, *refs):
    total = refs[0][...].astype(F32)
    for ref in refs[1:count]:
        total = total + ref[...].astype(F32)
    size = refs[count].shape[0]
    for i, ref in enumerate(refs[count:]):
        ref[...] = total[i * size : (i + 1) * size].astype(ref.dtype)


def add(arrays, dtypes):
    rows, cols = arrays[0].shape
    out = [shape((rows // len(dtypes), cols), dtype) for dtype in dtypes]
    return call(functools.partial(add_kernel, len(arrays)), out, arrays, "add")


def rows_kernel(info_ref, *refs):
    block_refs, (out_ref, rows_ref, sem) = refs[:-3], refs[-3:]
    size = block_refs[0].shape[0]
    copies = []
    for i, ref in enumerate(block_refs):
        rows_ref[i] = ref[...].astype(F32)
        to = pl.ds(pl.multiple_of((info_ref[1] ^ i) * size, size), size)
        copies.append(pltpu.make_async_copy(rows_ref.at[i], out_ref.at[to], sem.at[i]))
        copies[-1].start()
    for copy in copies:
        copy.wait()


def to_rows(info, blocks):
    count = len(blocks)
    rows, cols = blocks[0].shape
    return pl.pallas_call(
        rows_kernel,
        out_shape=shape((count * rows, cols), F32),
        in_specs=[SMEM] + [VMEM] * count,
        out_specs=pl.BlockSpec(memory_space=pl.ANY),
        scratch_shapes=[pltpu.VMEM((count, rows, cols), F32), pltpu.SemaphoreType.DMA((count,))],
        compiler_params=PARAMS,
        name="to_rows",
    )(info, *blocks)


def per_device(reps, blks, encoded, queries, classifiers, lengths, beam, logit_grad):
    labels, width = queries.shape
    docs, tokens, _ = encoded.shape
    total = reps * blks
    blk, rep = lax.axis_index("blk"), lax.axis_index("rep")
    info = jnp.stack([blk, (rep & 1) * 2 + ((rep >> 1) & 1)]).astype(jnp.int32)

    def swap(x, mask):
        return lax.ppermute(x, ("rep", "blk"), [(i, i ^ mask) for i in range(total)])

    core, ax = 1, 2
    ay, az, azz = blks, 2 * blks, 4 * blks
    turns = [0, az, ay, ay | az]

    qc = call(
        pack_kernel, shape((2, labels, width), BF16), [queries, classifiers], "pack",
        [pltpu.SemaphoreType.DMA((2,))], hbm=2,
    )
    encoded2, qc = lax.optimization_barrier((encoded, qc))
    far_qc = swap(qc, ax)
    encoded2, beam2, grad2 = swap(encoded2, core), swap(beam, core), swap(logit_grad, core)
    lengths2 = swap(lengths, core)
    lengths = pltpu.with_memory_space_constraint(lengths, pltpu.HBM)

    per_chunk = [
        shape((docs, tokens, labels), BF16),
        shape((docs, tokens, labels), BF16),
        shape((docs, labels), F32),
    ]
    gates = shape(beam.shape, F32)
    turned = shape((docs, width, tokens), BF16)
    block = shape((labels // GROUP, 2 * width), BF16)
    halves = [shape((labels // 2, 2 * width), dtype) for dtype in (F32, BF16)]
    rows = [pltpu.VMEM((labels, 2 * width), F32)]
    sums = [shape((width, labels), F32)] * 2
    estimate = functools.partial(cost, tokens=tokens, width=width, labels=labels)

    enc, gate, enct, attn, score, logit, *acc = call(
        own_kernel,
        [shape(encoded.shape, BF16), gates, turned] + per_chunk + sums,
        [encoded, beam, logit_grad, info, lengths, qc], "own_labels",
        [pltpu.VMEM(beam.shape, jnp.int32), pltpu.SemaphoreType.DMA((docs + 2,))],
        estimate(4, docs), hbm=3,
    )
    gate2, enct2, attn2, score2, logit2, keep, send = call(
        other_kernel, [gates, turned] + per_chunk + halves,
        [info, lengths2, beam2, grad2, encoded2, qc, *acc], "own_labels_other_docs",
        rows, estimate(4, docs),
    )
    received = swap(send, ay)
    far_attn, far_score, far_logit, far_attn2, far_score2, far_logit2, *far = call(
        far_kernel, per_chunk + per_chunk + [block] * GROUP,
        [info, lengths, lengths2, gate, gate2, enc, encoded2, enct, enct2, far_qc],
        "far_labels", rows, estimate(4, 2 * docs),
    )

    far, keep, received = lax.optimization_barrier((far, keep, received))
    keep, send = add([keep, received], [F32, BF16])
    far, send = lax.optimization_barrier((far, send))
    received = [swap(x, ax | mask) for x, mask in zip(far, turns)]
    near = swap(send, az)
    state2 = state_grad(
        info, gate2,
        [(attn2, score2, qc, logit2), (far_attn2, far_score2, far_qc, far_logit2)], [],
    )
    received, state2, near = lax.optimization_barrier((received, state2, near))
    state_in = swap(state2, core)
    (own,) = add([keep, near, *received], [BF16])
    far_attn, far_score, own = lax.optimization_barrier((far_attn, far_score, own))
    state, logits = state_grad(
        info, gate, [(attn, score, qc, logit), (far_attn, far_score, far_qc, far_logit)],
        [state_in],
    )
    received, state = lax.optimization_barrier((swap(own, azz), state))
    (own,) = add([own, received], [BF16])
    if reps > 8:
        members = [[i * 8 + j for i in range(reps // 8)] for j in range(8)]
        own = lax.psum(own.astype(F32), "rep", axis_index_groups=members).astype(BF16)

    label_grad = to_rows(info, [own] + [swap(own, mask) for mask in turns[1:]])
    return logits, state, label_grad


def solution(mesh):
    reps, blks = mesh.shape["rep"], mesh.shape["blk"]
    assert blks == 4 and reps >= 8 and reps & (reps - 1) == 0
    in_specs = (
        P(("rep", "blk"), None, None),
        P("blk", None),
        P("blk", None),
        P(("rep", "blk")),
        P(("rep", "blk"), None),
        P(("rep", "blk"), None),
    )
    out_specs = (P(("rep", "blk"), None), P(("rep", "blk"), None, None), P("blk", None))
    return jax.shard_map(
        functools.partial(per_device, reps, blks),
        mesh=mesh, in_specs=in_specs, out_specs=out_specs, check_vma=False,
    )
```

```python
import functools

import jax
import jax.numpy as jnp
from jax import lax
from jax.experimental import pallas as pl
from jax.experimental.pallas import tpu as pltpu
from jax.sharding import PartitionSpec as P

F32 = jnp.float32
BF16 = jnp.bfloat16
VMEM = pl.BlockSpec(memory_space=pltpu.VMEM)
SMEM = pl.BlockSpec(memory_space=pltpu.SMEM)
HBM = pl.BlockSpec(memory_space=pltpu.HBM)
PARAMS = pltpu.CompilerParams(vmem_limit_bytes=20 * 1024 * 1024)
GROUP = 4
EXTRA = 16


def shape(dims, dtype):
    return jax.ShapeDtypeStruct(dims, dtype)


def mm(a, b):
    return jnp.dot(a, b, preferred_element_type=F32)


def cost(products, docs, tokens, width, labels):
    return pl.CostEstimate(
        flops=2 * products * docs * tokens * width * labels,
        transcendentals=docs * tokens * labels,
        bytes_accessed=4 * docs * tokens * width,
    )


def call(kernel, out_shape, ins, name, scratch=(), estimate=None, hbm=0):
    single = not isinstance(out_shape, (list, tuple))
    ins = [pltpu.with_memory_space_constraint(x, pltpu.HBM) for x in ins[:hbm]] + list(ins[hbm:])
    return pl.pallas_call(
        kernel,
        out_shape=out_shape,
        in_specs=[
            HBM if i < hbm else SMEM if x.ndim == 1 else VMEM for i, x in enumerate(ins)
        ],
        out_specs=VMEM if single else [VMEM] * len(out_shape),
        scratch_shapes=scratch,
        compiler_params=PARAMS,
        cost_estimate=estimate,
        name=name,
    )(*ins)


def lanes_of(info_ref, k, labels):
    return pl.ds(pl.multiple_of((info_ref[0] ^ k) * labels, labels), labels)


def label_chunk(docs, q, c, lanes, sums):
    qt = q.T
    ct = c.T.astype(F32)
    labels = q.shape[0]

    def products(doc):
        load, enc_ref, enct_ref, gate_ref = doc[:4]
        load()
        enc = enc_ref[...]
        g = gate_ref[:, lanes]
        return g, mm(enc, qt), mm(enc, (ct * g).astype(BF16))

    query_grad, class_grad = sums
    ahead = products(docs[0])
    for i, (_, _, enct_ref, _, length, attn_ref, score_ref, logit_ref) in enumerate(docs):
        g, scores, attn_grad = ahead
        if i + 1 < len(docs):
            ahead = products(docs[i + 1])
        token = lax.broadcasted_iota(jnp.int32, scores.shape, 0)
        expo = jnp.where(token < length, jnp.exp(scores), 0.0)
        attn = expo * (1.0 / jnp.sum(expo, axis=0, keepdims=True))
        attn_b = attn.astype(BF16)
        attn_ref[...] = attn_b
        inner = jnp.sum(attn * attn_grad, axis=0, keepdims=True)
        score_grad = (attn * (attn_grad - inner)).astype(BF16)
        score_ref[...] = score_grad
        enct = enct_ref[...]
        context = mm(enct, attn_b)
        logit_ref[...] = jnp.sum(context * ct, axis=0, keepdims=True)
        part = context * g
        class_grad = part if class_grad is None else class_grad + part
        part = mm(enct, score_grad)
        query_grad = part if query_grad is None else query_grad + part
    return query_grad, class_grad


def doc_list(loads, enc_ref, enct_ref, gate_ref, lens_ref, attn_ref, score_ref, logit_ref):
    return [
        (loads[d], enc_ref.at[d], enct_ref.at[d], gate_ref.at[d : d + 1], lens_ref[d],
         attn_ref.at[d], score_ref.at[d], logit_ref.at[d : d + 1])
        for d in range(enc_ref.shape[0])
    ]


def turn_around(enc_ref, enct_ref, copies=None):
    def load(d):
        if copies is not None:
            copies[d].wait()
        enct_ref[d] = enc_ref[d].T

    return [functools.partial(load, d) for d in range(enc_ref.shape[0])]


def pack_kernel(q_in, c_in, qc_ref, sem):
    copies = [pltpu.make_async_copy(x, qc_ref.at[i], sem.at[i]) for i, x in enumerate((q_in, c_in))]
    for copy in copies:
        copy.start()
    for copy in copies:
        copy.wait()


def own_kernel(enc_in, beam_in, grad_in, info_ref, lens_ref, qc_ref, enc_ref, gate_ref, enct_ref,
               attn_ref, score_ref, logit_ref, qsum_ref, csum_ref, beam_ref, sem):
    docs = enc_ref.shape[0]
    small = [(beam_in, beam_ref), (grad_in, gate_ref)]
    small = [pltpu.make_async_copy(x, y, sem.at[docs + i]) for i, (x, y) in enumerate(small)]
    copies = [
        pltpu.make_async_copy(enc_in.at[d], enc_ref.at[d], sem.at[d]) for d in range(docs)
    ]
    for copy in copies[:1] + small + copies[1:]:
        copy.start()
    loads = turn_around(enc_ref, enct_ref, copies)

    def first_load():
        load()
        for copy in small:
            copy.wait()
        gate_ref[...] = gate_ref[...] * beam_ref[...].astype(F32)

    load, loads[0] = loads[0], first_load
    qsum_ref[...], csum_ref[...] = label_chunk(
        doc_list(loads, enc_ref, enct_ref, gate_ref, lens_ref, attn_ref, score_ref, logit_ref),
        qc_ref[0], qc_ref[1], lanes_of(info_ref, 0, qc_ref.shape[1]), (None, None),
    )


def to_blocks(info_ref, sums, rows_ref, out_refs):
    query_grad, class_grad = sums
    width = query_grad.shape[0]
    rows_ref[:, :width] = query_grad.T
    rows_ref[:, width:] = class_grad.T
    size = rows_ref.shape[0] // GROUP
    count = GROUP // len(out_refs)
    for i in range(GROUP):
        ref = out_refs[i // count]
        block = rows_ref[pl.ds(pl.multiple_of((info_ref[1] ^ i) * size, size), size), :]
        ref[(i % count) * size : (i % count + 1) * size, :] = block.astype(ref.dtype)


def other_kernel(info_ref, lens_ref, beam_ref, grad_ref, enc_ref, qc_ref, qsum_ref, csum_ref,
                 gate_ref, enct_ref, attn_ref, score_ref, logit_ref, *refs):
    gate_ref[...] = grad_ref[...] * beam_ref[...].astype(F32)
    sums = label_chunk(
        doc_list(turn_around(enc_ref, enct_ref), enc_ref, enct_ref, gate_ref, lens_ref,
                 attn_ref, score_ref, logit_ref),
        qc_ref[0], qc_ref[1], lanes_of(info_ref, 0, qc_ref.shape[1]),
        (qsum_ref[...], csum_ref[...]),
    )
    to_blocks(info_ref, sums, refs[-1], refs[:-1])


def far_kernel(info_ref, lens_ref, lens2_ref, gate_ref, gate2_ref, enc_ref, enc2_ref, enct_ref,
               enct2_ref, qc_ref, attn_ref, score_ref, logit_ref, attn2_ref, score2_ref,
               logit2_ref, *refs):
    loads = [lambda: None] * enc_ref.shape[0]
    sums = label_chunk(
        doc_list(loads, enc_ref, enct_ref, gate_ref, lens_ref, attn_ref, score_ref, logit_ref)
        + doc_list(loads, enc2_ref, enct2_ref, gate2_ref, lens2_ref, attn2_ref, score2_ref,
                   logit2_ref),
        qc_ref[0], qc_ref[1], lanes_of(info_ref, 2, qc_ref.shape[1]), (None, None),
    )
    to_blocks(info_ref, sums, refs[-1], refs[:-1])


def state_parts(ks, info_ref, gate_ref, chunks):
    docs, labels = gate_ref.shape[0], chunks[2].shape[1]
    ctx_grads = []
    for n, k in enumerate(ks):
        gate = gate_ref[:, lanes_of(info_ref, k, labels)]
        gate = jnp.concatenate([gate, jnp.zeros((128 - docs, labels), F32)], axis=0).T
        c = chunks[4 * n + 2][1].astype(F32)
        ctx_grads.append([(c * gate[:, d : d + 1]).astype(BF16) for d in range(docs)])
    for d in range(docs):
        total = None
        for n in range(len(ks)):
            attn_ref, score_ref, qc_ref = chunks[4 * n : 4 * n + 3]
            part = mm(attn_ref[d], ctx_grads[n][d]) + mm(score_ref[d], qc_ref[0])
            total = part if total is None else total + part
        yield d, total


def away_kernel(ks, info_ref, gate_ref, *refs):
    chunks, out_ref = refs[:-1], refs[-1]
    tokens, labels = chunks[0].shape[1:]
    for d, total in state_parts(ks, info_ref, gate_ref, chunks):
        out_ref[d, :tokens] = total.astype(BF16)
        for n in range(len(ks)):
            logit = chunks[4 * n + 3][d : d + 1, :]
            high = logit.astype(BF16).astype(F32)
            pad = jnp.zeros((EXTRA - 2, labels), F32)
            pair = jnp.concatenate([high, logit - high, pad], axis=0)
            out_ref[d, tokens:, n * labels : (n + 1) * labels] = pair.astype(BF16)


def home_kernel(ks, info_ref, gate_ref, *refs):
    chunks, (in_ref, out_ref, logit_ref, done_ref, sem) = refs[:-5], refs[-5:]
    tokens, labels = chunks[0].shape[1:]
    copies = []
    for d, total in state_parts(ks, info_ref, gate_ref, chunks):
        done_ref[d] = (total + in_ref[d, :tokens].astype(F32)).astype(BF16)
        copies.append(pltpu.make_async_copy(done_ref.at[d], out_ref.at[d], sem.at[d]))
        copies[-1].start()
        for n, k in enumerate(ks):
            pair = in_ref[d, tokens:, n * labels : (n + 1) * labels].astype(F32)
            logit_ref[d : d + 1, lanes_of(info_ref, k, labels)] = chunks[4 * n + 3][d : d + 1, :]
            logit_ref[d : d + 1, lanes_of(info_ref, k ^ 1, labels)] = pair[0:1] + pair[1:2]
    for copy in copies:
        copy.wait()


def state_grad(info, gate, parts, more):
    docs, tokens, labels = parts[0][0].shape
    width = parts[0][2].shape[2]
    ins = [info, gate, *parts[0], *parts[1], *more]
    estimate = cost(4, docs, tokens, width, labels)
    if not more:
        out = shape((docs, tokens + EXTRA, width), BF16)
        return call(functools.partial(away_kernel, (0, 2)), out, ins, "state_away", (), estimate)
    out = shape((docs, tokens, width), BF16)
    return pl.pallas_call(
        functools.partial(home_kernel, (0, 2)),
        out_shape=[out, shape(gate.shape, F32)],
        in_specs=[SMEM] + [VMEM] * (len(ins) - 1),
        out_specs=[pl.BlockSpec(memory_space=pl.ANY), VMEM],
        scratch_shapes=[pltpu.VMEM(out.shape, BF16), pltpu.SemaphoreType.DMA((docs,))],
        compiler_params=PARAMS,
        cost_estimate=estimate,
        name="state_home",
    )(*ins)


def add_kernel(count, *refs):
    total = refs[0][...].astype(F32)
    for ref in refs[1:count]:
        total = total + ref[...].astype(F32)
    size = refs[count].shape[0]
    for i, ref in enumerate(refs[count:]):
        ref[...] = total[i * size : (i + 1) * size].astype(ref.dtype)


def add(arrays, dtypes):
    rows, cols = arrays[0].shape
    out = [shape((rows // len(dtypes), cols), dtype) for dtype in dtypes]
    return call(functools.partial(add_kernel, len(arrays)), out, arrays, "add")


def rows_kernel(info_ref, *refs):
    block_refs, (out_ref, rows_ref, sem) = refs[:-3], refs[-3:]
    size = block_refs[0].shape[0]
    copies = []
    for i, ref in enumerate(block_refs):
        rows_ref[i] = ref[...].astype(F32)
        to = pl.ds(pl.multiple_of((info_ref[1] ^ i) * size, size), size)
        copies.append(pltpu.make_async_copy(rows_ref.at[i], out_ref.at[to], sem.at[i]))
        copies[-1].start()
    for copy in copies:
        copy.wait()


def to_rows(info, blocks):
    count = len(blocks)
    rows, cols = blocks[0].shape
    return pl.pallas_call(
        rows_kernel,
        out_shape=shape((count * rows, cols), F32),
        in_specs=[SMEM] + [VMEM] * count,
        out_specs=pl.BlockSpec(memory_space=pl.ANY),
        scratch_shapes=[pltpu.VMEM((count, rows, cols), F32), pltpu.SemaphoreType.DMA((count,))],
        compiler_params=PARAMS,
        name="to_rows",
    )(info, *blocks)


def per_device(reps, blks, encoded, queries, classifiers, lengths, beam, logit_grad):
    labels, width = queries.shape
    docs, tokens, _ = encoded.shape
    total = reps * blks
    blk, rep = lax.axis_index("blk"), lax.axis_index("rep")
    info = jnp.stack([blk, (rep & 1) * 2 + ((rep >> 1) & 1)]).astype(jnp.int32)

    def swap(x, mask):
        return lax.ppermute(x, ("rep", "blk"), [(i, i ^ mask) for i in range(total)])

    core, ax = 1, 2
    ay, az, azz = blks, 2 * blks, 4 * blks
    turns = [0, az, ay, ay | az]

    qc = call(
        pack_kernel, shape((2, labels, width), BF16), [queries, classifiers], "pack",
        [pltpu.SemaphoreType.DMA((2,))], hbm=2,
    )
    encoded2, qc = lax.optimization_barrier((encoded, qc))
    far_qc = swap(qc, ax)
    encoded2, beam2, grad2 = swap(encoded2, core), swap(beam, core), swap(logit_grad, core)
    lengths2 = swap(lengths, core)
    lengths = pltpu.with_memory_space_constraint(lengths, pltpu.HBM)

    per_chunk = [
        shape((docs, tokens, labels), BF16),
        shape((docs, tokens, labels), BF16),
        shape((docs, labels), F32),
    ]
    gates = shape(beam.shape, F32)
    turned = shape((docs, width, tokens), BF16)
    block = shape((labels // GROUP, 2 * width), BF16)
    halves = [shape((labels // 2, 2 * width), dtype) for dtype in (F32, BF16)]
    rows = [pltpu.VMEM((labels, 2 * width), F32)]
    sums = [shape((width, labels), F32)] * 2
    estimate = functools.partial(cost, tokens=tokens, width=width, labels=labels)

    enc, gate, enct, attn, score, logit, *acc = call(
        own_kernel,
        [shape(encoded.shape, BF16), gates, turned] + per_chunk + sums,
        [encoded, beam, logit_grad, info, lengths, qc], "own_labels",
        [pltpu.VMEM(beam.shape, jnp.int32), pltpu.SemaphoreType.DMA((docs + 2,))],
        estimate(4, docs), hbm=3,
    )
    gate2, enct2, attn2, score2, logit2, keep, send = call(
        other_kernel, [gates, turned] + per_chunk + halves,
        [info, lengths2, beam2, grad2, encoded2, qc, *acc], "own_labels_other_docs",
        rows, estimate(4, docs),
    )
    received = swap(send, ay)
    far_attn, far_score, far_logit, far_attn2, far_score2, far_logit2, *far = call(
        far_kernel, per_chunk + per_chunk + [shape(block.shape, F32)] + [block] * (GROUP - 1),
        [info, lengths, lengths2, gate, gate2, enc, encoded2, enct, enct2, far_qc],
        "far_labels", rows, estimate(4, 2 * docs),
    )

    far, keep, received = lax.optimization_barrier((far, keep, received))
    keep, send = add([keep, received], [F32, BF16])
    send, far = lax.optimization_barrier((send, far))
    relayed = swap(far[2], ay)
    received = [swap(far[3], ax | ay | az), swap(far[1], ax | az)]
    (first,) = add([far[0], relayed], [BF16])
    first, send, far_attn2 = lax.optimization_barrier((first, send, far_attn2))
    received.append(swap(first, ax))
    near = swap(send, az)
    state2 = state_grad(
        info, gate2,
        [(attn2, score2, qc, logit2), (far_attn2, far_score2, far_qc, far_logit2)], [],
    )
    received, state2, near = lax.optimization_barrier((received, state2, near))
    state_in = swap(state2, core)
    (own,) = add([keep, near, *received], [BF16])
    far_attn, far_score, own = lax.optimization_barrier((far_attn, far_score, own))
    state, logits = state_grad(
        info, gate, [(attn, score, qc, logit), (far_attn, far_score, far_qc, far_logit)],
        [state_in],
    )
    received, state = lax.optimization_barrier((swap(own, azz), state))
    (own,) = add([own, received], [BF16])
    if reps > 8:
        members = [[i * 8 + j for i in range(reps // 8)] for j in range(8)]
        own = lax.psum(own.astype(F32), "rep", axis_index_groups=members).astype(BF16)

    label_grad = to_rows(info, [own] + [swap(own, mask) for mask in turns[1:]])
    return logits, state, label_grad


def solution(mesh):
    reps, blks = mesh.shape["rep"], mesh.shape["blk"]
    assert blks == 4 and reps >= 8 and reps & (reps - 1) == 0
    in_specs = (
        P(("rep", "blk"), None, None),
        P("blk", None),
        P("blk", None),
        P(("rep", "blk")),
        P(("rep", "blk"), None),
        P(("rep", "blk"), None),
    )
    out_specs = (P(("rep", "blk"), None), P(("rep", "blk"), None, None), P("blk", None))
    return jax.shard_map(
        functools.partial(per_device, reps, blks),
        mesh=mesh, in_specs=in_specs, out_specs=out_specs, check_vma=False,
    )
```

```python
import functools

import jax
import jax.numpy as jnp
from jax import lax
from jax.experimental import pallas as pl
from jax.experimental.pallas import tpu as pltpu
from jax.sharding import PartitionSpec as P

F32 = jnp.float32
BF16 = jnp.bfloat16
VMEM = pl.BlockSpec(memory_space=pltpu.VMEM)
SMEM = pl.BlockSpec(memory_space=pltpu.SMEM)
HBM = pl.BlockSpec(memory_space=pltpu.HBM)
PARAMS = pltpu.CompilerParams(vmem_limit_bytes=20 * 1024 * 1024)
GROUP = 4
EXTRA = 16


def shape(dims, dtype):
    return jax.ShapeDtypeStruct(dims, dtype)


def mm(a, b):
    return jnp.dot(a, b, preferred_element_type=F32)


def cost(products, docs, tokens, width, labels):
    return pl.CostEstimate(
        flops=2 * products * docs * tokens * width * labels,
        transcendentals=docs * tokens * labels,
        bytes_accessed=4 * docs * tokens * width,
    )


def call(kernel, out_shape, ins, name, scratch=(), estimate=None, hbm=0):
    single = not isinstance(out_shape, (list, tuple))
    ins = [pltpu.with_memory_space_constraint(x, pltpu.HBM) for x in ins[:hbm]] + list(ins[hbm:])
    return pl.pallas_call(
        kernel,
        out_shape=out_shape,
        in_specs=[
            HBM if i < hbm else SMEM if x.ndim == 1 else VMEM for i, x in enumerate(ins)
        ],
        out_specs=VMEM if single else [VMEM] * len(out_shape),
        scratch_shapes=scratch,
        compiler_params=PARAMS,
        cost_estimate=estimate,
        name=name,
    )(*ins)


def lanes_of(info_ref, k, labels):
    return pl.ds(pl.multiple_of((info_ref[0] ^ k) * labels, labels), labels)


def label_chunk(docs, q, c, lanes, sums):
    qt = q.T
    ct = c.T.astype(F32)
    labels = q.shape[0]

    def products(doc):
        load, enc_ref, enct_ref, gate_ref = doc[:4]
        load()
        enc = enc_ref[...]
        g = gate_ref[:, lanes]
        both = mm(enc, jnp.concatenate([qt, (ct * g).astype(BF16)], axis=1))
        return g, both[:, :labels], both[:, labels:]

    query_grad, class_grad = sums
    ahead = products(docs[0])
    for i, (_, _, enct_ref, _, length, attn_ref, score_ref, logit_ref) in enumerate(docs):
        g, scores, attn_grad = ahead
        if i + 1 < len(docs):
            ahead = products(docs[i + 1])
        token = lax.broadcasted_iota(jnp.int32, scores.shape, 0)
        expo = jnp.where(token < length, jnp.exp(scores), 0.0)
        attn = expo * (1.0 / jnp.sum(expo, axis=0, keepdims=True))
        attn_b = attn.astype(BF16)
        attn_ref[...] = attn_b
        inner = jnp.sum(attn * attn_grad, axis=0, keepdims=True)
        score_grad = (attn * (attn_grad - inner)).astype(BF16)
        score_ref[...] = score_grad
        both = mm(enct_ref[...], jnp.concatenate([attn_b, score_grad], axis=1))
        context, part = both[:, :labels], both[:, labels:]
        query_grad = part if query_grad is None else query_grad + part
        logit_ref[...] = jnp.sum(context * ct, axis=0, keepdims=True)
        part = context * g
        class_grad = part if class_grad is None else class_grad + part
    return query_grad, class_grad


def doc_list(loads, enc_ref, enct_ref, gate_ref, lens_ref, attn_ref, score_ref, logit_ref):
    return [
        (loads[d], enc_ref.at[d], enct_ref.at[d], gate_ref.at[d : d + 1], lens_ref[d],
         attn_ref.at[d], score_ref.at[d], logit_ref.at[d : d + 1])
        for d in range(enc_ref.shape[0])
    ]


def turn_around(enc_ref, enct_ref, copies=None):
    def load(d):
        if copies is not None:
            copies[d].wait()
        enct_ref[d] = enc_ref[d].T

    return [functools.partial(load, d) for d in range(enc_ref.shape[0])]


def pack_kernel(q_in, c_in, qc_ref, sem):
    copies = [pltpu.make_async_copy(x, qc_ref.at[i], sem.at[i]) for i, x in enumerate((q_in, c_in))]
    for copy in copies:
        copy.start()
    for copy in copies:
        copy.wait()


def own_kernel(enc_in, beam_in, grad_in, info_ref, lens_ref, qc_ref, enc_ref, gate_ref, enct_ref,
               attn_ref, score_ref, logit_ref, qsum_ref, csum_ref, beam_ref, sem):
    docs = enc_ref.shape[0]
    small = [(beam_in, beam_ref), (grad_in, gate_ref)]
    small = [pltpu.make_async_copy(x, y, sem.at[docs + i]) for i, (x, y) in enumerate(small)]
    copies = [
        pltpu.make_async_copy(enc_in.at[d], enc_ref.at[d], sem.at[d]) for d in range(docs)
    ]
    for copy in copies[:1] + small + copies[1:]:
        copy.start()
    loads = turn_around(enc_ref, enct_ref, copies)

    def first_load():
        load()
        for copy in small:
            copy.wait()
        gate_ref[...] = gate_ref[...] * beam_ref[...].astype(F32)

    load, loads[0] = loads[0], first_load
    qsum_ref[...], csum_ref[...] = label_chunk(
        doc_list(loads, enc_ref, enct_ref, gate_ref, lens_ref, attn_ref, score_ref, logit_ref),
        qc_ref[0], qc_ref[1], lanes_of(info_ref, 0, qc_ref.shape[1]), (None, None),
    )


def to_blocks(info_ref, sums, rows_ref, out_refs):
    query_grad, class_grad = sums
    width = query_grad.shape[0]
    rows_ref[:, :width] = query_grad.T
    rows_ref[:, width:] = class_grad.T
    size = rows_ref.shape[0] // GROUP
    count = GROUP // len(out_refs)
    for i in range(GROUP):
        ref = out_refs[i // count]
        block = rows_ref[pl.ds(pl.multiple_of((info_ref[1] ^ i) * size, size), size), :]
        ref[(i % count) * size : (i % count + 1) * size, :] = block.astype(ref.dtype)


def other_kernel(info_ref, lens_ref, beam_ref, grad_ref, enc_ref, qc_ref, qsum_ref, csum_ref,
                 gate_ref, enct_ref, attn_ref, score_ref, logit_ref, *refs):
    gate_ref[...] = grad_ref[...] * beam_ref[...].astype(F32)
    sums = label_chunk(
        doc_list(turn_around(enc_ref, enct_ref), enc_ref, enct_ref, gate_ref, lens_ref,
                 attn_ref, score_ref, logit_ref),
        qc_ref[0], qc_ref[1], lanes_of(info_ref, 0, qc_ref.shape[1]),
        (qsum_ref[...], csum_ref[...]),
    )
    to_blocks(info_ref, sums, refs[-1], refs[:-1])


def far_kernel(info_ref, lens_ref, lens2_ref, gate_ref, gate2_ref, enc_ref, enc2_ref, enct_ref,
               enct2_ref, qc_ref, attn_ref, score_ref, logit_ref, attn2_ref, score2_ref,
               logit2_ref, *refs):
    loads = [lambda: None] * enc_ref.shape[0]
    sums = label_chunk(
        doc_list(loads, enc_ref, enct_ref, gate_ref, lens_ref, attn_ref, score_ref, logit_ref)
        + doc_list(loads, enc2_ref, enct2_ref, gate2_ref, lens2_ref, attn2_ref, score2_ref,
                   logit2_ref),
        qc_ref[0], qc_ref[1], lanes_of(info_ref, 2, qc_ref.shape[1]), (None, None),
    )
    to_blocks(info_ref, sums, refs[-1], refs[:-1])


def state_parts(ks, info_ref, gate_ref, chunks):
    docs, labels = gate_ref.shape[0], chunks[2].shape[1]
    ctx_grads = []
    for n, k in enumerate(ks):
        gate = gate_ref[:, lanes_of(info_ref, k, labels)]
        gate = jnp.concatenate([gate, jnp.zeros((128 - docs, labels), F32)], axis=0).T
        c = chunks[4 * n + 2][1].astype(F32)
        ctx_grads.append([(c * gate[:, d : d + 1]).astype(BF16) for d in range(docs)])
    for d in range(docs):
        total = None
        for n in range(len(ks)):
            attn_ref, score_ref, qc_ref = chunks[4 * n : 4 * n + 3]
            part = mm(attn_ref[d], ctx_grads[n][d]) + mm(score_ref[d], qc_ref[0])
            total = part if total is None else total + part
        yield d, total


def away_kernel(ks, info_ref, gate_ref, *refs):
    chunks, out_ref = refs[:-1], refs[-1]
    tokens, labels = chunks[0].shape[1:]
    for d, total in state_parts(ks, info_ref, gate_ref, chunks):
        out_ref[d, :tokens] = total.astype(BF16)
        for n in range(len(ks)):
            logit = chunks[4 * n + 3][d : d + 1, :]
            high = logit.astype(BF16).astype(F32)
            pad = jnp.zeros((EXTRA - 2, labels), F32)
            pair = jnp.concatenate([high, logit - high, pad], axis=0)
            out_ref[d, tokens:, n * labels : (n + 1) * labels] = pair.astype(BF16)


def home_kernel(ks, info_ref, gate_ref, *refs):
    chunks, (in_ref, out_ref, logit_ref, done_ref, sem) = refs[:-5], refs[-5:]
    tokens, labels = chunks[0].shape[1:]
    copies = []
    for d, total in state_parts(ks, info_ref, gate_ref, chunks):
        done_ref[d] = (total + in_ref[d, :tokens].astype(F32)).astype(BF16)
        copies.append(pltpu.make_async_copy(done_ref.at[d], out_ref.at[d], sem.at[d]))
        copies[-1].start()
        for n, k in enumerate(ks):
            pair = in_ref[d, tokens:, n * labels : (n + 1) * labels].astype(F32)
            logit_ref[d : d + 1, lanes_of(info_ref, k, labels)] = chunks[4 * n + 3][d : d + 1, :]
            logit_ref[d : d + 1, lanes_of(info_ref, k ^ 1, labels)] = pair[0:1] + pair[1:2]
    for copy in copies:
        copy.wait()


def state_grad(info, gate, parts, more):
    docs, tokens, labels = parts[0][0].shape
    width = parts[0][2].shape[2]
    ins = [info, gate, *parts[0], *parts[1], *more]
    estimate = cost(4, docs, tokens, width, labels)
    if not more:
        out = shape((docs, tokens + EXTRA, width), BF16)
        return call(functools.partial(away_kernel, (0, 2)), out, ins, "state_away", (), estimate)
    out = shape((docs, tokens, width), BF16)
    return pl.pallas_call(
        functools.partial(home_kernel, (0, 2)),
        out_shape=[out, shape(gate.shape, F32)],
        in_specs=[SMEM] + [VMEM] * (len(ins) - 1),
        out_specs=[pl.BlockSpec(memory_space=pl.ANY), VMEM],
        scratch_shapes=[pltpu.VMEM(out.shape, BF16), pltpu.SemaphoreType.DMA((docs,))],
        compiler_params=PARAMS,
        cost_estimate=estimate,
        name="state_home",
    )(*ins)


def add_kernel(count, *refs):
    total = refs[0][...].astype(F32)
    for ref in refs[1:count]:
        total = total + ref[...].astype(F32)
    size = refs[count].shape[0]
    for i, ref in enumerate(refs[count:]):
        ref[...] = total[i * size : (i + 1) * size].astype(ref.dtype)


def add(arrays, dtypes):
    rows, cols = arrays[0].shape
    out = [shape((rows // len(dtypes), cols), dtype) for dtype in dtypes]
    return call(functools.partial(add_kernel, len(arrays)), out, arrays, "add")


def rows_kernel(info_ref, *refs):
    block_refs, (out_ref, rows_ref, sem) = refs[:-3], refs[-3:]
    size = block_refs[0].shape[0]
    copies = []
    for i, ref in enumerate(block_refs):
        rows_ref[i] = ref[...].astype(F32)
        to = pl.ds(pl.multiple_of((info_ref[1] ^ i) * size, size), size)
        copies.append(pltpu.make_async_copy(rows_ref.at[i], out_ref.at[to], sem.at[i]))
        copies[-1].start()
    for copy in copies:
        copy.wait()


def to_rows(info, blocks):
    count = len(blocks)
    rows, cols = blocks[0].shape
    return pl.pallas_call(
        rows_kernel,
        out_shape=shape((count * rows, cols), F32),
        in_specs=[SMEM] + [VMEM] * count,
        out_specs=pl.BlockSpec(memory_space=pl.ANY),
        scratch_shapes=[pltpu.VMEM((count, rows, cols), F32), pltpu.SemaphoreType.DMA((count,))],
        compiler_params=PARAMS,
        name="to_rows",
    )(info, *blocks)


def per_device(reps, blks, encoded, queries, classifiers, lengths, beam, logit_grad):
    labels, width = queries.shape
    docs, tokens, _ = encoded.shape
    total = reps * blks
    blk, rep = lax.axis_index("blk"), lax.axis_index("rep")
    info = jnp.stack([blk, (rep & 1) * 2 + ((rep >> 1) & 1)]).astype(jnp.int32)

    def swap(x, mask):
        return lax.ppermute(x, ("rep", "blk"), [(i, i ^ mask) for i in range(total)])

    core, ax = 1, 2
    ay, az, azz = blks, 2 * blks, 4 * blks
    turns = [0, az, ay, ay | az]

    qc = call(
        pack_kernel, shape((2, labels, width), BF16), [queries, classifiers], "pack",
        [pltpu.SemaphoreType.DMA((2,))], hbm=2,
    )
    encoded2, qc = lax.optimization_barrier((encoded, qc))
    far_qc = swap(qc, ax)
    encoded2, beam2, grad2 = swap(encoded2, core), swap(beam, core), swap(logit_grad, core)
    lengths2 = swap(lengths, core)
    lengths = pltpu.with_memory_space_constraint(lengths, pltpu.HBM)

    per_chunk = [
        shape((docs, tokens, labels), BF16),
        shape((docs, tokens, labels), BF16),
        shape((docs, labels), F32),
    ]
    gates = shape(beam.shape, F32)
    turned = shape((docs, width, tokens), BF16)
    block = shape((labels // GROUP, 2 * width), BF16)
    halves = [shape((labels // 2, 2 * width), dtype) for dtype in (F32, BF16)]
    rows = [pltpu.VMEM((labels, 2 * width), F32)]
    sums = [shape((width, labels), F32)] * 2
    estimate = functools.partial(cost, tokens=tokens, width=width, labels=labels)

    enc, gate, enct, attn, score, logit, *acc = call(
        own_kernel,
        [shape(encoded.shape, BF16), gates, turned] + per_chunk + sums,
        [encoded, beam, logit_grad, info, lengths, qc], "own_labels",
        [pltpu.VMEM(beam.shape, jnp.int32), pltpu.SemaphoreType.DMA((docs + 2,))],
        estimate(4, docs), hbm=3,
    )
    gate2, enct2, attn2, score2, logit2, keep, send = call(
        other_kernel, [gates, turned] + per_chunk + halves,
        [info, lengths2, beam2, grad2, encoded2, qc, *acc], "own_labels_other_docs",
        rows, estimate(4, docs),
    )
    received = swap(send, ay)
    far_attn, far_score, far_logit, far_attn2, far_score2, far_logit2, *far = call(
        far_kernel, per_chunk + per_chunk + [shape(block.shape, F32)] + [block] * (GROUP - 1),
        [info, lengths, lengths2, gate, gate2, enc, encoded2, enct, enct2, far_qc],
        "far_labels", rows, estimate(4, 2 * docs),
    )

    far, keep, received = lax.optimization_barrier((far, keep, received))
    keep, send = add([keep, received], [F32, BF16])
    send, far = lax.optimization_barrier((send, far))
    relayed = swap(far[2], ay)
    received = [swap(far[3], ax | ay | az), swap(far[1], ax | az)]
    (first,) = add([far[0], relayed], [BF16])
    first, send, far_attn2 = lax.optimization_barrier((first, send, far_attn2))
    received.append(swap(first, ax))
    near = swap(send, az)
    state2 = state_grad(
        info, gate2,
        [(attn2, score2, qc, logit2), (far_attn2, far_score2, far_qc, far_logit2)], [],
    )
    received, state2, near = lax.optimization_barrier((received, state2, near))
    state_in = swap(state2, core)
    (own,) = add([keep, near, *received], [BF16])
    far_attn, far_score, own = lax.optimization_barrier((far_attn, far_score, own))
    state, logits = state_grad(
        info, gate, [(attn, score, qc, logit), (far_attn, far_score, far_qc, far_logit)],
        [state_in],
    )
    received, state = lax.optimization_barrier((swap(own, azz), state))
    (own,) = add([own, received], [BF16])
    if reps > 8:
        members = [[i * 8 + j for i in range(reps // 8)] for j in range(8)]
        own = lax.psum(own.astype(F32), "rep", axis_index_groups=members).astype(BF16)

    label_grad = to_rows(info, [own] + [swap(own, mask) for mask in turns[1:]])
    return logits, state, label_grad


def solution(mesh):
    reps, blks = mesh.shape["rep"], mesh.shape["blk"]
    assert blks == 4 and reps >= 8 and reps & (reps - 1) == 0
    in_specs = (
        P(("rep", "blk"), None, None),
        P("blk", None),
        P("blk", None),
        P(("rep", "blk")),
        P(("rep", "blk"), None),
        P(("rep", "blk"), None),
    )
    out_specs = (P(("rep", "blk"), None), P(("rep", "blk"), None, None), P("blk", None))
    return jax.shard_map(
        functools.partial(per_device, reps, blks),
        mesh=mesh, in_specs=in_specs, out_specs=out_specs, check_vma=False,
    )
```

```python
import functools

import jax
import jax.numpy as jnp
from jax import lax
from jax.experimental import pallas as pl
from jax.experimental.pallas import tpu as pltpu
from jax.sharding import PartitionSpec as P

F32 = jnp.float32
BF16 = jnp.bfloat16
VMEM = pl.BlockSpec(memory_space=pltpu.VMEM)
SMEM = pl.BlockSpec(memory_space=pltpu.SMEM)
HBM = pl.BlockSpec(memory_space=pltpu.HBM)
PARAMS = pltpu.CompilerParams(vmem_limit_bytes=20 * 1024 * 1024)
GROUP = 4
EXTRA = 16


LONG = pl.CostEstimate(flops=10**11, transcendentals=0, bytes_accessed=0)


def shape(dims, dtype):
    return jax.ShapeDtypeStruct(dims, dtype)


def mm(a, b):
    return jnp.dot(a, b, preferred_element_type=F32)


def cost(products, docs, tokens, width, labels):
    return pl.CostEstimate(
        flops=2 * products * docs * tokens * width * labels,
        transcendentals=docs * tokens * labels,
        bytes_accessed=4 * docs * tokens * width,
    )


def call(kernel, out_shape, ins, name, scratch=(), estimate=None, hbm=0):
    single = not isinstance(out_shape, (list, tuple))
    ins = [pltpu.with_memory_space_constraint(x, pltpu.HBM) for x in ins[:hbm]] + list(ins[hbm:])
    return pl.pallas_call(
        kernel,
        out_shape=out_shape,
        in_specs=[
            HBM if i < hbm else SMEM if x.ndim == 1 else VMEM for i, x in enumerate(ins)
        ],
        out_specs=VMEM if single else [VMEM] * len(out_shape),
        scratch_shapes=scratch,
        compiler_params=PARAMS,
        cost_estimate=estimate,
        name=name,
    )(*ins)


def lanes_of(info_ref, k, labels):
    return pl.ds(pl.multiple_of((info_ref[0] ^ k) * labels, labels), labels)


def label_chunk(docs, q, c, lanes, sums):
    qt = q.T
    ct = c.T.astype(F32)
    labels = q.shape[0]

    def products(doc):
        load, enc_ref, enct_ref, gate_ref = doc[:4]
        load()
        enc = enc_ref[...]
        g = gate_ref[:, lanes]
        both = mm(enc, jnp.concatenate([qt, (ct * g).astype(BF16)], axis=1))
        return g, both[:, :labels], both[:, labels:]

    query_grad, class_grad = sums
    ahead = products(docs[0])
    for i, (_, _, enct_ref, _, length, attn_ref, score_ref, logit_ref) in enumerate(docs):
        g, scores, attn_grad = ahead
        if i + 1 < len(docs):
            ahead = products(docs[i + 1])
        token = lax.broadcasted_iota(jnp.int32, scores.shape, 0)
        expo = jnp.where(token < length, jnp.exp(scores), 0.0)
        attn = expo * (1.0 / jnp.sum(expo, axis=0, keepdims=True))
        attn_b = attn.astype(BF16)
        attn_ref[...] = attn_b
        inner = jnp.sum(attn * attn_grad, axis=0, keepdims=True)
        score_grad = (attn * (attn_grad - inner)).astype(BF16)
        score_ref[...] = score_grad
        both = mm(enct_ref[...], jnp.concatenate([attn_b, score_grad], axis=1))
        context, part = both[:, :labels], both[:, labels:]
        query_grad = part if query_grad is None else query_grad + part
        logit_ref[...] = jnp.sum(context * ct, axis=0, keepdims=True)
        part = context * g
        class_grad = part if class_grad is None else class_grad + part
    return query_grad, class_grad


def doc_list(loads, enc_ref, enct_ref, gate_ref, lens_ref, attn_ref, score_ref, logit_ref):
    return [
        (loads[d], enc_ref.at[d], enct_ref.at[d], gate_ref.at[d : d + 1], lens_ref[d],
         attn_ref.at[d], score_ref.at[d], logit_ref.at[d : d + 1])
        for d in range(enc_ref.shape[0])
    ]


def turn_around(enc_ref, enct_ref, copies=None):
    def load(d):
        if copies is not None:
            copies[d].wait()
        enct_ref[d] = enc_ref[d].T

    return [functools.partial(load, d) for d in range(enc_ref.shape[0])]


def pack_kernel(q_in, c_in, qc_ref, sem):
    copies = [pltpu.make_async_copy(x, qc_ref.at[i], sem.at[i]) for i, x in enumerate((q_in, c_in))]
    for copy in copies:
        copy.start()
    for copy in copies:
        copy.wait()


def own_kernel(enc_in, beam_in, grad_in, info_ref, lens_ref, qc_ref, enc_ref, gate_ref, enct_ref,
               attn_ref, score_ref, logit_ref, qsum_ref, csum_ref, beam_ref, sem):
    docs = enc_ref.shape[0]
    small = [(beam_in, beam_ref), (grad_in, gate_ref)]
    small = [pltpu.make_async_copy(x, y, sem.at[docs + i]) for i, (x, y) in enumerate(small)]
    copies = [
        pltpu.make_async_copy(enc_in.at[d], enc_ref.at[d], sem.at[d]) for d in range(docs)
    ]
    for copy in copies[:1] + small + copies[1:]:
        copy.start()
    loads = turn_around(enc_ref, enct_ref, copies)

    def first_load():
        load()
        for copy in small:
            copy.wait()
        gate_ref[...] = gate_ref[...] * beam_ref[...].astype(F32)

    load, loads[0] = loads[0], first_load
    qsum_ref[...], csum_ref[...] = label_chunk(
        doc_list(loads, enc_ref, enct_ref, gate_ref, lens_ref, attn_ref, score_ref, logit_ref),
        qc_ref[0], qc_ref[1], lanes_of(info_ref, 0, qc_ref.shape[1]), (None, None),
    )


def to_blocks(info_ref, sums, rows_ref, out_refs):
    query_grad, class_grad = sums
    width = query_grad.shape[0]
    rows_ref[:, :width] = query_grad.T
    rows_ref[:, width:] = class_grad.T
    size = rows_ref.shape[0] // GROUP
    count = GROUP // len(out_refs)
    for i in range(GROUP):
        ref = out_refs[i // count]
        block = rows_ref[pl.ds(pl.multiple_of((info_ref[1] ^ i) * size, size), size), :]
        ref[(i % count) * size : (i % count + 1) * size, :] = block.astype(ref.dtype)


def other_kernel(info_ref, lens_ref, beam_ref, grad_ref, enc_ref, qc_ref, qsum_ref, csum_ref,
                 gate_ref, enct_ref, attn_ref, score_ref, logit_ref, *refs):
    gate_ref[...] = grad_ref[...] * beam_ref[...].astype(F32)
    sums = label_chunk(
        doc_list(turn_around(enc_ref, enct_ref), enc_ref, enct_ref, gate_ref, lens_ref,
                 attn_ref, score_ref, logit_ref),
        qc_ref[0], qc_ref[1], lanes_of(info_ref, 0, qc_ref.shape[1]),
        (qsum_ref[...], csum_ref[...]),
    )
    to_blocks(info_ref, sums, refs[-1], refs[:-1])


def far_kernel(info_ref, lens_ref, lens2_ref, gate_ref, gate2_ref, enc_ref, enc2_ref, enct_ref,
               enct2_ref, qc_ref, attn_ref, score_ref, logit_ref, attn2_ref, score2_ref,
               logit2_ref, *refs):
    loads = [lambda: None] * enc_ref.shape[0]
    sums = label_chunk(
        doc_list(loads, enc_ref, enct_ref, gate_ref, lens_ref, attn_ref, score_ref, logit_ref)
        + doc_list(loads, enc2_ref, enct2_ref, gate2_ref, lens2_ref, attn2_ref, score2_ref,
                   logit2_ref),
        qc_ref[0], qc_ref[1], lanes_of(info_ref, 2, qc_ref.shape[1]), (None, None),
    )
    to_blocks(info_ref, sums, refs[-1], refs[:-1])


def state_parts(ks, info_ref, gate_ref, chunks):
    docs, labels = gate_ref.shape[0], chunks[2].shape[1]
    ctx_grads = []
    for n, k in enumerate(ks):
        gate = gate_ref[:, lanes_of(info_ref, k, labels)]
        gate = jnp.concatenate([gate, jnp.zeros((128 - docs, labels), F32)], axis=0).T
        c = chunks[4 * n + 2][1].astype(F32)
        ctx_grads.append([(c * gate[:, d : d + 1]).astype(BF16) for d in range(docs)])
    for d in range(docs):
        total = None
        for n in range(len(ks)):
            attn_ref, score_ref, qc_ref = chunks[4 * n : 4 * n + 3]
            part = mm(attn_ref[d], ctx_grads[n][d]) + mm(score_ref[d], qc_ref[0])
            total = part if total is None else total + part
        yield d, total


def away_kernel(ks, info_ref, gate_ref, *refs):
    chunks, out_ref = refs[:-1], refs[-1]
    tokens, labels = chunks[0].shape[1:]
    for d, total in state_parts(ks, info_ref, gate_ref, chunks):
        out_ref[d, :tokens] = total.astype(BF16)
        for n in range(len(ks)):
            logit = chunks[4 * n + 3][d : d + 1, :]
            high = logit.astype(BF16).astype(F32)
            pad = jnp.zeros((EXTRA - 2, labels), F32)
            pair = jnp.concatenate([high, logit - high, pad], axis=0)
            out_ref[d, tokens:, n * labels : (n + 1) * labels] = pair.astype(BF16)


def home_kernel(ks, info_ref, gate_ref, *refs):
    chunks, (in_ref, out_ref, logit_ref, done_ref, sem) = refs[:-5], refs[-5:]
    tokens, labels = chunks[0].shape[1:]
    copies = []
    for d, total in state_parts(ks, info_ref, gate_ref, chunks):
        done_ref[d] = (total + in_ref[d, :tokens].astype(F32)).astype(BF16)
        copies.append(pltpu.make_async_copy(done_ref.at[d], out_ref.at[d], sem.at[d]))
        copies[-1].start()
        for n, k in enumerate(ks):
            pair = in_ref[d, tokens:, n * labels : (n + 1) * labels].astype(F32)
            logit_ref[d : d + 1, lanes_of(info_ref, k, labels)] = chunks[4 * n + 3][d : d + 1, :]
            logit_ref[d : d + 1, lanes_of(info_ref, k ^ 1, labels)] = pair[0:1] + pair[1:2]
    for copy in copies:
        copy.wait()


def state_grad(info, gate, parts, more):
    docs, tokens, labels = parts[0][0].shape
    width = parts[0][2].shape[2]
    ins = [info, gate, *parts[0], *parts[1], *more]
    estimate = cost(4, docs, tokens, width, labels)
    if not more:
        out = shape((docs, tokens + EXTRA, width), BF16)
        return call(functools.partial(away_kernel, (0, 2)), out, ins, "state_away", (), estimate)
    out = shape((docs, tokens, width), BF16)
    return pl.pallas_call(
        functools.partial(home_kernel, (0, 2)),
        out_shape=[out, shape(gate.shape, F32)],
        in_specs=[SMEM] + [VMEM] * (len(ins) - 1),
        out_specs=[pl.BlockSpec(memory_space=pl.ANY), VMEM],
        scratch_shapes=[pltpu.VMEM(out.shape, BF16), pltpu.SemaphoreType.DMA((docs,))],
        compiler_params=PARAMS,
        cost_estimate=estimate,
        name="state_home",
    )(*ins)


def add_kernel(count, *refs):
    total = refs[0][...].astype(F32)
    for ref in refs[1:count]:
        total = total + ref[...].astype(F32)
    size = refs[count].shape[0]
    for i, ref in enumerate(refs[count:]):
        ref[...] = total[i * size : (i + 1) * size].astype(ref.dtype)


def add(arrays, dtypes, estimate=None):
    rows, cols = arrays[0].shape
    out = [shape((rows // len(dtypes), cols), dtype) for dtype in dtypes]
    return call(
        functools.partial(add_kernel, len(arrays)), out, arrays, "add", estimate=estimate
    )


def rows_kernel(info_ref, *refs):
    block_refs, (out_ref, rows_ref, sem) = refs[:-3], refs[-3:]
    size = block_refs[0].shape[0]
    copies = []
    for i, ref in enumerate(block_refs):
        rows_ref[i] = ref[...].astype(F32)
        to = pl.ds(pl.multiple_of((info_ref[1] ^ i) * size, size), size)
        copies.append(pltpu.make_async_copy(rows_ref.at[i], out_ref.at[to], sem.at[i]))
        copies[-1].start()
    for copy in copies:
        copy.wait()


def to_rows(info, blocks):
    count = len(blocks)
    rows, cols = blocks[0].shape
    return pl.pallas_call(
        rows_kernel,
        out_shape=shape((count * rows, cols), F32),
        in_specs=[SMEM] + [VMEM] * count,
        out_specs=pl.BlockSpec(memory_space=pl.ANY),
        scratch_shapes=[pltpu.VMEM((count, rows, cols), F32), pltpu.SemaphoreType.DMA((count,))],
        compiler_params=PARAMS,
        name="to_rows",
    )(info, *blocks)


def per_device(reps, blks, encoded, queries, classifiers, lengths, beam, logit_grad):
    labels, width = queries.shape
    docs, tokens, _ = encoded.shape
    total = reps * blks
    blk, rep = lax.axis_index("blk"), lax.axis_index("rep")
    info = jnp.stack([blk, (rep & 1) * 2 + ((rep >> 1) & 1)]).astype(jnp.int32)

    def swap(x, mask):
        return lax.ppermute(x, ("rep", "blk"), [(i, i ^ mask) for i in range(total)])

    core, ax = 1, 2
    ay, az, azz = blks, 2 * blks, 4 * blks
    turns = [0, az, ay, ay | az]

    qc = call(
        pack_kernel, shape((2, labels, width), BF16), [queries, classifiers], "pack",
        [pltpu.SemaphoreType.DMA((2,))], hbm=2,
    )
    encoded2, qc = lax.optimization_barrier((encoded, qc))
    far_qc = swap(qc, ax)
    encoded2, beam2, grad2 = swap(encoded2, core), swap(beam, core), swap(logit_grad, core)
    lengths2 = swap(lengths, core)
    lengths = pltpu.with_memory_space_constraint(lengths, pltpu.HBM)

    per_chunk = [
        shape((docs, tokens, labels), BF16),
        shape((docs, tokens, labels), BF16),
        shape((docs, labels), F32),
    ]
    gates = shape(beam.shape, F32)
    turned = shape((docs, width, tokens), BF16)
    block = shape((labels // GROUP, 2 * width), BF16)
    halves = [shape((labels // 2, 2 * width), dtype) for dtype in (F32, BF16)]
    rows = [pltpu.VMEM((labels, 2 * width), F32)]
    sums = [shape((width, labels), F32)] * 2
    estimate = functools.partial(cost, tokens=tokens, width=width, labels=labels)

    enc, gate, enct, attn, score, logit, *acc = call(
        own_kernel,
        [shape(encoded.shape, BF16), gates, turned] + per_chunk + sums,
        [encoded, beam, logit_grad, info, lengths, qc], "own_labels",
        [pltpu.VMEM(beam.shape, jnp.int32), pltpu.SemaphoreType.DMA((docs + 2,))],
        estimate(4, docs), hbm=3,
    )
    gate2, enct2, attn2, score2, logit2, keep, send = call(
        other_kernel, [gates, turned] + per_chunk + halves,
        [info, lengths2, beam2, grad2, encoded2, qc, *acc], "own_labels_other_docs",
        rows, estimate(4, docs),
    )
    received = swap(send, ay)
    far_attn, far_score, far_logit, far_attn2, far_score2, far_logit2, *far = call(
        far_kernel, per_chunk + per_chunk + [shape(block.shape, F32)] + [block] * (GROUP - 1),
        [info, lengths, lengths2, gate, gate2, enc, encoded2, enct, enct2, far_qc],
        "far_labels", rows, estimate(4, 2 * docs),
    )

    far, keep, received = lax.optimization_barrier((far, keep, received))
    keep, send = add([keep, received], [F32, BF16])
    send, far = lax.optimization_barrier((send, far))
    relayed = swap(far[2], ay)
    received = [swap(far[3], ax | ay | az), swap(far[1], ax | az)]
    (first,) = add([far[0], relayed], [BF16])
    first, send, far_attn2 = lax.optimization_barrier((first, send, far_attn2))
    received.append(swap(first, ax))
    near = swap(send, az)
    state2 = state_grad(
        info, gate2,
        [(attn2, score2, qc, logit2), (far_attn2, far_score2, far_qc, far_logit2)], [],
    )
    received, near = lax.optimization_barrier((received, near))
    state_in = swap(state2, core)
    (own,) = add([keep, near, *received], [BF16], LONG)
    far_attn, far_score, own = lax.optimization_barrier((far_attn, far_score, own))
    state, logits = state_grad(
        info, gate, [(attn, score, qc, logit), (far_attn, far_score, far_qc, far_logit)],
        [state_in],
    )
    received, state = lax.optimization_barrier((swap(own, azz), state))
    (own,) = add([own, received], [BF16])
    if reps > 8:
        members = [[i * 8 + j for i in range(reps // 8)] for j in range(8)]
        own = lax.psum(own.astype(F32), "rep", axis_index_groups=members).astype(BF16)

    label_grad = to_rows(info, [own] + [swap(own, mask) for mask in turns[1:]])
    return logits, state, label_grad


def solution(mesh):
    reps, blks = mesh.shape["rep"], mesh.shape["blk"]
    assert blks == 4 and reps >= 8 and reps & (reps - 1) == 0
    in_specs = (
        P(("rep", "blk"), None, None),
        P("blk", None),
        P("blk", None),
        P(("rep", "blk")),
        P(("rep", "blk"), None),
        P(("rep", "blk"), None),
    )
    out_specs = (P(("rep", "blk"), None), P(("rep", "blk"), None, None), P("blk", None))
    return jax.shard_map(
        functools.partial(per_device, reps, blks),
        mesh=mesh, in_specs=in_specs, out_specs=out_specs, check_vma=False,
    )
```

```python
import functools

import jax
import jax.numpy as jnp
from jax import lax
from jax.experimental import pallas as pl
from jax.experimental.pallas import tpu as pltpu
from jax.sharding import PartitionSpec as P

F32 = jnp.float32
BF16 = jnp.bfloat16
VMEM = pl.BlockSpec(memory_space=pltpu.VMEM)
SMEM = pl.BlockSpec(memory_space=pltpu.SMEM)
HBM = pl.BlockSpec(memory_space=pltpu.HBM)
PARAMS = pltpu.CompilerParams(vmem_limit_bytes=20 * 1024 * 1024)
GROUP = 4
EXTRA = 16


LONG = pl.CostEstimate(flops=10**11, transcendentals=0, bytes_accessed=0)


def shape(dims, dtype):
    return jax.ShapeDtypeStruct(dims, dtype)


def mm(a, b):
    return jnp.dot(a, b, preferred_element_type=F32)


def cost(products, docs, tokens, width, labels):
    return pl.CostEstimate(
        flops=2 * products * docs * tokens * width * labels,
        transcendentals=docs * tokens * labels,
        bytes_accessed=4 * docs * tokens * width,
    )


def call(kernel, out_shape, ins, name, scratch=(), estimate=None, hbm=0):
    single = not isinstance(out_shape, (list, tuple))
    ins = [pltpu.with_memory_space_constraint(x, pltpu.HBM) for x in ins[:hbm]] + list(ins[hbm:])
    return pl.pallas_call(
        kernel,
        out_shape=out_shape,
        in_specs=[
            HBM if i < hbm else SMEM if x.ndim == 1 else VMEM for i, x in enumerate(ins)
        ],
        out_specs=VMEM if single else [VMEM] * len(out_shape),
        scratch_shapes=scratch,
        compiler_params=PARAMS,
        cost_estimate=estimate,
        name=name,
    )(*ins)


def lanes_of(info_ref, k, labels):
    return pl.ds(pl.multiple_of((info_ref[0] ^ k) * labels, labels), labels)


def label_chunk(docs, q, c, lanes, sums):
    qt = q.T
    ct = c.T.astype(F32)
    labels = q.shape[0]

    def products(doc):
        load, enc_ref, enct_ref, gate_ref = doc[:4]
        load()
        enc = enc_ref[...]
        g = gate_ref[:, lanes]
        both = mm(enc, jnp.concatenate([qt, (ct * g).astype(BF16)], axis=1))
        return g, both[:, :labels], both[:, labels:]

    query_grad, class_grad = sums
    ahead = products(docs[0])
    for i, (_, _, enct_ref, _, length, attn_ref, score_ref, logit_ref) in enumerate(docs):
        g, scores, attn_grad = ahead
        if i + 1 < len(docs):
            ahead = products(docs[i + 1])
        token = lax.broadcasted_iota(jnp.int32, scores.shape, 0)
        expo = jnp.where(token < length, jnp.exp(scores), 0.0)
        attn = expo * (1.0 / jnp.sum(expo, axis=0, keepdims=True))
        attn_b = attn.astype(BF16)
        attn_ref[...] = attn_b
        inner = jnp.sum(attn * attn_grad, axis=0, keepdims=True)
        score_grad = (attn * (attn_grad - inner)).astype(BF16)
        score_ref[...] = score_grad
        both = mm(enct_ref[...], jnp.concatenate([attn_b, score_grad], axis=1))
        context, part = both[:, :labels], both[:, labels:]
        query_grad = part if query_grad is None else query_grad + part
        logit_ref[...] = jnp.sum(context * ct, axis=0, keepdims=True)
        part = context * g
        class_grad = part if class_grad is None else class_grad + part
    return query_grad, class_grad


def doc_list(loads, enc_ref, enct_ref, gate_ref, lens_ref, attn_ref, score_ref, logit_ref):
    return [
        (loads[d], enc_ref.at[d], enct_ref.at[d], gate_ref.at[d : d + 1], lens_ref[d],
         attn_ref.at[d], score_ref.at[d], logit_ref.at[d : d + 1])
        for d in range(enc_ref.shape[0])
    ]


def turn_around(enc_ref, enct_ref, copies=None):
    def load(d):
        if copies is not None:
            copies[d].wait()
        enct_ref[d] = enc_ref[d].T

    return [functools.partial(load, d) for d in range(enc_ref.shape[0])]


def pack_kernel(q_in, c_in, qc_ref, sem):
    copies = [pltpu.make_async_copy(x, qc_ref.at[i], sem.at[i]) for i, x in enumerate((q_in, c_in))]
    for copy in copies:
        copy.start()
    for copy in copies:
        copy.wait()


def own_kernel(enc_in, beam_in, grad_in, info_ref, lens_ref, qc_ref, enc_ref, gate_ref, enct_ref,
               attn_ref, score_ref, logit_ref, qsum_ref, csum_ref, beam_ref, sem):
    docs = enc_ref.shape[0]
    small = [(beam_in, beam_ref), (grad_in, gate_ref)]
    small = [pltpu.make_async_copy(x, y, sem.at[docs + i]) for i, (x, y) in enumerate(small)]
    copies = [
        pltpu.make_async_copy(enc_in.at[d], enc_ref.at[d], sem.at[d]) for d in range(docs)
    ]
    for copy in copies[:1] + small + copies[1:]:
        copy.start()
    loads = turn_around(enc_ref, enct_ref, copies)

    def first_load():
        load()
        for copy in small:
            copy.wait()
        gate_ref[...] = gate_ref[...] * beam_ref[...].astype(F32)

    load, loads[0] = loads[0], first_load
    qsum_ref[...], csum_ref[...] = label_chunk(
        doc_list(loads, enc_ref, enct_ref, gate_ref, lens_ref, attn_ref, score_ref, logit_ref),
        qc_ref[0], qc_ref[1], lanes_of(info_ref, 0, qc_ref.shape[1]), (None, None),
    )


def to_blocks(info_ref, sums, rows_ref, out_refs):
    query_grad, class_grad = sums
    width = query_grad.shape[0]
    rows_ref[:, :width] = query_grad.T
    rows_ref[:, width:] = class_grad.T
    size = rows_ref.shape[0] // GROUP
    count = GROUP // len(out_refs)
    for i in range(GROUP):
        ref = out_refs[i // count]
        block = rows_ref[pl.ds(pl.multiple_of((info_ref[1] ^ i) * size, size), size), :]
        ref[(i % count) * size : (i % count + 1) * size, :] = block.astype(ref.dtype)


def other_kernel(info_ref, lens_ref, beam_ref, grad_ref, enc_ref, qc_ref, qsum_ref, csum_ref,
                 gate_ref, enct_ref, attn_ref, score_ref, logit_ref, *refs):
    gate_ref[...] = grad_ref[...] * beam_ref[...].astype(F32)
    sums = label_chunk(
        doc_list(turn_around(enc_ref, enct_ref), enc_ref, enct_ref, gate_ref, lens_ref,
                 attn_ref, score_ref, logit_ref),
        qc_ref[0], qc_ref[1], lanes_of(info_ref, 0, qc_ref.shape[1]),
        (qsum_ref[...], csum_ref[...]),
    )
    to_blocks(info_ref, sums, refs[-1], refs[:-1])


def far_kernel(info_ref, lens_ref, lens2_ref, gate_ref, gate2_ref, enc_ref, enc2_ref, enct_ref,
               enct2_ref, qc_ref, attn_ref, score_ref, logit_ref, attn2_ref, score2_ref,
               logit2_ref, *refs):
    loads = [lambda: None] * enc_ref.shape[0]
    sums = label_chunk(
        doc_list(loads, enc_ref, enct_ref, gate_ref, lens_ref, attn_ref, score_ref, logit_ref)
        + doc_list(loads, enc2_ref, enct2_ref, gate2_ref, lens2_ref, attn2_ref, score2_ref,
                   logit2_ref),
        qc_ref[0], qc_ref[1], lanes_of(info_ref, 2, qc_ref.shape[1]), (None, None),
    )
    to_blocks(info_ref, sums, refs[-1], refs[:-1])


def state_parts(ks, info_ref, gate_ref, chunks):
    docs, labels = gate_ref.shape[0], chunks[2].shape[1]
    ctx_grads = []
    for n, k in enumerate(ks):
        gate = gate_ref[:, lanes_of(info_ref, k, labels)]
        gate = jnp.concatenate([gate, jnp.zeros((128 - docs, labels), F32)], axis=0).T
        c = chunks[4 * n + 2][1].astype(F32)
        ctx_grads.append([(c * gate[:, d : d + 1]).astype(BF16) for d in range(docs)])
    for d in range(docs):
        total = None
        for n in range(len(ks)):
            attn_ref, score_ref, qc_ref = chunks[4 * n : 4 * n + 3]
            part = mm(attn_ref[d], ctx_grads[n][d]) + mm(score_ref[d], qc_ref[0])
            total = part if total is None else total + part
        yield d, total


def away_kernel(ks, info_ref, gate_ref, *refs):
    chunks, out_ref = refs[:-1], refs[-1]
    tokens, labels = chunks[0].shape[1:]
    for d, total in state_parts(ks, info_ref, gate_ref, chunks):
        out_ref[d, :tokens] = total.astype(BF16)
        for n in range(len(ks)):
            logit = chunks[4 * n + 3][d : d + 1, :]
            high = logit.astype(BF16).astype(F32)
            pad = jnp.zeros((EXTRA - 2, labels), F32)
            pair = jnp.concatenate([high, logit - high, pad], axis=0)
            out_ref[d, tokens:, n * labels : (n + 1) * labels] = pair.astype(BF16)


def home_kernel(ks, info_ref, gate_ref, *refs):
    chunks, (in_ref, out_ref, logit_ref, done_ref, sem) = refs[:-5], refs[-5:]
    tokens, labels = chunks[0].shape[1:]
    copies = []
    for d, total in state_parts(ks, info_ref, gate_ref, chunks):
        done_ref[d] = (total + in_ref[d, :tokens].astype(F32)).astype(BF16)
        copies.append(pltpu.make_async_copy(done_ref.at[d], out_ref.at[d], sem.at[d]))
        copies[-1].start()
        for n, k in enumerate(ks):
            pair = in_ref[d, tokens:, n * labels : (n + 1) * labels].astype(F32)
            logit_ref[d : d + 1, lanes_of(info_ref, k, labels)] = chunks[4 * n + 3][d : d + 1, :]
            logit_ref[d : d + 1, lanes_of(info_ref, k ^ 1, labels)] = pair[0:1] + pair[1:2]
    for copy in copies:
        copy.wait()


def state_grad(info, gate, parts, more):
    docs, tokens, labels = parts[0][0].shape
    width = parts[0][2].shape[2]
    ins = [info, gate, *parts[0], *parts[1], *more]
    estimate = cost(4, docs, tokens, width, labels)
    if not more:
        out = shape((docs, tokens + EXTRA, width), BF16)
        return call(functools.partial(away_kernel, (0, 2)), out, ins, "state_away", (), estimate)
    out = shape((docs, tokens, width), BF16)
    return pl.pallas_call(
        functools.partial(home_kernel, (0, 2)),
        out_shape=[out, shape(gate.shape, F32)],
        in_specs=[SMEM] + [VMEM] * (len(ins) - 1),
        out_specs=[pl.BlockSpec(memory_space=pl.ANY), VMEM],
        scratch_shapes=[pltpu.VMEM(out.shape, BF16), pltpu.SemaphoreType.DMA((docs,))],
        compiler_params=PARAMS,
        cost_estimate=estimate,
        name="state_home",
    )(*ins)


def add_kernel(count, *refs):
    total = refs[0][...].astype(F32)
    for ref in refs[1:count]:
        total = total + ref[...].astype(F32)
    size = refs[count].shape[0]
    for i, ref in enumerate(refs[count:]):
        ref[...] = total[i * size : (i + 1) * size].astype(ref.dtype)


def add(arrays, dtypes, estimate=None):
    rows, cols = arrays[0].shape
    out = [shape((rows // len(dtypes), cols), dtype) for dtype in dtypes]
    return call(
        functools.partial(add_kernel, len(arrays)), out, arrays, "add", estimate=estimate
    )


def rows_kernel(info_ref, *refs):
    block_refs, (out_ref, rows_ref, sem) = refs[:-3], refs[-3:]
    size = block_refs[0].shape[0]
    copies = []
    for i, ref in enumerate(block_refs):
        rows_ref[i] = ref[...].astype(F32)
        to = pl.ds(pl.multiple_of((info_ref[1] ^ i) * size, size), size)
        copies.append(pltpu.make_async_copy(rows_ref.at[i], out_ref.at[to], sem.at[i]))
        copies[-1].start()
    for copy in copies:
        copy.wait()


def to_rows(info, blocks):
    count = len(blocks)
    rows, cols = blocks[0].shape
    return pl.pallas_call(
        rows_kernel,
        out_shape=shape((count * rows, cols), F32),
        in_specs=[SMEM] + [VMEM] * count,
        out_specs=pl.BlockSpec(memory_space=pl.ANY),
        scratch_shapes=[pltpu.VMEM((count, rows, cols), F32), pltpu.SemaphoreType.DMA((count,))],
        compiler_params=PARAMS,
        name="to_rows",
    )(info, *blocks)


def per_device(reps, blks, encoded, queries, classifiers, lengths, beam, logit_grad):
    labels, width = queries.shape
    docs, tokens, _ = encoded.shape
    total = reps * blks
    blk, rep = lax.axis_index("blk"), lax.axis_index("rep")
    info = jnp.stack([blk, (rep & 1) * 2 + ((rep >> 1) & 1)]).astype(jnp.int32)

    def swap(x, mask):
        return lax.ppermute(x, ("rep", "blk"), [(i, i ^ mask) for i in range(total)])

    core, ax = 1, 2
    ay, az, azz = blks, 2 * blks, 4 * blks
    turns = [0, az, ay, ay | az]

    qc = call(
        pack_kernel, shape((2, labels, width), BF16), [queries, classifiers], "pack",
        [pltpu.SemaphoreType.DMA((2,))], hbm=2,
    )
    encoded2, qc = lax.optimization_barrier((encoded, qc))
    far_qc = swap(qc, ax)
    encoded2, beam2, grad2 = swap(encoded2, core), swap(beam, core), swap(logit_grad, core)
    lengths2 = swap(lengths, core)
    lengths = pltpu.with_memory_space_constraint(lengths, pltpu.HBM)

    per_chunk = [
        shape((docs, tokens, labels), BF16),
        shape((docs, tokens, labels), BF16),
        shape((docs, labels), F32),
    ]
    gates = shape(beam.shape, F32)
    turned = shape((docs, width, tokens), BF16)
    block = shape((labels // GROUP, 2 * width), BF16)
    halves = [shape((labels // 2, 2 * width), dtype) for dtype in (F32, BF16)]
    rows = [pltpu.VMEM((labels, 2 * width), F32)]
    sums = [shape((width, labels), F32)] * 2
    estimate = functools.partial(cost, tokens=tokens, width=width, labels=labels)

    enc, gate, enct, attn, score, logit, *acc = call(
        own_kernel,
        [shape(encoded.shape, BF16), gates, turned] + per_chunk + sums,
        [encoded, beam, logit_grad, info, lengths, qc], "own_labels",
        [pltpu.VMEM(beam.shape, jnp.int32), pltpu.SemaphoreType.DMA((docs + 2,))],
        estimate(4, docs), hbm=3,
    )
    gate2, enct2, attn2, score2, logit2, keep, send = call(
        other_kernel, [gates, turned] + per_chunk + halves,
        [info, lengths2, beam2, grad2, encoded2, qc, *acc], "own_labels_other_docs",
        rows, estimate(4, docs),
    )
    received = swap(send, ay)
    far_attn, far_score, far_logit, far_attn2, far_score2, far_logit2, *far = call(
        far_kernel, per_chunk + per_chunk + [shape(block.shape, F32)] + [block] * (GROUP - 1),
        [info, lengths, lengths2, gate, gate2, enc, encoded2, enct, enct2, far_qc],
        "far_labels", rows, estimate(4, 2 * docs),
    )

    far, keep, received = lax.optimization_barrier((far, keep, received))
    keep, send = add([keep, received], [F32, BF16])
    send, far = lax.optimization_barrier((send, far))
    relayed = swap(far[2], ay)
    received = [swap(far[3], ax | ay | az), swap(far[1], ax | az)]
    (first,) = add([far[0], relayed], [BF16])
    first, send, far_attn2 = lax.optimization_barrier((first, send, far_attn2))
    received.append(swap(first, ax))
    near = swap(send, az)
    state2 = state_grad(
        info, gate2,
        [(attn2, score2, qc, logit2), (far_attn2, far_score2, far_qc, far_logit2)], [],
    )
    received, near = lax.optimization_barrier((received, near))
    state_in = swap(state2, core)
    (own,) = add([keep, near, *received], [BF16], LONG)
    far_attn, far_score, own = lax.optimization_barrier((far_attn, far_score, own))
    state, logits = state_grad(
        info, gate, [(attn, score, qc, logit), (far_attn, far_score, far_qc, far_logit)],
        [state_in],
    )
    received, state = lax.optimization_barrier((swap(own, azz), state))
    (own,) = add([own, received], [BF16])
    if reps > 8:
        members = [[i * 8 + j for i in range(reps // 8)] for j in range(8)]
        own = lax.psum(own.astype(F32), "rep", axis_index_groups=members).astype(BF16)

    both, second, first = lax.optimization_barrier([swap(own, mask) for mask in turns[:0:-1]])
    label_grad = to_rows(info, [own, first, second, both])
    return logits, state, label_grad


def solution(mesh):
    reps, blks = mesh.shape["rep"], mesh.shape["blk"]
    assert blks == 4 and reps >= 8 and reps & (reps - 1) == 0
    in_specs = (
        P(("rep", "blk"), None, None),
        P("blk", None),
        P("blk", None),
        P(("rep", "blk")),
        P(("rep", "blk"), None),
        P(("rep", "blk"), None),
    )
    out_specs = (P(("rep", "blk"), None), P(("rep", "blk"), None, None), P("blk", None))
    return jax.shard_map(
        functools.partial(per_device, reps, blks),
        mesh=mesh, in_specs=in_specs, out_specs=out_specs, check_vma=False,
    )
```

```python
import functools

import jax
import jax.numpy as jnp
from jax import lax
from jax.experimental import pallas as pl
from jax.experimental.pallas import tpu as pltpu
from jax.sharding import PartitionSpec as P

F32 = jnp.float32
BF16 = jnp.bfloat16
VMEM = pl.BlockSpec(memory_space=pltpu.VMEM)
SMEM = pl.BlockSpec(memory_space=pltpu.SMEM)
HBM = pl.BlockSpec(memory_space=pltpu.HBM)
PARAMS = pltpu.CompilerParams(vmem_limit_bytes=20 * 1024 * 1024)
GROUP = 4
EXTRA = 16


LONG = pl.CostEstimate(flops=10**11, transcendentals=0, bytes_accessed=0)


def shape(dims, dtype):
    return jax.ShapeDtypeStruct(dims, dtype)


def mm(a, b):
    return jnp.dot(a, b, preferred_element_type=F32)


def cost(products, docs, tokens, width, labels):
    return pl.CostEstimate(
        flops=2 * products * docs * tokens * width * labels,
        transcendentals=docs * tokens * labels,
        bytes_accessed=4 * docs * tokens * width,
    )


def call(kernel, out_shape, ins, name, scratch=(), estimate=None, hbm=0):
    single = not isinstance(out_shape, (list, tuple))
    ins = [pltpu.with_memory_space_constraint(x, pltpu.HBM) for x in ins[:hbm]] + list(ins[hbm:])
    return pl.pallas_call(
        kernel,
        out_shape=out_shape,
        in_specs=[
            HBM if i < hbm else SMEM if x.ndim == 1 else VMEM for i, x in enumerate(ins)
        ],
        out_specs=VMEM if single else [VMEM] * len(out_shape),
        scratch_shapes=scratch,
        compiler_params=PARAMS,
        cost_estimate=estimate,
        name=name,
    )(*ins)


def lanes_of(info_ref, k, labels):
    return pl.ds(pl.multiple_of((info_ref[0] ^ k) * labels, labels), labels)


def label_chunk(docs, q, c, lanes, sums):
    qt = q.T
    ct = c.T.astype(F32)
    labels = q.shape[0]

    def products(doc):
        load, enc_ref, enct_ref, gate_ref = doc[:4]
        load()
        enc = enc_ref[...]
        g = gate_ref[:, lanes]
        both = mm(enc, jnp.concatenate([qt, (ct * g).astype(BF16)], axis=1))
        return g, both[:, :labels], both[:, labels:]

    query_grad, class_grad = sums
    ahead = products(docs[0])
    for i, (_, _, enct_ref, _, length, attn_ref, score_ref, logit_ref) in enumerate(docs):
        g, scores, attn_grad = ahead
        if i + 1 < len(docs):
            ahead = products(docs[i + 1])
        token = lax.broadcasted_iota(jnp.int32, scores.shape, 0)
        expo = jnp.where(token < length, jnp.exp(scores), 0.0)
        attn = expo * (1.0 / jnp.sum(expo, axis=0, keepdims=True))
        attn_b = attn.astype(BF16)
        attn_ref[...] = attn_b
        inner = jnp.sum(attn * attn_grad, axis=0, keepdims=True)
        score_grad = (attn * (attn_grad - inner)).astype(BF16)
        score_ref[...] = score_grad
        both = mm(enct_ref[...], jnp.concatenate([attn_b, score_grad], axis=1))
        context, part = both[:, :labels], both[:, labels:]
        query_grad = part if query_grad is None else query_grad + part
        logit_ref[...] = jnp.sum(context * ct, axis=0, keepdims=True)
        part = context * g
        class_grad = part if class_grad is None else class_grad + part
    return query_grad, class_grad


def doc_list(loads, enc_ref, enct_ref, gate_ref, lens_ref, attn_ref, score_ref, logit_ref):
    return [
        (loads[d], enc_ref.at[d], enct_ref.at[d], gate_ref.at[d : d + 1], lens_ref[d],
         attn_ref.at[d], score_ref.at[d], logit_ref.at[d : d + 1])
        for d in range(enc_ref.shape[0])
    ]


def turn_around(enc_ref, enct_ref, copies=None):
    def load(d):
        if copies is not None:
            copies[d].wait()
        enct_ref[d] = enc_ref[d].T

    return [functools.partial(load, d) for d in range(enc_ref.shape[0])]


def pack_kernel(q_in, c_in, qc_ref, sem):
    copies = [pltpu.make_async_copy(x, qc_ref.at[i], sem.at[i]) for i, x in enumerate((q_in, c_in))]
    for copy in copies:
        copy.start()
    for copy in copies:
        copy.wait()


def own_kernel(enc_in, beam_in, grad_in, info_ref, lens_ref, qc_ref, enc_ref, gate_ref, enct_ref,
               attn_ref, score_ref, logit_ref, qsum_ref, csum_ref, beam_ref, sem):
    docs = enc_ref.shape[0]
    small = [(beam_in, beam_ref), (grad_in, gate_ref)]
    small = [pltpu.make_async_copy(x, y, sem.at[docs + i]) for i, (x, y) in enumerate(small)]
    copies = [
        pltpu.make_async_copy(enc_in.at[d], enc_ref.at[d], sem.at[d]) for d in range(docs)
    ]
    for copy in copies[:1] + small + copies[1:]:
        copy.start()
    loads = turn_around(enc_ref, enct_ref, copies)

    def first_load():
        load()
        for copy in small:
            copy.wait()
        gate_ref[...] = gate_ref[...] * beam_ref[...].astype(F32)

    load, loads[0] = loads[0], first_load
    qsum_ref[...], csum_ref[...] = label_chunk(
        doc_list(loads, enc_ref, enct_ref, gate_ref, lens_ref, attn_ref, score_ref, logit_ref),
        qc_ref[0], qc_ref[1], lanes_of(info_ref, 0, qc_ref.shape[1]), (None, None),
    )


def to_blocks(info_ref, sums, rows_ref, out_refs):
    query_grad, class_grad = sums
    width = query_grad.shape[0]
    rows_ref[:, :width] = query_grad.T
    rows_ref[:, width:] = class_grad.T
    size = rows_ref.shape[0] // GROUP
    count = GROUP // len(out_refs)
    for i in range(GROUP):
        ref = out_refs[i // count]
        block = rows_ref[pl.ds(pl.multiple_of((info_ref[1] ^ i) * size, size), size), :]
        ref[(i % count) * size : (i % count + 1) * size, :] = block.astype(ref.dtype)


def other_kernel(info_ref, lens_ref, beam_ref, grad_ref, enc_ref, qc_ref, qsum_ref, csum_ref,
                 gate_ref, enct_ref, attn_ref, score_ref, logit_ref, *refs):
    gate_ref[...] = grad_ref[...] * beam_ref[...].astype(F32)
    sums = label_chunk(
        doc_list(turn_around(enc_ref, enct_ref), enc_ref, enct_ref, gate_ref, lens_ref,
                 attn_ref, score_ref, logit_ref),
        qc_ref[0], qc_ref[1], lanes_of(info_ref, 0, qc_ref.shape[1]),
        (qsum_ref[...], csum_ref[...]),
    )
    to_blocks(info_ref, sums, refs[-1], refs[:-1])


def far_kernel(info_ref, lens_ref, lens2_ref, gate_ref, gate2_ref, enc_ref, enc2_ref, enct_ref,
               enct2_ref, qc_ref, attn_ref, score_ref, logit_ref, attn2_ref, score2_ref,
               logit2_ref, *refs):
    loads = [lambda: None] * enc_ref.shape[0]
    sums = label_chunk(
        doc_list(loads, enc_ref, enct_ref, gate_ref, lens_ref, attn_ref, score_ref, logit_ref)
        + doc_list(loads, enc2_ref, enct2_ref, gate2_ref, lens2_ref, attn2_ref, score2_ref,
                   logit2_ref),
        qc_ref[0], qc_ref[1], lanes_of(info_ref, 2, qc_ref.shape[1]), (None, None),
    )
    to_blocks(info_ref, sums, refs[-1], refs[:-1])


def state_parts(ks, info_ref, gate_ref, chunks):
    docs, labels = gate_ref.shape[0], chunks[2].shape[1]
    ctx_grads = []
    for n, k in enumerate(ks):
        gate = gate_ref[:, lanes_of(info_ref, k, labels)]
        gate = jnp.concatenate([gate, jnp.zeros((128 - docs, labels), F32)], axis=0).T
        c = chunks[4 * n + 2][1].astype(F32)
        ctx_grads.append([(c * gate[:, d : d + 1]).astype(BF16) for d in range(docs)])
    for d in range(docs):
        total = None
        for n in range(len(ks)):
            attn_ref, score_ref, qc_ref = chunks[4 * n : 4 * n + 3]
            part = mm(attn_ref[d], ctx_grads[n][d]) + mm(score_ref[d], qc_ref[0])
            total = part if total is None else total + part
        yield d, total


def away_kernel(ks, info_ref, gate_ref, *refs):
    chunks, out_ref = refs[:-1], refs[-1]
    tokens, labels = chunks[0].shape[1:]
    for d, total in state_parts(ks, info_ref, gate_ref, chunks):
        out_ref[d, :tokens] = total.astype(BF16)
        for n in range(len(ks)):
            logit = chunks[4 * n + 3][d : d + 1, :]
            high = logit.astype(BF16).astype(F32)
            pad = jnp.zeros((EXTRA - 2, labels), F32)
            pair = jnp.concatenate([high, logit - high, pad], axis=0)
            out_ref[d, tokens:, n * labels : (n + 1) * labels] = pair.astype(BF16)


def home_kernel(ks, info_ref, gate_ref, *refs):
    chunks, (in_ref, out_ref, logit_ref, done_ref, sem) = refs[:-5], refs[-5:]
    tokens, labels = chunks[0].shape[1:]
    copies = []
    for d, total in state_parts(ks, info_ref, gate_ref, chunks):
        done_ref[d] = (total + in_ref[d, :tokens].astype(F32)).astype(BF16)
        copies.append(pltpu.make_async_copy(done_ref.at[d], out_ref.at[d], sem.at[d]))
        copies[-1].start()
        for n, k in enumerate(ks):
            pair = in_ref[d, tokens:, n * labels : (n + 1) * labels].astype(F32)
            logit_ref[d : d + 1, lanes_of(info_ref, k, labels)] = chunks[4 * n + 3][d : d + 1, :]
            logit_ref[d : d + 1, lanes_of(info_ref, k ^ 1, labels)] = pair[0:1] + pair[1:2]
    for copy in copies:
        copy.wait()


def state_grad(info, gate, parts, more):
    docs, tokens, labels = parts[0][0].shape
    width = parts[0][2].shape[2]
    ins = [info, gate, *parts[0], *parts[1], *more]
    estimate = cost(4, docs, tokens, width, labels)
    if not more:
        out = shape((docs, tokens + EXTRA, width), BF16)
        return call(functools.partial(away_kernel, (0, 2)), out, ins, "state_away", (), estimate)
    out = shape((docs, tokens, width), BF16)
    return pl.pallas_call(
        functools.partial(home_kernel, (0, 2)),
        out_shape=[out, shape(gate.shape, F32)],
        in_specs=[SMEM] + [VMEM] * (len(ins) - 1),
        out_specs=[pl.BlockSpec(memory_space=pl.ANY), VMEM],
        scratch_shapes=[pltpu.VMEM(out.shape, BF16), pltpu.SemaphoreType.DMA((docs,))],
        compiler_params=PARAMS,
        cost_estimate=estimate,
        name="state_home",
    )(*ins)


def add_kernel(count, *refs):
    total = refs[0][...].astype(F32)
    for ref in refs[1:count]:
        total = total + ref[...].astype(F32)
    size = refs[count].shape[0]
    for i, ref in enumerate(refs[count:]):
        ref[...] = total[i * size : (i + 1) * size].astype(ref.dtype)


def add(arrays, dtypes, estimate=None):
    rows, cols = arrays[0].shape
    out = [shape((rows // len(dtypes), cols), dtype) for dtype in dtypes]
    return call(
        functools.partial(add_kernel, len(arrays)), out, arrays, "add", estimate=estimate
    )


def rows_kernel(blocks_ref, out_ref, rows_ref, sem):
    count, size, _ = blocks_ref.shape
    copies = []
    for i in range(count):
        rows_ref[i] = blocks_ref[i].astype(F32)
        to = pl.ds(((i & 1) * 2 + (i >> 1)) * size, size)
        copies.append(pltpu.make_async_copy(rows_ref.at[i], out_ref.at[to], sem.at[i]))
        copies[-1].start()
    for copy in copies:
        copy.wait()


def to_rows(blocks):
    count, rows, cols = blocks.shape
    return pl.pallas_call(
        rows_kernel,
        out_shape=shape((count * rows, cols), F32),
        in_specs=[VMEM],
        out_specs=pl.BlockSpec(memory_space=pl.ANY),
        scratch_shapes=[pltpu.VMEM((count, rows, cols), F32), pltpu.SemaphoreType.DMA((count,))],
        compiler_params=PARAMS,
        name="to_rows",
    )(blocks)


def per_device(reps, blks, encoded, queries, classifiers, lengths, beam, logit_grad):
    labels, width = queries.shape
    docs, tokens, _ = encoded.shape
    total = reps * blks
    blk, rep = lax.axis_index("blk"), lax.axis_index("rep")
    info = jnp.stack([blk, (rep & 1) * 2 + ((rep >> 1) & 1)]).astype(jnp.int32)

    def swap(x, mask):
        return lax.ppermute(x, ("rep", "blk"), [(i, i ^ mask) for i in range(total)])

    core, ax = 1, 2
    ay, az, azz = blks, 2 * blks, 4 * blks
    turns = [0, az, ay, ay | az]

    qc = call(
        pack_kernel, shape((2, labels, width), BF16), [queries, classifiers], "pack",
        [pltpu.SemaphoreType.DMA((2,))], hbm=2,
    )
    encoded2, qc = lax.optimization_barrier((encoded, qc))
    far_qc = swap(qc, ax)
    encoded2, beam2, grad2 = swap(encoded2, core), swap(beam, core), swap(logit_grad, core)
    lengths2 = swap(lengths, core)
    lengths = pltpu.with_memory_space_constraint(lengths, pltpu.HBM)

    per_chunk = [
        shape((docs, tokens, labels), BF16),
        shape((docs, tokens, labels), BF16),
        shape((docs, labels), F32),
    ]
    gates = shape(beam.shape, F32)
    turned = shape((docs, width, tokens), BF16)
    block = shape((labels // GROUP, 2 * width), BF16)
    halves = [shape((labels // 2, 2 * width), dtype) for dtype in (F32, BF16)]
    rows = [pltpu.VMEM((labels, 2 * width), F32)]
    sums = [shape((width, labels), F32)] * 2
    estimate = functools.partial(cost, tokens=tokens, width=width, labels=labels)

    enc, gate, enct, attn, score, logit, *acc = call(
        own_kernel,
        [shape(encoded.shape, BF16), gates, turned] + per_chunk + sums,
        [encoded, beam, logit_grad, info, lengths, qc], "own_labels",
        [pltpu.VMEM(beam.shape, jnp.int32), pltpu.SemaphoreType.DMA((docs + 2,))],
        estimate(4, docs), hbm=3,
    )
    gate2, enct2, attn2, score2, logit2, keep, send = call(
        other_kernel, [gates, turned] + per_chunk + halves,
        [info, lengths2, beam2, grad2, encoded2, qc, *acc], "own_labels_other_docs",
        rows, estimate(4, docs),
    )
    received = swap(send, ay)
    far_attn, far_score, far_logit, far_attn2, far_score2, far_logit2, *far = call(
        far_kernel, per_chunk + per_chunk + [shape(block.shape, F32)] + [block] * (GROUP - 1),
        [info, lengths, lengths2, gate, gate2, enc, encoded2, enct, enct2, far_qc],
        "far_labels", rows, estimate(4, 2 * docs),
    )

    far, keep, received = lax.optimization_barrier((far, keep, received))
    keep, send = add([keep, received], [F32, BF16])
    send, far = lax.optimization_barrier((send, far))
    relayed = swap(far[2], ay)
    received = [swap(far[3], ax | ay | az), swap(far[1], ax | az)]
    (first,) = add([far[0], relayed], [BF16])
    first, send, far_attn2 = lax.optimization_barrier((first, send, far_attn2))
    received.append(swap(first, ax))
    near = swap(send, az)
    state2 = state_grad(
        info, gate2,
        [(attn2, score2, qc, logit2), (far_attn2, far_score2, far_qc, far_logit2)], [],
    )
    received, near = lax.optimization_barrier((received, near))
    state_in = swap(state2, core)
    (own,) = add([keep, near, *received], [BF16], LONG)
    far_attn, far_score, own = lax.optimization_barrier((far_attn, far_score, own))
    state, logits = state_grad(
        info, gate, [(attn, score, qc, logit), (far_attn, far_score, far_qc, far_logit)],
        [state_in],
    )
    received, state = lax.optimization_barrier((swap(own, azz), state))
    (own,) = add([own, received], [BF16])
    if reps > 8:
        members = [[i * 8 + j for i in range(reps // 8)] for j in range(8)]
        own = lax.psum(own.astype(F32), "rep", axis_index_groups=members).astype(BF16)

    groups = [[GROUP * i + j for j in range(GROUP)] for i in range(reps // GROUP)]
    copies = jnp.broadcast_to(own, (GROUP, *own.shape))
    blocks = lax.all_to_all(copies, "rep", 0, 0, axis_index_groups=groups, tiled=True)
    label_grad = to_rows(blocks)
    return logits, state, label_grad


def solution(mesh):
    reps, blks = mesh.shape["rep"], mesh.shape["blk"]
    assert blks == 4 and reps >= 8 and reps & (reps - 1) == 0
    in_specs = (
        P(("rep", "blk"), None, None),
        P("blk", None),
        P("blk", None),
        P(("rep", "blk")),
        P(("rep", "blk"), None),
        P(("rep", "blk"), None),
    )
    out_specs = (P(("rep", "blk"), None), P(("rep", "blk"), None, None), P("blk", None))
    return jax.shard_map(
        functools.partial(per_device, reps, blks),
        mesh=mesh, in_specs=in_specs, out_specs=out_specs, check_vma=False,
    )
```

```python
import functools

import jax
import jax.numpy as jnp
from jax import lax
from jax.experimental import pallas as pl
from jax.experimental.pallas import tpu as pltpu
from jax.sharding import PartitionSpec as P

F32 = jnp.float32
BF16 = jnp.bfloat16
VMEM = pl.BlockSpec(memory_space=pltpu.VMEM)
SMEM = pl.BlockSpec(memory_space=pltpu.SMEM)
HBM = pl.BlockSpec(memory_space=pltpu.HBM)
PARAMS = pltpu.CompilerParams(vmem_limit_bytes=20 * 1024 * 1024)
GROUP = 4
LANES = 128
EXTRA = 16


LONG = pl.CostEstimate(flops=10**11, transcendentals=0, bytes_accessed=0)


def shape(dims, dtype):
    return jax.ShapeDtypeStruct(dims, dtype)


def mm(a, b):
    return jnp.dot(a, b, preferred_element_type=F32)


def cost(products, docs, tokens, width, labels):
    return pl.CostEstimate(
        flops=2 * products * docs * tokens * width * labels,
        transcendentals=docs * tokens * labels,
        bytes_accessed=4 * docs * tokens * width,
    )


def call(kernel, out_shape, ins, name, scratch=(), estimate=None, hbm=0):
    single = not isinstance(out_shape, (list, tuple))
    ins = [pltpu.with_memory_space_constraint(x, pltpu.HBM) for x in ins[:hbm]] + list(ins[hbm:])
    return pl.pallas_call(
        kernel,
        out_shape=out_shape,
        in_specs=[
            HBM if i < hbm else SMEM if x.ndim == 1 else VMEM for i, x in enumerate(ins)
        ],
        out_specs=VMEM if single else [VMEM] * len(out_shape),
        scratch_shapes=scratch,
        compiler_params=PARAMS,
        cost_estimate=estimate,
        name=name,
    )(*ins)


def lanes_of(k, labels):
    return pl.ds(pl.multiple_of((lax.axis_index("blk") ^ k) * labels, labels), labels)


def turn():
    rep = lax.axis_index("rep")
    return (rep & 1) * 2 + ((rep >> 1) & 1)


def label_chunk(docs, q, c, lanes, sums):
    qt = q.T
    ct = c.T.astype(F32)
    labels = q.shape[0]

    def products(doc):
        load, enc_ref, enct_ref, gate_ref = doc[:4]
        load()
        enc = enc_ref[...]
        g = gate_ref[:, lanes]
        both = mm(enc, jnp.concatenate([qt, (ct * g).astype(BF16)], axis=1))
        return g, both[:, :labels], both[:, labels:]

    query_grad, class_grad = sums
    ahead = products(docs[0])
    for i, (_, _, enct_ref, gate_ref, attn_ref, score_ref, logit_ref) in enumerate(docs):
        g, scores, attn_grad = ahead
        if i + 1 < len(docs):
            ahead = products(docs[i + 1])
        length = gate_ref[:, gate_ref.shape[1] - LANES :][:, :1]
        token = lax.broadcasted_iota(jnp.int32, scores.shape, 0).astype(F32)
        expo = jnp.where(token < length, jnp.exp(scores), 0.0)
        attn = expo * (1.0 / jnp.sum(expo, axis=0, keepdims=True))
        attn_b = attn.astype(BF16)
        attn_ref[...] = attn_b
        inner = jnp.sum(attn * attn_grad, axis=0, keepdims=True)
        score_grad = (attn * (attn_grad - inner)).astype(BF16)
        score_ref[...] = score_grad
        both = mm(enct_ref[...], jnp.concatenate([attn_b, score_grad], axis=1))
        context, part = both[:, :labels], both[:, labels:]
        query_grad = part if query_grad is None else query_grad + part
        logit_ref[...] = jnp.sum(context * ct, axis=0, keepdims=True)
        part = context * g
        class_grad = part if class_grad is None else class_grad + part
    return query_grad, class_grad


def doc_list(loads, enc_ref, enct_ref, gate_ref, attn_ref, score_ref, logit_ref):
    return [
        (loads[d], enc_ref.at[d], enct_ref.at[d], gate_ref.at[d : d + 1], attn_ref.at[d],
         score_ref.at[d], logit_ref.at[d : d + 1])
        for d in range(enc_ref.shape[0])
    ]


def turn_around(enc_ref, enct_ref, copies=None):
    def load(d):
        if copies is not None:
            copies[d].wait()
        enct_ref[d] = enc_ref[d].T

    return [functools.partial(load, d) for d in range(enc_ref.shape[0])]


def pack_kernel(q_in, c_in, qc_ref, sem):
    copies = [pltpu.make_async_copy(x, qc_ref.at[i], sem.at[i]) for i, x in enumerate((q_in, c_in))]
    for copy in copies:
        copy.start()
    for copy in copies:
        copy.wait()


def make_gates(gate_ref, grad_ref, beam_ref, lens_ref):
    docs, labels = beam_ref.shape
    gate_ref[:, :labels] = grad_ref[...] * beam_ref[...].astype(F32)
    for d in range(docs):
        gate_ref[d : d + 1, labels:] = jnp.full((1, LANES), lens_ref[d], jnp.int32).astype(F32)


def own_kernel(enc_in, beam_in, grad_in, lens_ref, qc_ref, enc_ref, gate_ref, enct_ref,
               attn_ref, score_ref, logit_ref, qsum_ref, csum_ref, beam_ref, grad_ref, sem):
    docs = enc_ref.shape[0]
    small = [(beam_in, beam_ref), (grad_in, grad_ref)]
    small = [pltpu.make_async_copy(x, y, sem.at[docs + i]) for i, (x, y) in enumerate(small)]
    copies = [
        pltpu.make_async_copy(enc_in.at[d], enc_ref.at[d], sem.at[d]) for d in range(docs)
    ]
    for copy in copies[:1] + small + copies[1:]:
        copy.start()
    loads = turn_around(enc_ref, enct_ref, copies)

    def first_load():
        load()
        for copy in small:
            copy.wait()
        make_gates(gate_ref, grad_ref, beam_ref, lens_ref)

    load, loads[0] = loads[0], first_load
    qsum_ref[...], csum_ref[...] = label_chunk(
        doc_list(loads, enc_ref, enct_ref, gate_ref, attn_ref, score_ref, logit_ref),
        qc_ref[0], qc_ref[1], lanes_of(0, qc_ref.shape[1]), (None, None),
    )


def to_blocks(sums, rows_ref, out_refs):
    query_grad, class_grad = sums
    width = query_grad.shape[0]
    rows_ref[:, :width] = query_grad.T
    rows_ref[:, width:] = class_grad.T
    size = rows_ref.shape[0] // GROUP
    count = GROUP // len(out_refs)
    for i in range(GROUP):
        ref = out_refs[i // count]
        block = rows_ref[pl.ds(pl.multiple_of((turn() ^ i) * size, size), size), :]
        ref[(i % count) * size : (i % count + 1) * size, :] = block.astype(ref.dtype)


def other_kernel(lens_ref, beam_ref, grad_ref, enc_ref, qc_ref, qsum_ref, csum_ref,
                 gate_ref, enct_ref, attn_ref, score_ref, logit_ref, *refs):
    make_gates(gate_ref, grad_ref, beam_ref, lens_ref)
    sums = label_chunk(
        doc_list(turn_around(enc_ref, enct_ref), enc_ref, enct_ref, gate_ref,
                 attn_ref, score_ref, logit_ref),
        qc_ref[0], qc_ref[1], lanes_of(0, qc_ref.shape[1]),
        (qsum_ref[...], csum_ref[...]),
    )
    to_blocks(sums, refs[-1], refs[:-1])


def far_kernel(gate_ref, gate2_ref, enc_ref, enc2_ref, enct_ref,
               enct2_ref, qc_ref, attn_ref, score_ref, logit_ref, attn2_ref, score2_ref,
               logit2_ref, *refs):
    loads = [lambda: None] * enc_ref.shape[0]
    sums = label_chunk(
        doc_list(loads, enc_ref, enct_ref, gate_ref, attn_ref, score_ref, logit_ref)
        + doc_list(loads, enc2_ref, enct2_ref, gate2_ref, attn2_ref, score2_ref,
                   logit2_ref),
        qc_ref[0], qc_ref[1], lanes_of(2, qc_ref.shape[1]), (None, None),
    )
    to_blocks(sums, refs[-1], refs[:-1])


def state_parts(ks, gate_ref, chunks):
    docs, labels = gate_ref.shape[0], chunks[2].shape[1]
    ctx_grads = []
    for n, k in enumerate(ks):
        gate = gate_ref[:, lanes_of(k, labels)]
        gate = jnp.concatenate([gate, jnp.zeros((128 - docs, labels), F32)], axis=0).T
        c = chunks[4 * n + 2][1].astype(F32)
        ctx_grads.append([(c * gate[:, d : d + 1]).astype(BF16) for d in range(docs)])
    for d in range(docs):
        total = None
        for n in range(len(ks)):
            attn_ref, score_ref, qc_ref = chunks[4 * n : 4 * n + 3]
            part = mm(attn_ref[d], ctx_grads[n][d]) + mm(score_ref[d], qc_ref[0])
            total = part if total is None else total + part
        yield d, total


def away_kernel(ks, gate_ref, *refs):
    chunks, out_ref = refs[:-1], refs[-1]
    tokens, labels = chunks[0].shape[1:]
    for d, total in state_parts(ks, gate_ref, chunks):
        out_ref[d, :tokens] = total.astype(BF16)
        for n in range(len(ks)):
            logit = chunks[4 * n + 3][d : d + 1, :]
            high = logit.astype(BF16).astype(F32)
            pad = jnp.zeros((EXTRA - 2, labels), F32)
            pair = jnp.concatenate([high, logit - high, pad], axis=0)
            out_ref[d, tokens:, n * labels : (n + 1) * labels] = pair.astype(BF16)


def home_kernel(ks, gate_ref, *refs):
    chunks, (in_ref, out_ref, logit_ref, done_ref, sem) = refs[:-5], refs[-5:]
    tokens, labels = chunks[0].shape[1:]
    copies = []
    for d, total in state_parts(ks, gate_ref, chunks):
        done_ref[d] = (total + in_ref[d, :tokens].astype(F32)).astype(BF16)
        copies.append(pltpu.make_async_copy(done_ref.at[d], out_ref.at[d], sem.at[d]))
        copies[-1].start()
        for n, k in enumerate(ks):
            pair = in_ref[d, tokens:, n * labels : (n + 1) * labels].astype(F32)
            logit_ref[d : d + 1, lanes_of(k, labels)] = chunks[4 * n + 3][d : d + 1, :]
            logit_ref[d : d + 1, lanes_of(k ^ 1, labels)] = pair[0:1] + pair[1:2]
    for copy in copies:
        copy.wait()


def state_grad(gate, parts, more):
    docs, tokens, labels = parts[0][0].shape
    width = parts[0][2].shape[2]
    ins = [gate, *parts[0], *parts[1], *more]
    estimate = cost(4, docs, tokens, width, labels)
    if not more:
        out = shape((docs, tokens + EXTRA, width), BF16)
        return call(functools.partial(away_kernel, (0, 2)), out, ins, "state_away", (), estimate)
    out = shape((docs, tokens, width), BF16)
    return pl.pallas_call(
        functools.partial(home_kernel, (0, 2)),
        out_shape=[out, shape((docs, gate.shape[1] - LANES), F32)],
        in_specs=[VMEM] * len(ins),
        out_specs=[pl.BlockSpec(memory_space=pl.ANY), VMEM],
        scratch_shapes=[pltpu.VMEM(out.shape, BF16), pltpu.SemaphoreType.DMA((docs,))],
        compiler_params=PARAMS,
        cost_estimate=estimate,
        name="state_home",
    )(*ins)


def add_kernel(count, *refs):
    total = refs[0][...].astype(F32)
    for ref in refs[1:count]:
        total = total + ref[...].astype(F32)
    size = refs[count].shape[0]
    for i, ref in enumerate(refs[count:]):
        ref[...] = total[i * size : (i + 1) * size].astype(ref.dtype)


def add(arrays, dtypes, estimate=None):
    rows, cols = arrays[0].shape
    out = [shape((rows // len(dtypes), cols), dtype) for dtype in dtypes]
    return call(
        functools.partial(add_kernel, len(arrays)), out, arrays, "add", estimate=estimate
    )


def rows_kernel(*refs):
    block_refs, (out_ref, rows_ref, sem) = refs[:-3], refs[-3:]
    size = block_refs[0].shape[0]
    copies = []
    for i, ref in enumerate(block_refs):
        rows_ref[i] = ref[...].astype(F32)
        to = pl.ds(pl.multiple_of((turn() ^ i) * size, size), size)
        copies.append(pltpu.make_async_copy(rows_ref.at[i], out_ref.at[to], sem.at[i]))
        copies[-1].start()
    for copy in copies:
        copy.wait()


def to_rows(blocks):
    count = len(blocks)
    rows, cols = blocks[0].shape
    return pl.pallas_call(
        rows_kernel,
        out_shape=shape((count * rows, cols), F32),
        in_specs=[VMEM] * count,
        out_specs=pl.BlockSpec(memory_space=pl.ANY),
        scratch_shapes=[pltpu.VMEM((count, rows, cols), F32), pltpu.SemaphoreType.DMA((count,))],
        compiler_params=PARAMS,
        name="to_rows",
    )(*blocks)


def per_device(reps, blks, encoded, queries, classifiers, lengths, beam, logit_grad):
    labels, width = queries.shape
    docs, tokens, _ = encoded.shape
    total = reps * blks

    def swap(x, mask):
        return lax.ppermute(x, ("rep", "blk"), [(i, i ^ mask) for i in range(total)])

    core, ax = 1, 2
    ay, az, azz = blks, 2 * blks, 4 * blks
    turns = [0, az, ay, ay | az]

    qc = call(
        pack_kernel, shape((2, labels, width), BF16), [queries, classifiers], "pack",
        [pltpu.SemaphoreType.DMA((2,))], hbm=2,
    )
    encoded2, qc = lax.optimization_barrier((encoded, qc))
    far_qc = swap(qc, ax)
    encoded2, beam2, grad2 = swap(encoded2, core), swap(beam, core), swap(logit_grad, core)
    lengths2 = swap(lengths, core)
    lengths = pltpu.with_memory_space_constraint(lengths, pltpu.HBM)

    per_chunk = [
        shape((docs, tokens, labels), BF16),
        shape((docs, tokens, labels), BF16),
        shape((docs, labels), F32),
    ]
    gates = shape((docs, beam.shape[1] + LANES), F32)
    turned = shape((docs, width, tokens), BF16)
    block = shape((labels // GROUP, 2 * width), BF16)
    halves = [shape((labels // 2, 2 * width), dtype) for dtype in (F32, BF16)]
    rows = [pltpu.VMEM((labels, 2 * width), F32)]
    sums = [shape((width, labels), F32)] * 2
    estimate = functools.partial(cost, tokens=tokens, width=width, labels=labels)

    enc, gate, enct, attn, score, logit, *acc = call(
        own_kernel,
        [shape(encoded.shape, BF16), gates, turned] + per_chunk + sums,
        [encoded, beam, logit_grad, lengths, qc], "own_labels",
        [pltpu.VMEM(beam.shape, jnp.int32), pltpu.VMEM(beam.shape, F32),
         pltpu.SemaphoreType.DMA((docs + 2,))],
        estimate(4, docs), hbm=3,
    )
    gate2, enct2, attn2, score2, logit2, keep, send = call(
        other_kernel, [gates, turned] + per_chunk + halves,
        [lengths2, beam2, grad2, encoded2, qc, *acc], "own_labels_other_docs",
        rows, estimate(4, docs),
    )
    received = swap(send, ay)
    far_attn, far_score, far_logit, far_attn2, far_score2, far_logit2, *far = call(
        far_kernel, per_chunk + per_chunk + [shape(block.shape, F32)] + [block] * (GROUP - 1),
        [gate, gate2, enc, encoded2, enct, enct2, far_qc],
        "far_labels", rows, estimate(4, 2 * docs),
    )

    far, keep, received = lax.optimization_barrier((far, keep, received))
    keep, send = add([keep, received], [F32, BF16])
    send, far = lax.optimization_barrier((send, far))
    relayed = swap(far[2], ay)
    received = [swap(far[3], ax | ay | az), swap(far[1], ax | az)]
    (first,) = add([far[0], relayed], [BF16])
    first, send, far_attn2 = lax.optimization_barrier((first, send, far_attn2))
    received.append(swap(first, ax))
    near = swap(send, az)
    state2 = state_grad(
        gate2,
        [(attn2, score2, qc, logit2), (far_attn2, far_score2, far_qc, far_logit2)], [],
    )
    received, near = lax.optimization_barrier((received, near))
    state_in = swap(state2, core)
    (own,) = add([keep, near, *received], [BF16], LONG)
    far_attn, far_score, own = lax.optimization_barrier((far_attn, far_score, own))
    state, logits = state_grad(
        gate, [(attn, score, qc, logit), (far_attn, far_score, far_qc, far_logit)],
        [state_in],
    )
    received, state = lax.optimization_barrier((swap(own, azz), state))
    (own,) = add([own, received], [BF16])
    if reps > 8:
        members = [[i * 8 + j for i in range(reps // 8)] for j in range(8)]
        own = lax.psum(own.astype(F32), "rep", axis_index_groups=members).astype(BF16)

    both, second, first = lax.optimization_barrier([swap(own, mask) for mask in turns[:0:-1]])
    label_grad = to_rows([own, first, second, both])
    return logits, state, label_grad


def solution(mesh):
    reps, blks = mesh.shape["rep"], mesh.shape["blk"]
    assert blks == 4 and reps >= 8 and reps & (reps - 1) == 0
    in_specs = (
        P(("rep", "blk"), None, None),
        P("blk", None),
        P("blk", None),
        P(("rep", "blk")),
        P(("rep", "blk"), None),
        P(("rep", "blk"), None),
    )
    out_specs = (P(("rep", "blk"), None), P(("rep", "blk"), None, None), P("blk", None))
    return jax.shard_map(
        functools.partial(per_device, reps, blks),
        mesh=mesh, in_specs=in_specs, out_specs=out_specs, check_vma=False,
    )
```

```python
import functools

import jax
import jax.numpy as jnp
from jax import lax
from jax.experimental import pallas as pl
from jax.experimental.pallas import tpu as pltpu
from jax.sharding import PartitionSpec as P

F32 = jnp.float32
BF16 = jnp.bfloat16
VMEM = pl.BlockSpec(memory_space=pltpu.VMEM)
SMEM = pl.BlockSpec(memory_space=pltpu.SMEM)
HBM = pl.BlockSpec(memory_space=pltpu.HBM)
PARAMS = pltpu.CompilerParams(vmem_limit_bytes=20 * 1024 * 1024)
GROUP = 4
LANES = 128
EXTRA = 16


LONG = pl.CostEstimate(flops=10**11, transcendentals=0, bytes_accessed=0)


def shape(dims, dtype):
    return jax.ShapeDtypeStruct(dims, dtype)


def mm(a, b):
    return jnp.dot(a, b, preferred_element_type=F32)


def cost(products, docs, tokens, width, labels):
    return pl.CostEstimate(
        flops=2 * products * docs * tokens * width * labels,
        transcendentals=docs * tokens * labels,
        bytes_accessed=4 * docs * tokens * width,
    )


def call(kernel, out_shape, ins, name, scratch=(), estimate=None, hbm=0):
    single = not isinstance(out_shape, (list, tuple))
    ins = [pltpu.with_memory_space_constraint(x, pltpu.HBM) for x in ins[:hbm]] + list(ins[hbm:])
    return pl.pallas_call(
        kernel,
        out_shape=out_shape,
        in_specs=[
            HBM if i < hbm else SMEM if x.ndim == 1 else VMEM for i, x in enumerate(ins)
        ],
        out_specs=VMEM if single else [VMEM] * len(out_shape),
        scratch_shapes=scratch,
        compiler_params=PARAMS,
        cost_estimate=estimate,
        name=name,
    )(*ins)


def lanes_of(k, labels):
    return pl.ds(pl.multiple_of((lax.axis_index("blk") ^ k) * labels, labels), labels)


def turn():
    rep = lax.axis_index("rep")
    return (rep & 1) * 2 + ((rep >> 1) & 1)


def label_chunk(docs, q, c, lanes, sums):
    qt = q.T
    ct = c.T.astype(F32)
    labels = q.shape[0]

    def products(doc):
        load, enc_ref, enct_ref, gate_ref = doc[:4]
        load()
        enc = enc_ref[...]
        g = gate_ref[:, lanes]
        both = mm(enc, jnp.concatenate([qt, (ct * g).astype(BF16)], axis=1))
        return g, both[:, :labels], both[:, labels:]

    query_grad, class_grad = sums
    ahead = products(docs[0])
    for i, (_, _, enct_ref, gate_ref, attn_ref, score_ref, logit_ref) in enumerate(docs):
        g, scores, attn_grad = ahead
        if i + 1 < len(docs):
            ahead = products(docs[i + 1])
        length = gate_ref[:, gate_ref.shape[1] - LANES :][:, :1]
        token = lax.broadcasted_iota(jnp.int32, scores.shape, 0).astype(F32)
        expo = jnp.where(token < length, jnp.exp(scores), 0.0)
        attn = expo * (1.0 / jnp.sum(expo, axis=0, keepdims=True))
        attn_b = attn.astype(BF16)
        attn_ref[...] = attn_b
        inner = jnp.sum(attn * attn_grad, axis=0, keepdims=True)
        score_grad = (attn * (attn_grad - inner)).astype(BF16)
        score_ref[...] = score_grad
        both = mm(enct_ref[...], jnp.concatenate([attn_b, score_grad], axis=1))
        context, part = both[:, :labels], both[:, labels:]
        query_grad = part if query_grad is None else query_grad + part
        logit_ref[...] = jnp.sum(context * ct, axis=0, keepdims=True)
        part = context * g
        class_grad = part if class_grad is None else class_grad + part
    return query_grad, class_grad


def doc_list(loads, enc_ref, enct_ref, gate_ref, attn_ref, score_ref, logit_ref):
    return [
        (loads[d], enc_ref.at[d], enct_ref.at[d], gate_ref.at[d : d + 1], attn_ref.at[d],
         score_ref.at[d], logit_ref.at[d : d + 1])
        for d in range(enc_ref.shape[0])
    ]


def turn_around(enc_ref, enct_ref, copies=None):
    def load(d):
        if copies is not None:
            copies[d].wait()
        enct_ref[d] = enc_ref[d].T

    return [functools.partial(load, d) for d in range(enc_ref.shape[0])]


def pack_kernel(q_in, c_in, qc_ref, sem):
    copies = [pltpu.make_async_copy(x, qc_ref.at[i], sem.at[i]) for i, x in enumerate((q_in, c_in))]
    for copy in copies:
        copy.start()
    for copy in copies:
        copy.wait()


def after_first(loads, then):
    load = loads[0]

    def both():
        load()
        then()

    loads[0] = both


def make_gates(gate_ref, grad_ref, beam_ref, lens_ref):
    docs, labels = beam_ref.shape
    gate_ref[:, :labels] = grad_ref[...] * beam_ref[...].astype(F32)
    for d in range(docs):
        gate_ref[d : d + 1, labels:] = jnp.full((1, LANES), lens_ref[d], jnp.int32).astype(F32)


def own_kernel(enc_in, beam_in, grad_in, lens_in, qc_ref, enc_ref, gate_ref, enct_ref, attn_ref,
               score_ref, logit_ref, qsum_ref, csum_ref, beam_ref, grad_ref, lens_ref, sem):
    docs = enc_ref.shape[0]
    small = [(beam_in, beam_ref), (grad_in, grad_ref), (lens_in, lens_ref)]
    small = [pltpu.make_async_copy(x, y, sem.at[docs + i]) for i, (x, y) in enumerate(small)]
    copies = [
        pltpu.make_async_copy(enc_in.at[d], enc_ref.at[d], sem.at[d]) for d in range(docs)
    ]
    for copy in copies[:1] + small + copies[1:]:
        copy.start()
    loads = turn_around(enc_ref, enct_ref, copies)

    def gates():
        for copy in small:
            copy.wait()
        make_gates(gate_ref, grad_ref, beam_ref, lens_ref)

    after_first(loads, gates)
    qsum_ref[...], csum_ref[...] = label_chunk(
        doc_list(loads, enc_ref, enct_ref, gate_ref, attn_ref, score_ref, logit_ref),
        qc_ref[0], qc_ref[1], lanes_of(0, qc_ref.shape[1]), (None, None),
    )


def to_blocks(sums, rows_ref, out_refs):
    query_grad, class_grad = sums
    width = query_grad.shape[0]
    rows_ref[:, :width] = query_grad.T
    rows_ref[:, width:] = class_grad.T
    size = rows_ref.shape[0] // GROUP
    count = GROUP // len(out_refs)
    for i in range(GROUP):
        ref = out_refs[i // count]
        block = rows_ref[pl.ds(pl.multiple_of((turn() ^ i) * size, size), size), :]
        ref[(i % count) * size : (i % count + 1) * size, :] = block.astype(ref.dtype)


def other_kernel(lens_in, beam_ref, grad_ref, enc_ref, qc_ref, qsum_ref, csum_ref, gate_ref,
                 enct_ref, attn_ref, score_ref, logit_ref, *refs):
    refs, (lens_ref, sem) = refs[:-2], refs[-2:]
    copy = pltpu.make_async_copy(lens_in, lens_ref, sem)
    copy.start()

    def gates():
        copy.wait()
        make_gates(gate_ref, grad_ref, beam_ref, lens_ref)

    loads = turn_around(enc_ref, enct_ref)
    after_first(loads, gates)
    sums = label_chunk(
        doc_list(loads, enc_ref, enct_ref, gate_ref, attn_ref, score_ref, logit_ref),
        qc_ref[0], qc_ref[1], lanes_of(0, qc_ref.shape[1]), (qsum_ref[...], csum_ref[...]),
    )
    to_blocks(sums, refs[-1], refs[:-1])


def far_kernel(gate_ref, gate2_ref, enc_ref, enc2_ref, enct_ref,
               enct2_ref, qc_ref, attn_ref, score_ref, logit_ref, attn2_ref, score2_ref,
               logit2_ref, *refs):
    loads = [lambda: None] * enc_ref.shape[0]
    sums = label_chunk(
        doc_list(loads, enc_ref, enct_ref, gate_ref, attn_ref, score_ref, logit_ref)
        + doc_list(loads, enc2_ref, enct2_ref, gate2_ref, attn2_ref, score2_ref,
                   logit2_ref),
        qc_ref[0], qc_ref[1], lanes_of(2, qc_ref.shape[1]), (None, None),
    )
    to_blocks(sums, refs[-1], refs[:-1])


def state_parts(ks, gate_ref, chunks):
    docs, labels = gate_ref.shape[0], chunks[2].shape[1]
    ctx_grads = []
    for n, k in enumerate(ks):
        gate = gate_ref[:, lanes_of(k, labels)]
        gate = jnp.concatenate([gate, jnp.zeros((128 - docs, labels), F32)], axis=0).T
        c = chunks[4 * n + 2][1].astype(F32)
        ctx_grads.append([(c * gate[:, d : d + 1]).astype(BF16) for d in range(docs)])
    for d in range(docs):
        total = None
        for n in range(len(ks)):
            attn_ref, score_ref, qc_ref = chunks[4 * n : 4 * n + 3]
            part = mm(attn_ref[d], ctx_grads[n][d]) + mm(score_ref[d], qc_ref[0])
            total = part if total is None else total + part
        yield d, total


def away_kernel(ks, gate_ref, *refs):
    chunks, out_ref = refs[:-1], refs[-1]
    tokens, labels = chunks[0].shape[1:]
    for d, total in state_parts(ks, gate_ref, chunks):
        out_ref[d, :tokens] = total.astype(BF16)
        for n in range(len(ks)):
            logit = chunks[4 * n + 3][d : d + 1, :]
            high = logit.astype(BF16).astype(F32)
            pad = jnp.zeros((EXTRA - 2, labels), F32)
            pair = jnp.concatenate([high, logit - high, pad], axis=0)
            out_ref[d, tokens:, n * labels : (n + 1) * labels] = pair.astype(BF16)


def home_kernel(ks, gate_ref, *refs):
    chunks, (in_ref, out_ref, logit_ref, done_ref, sem) = refs[:-5], refs[-5:]
    tokens, labels = chunks[0].shape[1:]
    copies = []
    for d, total in state_parts(ks, gate_ref, chunks):
        done_ref[d] = (total + in_ref[d, :tokens].astype(F32)).astype(BF16)
        copies.append(pltpu.make_async_copy(done_ref.at[d], out_ref.at[d], sem.at[d]))
        copies[-1].start()
        for n, k in enumerate(ks):
            pair = in_ref[d, tokens:, n * labels : (n + 1) * labels].astype(F32)
            logit_ref[d : d + 1, lanes_of(k, labels)] = chunks[4 * n + 3][d : d + 1, :]
            logit_ref[d : d + 1, lanes_of(k ^ 1, labels)] = pair[0:1] + pair[1:2]
    for copy in copies:
        copy.wait()


def state_grad(gate, parts, more):
    docs, tokens, labels = parts[0][0].shape
    width = parts[0][2].shape[2]
    ins = [gate, *parts[0], *parts[1], *more]
    estimate = cost(4, docs, tokens, width, labels)
    if not more:
        out = shape((docs, tokens + EXTRA, width), BF16)
        return call(functools.partial(away_kernel, (0, 2)), out, ins, "state_away", (), estimate)
    out = shape((docs, tokens, width), BF16)
    return pl.pallas_call(
        functools.partial(home_kernel, (0, 2)),
        out_shape=[out, shape((docs, gate.shape[1] - LANES), F32)],
        in_specs=[VMEM] * len(ins),
        out_specs=[pl.BlockSpec(memory_space=pl.ANY), VMEM],
        scratch_shapes=[pltpu.VMEM(out.shape, BF16), pltpu.SemaphoreType.DMA((docs,))],
        compiler_params=PARAMS,
        cost_estimate=estimate,
        name="state_home",
    )(*ins)


def add_kernel(count, *refs):
    total = refs[0][...].astype(F32)
    for ref in refs[1:count]:
        total = total + ref[...].astype(F32)
    size = refs[count].shape[0]
    for i, ref in enumerate(refs[count:]):
        ref[...] = total[i * size : (i + 1) * size].astype(ref.dtype)


def add(arrays, dtypes, estimate=None):
    rows, cols = arrays[0].shape
    out = [shape((rows // len(dtypes), cols), dtype) for dtype in dtypes]
    return call(
        functools.partial(add_kernel, len(arrays)), out, arrays, "add", estimate=estimate
    )


def rows_kernel(*refs):
    block_refs, (out_ref, rows_ref, sem) = refs[:-3], refs[-3:]
    size = block_refs[0].shape[0]
    copies = []
    for i, ref in enumerate(block_refs):
        rows_ref[i] = ref[...].astype(F32)
        to = pl.ds(pl.multiple_of((turn() ^ i) * size, size), size)
        copies.append(pltpu.make_async_copy(rows_ref.at[i], out_ref.at[to], sem.at[i]))
        copies[-1].start()
    for copy in copies:
        copy.wait()


def to_rows(blocks):
    count = len(blocks)
    rows, cols = blocks[0].shape
    return pl.pallas_call(
        rows_kernel,
        out_shape=shape((count * rows, cols), F32),
        in_specs=[VMEM] * count,
        out_specs=pl.BlockSpec(memory_space=pl.ANY),
        scratch_shapes=[pltpu.VMEM((count, rows, cols), F32), pltpu.SemaphoreType.DMA((count,))],
        compiler_params=PARAMS,
        name="to_rows",
    )(*blocks)


def per_device(reps, blks, encoded, queries, classifiers, lengths, beam, logit_grad):
    labels, width = queries.shape
    docs, tokens, _ = encoded.shape
    total = reps * blks

    def swap(x, mask):
        return lax.ppermute(x, ("rep", "blk"), [(i, i ^ mask) for i in range(total)])

    core, ax = 1, 2
    ay, az, azz = blks, 2 * blks, 4 * blks
    turns = [0, az, ay, ay | az]

    qc = call(
        pack_kernel, shape((2, labels, width), BF16), [queries, classifiers], "pack",
        [pltpu.SemaphoreType.DMA((2,))], hbm=2,
    )
    encoded2, qc = lax.optimization_barrier((encoded, qc))
    far_qc = swap(qc, ax)
    encoded2, beam2, grad2 = swap(encoded2, core), swap(beam, core), swap(logit_grad, core)
    lengths2 = swap(lengths, core)

    per_chunk = [
        shape((docs, tokens, labels), BF16),
        shape((docs, tokens, labels), BF16),
        shape((docs, labels), F32),
    ]
    gates = shape((docs, beam.shape[1] + LANES), F32)
    turned = shape((docs, width, tokens), BF16)
    block = shape((labels // GROUP, 2 * width), BF16)
    halves = [shape((labels // 2, 2 * width), dtype) for dtype in (F32, BF16)]
    rows = [pltpu.VMEM((labels, 2 * width), F32)]
    sums = [shape((width, labels), F32)] * 2
    estimate = functools.partial(cost, tokens=tokens, width=width, labels=labels)

    enc, gate, enct, attn, score, logit, *acc = call(
        own_kernel,
        [shape(encoded.shape, BF16), gates, turned] + per_chunk + sums,
        [encoded, beam, logit_grad, lengths, qc], "own_labels",
        [pltpu.VMEM(beam.shape, jnp.int32), pltpu.VMEM(beam.shape, F32),
         pltpu.SMEM((docs,), jnp.int32), pltpu.SemaphoreType.DMA((docs + 3,))],
        estimate(4, docs), hbm=4,
    )
    gate2, enct2, attn2, score2, logit2, keep, send = call(
        other_kernel, [gates, turned] + per_chunk + halves,
        [lengths2, beam2, grad2, encoded2, qc, *acc], "own_labels_other_docs",
        rows + [pltpu.SMEM((docs,), jnp.int32), pltpu.SemaphoreType.DMA(())],
        estimate(4, docs), hbm=1,
    )
    received = swap(send, ay)
    far_attn, far_score, far_logit, far_attn2, far_score2, far_logit2, *far = call(
        far_kernel, per_chunk + per_chunk + [shape(block.shape, F32)] + [block] * (GROUP - 1),
        [gate, gate2, enc, encoded2, enct, enct2, far_qc],
        "far_labels", rows, estimate(4, 2 * docs),
    )

    far, keep, received = lax.optimization_barrier((far, keep, received))
    keep, send = add([keep, received], [F32, BF16])
    send, far = lax.optimization_barrier((send, far))
    relayed = swap(far[2], ay)
    received = [swap(far[1], ax | az), swap(far[3], ax | ay | az)]
    (first,) = add([far[0], relayed], [BF16])
    first, send, far_attn2 = lax.optimization_barrier((first, send, far_attn2))
    received.append(swap(first, ax))
    near = swap(send, az)
    state2 = state_grad(
        gate2,
        [(attn2, score2, qc, logit2), (far_attn2, far_score2, far_qc, far_logit2)], [],
    )
    received, near = lax.optimization_barrier((received, near))
    state_in = swap(state2, core)
    (own,) = add([keep, near, *received], [BF16], LONG)
    far_attn, far_score, own = lax.optimization_barrier((far_attn, far_score, own))
    state, logits = state_grad(
        gate, [(attn, score, qc, logit), (far_attn, far_score, far_qc, far_logit)],
        [state_in],
    )
    received, state = lax.optimization_barrier((swap(own, azz), state))
    (own,) = add([own, received], [BF16])
    if reps > 8:
        members = [[i * 8 + j for i in range(reps // 8)] for j in range(8)]
        own = lax.psum(own.astype(F32), "rep", axis_index_groups=members).astype(BF16)

    both, second, first = lax.optimization_barrier([swap(own, mask) for mask in turns[:0:-1]])
    label_grad = to_rows([own, first, second, both])
    return logits, state, label_grad


def solution(mesh):
    reps, blks = mesh.shape["rep"], mesh.shape["blk"]
    assert blks == 4 and reps >= 8 and reps & (reps - 1) == 0
    in_specs = (
        P(("rep", "blk"), None, None),
        P("blk", None),
        P("blk", None),
        P(("rep", "blk")),
        P(("rep", "blk"), None),
        P(("rep", "blk"), None),
    )
    out_specs = (P(("rep", "blk"), None), P(("rep", "blk"), None, None), P("blk", None))
    return jax.shard_map(
        functools.partial(per_device, reps, blks),
        mesh=mesh, in_specs=in_specs, out_specs=out_specs, check_vma=False,
    )
```

```python
import functools

import jax
import jax.numpy as jnp
from jax import lax
from jax.experimental import pallas as pl
from jax.experimental.pallas import tpu as pltpu
from jax.sharding import PartitionSpec as P

F32 = jnp.float32
BF16 = jnp.bfloat16
VMEM = pl.BlockSpec(memory_space=pltpu.VMEM)
SMEM = pl.BlockSpec(memory_space=pltpu.SMEM)
HBM = pl.BlockSpec(memory_space=pltpu.HBM)
PARAMS = pltpu.CompilerParams(vmem_limit_bytes=20 * 1024 * 1024)
GROUP = 4
LANES = 128
EXTRA = 16


LONG = pl.CostEstimate(flops=10**11, transcendentals=0, bytes_accessed=0)


def shape(dims, dtype):
    return jax.ShapeDtypeStruct(dims, dtype)


def mm(a, b):
    return jnp.dot(a, b, preferred_element_type=F32)


def cost(products, docs, tokens, width, labels):
    return pl.CostEstimate(
        flops=2 * products * docs * tokens * width * labels,
        transcendentals=docs * tokens * labels,
        bytes_accessed=4 * docs * tokens * width,
    )


def call(kernel, out_shape, ins, name, scratch=(), estimate=None, hbm=0):
    single = not isinstance(out_shape, (list, tuple))
    ins = [pltpu.with_memory_space_constraint(x, pltpu.HBM) for x in ins[:hbm]] + list(ins[hbm:])
    return pl.pallas_call(
        kernel,
        out_shape=out_shape,
        in_specs=[
            HBM if i < hbm else SMEM if x.ndim == 1 else VMEM for i, x in enumerate(ins)
        ],
        out_specs=VMEM if single else [VMEM] * len(out_shape),
        scratch_shapes=scratch,
        compiler_params=PARAMS,
        cost_estimate=estimate,
        name=name,
    )(*ins)


def lanes_of(k, labels):
    return pl.ds(pl.multiple_of((lax.axis_index("blk") ^ k) * labels, labels), labels)


def turn():
    rep = lax.axis_index("rep")
    return (rep & 1) * 2 + ((rep >> 1) & 1)


def label_chunk(docs, q, c, lanes, sums):
    qt = q.T
    ct = c.T.astype(F32)
    labels = q.shape[0]

    def products(doc):
        load, enc_ref, enct_ref, gate_ref = doc[:4]
        load()
        enc = enc_ref[...]
        g = gate_ref[:, lanes]
        both = mm(enc, jnp.concatenate([qt, (ct * g).astype(BF16)], axis=1))
        return g, both[:, :labels], both[:, labels:]

    query_grad, class_grad = sums
    ahead = products(docs[0])
    for i, (_, _, enct_ref, gate_ref, attn_ref, score_ref, logit_ref) in enumerate(docs):
        g, scores, attn_grad = ahead
        if i + 1 < len(docs):
            ahead = products(docs[i + 1])
        length = gate_ref[:, gate_ref.shape[1] - LANES :][:, :1]
        token = lax.broadcasted_iota(jnp.int32, scores.shape, 0).astype(F32)
        expo = jnp.where(token < length, jnp.exp(scores), 0.0)
        attn = expo * (1.0 / jnp.sum(expo, axis=0, keepdims=True))
        attn_b = attn.astype(BF16)
        attn_ref[...] = attn_b
        inner = jnp.sum(attn * attn_grad, axis=0, keepdims=True)
        score_grad = (attn * (attn_grad - inner)).astype(BF16)
        score_ref[...] = score_grad
        both = mm(enct_ref[...], jnp.concatenate([attn_b, score_grad], axis=1))
        context, part = both[:, :labels], both[:, labels:]
        query_grad = part if query_grad is None else query_grad + part
        logit_ref[...] = jnp.sum(context * ct, axis=0, keepdims=True)
        part = context * g
        class_grad = part if class_grad is None else class_grad + part
    return query_grad, class_grad


def doc_list(loads, enc_ref, enct_ref, gate_ref, attn_ref, score_ref, logit_ref):
    return [
        (loads[d], enc_ref.at[d], enct_ref.at[d], gate_ref.at[d : d + 1], attn_ref.at[d],
         score_ref.at[d], logit_ref.at[d : d + 1])
        for d in range(enc_ref.shape[0])
    ]


def turn_around(enc_ref, enct_ref, copies=None):
    def load(d):
        if copies is not None:
            copies[d].wait()
        enct_ref[d] = enc_ref[d].T

    return [functools.partial(load, d) for d in range(enc_ref.shape[0])]


def pack_kernel(q_in, c_in, qc_ref, sem):
    copies = [pltpu.make_async_copy(x, qc_ref.at[i], sem.at[i]) for i, x in enumerate((q_in, c_in))]
    for copy in copies:
        copy.start()
    for copy in copies:
        copy.wait()


def after_first(loads, then):
    load = loads[0]

    def both():
        load()
        then()

    loads[0] = both


def make_gates(gate_ref, grad_ref, beam_ref, lens_ref):
    docs, labels = beam_ref.shape
    gate_ref[:, :labels] = grad_ref[...] * beam_ref[...].astype(F32)
    for d in range(docs):
        gate_ref[d : d + 1, labels:] = jnp.full((1, LANES), lens_ref[d], jnp.int32).astype(F32)


def own_kernel(enc_in, beam_in, grad_in, lens_in, qc_ref, enc_ref, gate_ref, enct_ref, attn_ref,
               score_ref, logit_ref, qsum_ref, csum_ref, beam_ref, grad_ref, lens_ref, sem):
    docs = enc_ref.shape[0]
    small = [(beam_in, beam_ref), (grad_in, grad_ref), (lens_in, lens_ref)]
    small = [pltpu.make_async_copy(x, y, sem.at[docs + i]) for i, (x, y) in enumerate(small)]
    copies = [
        pltpu.make_async_copy(enc_in.at[d], enc_ref.at[d], sem.at[d]) for d in range(docs)
    ]
    for copy in copies[:1] + small + copies[1:]:
        copy.start()
    loads = turn_around(enc_ref, enct_ref, copies)

    def gates():
        for copy in small:
            copy.wait()
        make_gates(gate_ref, grad_ref, beam_ref, lens_ref)

    after_first(loads, gates)
    qsum_ref[...], csum_ref[...] = label_chunk(
        doc_list(loads, enc_ref, enct_ref, gate_ref, attn_ref, score_ref, logit_ref),
        qc_ref[0], qc_ref[1], lanes_of(0, qc_ref.shape[1]), (None, None),
    )


def to_blocks(sums, rows_ref, out_refs):
    query_grad, class_grad = sums
    width = query_grad.shape[0]
    rows_ref[:, :width] = query_grad.T
    rows_ref[:, width:] = class_grad.T
    size = rows_ref.shape[0] // GROUP
    count = GROUP // len(out_refs)
    for i in range(GROUP):
        ref = out_refs[i // count]
        block = rows_ref[pl.ds(pl.multiple_of((turn() ^ i) * size, size), size), :]
        ref[(i % count) * size : (i % count + 1) * size, :] = block.astype(ref.dtype)


def other_kernel(lens_in, beam_ref, grad_ref, enc_ref, qc_ref, qsum_ref, csum_ref, gate_ref,
                 enct_ref, attn_ref, score_ref, logit_ref, *refs):
    refs, (lens_ref, sem) = refs[:-2], refs[-2:]
    copy = pltpu.make_async_copy(lens_in, lens_ref, sem)
    copy.start()

    def gates():
        copy.wait()
        make_gates(gate_ref, grad_ref, beam_ref, lens_ref)

    loads = turn_around(enc_ref, enct_ref)
    after_first(loads, gates)
    sums = label_chunk(
        doc_list(loads, enc_ref, enct_ref, gate_ref, attn_ref, score_ref, logit_ref),
        qc_ref[0], qc_ref[1], lanes_of(0, qc_ref.shape[1]), (qsum_ref[...], csum_ref[...]),
    )
    to_blocks(sums, refs[-1], refs[:-1])


def far_kernel(gate_ref, gate2_ref, enc_ref, enc2_ref, enct_ref,
               enct2_ref, qc_ref, attn_ref, score_ref, logit_ref, attn2_ref, score2_ref,
               logit2_ref, *refs):
    loads = [lambda: None] * enc_ref.shape[0]
    sums = label_chunk(
        doc_list(loads, enc_ref, enct_ref, gate_ref, attn_ref, score_ref, logit_ref)
        + doc_list(loads, enc2_ref, enct2_ref, gate2_ref, attn2_ref, score2_ref,
                   logit2_ref),
        qc_ref[0], qc_ref[1], lanes_of(2, qc_ref.shape[1]), (None, None),
    )
    to_blocks(sums, refs[-1], refs[:-1])


def state_parts(ks, gate_ref, chunks):
    docs, labels = gate_ref.shape[0], chunks[2].shape[1]
    ctx_grads = []
    for n, k in enumerate(ks):
        gate = gate_ref[:, lanes_of(k, labels)]
        gate = jnp.concatenate([gate, jnp.zeros((128 - docs, labels), F32)], axis=0).T
        c = chunks[4 * n + 2][1].astype(F32)
        ctx_grads.append([(c * gate[:, d : d + 1]).astype(BF16) for d in range(docs)])
    for d in range(docs):
        total = None
        for n in range(len(ks)):
            attn_ref, score_ref, qc_ref = chunks[4 * n : 4 * n + 3]
            part = mm(attn_ref[d], ctx_grads[n][d]) + mm(score_ref[d], qc_ref[0])
            total = part if total is None else total + part
        yield d, total


def away_kernel(ks, gate_ref, *refs):
    chunks, out_ref = refs[:-1], refs[-1]
    tokens, labels = chunks[0].shape[1:]
    for d, total in state_parts(ks, gate_ref, chunks):
        out_ref[d, :tokens] = total.astype(BF16)
        for n in range(len(ks)):
            logit = chunks[4 * n + 3][d : d + 1, :]
            high = logit.astype(BF16).astype(F32)
            pad = jnp.zeros((EXTRA - 2, labels), F32)
            pair = jnp.concatenate([high, logit - high, pad], axis=0)
            out_ref[d, tokens:, n * labels : (n + 1) * labels] = pair.astype(BF16)


def home_kernel(ks, gate_ref, *refs):
    chunks, (in_ref, out_ref, logit_ref, done_ref, sem) = refs[:-5], refs[-5:]
    tokens, labels = chunks[0].shape[1:]
    copies = []
    for d, total in state_parts(ks, gate_ref, chunks):
        done_ref[d] = (total + in_ref[d, :tokens].astype(F32)).astype(BF16)
        copies.append(pltpu.make_async_copy(done_ref.at[d], out_ref.at[d], sem.at[d]))
        copies[-1].start()
        for n, k in enumerate(ks):
            pair = in_ref[d, tokens:, n * labels : (n + 1) * labels].astype(F32)
            logit_ref[d : d + 1, lanes_of(k, labels)] = chunks[4 * n + 3][d : d + 1, :]
            logit_ref[d : d + 1, lanes_of(k ^ 1, labels)] = pair[0:1] + pair[1:2]
    for copy in copies:
        copy.wait()


def state_grad(gate, parts, more):
    docs, tokens, labels = parts[0][0].shape
    width = parts[0][2].shape[2]
    ins = [gate, *parts[0], *parts[1], *more]
    estimate = cost(4, docs, tokens, width, labels)
    if not more:
        out = shape((docs, tokens + EXTRA, width), BF16)
        return call(functools.partial(away_kernel, (0, 2)), out, ins, "state_away", (), estimate)
    out = shape((docs, tokens, width), BF16)
    return pl.pallas_call(
        functools.partial(home_kernel, (0, 2)),
        out_shape=[out, shape((docs, gate.shape[1] - LANES), F32)],
        in_specs=[VMEM] * len(ins),
        out_specs=[pl.BlockSpec(memory_space=pl.ANY), VMEM],
        scratch_shapes=[pltpu.VMEM(out.shape, BF16), pltpu.SemaphoreType.DMA((docs,))],
        compiler_params=PARAMS,
        cost_estimate=estimate,
        name="state_home",
    )(*ins)


def add_kernel(count, *refs):
    total = refs[0][...].astype(F32)
    for ref in refs[1:count]:
        total = total + ref[...].astype(F32)
    size = refs[count].shape[0]
    for i, ref in enumerate(refs[count:]):
        ref[...] = total[i * size : (i + 1) * size].astype(ref.dtype)


def add(arrays, dtypes, estimate=None):
    rows, cols = arrays[0].shape
    out = [shape((rows // len(dtypes), cols), dtype) for dtype in dtypes]
    return call(
        functools.partial(add_kernel, len(arrays)), out, arrays, "add", estimate=estimate
    )


def rows_kernel(*refs):
    block_refs, (out_ref, rows_ref, sem) = refs[:-3], refs[-3:]
    size = block_refs[0].shape[0]
    core = lax.axis_index("blk") & 1
    copies = []
    for i, (ref, block) in enumerate(zip(block_refs, (0, 1 + core, 2 - core, 3))):
        rows_ref[i] = ref[...].astype(F32)
        to = pl.ds(pl.multiple_of((turn() ^ block) * size, size), size)
        copies.append(pltpu.make_async_copy(rows_ref.at[i], out_ref.at[to], sem.at[i]))
        copies[-1].start()
    for copy in copies:
        copy.wait()


def to_rows(blocks):
    count = len(blocks)
    rows, cols = blocks[0].shape
    return pl.pallas_call(
        rows_kernel,
        out_shape=shape((count * rows, cols), F32),
        in_specs=[VMEM] * count,
        out_specs=pl.BlockSpec(memory_space=pl.ANY),
        scratch_shapes=[pltpu.VMEM((count, rows, cols), F32), pltpu.SemaphoreType.DMA((count,))],
        compiler_params=PARAMS,
        name="to_rows",
    )(*blocks)


def per_device(reps, blks, encoded, queries, classifiers, lengths, beam, logit_grad):
    labels, width = queries.shape
    docs, tokens, _ = encoded.shape
    total = reps * blks

    def swap(x, mask, other=None):
        masks = (mask, mask if other is None else other)
        return lax.ppermute(x, ("rep", "blk"), [(i, i ^ masks[i & 1]) for i in range(total)])

    core, ax = 1, 2
    ay, az, azz = blks, 2 * blks, 4 * blks
    turns = [0, az, ay, ay | az]

    qc = call(
        pack_kernel, shape((2, labels, width), BF16), [queries, classifiers], "pack",
        [pltpu.SemaphoreType.DMA((2,))], hbm=2,
    )
    encoded2, qc = lax.optimization_barrier((encoded, qc))
    far_qc = swap(qc, ax)
    encoded2, beam2, grad2 = swap(encoded2, core), swap(beam, core), swap(logit_grad, core)
    lengths2 = swap(lengths, core)

    per_chunk = [
        shape((docs, tokens, labels), BF16),
        shape((docs, tokens, labels), BF16),
        shape((docs, labels), F32),
    ]
    gates = shape((docs, beam.shape[1] + LANES), F32)
    turned = shape((docs, width, tokens), BF16)
    block = shape((labels // GROUP, 2 * width), BF16)
    halves = [shape((labels // 2, 2 * width), dtype) for dtype in (F32, BF16)]
    rows = [pltpu.VMEM((labels, 2 * width), F32)]
    sums = [shape((width, labels), F32)] * 2
    estimate = functools.partial(cost, tokens=tokens, width=width, labels=labels)

    enc, gate, enct, attn, score, logit, *acc = call(
        own_kernel,
        [shape(encoded.shape, BF16), gates, turned] + per_chunk + sums,
        [encoded, beam, logit_grad, lengths, qc], "own_labels",
        [pltpu.VMEM(beam.shape, jnp.int32), pltpu.VMEM(beam.shape, F32),
         pltpu.SMEM((docs,), jnp.int32), pltpu.SemaphoreType.DMA((docs + 3,))],
        estimate(4, docs), hbm=4,
    )
    gate2, enct2, attn2, score2, logit2, keep, send = call(
        other_kernel, [gates, turned] + per_chunk + halves,
        [lengths2, beam2, grad2, encoded2, qc, *acc], "own_labels_other_docs",
        rows + [pltpu.SMEM((docs,), jnp.int32), pltpu.SemaphoreType.DMA(())],
        estimate(4, docs), hbm=1,
    )
    received = swap(send, ay)
    far_attn, far_score, far_logit, far_attn2, far_score2, far_logit2, *far = call(
        far_kernel, per_chunk + per_chunk + [shape(block.shape, F32)] + [block] * (GROUP - 1),
        [gate, gate2, enc, encoded2, enct, enct2, far_qc],
        "far_labels", rows, estimate(4, 2 * docs),
    )

    far, keep, received = lax.optimization_barrier((far, keep, received))
    keep, send = add([keep, received], [F32, BF16])
    send, far = lax.optimization_barrier((send, far))
    relayed = swap(far[2], ay)
    received = [swap(far[1], ax | az), swap(far[3], ax | ay | az)]
    (first,) = add([far[0], relayed], [BF16])
    first, send, far_attn2 = lax.optimization_barrier((first, send, far_attn2))
    received.append(swap(first, ax))
    near = swap(send, az)
    state2 = state_grad(
        gate2,
        [(attn2, score2, qc, logit2), (far_attn2, far_score2, far_qc, far_logit2)], [],
    )
    received, near = lax.optimization_barrier((received, near))
    state_in = swap(state2, core)
    (own,) = add([keep, near, *received], [BF16], LONG)
    far_attn, far_score, own = lax.optimization_barrier((far_attn, far_score, own))
    state, logits = state_grad(
        gate, [(attn, score, qc, logit), (far_attn, far_score, far_qc, far_logit)],
        [state_in],
    )
    received, state = lax.optimization_barrier((swap(own, azz), state))
    (own,) = add([own, received], [BF16])
    if reps > 8:
        members = [[i * 8 + j for i in range(reps // 8)] for j in range(8)]
        own = lax.psum(own.astype(F32), "rep", axis_index_groups=members).astype(BF16)

    both, second, first = lax.optimization_barrier(
        [swap(own, ay | az), swap(own, ay, az), swap(own, az, ay)]
    )
    label_grad = to_rows([own, first, second, both])
    return logits, state, label_grad


def solution(mesh):
    reps, blks = mesh.shape["rep"], mesh.shape["blk"]
    assert blks == 4 and reps >= 8 and reps & (reps - 1) == 0
    in_specs = (
        P(("rep", "blk"), None, None),
        P("blk", None),
        P("blk", None),
        P(("rep", "blk")),
        P(("rep", "blk"), None),
        P(("rep", "blk"), None),
    )
    out_specs = (P(("rep", "blk"), None), P(("rep", "blk"), None, None), P("blk", None))
    return jax.shard_map(
        functools.partial(per_device, reps, blks),
        mesh=mesh, in_specs=in_specs, out_specs=out_specs, check_vma=False,
    )
```

```python
import functools

import jax
import jax.numpy as jnp
from jax import lax
from jax.experimental import pallas as pl
from jax.experimental.pallas import tpu as pltpu
from jax.sharding import PartitionSpec as P

F32 = jnp.float32
BF16 = jnp.bfloat16
VMEM = pl.BlockSpec(memory_space=pltpu.VMEM)
SMEM = pl.BlockSpec(memory_space=pltpu.SMEM)
HBM = pl.BlockSpec(memory_space=pltpu.HBM)
PARAMS = pltpu.CompilerParams(vmem_limit_bytes=20 * 1024 * 1024)
GROUP = 4
LANES = 128
EXTRA = 16


LONG = pl.CostEstimate(flops=10**11, transcendentals=0, bytes_accessed=0)


def shape(dims, dtype):
    return jax.ShapeDtypeStruct(dims, dtype)


def mm(a, b):
    return jnp.dot(a, b, preferred_element_type=F32)


def cost(products, docs, tokens, width, labels):
    return pl.CostEstimate(
        flops=2 * products * docs * tokens * width * labels,
        transcendentals=docs * tokens * labels,
        bytes_accessed=4 * docs * tokens * width,
    )


def call(kernel, out_shape, ins, name, scratch=(), estimate=None, hbm=0):
    single = not isinstance(out_shape, (list, tuple))
    ins = [pltpu.with_memory_space_constraint(x, pltpu.HBM) for x in ins[:hbm]] + list(ins[hbm:])
    return pl.pallas_call(
        kernel,
        out_shape=out_shape,
        in_specs=[
            HBM if i < hbm else SMEM if x.ndim == 1 else VMEM for i, x in enumerate(ins)
        ],
        out_specs=VMEM if single else [VMEM] * len(out_shape),
        scratch_shapes=scratch,
        compiler_params=PARAMS,
        cost_estimate=estimate,
        name=name,
    )(*ins)


def lanes_of(k, labels):
    return pl.ds(pl.multiple_of((lax.axis_index("blk") ^ k) * labels, labels), labels)


def turn():
    rep = lax.axis_index("rep")
    return (rep & 1) * 2 + ((rep >> 1) & 1)


def label_chunk(docs, q, c, lanes, sums):
    qt = q.T
    ct = c.T.astype(F32)
    labels = q.shape[0]

    def products(doc):
        load, enc_ref, enct_ref, gate_ref = doc[:4]
        load()
        enc = enc_ref[...]
        g = gate_ref[:, lanes]
        both = mm(enc, jnp.concatenate([qt, (ct * g).astype(BF16)], axis=1))
        return g, both[:, :labels], both[:, labels:]

    query_grad, class_grad = sums
    ahead = products(docs[0])
    for i, (_, _, enct_ref, gate_ref, attn_ref, score_ref, logit_ref) in enumerate(docs):
        g, scores, attn_grad = ahead
        if i + 1 < len(docs):
            ahead = products(docs[i + 1])
        length = gate_ref[:, gate_ref.shape[1] - LANES :][:, :1]
        token = lax.broadcasted_iota(jnp.int32, scores.shape, 0).astype(F32)
        expo = jnp.where(token < length, jnp.exp(scores), 0.0)
        attn = expo * (1.0 / jnp.sum(expo, axis=0, keepdims=True))
        attn_b = attn.astype(BF16)
        attn_ref[...] = attn_b
        inner = jnp.sum(attn * attn_grad, axis=0, keepdims=True)
        score_grad = (attn * (attn_grad - inner)).astype(BF16)
        score_ref[...] = score_grad
        both = mm(enct_ref[...], jnp.concatenate([attn_b, score_grad], axis=1))
        context, part = both[:, :labels], both[:, labels:]
        query_grad = part if query_grad is None else query_grad + part
        logit_ref[...] = jnp.sum(context * ct, axis=0, keepdims=True)
        part = context * g
        class_grad = part if class_grad is None else class_grad + part
    return query_grad, class_grad


def doc_list(loads, enc_ref, enct_ref, gate_ref, attn_ref, score_ref, logit_ref):
    return [
        (loads[d], enc_ref.at[d], enct_ref.at[d], gate_ref.at[d : d + 1], attn_ref.at[d],
         score_ref.at[d], logit_ref.at[d : d + 1])
        for d in range(enc_ref.shape[0])
    ]


def turn_around(enc_ref, enct_ref, copies=None):
    def load(d):
        if copies is not None:
            copies[d].wait()
        enct_ref[d] = enc_ref[d].T

    return [functools.partial(load, d) for d in range(enc_ref.shape[0])]


def pack_kernel(q_in, c_in, qc_ref, sem):
    copies = [pltpu.make_async_copy(x, qc_ref.at[i], sem.at[i]) for i, x in enumerate((q_in, c_in))]
    for copy in copies:
        copy.start()
    for copy in copies:
        copy.wait()


def after_first(loads, then):
    load = loads[0]

    def both():
        load()
        then()

    loads[0] = both


def make_gates(gate_ref, grad_ref, beam_ref, lens_ref):
    docs, labels = beam_ref.shape
    gate_ref[:, :labels] = grad_ref[...] * beam_ref[...].astype(F32)
    for d in range(docs):
        gate_ref[d : d + 1, labels:] = jnp.full((1, LANES), lens_ref[d], jnp.int32).astype(F32)


def own_kernel(enc_in, beam_in, grad_in, lens_in, qc_ref, enc_ref, gate_ref, enct_ref, attn_ref,
               score_ref, logit_ref, qsum_ref, csum_ref, beam_ref, grad_ref, lens_ref, sem):
    docs = enc_ref.shape[0]
    small = [(beam_in, beam_ref), (grad_in, grad_ref), (lens_in, lens_ref)]
    small = [pltpu.make_async_copy(x, y, sem.at[docs + i]) for i, (x, y) in enumerate(small)]
    copies = [
        pltpu.make_async_copy(enc_in.at[d], enc_ref.at[d], sem.at[d]) for d in range(docs)
    ]
    for copy in copies[:1] + small + copies[1:]:
        copy.start()
    loads = turn_around(enc_ref, enct_ref, copies)

    def gates():
        for copy in small:
            copy.wait()
        make_gates(gate_ref, grad_ref, beam_ref, lens_ref)

    after_first(loads, gates)
    qsum_ref[...], csum_ref[...] = label_chunk(
        doc_list(loads, enc_ref, enct_ref, gate_ref, attn_ref, score_ref, logit_ref),
        qc_ref[0], qc_ref[1], lanes_of(0, qc_ref.shape[1]), (None, None),
    )


def to_blocks(sums, rows_ref, out_refs):
    query_grad, class_grad = sums
    width = query_grad.shape[0]
    rows_ref[:, :width] = query_grad.T
    rows_ref[:, width:] = class_grad.T
    size = rows_ref.shape[0] // GROUP
    count = GROUP // len(out_refs)
    for i in range(GROUP):
        ref = out_refs[i // count]
        block = rows_ref[pl.ds(pl.multiple_of((turn() ^ i) * size, size), size), :]
        ref[(i % count) * size : (i % count + 1) * size, :] = block.astype(ref.dtype)


def other_kernel(lens_in, beam_ref, grad_ref, enc_ref, qc_ref, qsum_ref, csum_ref, gate_ref,
                 enct_ref, attn_ref, score_ref, logit_ref, *refs):
    refs, (lens_ref, sem) = refs[:-2], refs[-2:]
    copy = pltpu.make_async_copy(lens_in, lens_ref, sem)
    copy.start()

    def gates():
        copy.wait()
        make_gates(gate_ref, grad_ref, beam_ref, lens_ref)

    loads = turn_around(enc_ref, enct_ref)
    after_first(loads, gates)
    sums = label_chunk(
        doc_list(loads, enc_ref, enct_ref, gate_ref, attn_ref, score_ref, logit_ref),
        qc_ref[0], qc_ref[1], lanes_of(0, qc_ref.shape[1]), (qsum_ref[...], csum_ref[...]),
    )
    to_blocks(sums, refs[-1], refs[:-1])


def far_kernel(gate_ref, gate2_ref, enc_ref, enc2_ref, enct_ref,
               enct2_ref, qc_ref, attn_ref, score_ref, logit_ref, attn2_ref, score2_ref,
               logit2_ref, *refs):
    loads = [lambda: None] * enc_ref.shape[0]
    sums = label_chunk(
        doc_list(loads, enc_ref, enct_ref, gate_ref, attn_ref, score_ref, logit_ref)
        + doc_list(loads, enc2_ref, enct2_ref, gate2_ref, attn2_ref, score2_ref,
                   logit2_ref),
        qc_ref[0], qc_ref[1], lanes_of(2, qc_ref.shape[1]), (None, None),
    )
    to_blocks(sums, refs[-1], refs[:-1])


def state_parts(ks, gate_ref, chunks):
    docs, labels = gate_ref.shape[0], chunks[2].shape[1]
    ctx_grads = []
    for n, k in enumerate(ks):
        gate = gate_ref[:, lanes_of(k, labels)]
        gate = jnp.concatenate([gate, jnp.zeros((128 - docs, labels), F32)], axis=0).T
        c = chunks[4 * n + 2][1].astype(F32)
        ctx_grads.append([(c * gate[:, d : d + 1]).astype(BF16) for d in range(docs)])
    for d in range(docs):
        total = None
        for n in range(len(ks)):
            attn_ref, score_ref, qc_ref = chunks[4 * n : 4 * n + 3]
            part = mm(attn_ref[d], ctx_grads[n][d]) + mm(score_ref[d], qc_ref[0])
            total = part if total is None else total + part
        yield d, total


def away_kernel(ks, gate_ref, *refs):
    chunks, out_ref = refs[:-1], refs[-1]
    tokens, labels = chunks[0].shape[1:]
    for d, total in state_parts(ks, gate_ref, chunks):
        out_ref[d, :tokens] = total.astype(BF16)
        for n in range(len(ks)):
            logit = chunks[4 * n + 3][d : d + 1, :]
            high = logit.astype(BF16).astype(F32)
            pad = jnp.zeros((EXTRA - 2, labels), F32)
            pair = jnp.concatenate([high, logit - high, pad], axis=0)
            out_ref[d, tokens:, n * labels : (n + 1) * labels] = pair.astype(BF16)


def home_kernel(ks, gate_ref, *refs):
    chunks, (in_ref, out_ref, logit_ref, done_ref, sem) = refs[:-5], refs[-5:]
    tokens, labels = chunks[0].shape[1:]
    copies = []
    for d, total in state_parts(ks, gate_ref, chunks):
        done_ref[d] = (total + in_ref[d, :tokens].astype(F32)).astype(BF16)
        copies.append(pltpu.make_async_copy(done_ref.at[d], out_ref.at[d], sem.at[d]))
        copies[-1].start()
        for n, k in enumerate(ks):
            pair = in_ref[d, tokens:, n * labels : (n + 1) * labels].astype(F32)
            logit_ref[d : d + 1, lanes_of(k, labels)] = chunks[4 * n + 3][d : d + 1, :]
            logit_ref[d : d + 1, lanes_of(k ^ 1, labels)] = pair[0:1] + pair[1:2]
    for copy in copies:
        copy.wait()


def state_grad(gate, parts, more):
    docs, tokens, labels = parts[0][0].shape
    width = parts[0][2].shape[2]
    ins = [gate, *parts[0], *parts[1], *more]
    estimate = cost(4, docs, tokens, width, labels)
    if not more:
        out = shape((docs, tokens + EXTRA, width), BF16)
        return call(functools.partial(away_kernel, (0, 2)), out, ins, "state_away", (), estimate)
    out = shape((docs, tokens, width), BF16)
    return pl.pallas_call(
        functools.partial(home_kernel, (0, 2)),
        out_shape=[out, shape((docs, gate.shape[1] - LANES), F32)],
        in_specs=[VMEM] * len(ins),
        out_specs=[pl.BlockSpec(memory_space=pl.ANY), VMEM],
        scratch_shapes=[pltpu.VMEM(out.shape, BF16), pltpu.SemaphoreType.DMA((docs,))],
        compiler_params=PARAMS,
        cost_estimate=estimate,
        name="state_home",
    )(*ins)


def add_kernel(count, *refs):
    total = refs[0][...].astype(F32)
    for ref in refs[1:count]:
        total = total + ref[...].astype(F32)
    size = refs[count].shape[0]
    for i, ref in enumerate(refs[count:]):
        ref[...] = total[i * size : (i + 1) * size].astype(ref.dtype)


def add(arrays, dtypes, estimate=None):
    rows, cols = arrays[0].shape
    out = [shape((rows // len(dtypes), cols), dtype) for dtype in dtypes]
    return call(
        functools.partial(add_kernel, len(arrays)), out, arrays, "add", estimate=estimate
    )


def rows_kernel(*refs):
    block_refs, (out_ref, rows_ref, sem) = refs[:-3], refs[-3:]
    size = block_refs[0].shape[0]
    core = lax.axis_index("blk") & 1
    copies = []
    for i, (ref, block) in enumerate(zip(block_refs, (0, 1 + core, 2 - core, 3))):
        rows_ref[i] = ref[...].astype(F32)
        to = pl.ds(pl.multiple_of((turn() ^ block) * size, size), size)
        copies.append(pltpu.make_async_copy(rows_ref.at[i], out_ref.at[to], sem.at[i]))
        copies[-1].start()
    for copy in copies:
        copy.wait()


def to_rows(blocks):
    count = len(blocks)
    rows, cols = blocks[0].shape
    return pl.pallas_call(
        rows_kernel,
        out_shape=shape((count * rows, cols), F32),
        in_specs=[VMEM] * count,
        out_specs=pl.BlockSpec(memory_space=pl.ANY),
        scratch_shapes=[pltpu.VMEM((count, rows, cols), F32), pltpu.SemaphoreType.DMA((count,))],
        compiler_params=PARAMS,
        name="to_rows",
    )(*blocks)


def per_device(reps, blks, encoded, queries, classifiers, lengths, beam, logit_grad):
    labels, width = queries.shape
    docs, tokens, _ = encoded.shape
    total = reps * blks

    def swap(x, mask, other=None):
        masks = (mask, mask if other is None else other)
        return lax.ppermute(x, ("rep", "blk"), [(i, i ^ masks[i & 1]) for i in range(total)])

    core, ax = 1, 2
    ay, az, azz = blks, 2 * blks, 4 * blks
    turns = [0, az, ay, ay | az]

    qc = call(
        pack_kernel, shape((2, labels, width), BF16), [queries, classifiers], "pack",
        [pltpu.SemaphoreType.DMA((2,))], hbm=2,
    )
    encoded2, qc = lax.optimization_barrier((encoded, qc))
    far_qc = swap(qc, ax)
    encoded2, beam2, grad2 = swap(encoded2, core), swap(beam, core), swap(logit_grad, core)
    lengths2 = swap(lengths, core)

    per_chunk = [
        shape((docs, tokens, labels), BF16),
        shape((docs, tokens, labels), BF16),
        shape((docs, labels), F32),
    ]
    gates = shape((docs, beam.shape[1] + LANES), F32)
    turned = shape((docs, width, tokens), BF16)
    block = shape((labels // GROUP, 2 * width), BF16)
    halves = [shape((labels // 2, 2 * width), dtype) for dtype in (F32, BF16)]
    rows = [pltpu.VMEM((labels, 2 * width), F32)]
    sums = [shape((width, labels), F32)] * 2
    estimate = functools.partial(cost, tokens=tokens, width=width, labels=labels)

    enc, gate, enct, attn, score, logit, *acc = call(
        own_kernel,
        [shape(encoded.shape, BF16), gates, turned] + per_chunk + sums,
        [encoded, beam, logit_grad, lengths, qc], "own_labels",
        [pltpu.VMEM(beam.shape, jnp.int32), pltpu.VMEM(beam.shape, F32),
         pltpu.SMEM((docs,), jnp.int32), pltpu.SemaphoreType.DMA((docs + 3,))],
        estimate(4, docs), hbm=4,
    )
    gate2, enct2, attn2, score2, logit2, keep, send = call(
        other_kernel, [gates, turned] + per_chunk + halves,
        [lengths2, beam2, grad2, encoded2, qc, *acc], "own_labels_other_docs",
        rows + [pltpu.SMEM((docs,), jnp.int32), pltpu.SemaphoreType.DMA(())],
        estimate(4, docs), hbm=1,
    )
    received = swap(send, ay)
    far_attn, far_score, far_logit, far_attn2, far_score2, far_logit2, *far = call(
        far_kernel, per_chunk + per_chunk + [shape(block.shape, F32)] + [block] * (GROUP - 1),
        [gate, gate2, enc, encoded2, enct, enct2, far_qc],
        "far_labels", rows, estimate(4, 2 * docs),
    )

    far, keep, received = lax.optimization_barrier((far, keep, received))
    keep, send = add([keep, received], [F32, BF16])
    send, far = lax.optimization_barrier((send, far))
    relayed = swap(far[2], ay)
    received = [swap(far[1], ax | az), swap(far[3], ax | ay | az)]
    (first,) = add([far[0], relayed], [BF16])
    first, send, far_attn2 = lax.optimization_barrier((first, send, far_attn2))
    received.append(swap(first, ax))
    near = swap(send, az)
    state2 = state_grad(
        gate2,
        [(attn2, score2, qc, logit2), (far_attn2, far_score2, far_qc, far_logit2)], [],
    )
    received, near = lax.optimization_barrier((received, near))
    state_in = swap(state2, core)
    (own,) = add([keep, near, *received], [BF16], LONG)
    far_attn, far_score, own = lax.optimization_barrier((far_attn, far_score, own))
    state, logits = state_grad(
        gate, [(attn, score, qc, logit), (far_attn, far_score, far_qc, far_logit)],
        [state_in],
    )
    received, state = lax.optimization_barrier((swap(own, azz), state))
    (own,) = add([own, received], [BF16])
    if reps > 8:
        members = [[i * 8 + j for i in range(reps // 8)] for j in range(8)]
        own = lax.psum(own.astype(F32), "rep", axis_index_groups=members).astype(BF16)

    second, first = lax.optimization_barrier([swap(own, ay, az), swap(own, az, ay)])
    label_grad = to_rows([own, first, second, swap(first, ay, az)])
    return logits, state, label_grad


def solution(mesh):
    reps, blks = mesh.shape["rep"], mesh.shape["blk"]
    assert blks == 4 and reps >= 8 and reps & (reps - 1) == 0
    in_specs = (
        P(("rep", "blk"), None, None),
        P("blk", None),
        P("blk", None),
        P(("rep", "blk")),
        P(("rep", "blk"), None),
        P(("rep", "blk"), None),
    )
    out_specs = (P(("rep", "blk"), None), P(("rep", "blk"), None, None), P("blk", None))
    return jax.shard_map(
        functools.partial(per_device, reps, blks),
        mesh=mesh, in_specs=in_specs, out_specs=out_specs, check_vma=False,
    )
```

```python
import functools

import jax
import jax.numpy as jnp
from jax import lax
from jax.experimental import pallas as pl
from jax.experimental.pallas import tpu as pltpu
from jax.sharding import PartitionSpec as P

F32 = jnp.float32
BF16 = jnp.bfloat16
VMEM = pl.BlockSpec(memory_space=pltpu.VMEM)
SMEM = pl.BlockSpec(memory_space=pltpu.SMEM)
HBM = pl.BlockSpec(memory_space=pltpu.HBM)
PARAMS = pltpu.CompilerParams(vmem_limit_bytes=20 * 1024 * 1024)
GROUP = 4
LANES = 128
EXTRA = 16


LONG = pl.CostEstimate(flops=10**11, transcendentals=0, bytes_accessed=0)


def shape(dims, dtype):
    return jax.ShapeDtypeStruct(dims, dtype)


def mm(a, b):
    return jnp.dot(a, b, preferred_element_type=F32)


def cost(products, docs, tokens, width, labels):
    return pl.CostEstimate(
        flops=2 * products * docs * tokens * width * labels,
        transcendentals=docs * tokens * labels,
        bytes_accessed=4 * docs * tokens * width,
    )


def call(kernel, out_shape, ins, name, scratch=(), estimate=None, hbm=0):
    single = not isinstance(out_shape, (list, tuple))
    ins = [pltpu.with_memory_space_constraint(x, pltpu.HBM) for x in ins[:hbm]] + list(ins[hbm:])
    return pl.pallas_call(
        kernel,
        out_shape=out_shape,
        in_specs=[
            HBM if i < hbm else SMEM if x.ndim == 1 else VMEM for i, x in enumerate(ins)
        ],
        out_specs=VMEM if single else [VMEM] * len(out_shape),
        scratch_shapes=scratch,
        compiler_params=PARAMS,
        cost_estimate=estimate,
        name=name,
    )(*ins)


def lanes_of(k, labels):
    return pl.ds(pl.multiple_of((lax.axis_index("blk") ^ k) * labels, labels), labels)


def turn():
    rep = lax.axis_index("rep")
    return (rep & 1) * 2 + ((rep >> 1) & 1)


def label_chunk(docs, q, c, lanes, sums):
    qt = q.T
    ct = c.T.astype(F32)
    labels = q.shape[0]

    def products(doc):
        load, enc_ref, enct_ref, gate_ref = doc[:4]
        load()
        enc = enc_ref[...]
        g = gate_ref[:, lanes]
        both = mm(enc, jnp.concatenate([qt, (ct * g).astype(BF16)], axis=1))
        return g, both[:, :labels], both[:, labels:]

    query_grad, class_grad = sums
    ahead = products(docs[0])
    for i, (_, _, enct_ref, gate_ref, attn_ref, score_ref, logit_ref) in enumerate(docs):
        g, scores, attn_grad = ahead
        if i + 1 < len(docs):
            ahead = products(docs[i + 1])
        length = gate_ref[:, gate_ref.shape[1] - LANES :][:, :1]
        token = lax.broadcasted_iota(jnp.int32, scores.shape, 0).astype(F32)
        expo = jnp.where(token < length, jnp.exp(scores), 0.0)
        attn = expo * (1.0 / jnp.sum(expo, axis=0, keepdims=True))
        attn_b = attn.astype(BF16)
        attn_ref[...] = attn_b
        inner = jnp.sum(attn * attn_grad, axis=0, keepdims=True)
        score_grad = (attn * (attn_grad - inner)).astype(BF16)
        score_ref[...] = score_grad
        both = mm(enct_ref[...], jnp.concatenate([attn_b, score_grad], axis=1))
        context, part = both[:, :labels], both[:, labels:]
        query_grad = part if query_grad is None else query_grad + part
        logit_ref[...] = jnp.sum(context * ct, axis=0, keepdims=True)
        part = context * g
        class_grad = part if class_grad is None else class_grad + part
    return query_grad, class_grad


def doc_list(loads, enc_ref, enct_ref, gate_ref, attn_ref, score_ref, logit_ref):
    return [
        (loads[d], enc_ref.at[d], enct_ref.at[d], gate_ref.at[d : d + 1], attn_ref.at[d],
         score_ref.at[d], logit_ref.at[d : d + 1])
        for d in range(enc_ref.shape[0])
    ]


def turn_around(enc_ref, enct_ref, copies=None):
    def load(d):
        if copies is not None:
            copies[d].wait()
        enct_ref[d] = enc_ref[d].T

    return [functools.partial(load, d) for d in range(enc_ref.shape[0])]


def pack_kernel(q_in, c_in, qc_ref, sem):
    copies = [pltpu.make_async_copy(x, qc_ref.at[i], sem.at[i]) for i, x in enumerate((q_in, c_in))]
    for copy in copies:
        copy.start()
    for copy in copies:
        copy.wait()


def after_first(loads, then):
    load = loads[0]

    def both():
        load()
        then()

    loads[0] = both


def make_gates(gate_ref, grad_ref, beam_ref, lens_ref):
    docs, labels = beam_ref.shape
    gate_ref[:, :labels] = grad_ref[...] * beam_ref[...].astype(F32)
    for d in range(docs):
        gate_ref[d : d + 1, labels:] = jnp.full((1, LANES), lens_ref[d], jnp.int32).astype(F32)


def own_kernel(enc_in, beam_in, grad_in, lens_in, qc_ref, enc_ref, gate_ref, enct_ref, attn_ref,
               score_ref, logit_ref, qsum_ref, csum_ref, beam_ref, grad_ref, lens_ref, sem):
    docs = enc_ref.shape[0]
    small = [(beam_in, beam_ref), (grad_in, grad_ref), (lens_in, lens_ref)]
    small = [pltpu.make_async_copy(x, y, sem.at[docs + i]) for i, (x, y) in enumerate(small)]
    copies = [
        pltpu.make_async_copy(enc_in.at[d], enc_ref.at[d], sem.at[d]) for d in range(docs)
    ]
    for copy in copies[:1] + small + copies[1:]:
        copy.start()
    loads = turn_around(enc_ref, enct_ref, copies)

    def gates():
        for copy in small:
            copy.wait()
        make_gates(gate_ref, grad_ref, beam_ref, lens_ref)

    after_first(loads, gates)
    qsum_ref[...], csum_ref[...] = label_chunk(
        doc_list(loads, enc_ref, enct_ref, gate_ref, attn_ref, score_ref, logit_ref),
        qc_ref[0], qc_ref[1], lanes_of(0, qc_ref.shape[1]), (None, None),
    )


def to_blocks(sums, rows_ref, out_refs):
    query_grad, class_grad = sums
    width = query_grad.shape[0]
    rows_ref[:, :width] = query_grad.astype(BF16).T
    rows_ref[:, width:] = class_grad.astype(BF16).T
    size = rows_ref.shape[0] // GROUP
    count = GROUP // len(out_refs)
    for i in range(GROUP):
        ref = out_refs[i // count]
        block = rows_ref[pl.ds(pl.multiple_of((turn() ^ i) * size, size), size), :]
        ref[(i % count) * size : (i % count + 1) * size, :] = block.astype(ref.dtype)


def other_kernel(lens_in, beam_ref, grad_ref, enc_ref, qc_ref, qsum_ref, csum_ref, gate_ref,
                 enct_ref, attn_ref, score_ref, logit_ref, *refs):
    refs, (lens_ref, sem) = refs[:-2], refs[-2:]
    copy = pltpu.make_async_copy(lens_in, lens_ref, sem)
    copy.start()

    def gates():
        copy.wait()
        make_gates(gate_ref, grad_ref, beam_ref, lens_ref)

    loads = turn_around(enc_ref, enct_ref)
    after_first(loads, gates)
    sums = label_chunk(
        doc_list(loads, enc_ref, enct_ref, gate_ref, attn_ref, score_ref, logit_ref),
        qc_ref[0], qc_ref[1], lanes_of(0, qc_ref.shape[1]), (qsum_ref[...], csum_ref[...]),
    )
    to_blocks(sums, refs[-1], refs[:-1])


def far_kernel(gate_ref, gate2_ref, enc_ref, enc2_ref, enct_ref,
               enct2_ref, qc_ref, attn_ref, score_ref, logit_ref, attn2_ref, score2_ref,
               logit2_ref, *refs):
    loads = [lambda: None] * enc_ref.shape[0]
    sums = label_chunk(
        doc_list(loads, enc_ref, enct_ref, gate_ref, attn_ref, score_ref, logit_ref)
        + doc_list(loads, enc2_ref, enct2_ref, gate2_ref, attn2_ref, score2_ref,
                   logit2_ref),
        qc_ref[0], qc_ref[1], lanes_of(2, qc_ref.shape[1]), (None, None),
    )
    to_blocks(sums, refs[-1], refs[:-1])


def state_parts(ks, gate_ref, chunks):
    docs, labels = gate_ref.shape[0], chunks[2].shape[1]
    ctx_grads = []
    for n, k in enumerate(ks):
        gate = gate_ref[:, lanes_of(k, labels)]
        gate = jnp.concatenate([gate, jnp.zeros((128 - docs, labels), F32)], axis=0).T
        c = chunks[4 * n + 2][1].astype(F32)
        ctx_grads.append([(c * gate[:, d : d + 1]).astype(BF16) for d in range(docs)])
    for d in range(docs):
        total = None
        for n in range(len(ks)):
            attn_ref, score_ref, qc_ref = chunks[4 * n : 4 * n + 3]
            part = mm(attn_ref[d], ctx_grads[n][d]) + mm(score_ref[d], qc_ref[0])
            total = part if total is None else total + part
        yield d, total


def away_kernel(ks, gate_ref, *refs):
    chunks, out_ref = refs[:-1], refs[-1]
    tokens, labels = chunks[0].shape[1:]
    for d, total in state_parts(ks, gate_ref, chunks):
        out_ref[d, :tokens] = total.astype(BF16)
        for n in range(len(ks)):
            logit = chunks[4 * n + 3][d : d + 1, :]
            high = logit.astype(BF16).astype(F32)
            pad = jnp.zeros((EXTRA - 2, labels), F32)
            pair = jnp.concatenate([high, logit - high, pad], axis=0)
            out_ref[d, tokens:, n * labels : (n + 1) * labels] = pair.astype(BF16)


def home_kernel(ks, gate_ref, *refs):
    chunks, (in_ref, out_ref, logit_ref, done_ref, sem) = refs[:-5], refs[-5:]
    tokens, labels = chunks[0].shape[1:]
    copies = []
    for d, total in state_parts(ks, gate_ref, chunks):
        done_ref[d] = (total + in_ref[d, :tokens].astype(F32)).astype(BF16)
        copies.append(pltpu.make_async_copy(done_ref.at[d], out_ref.at[d], sem.at[d]))
        copies[-1].start()
        for n, k in enumerate(ks):
            pair = in_ref[d, tokens:, n * labels : (n + 1) * labels].astype(F32)
            logit_ref[d : d + 1, lanes_of(k, labels)] = chunks[4 * n + 3][d : d + 1, :]
            logit_ref[d : d + 1, lanes_of(k ^ 1, labels)] = pair[0:1] + pair[1:2]
    for copy in copies:
        copy.wait()


def state_grad(gate, parts, more):
    docs, tokens, labels = parts[0][0].shape
    width = parts[0][2].shape[2]
    ins = [gate, *parts[0], *parts[1], *more]
    estimate = cost(4, docs, tokens, width, labels)
    if not more:
        out = shape((docs, tokens + EXTRA, width), BF16)
        return call(functools.partial(away_kernel, (0, 2)), out, ins, "state_away", (), estimate)
    out = shape((docs, tokens, width), BF16)
    return pl.pallas_call(
        functools.partial(home_kernel, (0, 2)),
        out_shape=[out, shape((docs, gate.shape[1] - LANES), F32)],
        in_specs=[VMEM] * len(ins),
        out_specs=[pl.BlockSpec(memory_space=pl.ANY), VMEM],
        scratch_shapes=[pltpu.VMEM(out.shape, BF16), pltpu.SemaphoreType.DMA((docs,))],
        compiler_params=PARAMS,
        cost_estimate=estimate,
        name="state_home",
    )(*ins)


def add_kernel(count, *refs):
    total = refs[0][...].astype(F32)
    for ref in refs[1:count]:
        total = total + ref[...].astype(F32)
    size = refs[count].shape[0]
    for i, ref in enumerate(refs[count:]):
        ref[...] = total[i * size : (i + 1) * size].astype(ref.dtype)


def add(arrays, dtypes, estimate=None):
    rows, cols = arrays[0].shape
    out = [shape((rows // len(dtypes), cols), dtype) for dtype in dtypes]
    return call(
        functools.partial(add_kernel, len(arrays)), out, arrays, "add", estimate=estimate
    )


def rows_kernel(*refs):
    block_refs, (out_ref, rows_ref, sem) = refs[:-3], refs[-3:]
    size = block_refs[0].shape[0]
    copies = []
    for i, ref in enumerate(block_refs):
        rows_ref[i] = ref[...].astype(F32)
        to = pl.ds(pl.multiple_of((turn() ^ i) * size, size), size)
        copies.append(pltpu.make_async_copy(rows_ref.at[i], out_ref.at[to], sem.at[i]))
        copies[-1].start()
    for copy in copies:
        copy.wait()


def to_rows(blocks):
    count = len(blocks)
    rows, cols = blocks[0].shape
    return pl.pallas_call(
        rows_kernel,
        out_shape=shape((count * rows, cols), F32),
        in_specs=[VMEM] * count,
        out_specs=pl.BlockSpec(memory_space=pl.ANY),
        scratch_shapes=[pltpu.VMEM((count, rows, cols), F32), pltpu.SemaphoreType.DMA((count,))],
        compiler_params=PARAMS,
        name="to_rows",
    )(*blocks)


def per_device(reps, blks, encoded, queries, classifiers, lengths, beam, logit_grad):
    labels, width = queries.shape
    docs, tokens, _ = encoded.shape
    total = reps * blks

    def swap(x, mask):
        return lax.ppermute(x, ("rep", "blk"), [(i, i ^ mask) for i in range(total)])

    core, ax = 1, 2
    ay, az, azz = blks, 2 * blks, 4 * blks
    turns = [0, az, ay, ay | az]

    qc = call(
        pack_kernel, shape((2, labels, width), BF16), [queries, classifiers], "pack",
        [pltpu.SemaphoreType.DMA((2,))], hbm=2,
    )
    encoded2, qc = lax.optimization_barrier((encoded, qc))
    far_qc = swap(qc, ax)
    encoded2, beam2, grad2 = swap(encoded2, core), swap(beam, core), swap(logit_grad, core)
    lengths2 = swap(lengths, core)

    per_chunk = [
        shape((docs, tokens, labels), BF16),
        shape((docs, tokens, labels), BF16),
        shape((docs, labels), F32),
    ]
    gates = shape((docs, beam.shape[1] + LANES), F32)
    turned = shape((docs, width, tokens), BF16)
    block = shape((labels // GROUP, 2 * width), BF16)
    halves = [shape((labels // 2, 2 * width), BF16)] * 2
    rows = [pltpu.VMEM((labels, 2 * width), BF16)]
    sums = [shape((width, labels), F32)] * 2
    estimate = functools.partial(cost, tokens=tokens, width=width, labels=labels)

    enc, gate, enct, attn, score, logit, *acc = call(
        own_kernel,
        [shape(encoded.shape, BF16), gates, turned] + per_chunk + sums,
        [encoded, beam, logit_grad, lengths, qc], "own_labels",
        [pltpu.VMEM(beam.shape, jnp.int32), pltpu.VMEM(beam.shape, F32),
         pltpu.SMEM((docs,), jnp.int32), pltpu.SemaphoreType.DMA((docs + 3,))],
        estimate(4, docs), hbm=4,
    )
    gate2, enct2, attn2, score2, logit2, keep, send = call(
        other_kernel, [gates, turned] + per_chunk + halves,
        [lengths2, beam2, grad2, encoded2, qc, *acc], "own_labels_other_docs",
        rows + [pltpu.SMEM((docs,), jnp.int32), pltpu.SemaphoreType.DMA(())],
        estimate(4, docs), hbm=1,
    )
    received = swap(send, ay)
    far_attn, far_score, far_logit, far_attn2, far_score2, far_logit2, *far = call(
        far_kernel, per_chunk + per_chunk + [block] * GROUP,
        [gate, gate2, enc, encoded2, enct, enct2, far_qc],
        "far_labels", rows, estimate(4, 2 * docs),
    )

    far, keep, received = lax.optimization_barrier((far, keep, received))
    keep, send = add([keep, received], [F32, BF16])
    send, far = lax.optimization_barrier((send, far))
    relayed = swap(far[2], ay)
    received = [swap(far[1], ax | az), swap(far[3], ax | ay | az)]
    (first,) = add([far[0], relayed], [BF16])
    first, send, far_attn2 = lax.optimization_barrier((first, send, far_attn2))
    received.append(swap(first, ax))
    near = swap(send, az)
    state2 = state_grad(
        gate2,
        [(attn2, score2, qc, logit2), (far_attn2, far_score2, far_qc, far_logit2)], [],
    )
    received, near = lax.optimization_barrier((received, near))
    state_in = swap(state2, core)
    (own,) = add([keep, near, *received], [BF16], LONG)
    far_attn, far_score, own = lax.optimization_barrier((far_attn, far_score, own))
    state, logits = state_grad(
        gate, [(attn, score, qc, logit), (far_attn, far_score, far_qc, far_logit)],
        [state_in],
    )
    received, state = lax.optimization_barrier((swap(own, azz), state))
    (own,) = add([own, received], [BF16])
    if reps > 8:
        members = [[i * 8 + j for i in range(reps // 8)] for j in range(8)]
        own = lax.psum(own.astype(F32), "rep", axis_index_groups=members).astype(BF16)

    both, second, first = lax.optimization_barrier([swap(own, mask) for mask in turns[:0:-1]])
    label_grad = to_rows([own, first, second, both])
    return logits, state, label_grad


def solution(mesh):
    reps, blks = mesh.shape["rep"], mesh.shape["blk"]
    assert blks == 4 and reps >= 8 and reps & (reps - 1) == 0
    in_specs = (
        P(("rep", "blk"), None, None),
        P("blk", None),
        P("blk", None),
        P(("rep", "blk")),
        P(("rep", "blk"), None),
        P(("rep", "blk"), None),
    )
    out_specs = (P(("rep", "blk"), None), P(("rep", "blk"), None, None), P("blk", None))
    return jax.shard_map(
        functools.partial(per_device, reps, blks),
        mesh=mesh, in_specs=in_specs, out_specs=out_specs, check_vma=False,
    )
```

```python
import functools

import jax
import jax.numpy as jnp
from jax import lax
from jax.experimental import pallas as pl
from jax.experimental.pallas import tpu as pltpu
from jax.sharding import PartitionSpec as P

F32 = jnp.float32
BF16 = jnp.bfloat16
VMEM = pl.BlockSpec(memory_space=pltpu.VMEM)
SMEM = pl.BlockSpec(memory_space=pltpu.SMEM)
HBM = pl.BlockSpec(memory_space=pltpu.HBM)
PARAMS = pltpu.CompilerParams(vmem_limit_bytes=20 * 1024 * 1024)
GROUP = 4
LANES = 128
EXTRA = 16


LONG = pl.CostEstimate(flops=10**11, transcendentals=0, bytes_accessed=0)


def shape(dims, dtype):
    return jax.ShapeDtypeStruct(dims, dtype)


def mm(a, b):
    return jnp.dot(a, b, preferred_element_type=F32)


def cost(products, docs, tokens, width, labels):
    return pl.CostEstimate(
        flops=2 * products * docs * tokens * width * labels,
        transcendentals=docs * tokens * labels,
        bytes_accessed=4 * docs * tokens * width,
    )


def call(kernel, out_shape, ins, name, scratch=(), estimate=None, hbm=0):
    single = not isinstance(out_shape, (list, tuple))
    ins = [pltpu.with_memory_space_constraint(x, pltpu.HBM) for x in ins[:hbm]] + list(ins[hbm:])
    return pl.pallas_call(
        kernel,
        out_shape=out_shape,
        in_specs=[
            HBM if i < hbm else SMEM if x.ndim == 1 else VMEM for i, x in enumerate(ins)
        ],
        out_specs=VMEM if single else [VMEM] * len(out_shape),
        scratch_shapes=scratch,
        compiler_params=PARAMS,
        cost_estimate=estimate,
        name=name,
    )(*ins)


def lanes_of(k, labels):
    return pl.ds(pl.multiple_of((lax.axis_index("blk") ^ k) * labels, labels), labels)


def turn():
    rep = lax.axis_index("rep")
    return (rep & 1) * 2 + ((rep >> 1) & 1)


def label_chunk(docs, q, c, lanes, sums):
    qt = q.T
    ct = c.T.astype(F32)
    labels = q.shape[0]

    def products(doc):
        load, enc_ref, enct_ref, gate_ref = doc[:4]
        load()
        enc = enc_ref[...]
        g = gate_ref[:, lanes]
        both = mm(enc, jnp.concatenate([qt, (ct * g).astype(BF16)], axis=1))
        return g, both[:, :labels], both[:, labels:]

    query_grad, class_grad = sums
    ahead = products(docs[0])
    for i, (_, _, enct_ref, gate_ref, attn_ref, score_ref, logit_ref) in enumerate(docs):
        g, scores, attn_grad = ahead
        if i + 1 < len(docs):
            ahead = products(docs[i + 1])
        length = gate_ref[:, gate_ref.shape[1] - LANES :][:, :1]
        token = lax.broadcasted_iota(jnp.int32, scores.shape, 0).astype(F32)
        expo = jnp.where(token < length, jnp.exp(scores), 0.0)
        attn = expo * (1.0 / jnp.sum(expo, axis=0, keepdims=True))
        attn_b = attn.astype(BF16)
        attn_ref[...] = attn_b
        inner = jnp.sum(attn * attn_grad, axis=0, keepdims=True)
        score_grad = (attn * (attn_grad - inner)).astype(BF16)
        score_ref[...] = score_grad
        both = mm(enct_ref[...], jnp.concatenate([attn_b, score_grad], axis=1))
        context, part = both[:, :labels], both[:, labels:]
        query_grad = part if query_grad is None else query_grad + part
        logit_ref[...] = jnp.sum(context * ct, axis=0, keepdims=True)
        part = context * g
        class_grad = part if class_grad is None else class_grad + part
    return query_grad, class_grad


def doc_list(loads, enc_ref, enct_ref, gate_ref, attn_ref, score_ref, logit_ref):
    return [
        (loads[d], enc_ref.at[d], enct_ref.at[d], gate_ref.at[d : d + 1], attn_ref.at[d],
         score_ref.at[d], logit_ref.at[d : d + 1])
        for d in range(enc_ref.shape[0])
    ]


def turn_around(enc_ref, enct_ref, copies=None):
    def load(d):
        if copies is not None:
            copies[d].wait()
        enct_ref[d] = enc_ref[d].T

    return [functools.partial(load, d) for d in range(enc_ref.shape[0])]


def pack_kernel(q_in, c_in, qc_ref, sem):
    copies = [pltpu.make_async_copy(x, qc_ref.at[i], sem.at[i]) for i, x in enumerate((q_in, c_in))]
    for copy in copies:
        copy.start()
    for copy in copies:
        copy.wait()


def after_first(loads, then):
    load = loads[0]

    def both():
        load()
        then()

    loads[0] = both


def make_gates(gate_ref, grad_ref, beam_ref, lens_ref):
    docs, labels = beam_ref.shape
    gate_ref[:, :labels] = grad_ref[...] * beam_ref[...].astype(F32)
    for d in range(docs):
        gate_ref[d : d + 1, labels:] = jnp.full((1, LANES), lens_ref[d], jnp.int32).astype(F32)


def own_kernel(enc_in, beam_in, grad_in, lens_in, qc_ref, enc_ref, gate_ref, enct_ref, attn_ref,
               score_ref, logit_ref, qsum_ref, csum_ref, beam_ref, grad_ref, lens_ref, sem):
    docs = enc_ref.shape[0]
    small = [(beam_in, beam_ref), (grad_in, grad_ref), (lens_in, lens_ref)]
    small = [pltpu.make_async_copy(x, y, sem.at[docs + i]) for i, (x, y) in enumerate(small)]
    copies = [
        pltpu.make_async_copy(enc_in.at[d], enc_ref.at[d], sem.at[d]) for d in range(docs)
    ]
    for copy in copies[:1] + small + copies[1:]:
        copy.start()
    loads = turn_around(enc_ref, enct_ref, copies)

    def gates():
        for copy in small:
            copy.wait()
        make_gates(gate_ref, grad_ref, beam_ref, lens_ref)

    after_first(loads, gates)
    qsum_ref[...], csum_ref[...] = label_chunk(
        doc_list(loads, enc_ref, enct_ref, gate_ref, attn_ref, score_ref, logit_ref),
        qc_ref[0], qc_ref[1], lanes_of(0, qc_ref.shape[1]), (None, None),
    )


def to_blocks(sums, rows_ref, out_refs):
    query_grad, class_grad = sums
    width = query_grad.shape[0]
    rows_ref[:, :width] = query_grad.astype(BF16).T
    rows_ref[:, width:] = class_grad.astype(BF16).T
    size = rows_ref.shape[0] // GROUP
    count = GROUP // len(out_refs)
    for i in range(GROUP):
        ref = out_refs[i // count]
        block = rows_ref[pl.ds(pl.multiple_of((turn() ^ i) * size, size), size), :]
        ref[(i % count) * size : (i % count + 1) * size, :] = block.astype(ref.dtype)


def other_kernel(lens_in, beam_ref, grad_ref, enc_ref, qc_ref, qsum_ref, csum_ref, gate_ref,
                 enct_ref, attn_ref, score_ref, logit_ref, *refs):
    refs, (lens_ref, sem) = refs[:-2], refs[-2:]
    copy = pltpu.make_async_copy(lens_in, lens_ref, sem)
    copy.start()

    def gates():
        copy.wait()
        make_gates(gate_ref, grad_ref, beam_ref, lens_ref)

    loads = turn_around(enc_ref, enct_ref)
    after_first(loads, gates)
    sums = label_chunk(
        doc_list(loads, enc_ref, enct_ref, gate_ref, attn_ref, score_ref, logit_ref),
        qc_ref[0], qc_ref[1], lanes_of(0, qc_ref.shape[1]), (qsum_ref[...], csum_ref[...]),
    )
    to_blocks(sums, refs[-1], refs[:-1])


def far_kernel(gate_ref, gate2_ref, enc_ref, enc2_ref, enct_ref,
               enct2_ref, qc_ref, attn_ref, score_ref, logit_ref, attn2_ref, score2_ref,
               logit2_ref, *refs):
    loads = [lambda: None] * enc_ref.shape[0]
    sums = label_chunk(
        doc_list(loads, enc_ref, enct_ref, gate_ref, attn_ref, score_ref, logit_ref)
        + doc_list(loads, enc2_ref, enct2_ref, gate2_ref, attn2_ref, score2_ref,
                   logit2_ref),
        qc_ref[0], qc_ref[1], lanes_of(2, qc_ref.shape[1]), (None, None),
    )
    to_blocks(sums, refs[-1], refs[:-1])


def state_parts(ks, gate_ref, chunks):
    docs, labels = gate_ref.shape[0], chunks[2].shape[1]
    ctx_grads = []
    for n, k in enumerate(ks):
        gate = gate_ref[:, lanes_of(k, labels)]
        gate = jnp.concatenate([gate, jnp.zeros((128 - docs, labels), F32)], axis=0).T
        c = chunks[4 * n + 2][1].astype(F32)
        ctx_grads.append([(c * gate[:, d : d + 1]).astype(BF16) for d in range(docs)])
    for d in range(docs):
        total = None
        for n in range(len(ks)):
            attn_ref, score_ref, qc_ref = chunks[4 * n : 4 * n + 3]
            part = mm(attn_ref[d], ctx_grads[n][d]) + mm(score_ref[d], qc_ref[0])
            total = part if total is None else total + part
        yield d, total


def away_kernel(ks, gate_ref, *refs):
    chunks, out_ref = refs[:-1], refs[-1]
    tokens, labels = chunks[0].shape[1:]
    for d, total in state_parts(ks, gate_ref, chunks):
        out_ref[d, :tokens] = total.astype(BF16)
        for n in range(len(ks)):
            logit = chunks[4 * n + 3][d : d + 1, :]
            high = logit.astype(BF16).astype(F32)
            pad = jnp.zeros((EXTRA - 2, labels), F32)
            pair = jnp.concatenate([high, logit - high, pad], axis=0)
            out_ref[d, tokens:, n * labels : (n + 1) * labels] = pair.astype(BF16)


def home_kernel(ks, gate_ref, *refs):
    chunks, (in_ref, out_ref, logit_ref, done_ref, sem) = refs[:-5], refs[-5:]
    tokens, labels = chunks[0].shape[1:]
    copies = []
    for d, total in state_parts(ks, gate_ref, chunks):
        done_ref[d] = (total + in_ref[d, :tokens].astype(F32)).astype(BF16)
        copies.append(pltpu.make_async_copy(done_ref.at[d], out_ref.at[d], sem.at[d]))
        copies[-1].start()
        for n, k in enumerate(ks):
            pair = in_ref[d, tokens:, n * labels : (n + 1) * labels].astype(F32)
            logit_ref[d : d + 1, lanes_of(k, labels)] = chunks[4 * n + 3][d : d + 1, :]
            logit_ref[d : d + 1, lanes_of(k ^ 1, labels)] = pair[0:1] + pair[1:2]
    for copy in copies:
        copy.wait()


def state_grad(gate, parts, more):
    docs, tokens, labels = parts[0][0].shape
    width = parts[0][2].shape[2]
    ins = [gate, *parts[0], *parts[1], *more]
    estimate = cost(4, docs, tokens, width, labels)
    if not more:
        out = shape((docs, tokens + EXTRA, width), BF16)
        return call(functools.partial(away_kernel, (0, 2)), out, ins, "state_away", (), estimate)
    out = shape((docs, tokens, width), BF16)
    return pl.pallas_call(
        functools.partial(home_kernel, (0, 2)),
        out_shape=[out, shape((docs, gate.shape[1] - LANES), F32)],
        in_specs=[VMEM] * len(ins),
        out_specs=[pl.BlockSpec(memory_space=pl.ANY), VMEM],
        scratch_shapes=[pltpu.VMEM(out.shape, BF16), pltpu.SemaphoreType.DMA((docs,))],
        compiler_params=PARAMS,
        cost_estimate=estimate,
        name="state_home",
    )(*ins)


def add_kernel(count, *refs):
    total = refs[0][...].astype(F32)
    for ref in refs[1:count]:
        total = total + ref[...].astype(F32)
    size = refs[count].shape[0]
    for i, ref in enumerate(refs[count:]):
        ref[...] = total[i * size : (i + 1) * size].astype(ref.dtype)


def add(arrays, dtypes, estimate=None):
    rows, cols = arrays[0].shape
    out = [shape((rows // len(dtypes), cols), dtype) for dtype in dtypes]
    return call(
        functools.partial(add_kernel, len(arrays)), out, arrays, "add", estimate=estimate
    )


def rows_kernel(*refs):
    block_refs, (out_ref, rows_ref, sem) = refs[:-3], refs[-3:]
    size = block_refs[0].shape[0]
    copies = []
    for i, ref in enumerate(block_refs):
        rows_ref[i] = ref[...].astype(F32)
        to = pl.ds(pl.multiple_of((turn() ^ i) * size, size), size)
        copies.append(pltpu.make_async_copy(rows_ref.at[i], out_ref.at[to], sem.at[i]))
        copies[-1].start()
    for copy in copies:
        copy.wait()


def to_rows(blocks):
    count = len(blocks)
    rows, cols = blocks[0].shape
    return pl.pallas_call(
        rows_kernel,
        out_shape=shape((count * rows, cols), F32),
        in_specs=[VMEM] * count,
        out_specs=pl.BlockSpec(memory_space=pl.ANY),
        scratch_shapes=[pltpu.VMEM((count, rows, cols), F32), pltpu.SemaphoreType.DMA((count,))],
        compiler_params=PARAMS,
        name="to_rows",
    )(*blocks)


def per_device(reps, blks, encoded, queries, classifiers, lengths, beam, logit_grad):
    labels, width = queries.shape
    docs, tokens, _ = encoded.shape
    total = reps * blks

    def swap(x, mask):
        return lax.ppermute(x, ("rep", "blk"), [(i, i ^ mask) for i in range(total)])

    core, ax = 1, 2
    ay, az, azz = blks, 2 * blks, 4 * blks
    turns = [0, az, ay, ay | az]

    qc = call(
        pack_kernel, shape((2, labels, width), BF16), [queries, classifiers], "pack",
        [pltpu.SemaphoreType.DMA((2,))], hbm=2,
    )
    encoded2, qc = lax.optimization_barrier((encoded, qc))
    far_qc = swap(qc, ax)
    encoded2, beam2, grad2 = swap(encoded2, core), swap(beam, core), swap(logit_grad, core)
    lengths2 = swap(lengths, core)

    per_chunk = [
        shape((docs, tokens, labels), BF16),
        shape((docs, tokens, labels), BF16),
        shape((docs, labels), F32),
    ]
    gates = shape((docs, beam.shape[1] + LANES), F32)
    turned = shape((docs, width, tokens), BF16)
    block = shape((labels // GROUP, 2 * width), BF16)
    halves = [shape((labels // 2, 2 * width), BF16)] * 2
    rows = [pltpu.VMEM((labels, 2 * width), BF16)]
    sums = [shape((width, labels), F32)] * 2
    estimate = functools.partial(cost, tokens=tokens, width=width, labels=labels)

    enc, gate, enct, attn, score, logit, *acc = call(
        own_kernel,
        [shape(encoded.shape, BF16), gates, turned] + per_chunk + sums,
        [encoded, beam, logit_grad, lengths, qc], "own_labels",
        [pltpu.VMEM(beam.shape, jnp.int32), pltpu.VMEM(beam.shape, F32),
         pltpu.SMEM((docs,), jnp.int32), pltpu.SemaphoreType.DMA((docs + 3,))],
        estimate(4, docs), hbm=4,
    )
    gate2, enct2, attn2, score2, logit2, keep, send = call(
        other_kernel, [gates, turned] + per_chunk + halves,
        [lengths2, beam2, grad2, encoded2, qc, *acc], "own_labels_other_docs",
        rows + [pltpu.SMEM((docs,), jnp.int32), pltpu.SemaphoreType.DMA(())],
        estimate(4, docs), hbm=1,
    )
    received = swap(send, ay)
    far_attn, far_score, far_logit, far_attn2, far_score2, far_logit2, *far = call(
        far_kernel, per_chunk + per_chunk + [block] * GROUP,
        [gate, gate2, enc, encoded2, enct, enct2, far_qc],
        "far_labels", rows, estimate(4, 2 * docs),
    )

    far, keep, received = lax.optimization_barrier((far, keep, received))
    keep, send = add([keep, received], [F32, BF16])
    send, far = lax.optimization_barrier((send, far))
    relayed = swap(far[3], ay)
    received = [swap(far[0], ax), swap(far[2], ax | ay)]
    (first,) = add([far[1], relayed], [BF16])
    first, send, far_attn2 = lax.optimization_barrier((first, send, far_attn2))
    received.append(swap(first, ax | az))
    near = swap(send, az)
    state2 = state_grad(
        gate2,
        [(attn2, score2, qc, logit2), (far_attn2, far_score2, far_qc, far_logit2)], [],
    )
    received, near = lax.optimization_barrier((received, near))
    state_in = swap(state2, core)
    (own,) = add([keep, near, *received], [BF16], LONG)
    far_attn, far_score, own = lax.optimization_barrier((far_attn, far_score, own))
    state, logits = state_grad(
        gate, [(attn, score, qc, logit), (far_attn, far_score, far_qc, far_logit)],
        [state_in],
    )
    received, state = lax.optimization_barrier((swap(own, azz), state))
    (own,) = add([own, received], [BF16])
    if reps > 8:
        members = [[i * 8 + j for i in range(reps // 8)] for j in range(8)]
        own = lax.psum(own.astype(F32), "rep", axis_index_groups=members).astype(BF16)

    both, second, first = lax.optimization_barrier([swap(own, mask) for mask in turns[:0:-1]])
    label_grad = to_rows([own, first, second, both])
    return logits, state, label_grad


def solution(mesh):
    reps, blks = mesh.shape["rep"], mesh.shape["blk"]
    assert blks == 4 and reps >= 8 and reps & (reps - 1) == 0
    in_specs = (
        P(("rep", "blk"), None, None),
        P("blk", None),
        P("blk", None),
        P(("rep", "blk")),
        P(("rep", "blk"), None),
        P(("rep", "blk"), None),
    )
    out_specs = (P(("rep", "blk"), None), P(("rep", "blk"), None, None), P("blk", None))
    return jax.shard_map(
        functools.partial(per_device, reps, blks),
        mesh=mesh, in_specs=in_specs, out_specs=out_specs, check_vma=False,
    )
```

```python
import functools

import jax
import jax.numpy as jnp
from jax import lax
from jax.experimental import pallas as pl
from jax.experimental.pallas import tpu as pltpu
from jax.sharding import PartitionSpec as P

F32 = jnp.float32
BF16 = jnp.bfloat16
VMEM = pl.BlockSpec(memory_space=pltpu.VMEM)
SMEM = pl.BlockSpec(memory_space=pltpu.SMEM)
HBM = pl.BlockSpec(memory_space=pltpu.HBM)
PARAMS = pltpu.CompilerParams(vmem_limit_bytes=20 * 1024 * 1024)
GROUP = 4
LANES = 128
EXTRA = 16


LONG = pl.CostEstimate(flops=10**11, transcendentals=0, bytes_accessed=0)


def shape(dims, dtype):
    return jax.ShapeDtypeStruct(dims, dtype)


def mm(a, b):
    return jnp.dot(a, b, preferred_element_type=F32)


def cost(products, docs, tokens, width, labels):
    return pl.CostEstimate(
        flops=2 * products * docs * tokens * width * labels,
        transcendentals=docs * tokens * labels,
        bytes_accessed=4 * docs * tokens * width,
    )


def call(kernel, out_shape, ins, name, scratch=(), estimate=None, hbm=0):
    single = not isinstance(out_shape, (list, tuple))
    ins = [pltpu.with_memory_space_constraint(x, pltpu.HBM) for x in ins[:hbm]] + list(ins[hbm:])
    return pl.pallas_call(
        kernel,
        out_shape=out_shape,
        in_specs=[
            HBM if i < hbm else SMEM if x.ndim == 1 else VMEM for i, x in enumerate(ins)
        ],
        out_specs=VMEM if single else [VMEM] * len(out_shape),
        scratch_shapes=scratch,
        compiler_params=PARAMS,
        cost_estimate=estimate,
        name=name,
    )(*ins)


def lanes_of(k, labels):
    return pl.ds(pl.multiple_of((lax.axis_index("blk") ^ k) * labels, labels), labels)


def turn():
    rep = lax.axis_index("rep")
    return (rep & 1) * 2 + ((rep >> 1) & 1)


def label_chunk(docs, q, c, lanes, sums):
    qt = q.T
    ct = c.T.astype(F32)
    labels = q.shape[0]

    def products(doc):
        load, enc_ref, enct_ref, gate_ref = doc[:4]
        load()
        enc = enc_ref[...]
        g = gate_ref[:, lanes]
        both = mm(enc, jnp.concatenate([qt, (ct * g).astype(BF16)], axis=1))
        return g, both[:, :labels], both[:, labels:]

    query_grad, class_grad = sums
    ahead = products(docs[0])
    for i, (_, _, enct_ref, gate_ref, attn_ref, score_ref, logit_ref) in enumerate(docs):
        g, scores, attn_grad = ahead
        if i + 1 < len(docs):
            ahead = products(docs[i + 1])
        length = gate_ref[:, gate_ref.shape[1] - LANES :][:, :1]
        token = lax.broadcasted_iota(jnp.int32, scores.shape, 0).astype(F32)
        expo = jnp.where(token < length, jnp.exp(scores), 0.0)
        attn = expo * (1.0 / jnp.sum(expo, axis=0, keepdims=True))
        attn_b = attn.astype(BF16)
        attn_ref[...] = attn_b
        inner = jnp.sum(attn * attn_grad, axis=0, keepdims=True)
        score_grad = (attn * (attn_grad - inner)).astype(BF16)
        score_ref[...] = score_grad
        both = mm(enct_ref[...], jnp.concatenate([attn_b, score_grad], axis=1))
        context, part = both[:, :labels], both[:, labels:]
        query_grad = part if query_grad is None else query_grad + part
        logit_ref[...] = jnp.sum(context * ct, axis=0, keepdims=True)
        part = context * g
        class_grad = part if class_grad is None else class_grad + part
    return query_grad, class_grad


def doc_list(loads, enc_ref, enct_ref, gate_ref, attn_ref, score_ref, logit_ref):
    return [
        (loads[d], enc_ref.at[d], enct_ref.at[d], gate_ref.at[d : d + 1], attn_ref.at[d],
         score_ref.at[d], logit_ref.at[d : d + 1])
        for d in range(enc_ref.shape[0])
    ]


def turn_around(enc_ref, enct_ref, copies=None):
    def load(d):
        if copies is not None:
            copies[d].wait()
        enct_ref[d] = enc_ref[d].T

    return [functools.partial(load, d) for d in range(enc_ref.shape[0])]


def pack_kernel(q_in, c_in, qc_ref, sem):
    copies = [pltpu.make_async_copy(x, qc_ref.at[i], sem.at[i]) for i, x in enumerate((q_in, c_in))]
    for copy in copies:
        copy.start()
    for copy in copies:
        copy.wait()


def after_first(loads, then):
    load = loads[0]

    def both():
        load()
        then()

    loads[0] = both


def make_gates(gate_ref, grad_ref, beam_ref, lens_ref):
    docs, labels = beam_ref.shape
    gate_ref[:, :labels] = grad_ref[...] * beam_ref[...].astype(F32)
    for d in range(docs):
        gate_ref[d : d + 1, labels:] = jnp.full((1, LANES), lens_ref[d], jnp.int32).astype(F32)


def own_kernel(enc_in, beam_in, grad_in, lens_in, qc_ref, enc_ref, gate_ref, enct_ref, attn_ref,
               score_ref, logit_ref, qsum_ref, csum_ref, beam_ref, grad_ref, lens_ref, sem):
    docs = enc_ref.shape[0]
    small = [(beam_in, beam_ref), (grad_in, grad_ref), (lens_in, lens_ref)]
    small = [pltpu.make_async_copy(x, y, sem.at[docs + i]) for i, (x, y) in enumerate(small)]
    copies = [
        pltpu.make_async_copy(enc_in.at[d], enc_ref.at[d], sem.at[d]) for d in range(docs)
    ]
    for copy in copies[:1] + small + copies[1:]:
        copy.start()
    loads = turn_around(enc_ref, enct_ref, copies)

    def gates():
        for copy in small:
            copy.wait()
        make_gates(gate_ref, grad_ref, beam_ref, lens_ref)

    after_first(loads, gates)
    qsum_ref[...], csum_ref[...] = label_chunk(
        doc_list(loads, enc_ref, enct_ref, gate_ref, attn_ref, score_ref, logit_ref),
        qc_ref[0], qc_ref[1], lanes_of(0, qc_ref.shape[1]), (None, None),
    )


def to_blocks(sums, rows_ref, out_refs):
    query_grad, class_grad = sums
    width = query_grad.shape[0]
    rows_ref[:, :width] = query_grad.astype(BF16).T
    rows_ref[:, width:] = class_grad.astype(BF16).T
    size = rows_ref.shape[0] // GROUP
    count = GROUP // len(out_refs)
    for i in range(GROUP):
        ref = out_refs[i // count]
        block = rows_ref[pl.ds(pl.multiple_of((turn() ^ i) * size, size), size), :]
        ref[(i % count) * size : (i % count + 1) * size, :] = block.astype(ref.dtype)


def other_kernel(lens_in, beam_ref, grad_ref, enc_ref, qc_ref, qsum_ref, csum_ref, gate_ref,
                 enct_ref, attn_ref, score_ref, logit_ref, *refs):
    refs, (lens_ref, sem) = refs[:-2], refs[-2:]
    copy = pltpu.make_async_copy(lens_in, lens_ref, sem)
    copy.start()

    def gates():
        copy.wait()
        make_gates(gate_ref, grad_ref, beam_ref, lens_ref)

    loads = turn_around(enc_ref, enct_ref)
    after_first(loads, gates)
    sums = label_chunk(
        doc_list(loads, enc_ref, enct_ref, gate_ref, attn_ref, score_ref, logit_ref),
        qc_ref[0], qc_ref[1], lanes_of(0, qc_ref.shape[1]), (qsum_ref[...], csum_ref[...]),
    )
    to_blocks(sums, refs[-1], refs[:-1])


def far_kernel(gate_ref, gate2_ref, enc_ref, enc2_ref, enct_ref,
               enct2_ref, qc_ref, attn_ref, score_ref, logit_ref, attn2_ref, score2_ref,
               logit2_ref, *refs):
    loads = [lambda: None] * enc_ref.shape[0]
    sums = label_chunk(
        doc_list(loads, enc_ref, enct_ref, gate_ref, attn_ref, score_ref, logit_ref)
        + doc_list(loads, enc2_ref, enct2_ref, gate2_ref, attn2_ref, score2_ref,
                   logit2_ref),
        qc_ref[0], qc_ref[1], lanes_of(2, qc_ref.shape[1]), (None, None),
    )
    to_blocks(sums, refs[-1], refs[:-1])


def state_parts(ks, gate_ref, chunks):
    docs, labels = gate_ref.shape[0], chunks[2].shape[1]
    ctx_grads = []
    for n, k in enumerate(ks):
        gate = gate_ref[:, lanes_of(k, labels)]
        gate = jnp.concatenate([gate, jnp.zeros((128 - docs, labels), F32)], axis=0).T
        c = chunks[4 * n + 2][1].astype(F32)
        ctx_grads.append([(c * gate[:, d : d + 1]).astype(BF16) for d in range(docs)])
    for d in range(docs):
        total = None
        for n in range(len(ks)):
            attn_ref, score_ref, qc_ref = chunks[4 * n : 4 * n + 3]
            part = mm(attn_ref[d], ctx_grads[n][d]) + mm(score_ref[d], qc_ref[0])
            total = part if total is None else total + part
        yield d, total


def away_kernel(ks, gate_ref, *refs):
    chunks, out_ref = refs[:-1], refs[-1]
    tokens, labels = chunks[0].shape[1:]
    for d, total in state_parts(ks, gate_ref, chunks):
        out_ref[d, :tokens] = total.astype(BF16)
        for n in range(len(ks)):
            logit = chunks[4 * n + 3][d : d + 1, :]
            high = logit.astype(BF16).astype(F32)
            pad = jnp.zeros((EXTRA - 2, labels), F32)
            pair = jnp.concatenate([high, logit - high, pad], axis=0)
            out_ref[d, tokens:, n * labels : (n + 1) * labels] = pair.astype(BF16)


def home_kernel(ks, gate_ref, *refs):
    chunks, (in_ref, out_ref, logit_ref, done_ref, sem) = refs[:-5], refs[-5:]
    tokens, labels = chunks[0].shape[1:]
    copies = []
    for d, total in state_parts(ks, gate_ref, chunks):
        done_ref[d] = (total + in_ref[d, :tokens].astype(F32)).astype(BF16)
        copies.append(pltpu.make_async_copy(done_ref.at[d], out_ref.at[d], sem.at[d]))
        copies[-1].start()
        for n, k in enumerate(ks):
            pair = in_ref[d, tokens:, n * labels : (n + 1) * labels].astype(F32)
            logit_ref[d : d + 1, lanes_of(k, labels)] = chunks[4 * n + 3][d : d + 1, :]
            logit_ref[d : d + 1, lanes_of(k ^ 1, labels)] = pair[0:1] + pair[1:2]
    for copy in copies:
        copy.wait()


def state_grad(gate, parts, more):
    docs, tokens, labels = parts[0][0].shape
    width = parts[0][2].shape[2]
    ins = [gate, *parts[0], *parts[1], *more]
    estimate = cost(4, docs, tokens, width, labels)
    if not more:
        out = shape((docs, tokens + EXTRA, width), BF16)
        return call(functools.partial(away_kernel, (0, 2)), out, ins, "state_away", (), estimate)
    out = shape((docs, tokens, width), BF16)
    return pl.pallas_call(
        functools.partial(home_kernel, (0, 2)),
        out_shape=[out, shape((docs, gate.shape[1] - LANES), F32)],
        in_specs=[VMEM] * len(ins),
        out_specs=[pl.BlockSpec(memory_space=pl.ANY), VMEM],
        scratch_shapes=[pltpu.VMEM(out.shape, BF16), pltpu.SemaphoreType.DMA((docs,))],
        compiler_params=PARAMS,
        cost_estimate=estimate,
        name="state_home",
    )(*ins)


def add_kernel(count, *refs):
    total = refs[0][...].astype(F32)
    for ref in refs[1:count]:
        total = total + ref[...].astype(F32)
    size = refs[count].shape[0]
    for i, ref in enumerate(refs[count:]):
        ref[...] = total[i * size : (i + 1) * size].astype(ref.dtype)


def add(arrays, dtypes, estimate=None):
    rows, cols = arrays[0].shape
    out = [shape((rows // len(dtypes), cols), dtype) for dtype in dtypes]
    return call(
        functools.partial(add_kernel, len(arrays)), out, arrays, "add", estimate=estimate
    )


def rows_kernel(*refs):
    block_refs, (out_ref, rows_ref, sem) = refs[:-3], refs[-3:]
    size = block_refs[0].shape[0]
    copies = []
    for i, ref in enumerate(block_refs):
        rows_ref[i] = ref[...].astype(F32)
        to = pl.ds(pl.multiple_of((turn() ^ i) * size, size), size)
        copies.append(pltpu.make_async_copy(rows_ref.at[i], out_ref.at[to], sem.at[i]))
        copies[-1].start()
    for copy in copies:
        copy.wait()


def to_rows(blocks):
    count = len(blocks)
    rows, cols = blocks[0].shape
    return pl.pallas_call(
        rows_kernel,
        out_shape=shape((count * rows, cols), F32),
        in_specs=[VMEM] * count,
        out_specs=pl.BlockSpec(memory_space=pl.ANY),
        scratch_shapes=[pltpu.VMEM((count, rows, cols), F32), pltpu.SemaphoreType.DMA((count,))],
        compiler_params=PARAMS,
        name="to_rows",
    )(*blocks)


def per_device(reps, blks, encoded, queries, classifiers, lengths, beam, logit_grad):
    labels, width = queries.shape
    docs, tokens, _ = encoded.shape
    total = reps * blks

    def swap(x, mask):
        return lax.ppermute(x, ("rep", "blk"), [(i, i ^ mask) for i in range(total)])

    core, ax = 1, 2
    ay, az, azz = blks, 2 * blks, 4 * blks
    turns = [0, az, ay, ay | az]

    qc = call(
        pack_kernel, shape((2, labels, width), BF16), [queries, classifiers], "pack",
        [pltpu.SemaphoreType.DMA((2,))], hbm=2,
    )
    encoded2, qc = lax.optimization_barrier((encoded, qc))
    far_qc = swap(qc, ax)
    encoded2, beam2, grad2 = swap(encoded2, core), swap(beam, core), swap(logit_grad, core)
    lengths2 = swap(lengths, core)

    per_chunk = [
        shape((docs, tokens, labels), BF16),
        shape((docs, tokens, labels), BF16),
        shape((docs, labels), F32),
    ]
    gates = shape((docs, beam.shape[1] + LANES), F32)
    turned = shape((docs, width, tokens), BF16)
    block = shape((labels // GROUP, 2 * width), BF16)
    halves = [shape((labels // 2, 2 * width), BF16)] * 2
    rows = [pltpu.VMEM((labels, 2 * width), BF16)]
    sums = [shape((width, labels), F32)] * 2
    estimate = functools.partial(cost, tokens=tokens, width=width, labels=labels)

    enc, gate, enct, attn, score, logit, *acc = call(
        own_kernel,
        [shape(encoded.shape, BF16), gates, turned] + per_chunk + sums,
        [encoded, beam, logit_grad, lengths, qc], "own_labels",
        [pltpu.VMEM(beam.shape, jnp.int32), pltpu.VMEM(beam.shape, F32),
         pltpu.SMEM((docs,), jnp.int32), pltpu.SemaphoreType.DMA((docs + 3,))],
        estimate(4, docs), hbm=4,
    )
    gate2, enct2, attn2, score2, logit2, keep, send = call(
        other_kernel, [gates, turned] + per_chunk + halves,
        [lengths2, beam2, grad2, encoded2, qc, *acc], "own_labels_other_docs",
        rows + [pltpu.SMEM((docs,), jnp.int32), pltpu.SemaphoreType.DMA(())],
        estimate(4, docs), hbm=1,
    )
    received = swap(send, ay)
    far_attn, far_score, far_logit, far_attn2, far_score2, far_logit2, *far = call(
        far_kernel, per_chunk + per_chunk + [block] * GROUP,
        [gate, gate2, enc, encoded2, enct, enct2, far_qc],
        "far_labels", rows, estimate(4, 2 * docs),
    )

    far, keep, received = lax.optimization_barrier((far, keep, received))
    keep, send = add([keep, received], [F32, BF16])
    send, far = lax.optimization_barrier((send, far))
    relayed = swap(far[3], ay)
    received = [swap(far[0], ax), swap(far[2], ax | ay)]
    (first,) = add([far[1], relayed], [BF16])
    first, far_attn2 = lax.optimization_barrier((first, far_attn2))
    received.append(swap(first, ax | az))
    near = swap(send, az)
    state2 = state_grad(
        gate2,
        [(attn2, score2, qc, logit2), (far_attn2, far_score2, far_qc, far_logit2)], [],
    )
    received, near = lax.optimization_barrier((received, near))
    state_in = swap(state2, core)
    (own,) = add([keep, near, *received], [BF16], LONG)
    far_attn, far_score, own = lax.optimization_barrier((far_attn, far_score, own))
    state, logits = state_grad(
        gate, [(attn, score, qc, logit), (far_attn, far_score, far_qc, far_logit)],
        [state_in],
    )
    received, state = lax.optimization_barrier((swap(own, azz), state))
    (own,) = add([own, received], [BF16])
    if reps > 8:
        members = [[i * 8 + j for i in range(reps // 8)] for j in range(8)]
        own = lax.psum(own.astype(F32), "rep", axis_index_groups=members).astype(BF16)

    both, second, first = lax.optimization_barrier([swap(own, mask) for mask in turns[:0:-1]])
    label_grad = to_rows([own, first, second, both])
    return logits, state, label_grad


def solution(mesh):
    reps, blks = mesh.shape["rep"], mesh.shape["blk"]
    assert blks == 4 and reps >= 8 and reps & (reps - 1) == 0
    in_specs = (
        P(("rep", "blk"), None, None),
        P("blk", None),
        P("blk", None),
        P(("rep", "blk")),
        P(("rep", "blk"), None),
        P(("rep", "blk"), None),
    )
    out_specs = (P(("rep", "blk"), None), P(("rep", "blk"), None, None), P("blk", None))
    return jax.shard_map(
        functools.partial(per_device, reps, blks),
        mesh=mesh, in_specs=in_specs, out_specs=out_specs, check_vma=False,
    )
```

```python
import functools

import jax
import jax.numpy as jnp
from jax import lax
from jax.experimental import pallas as pl
from jax.experimental.pallas import tpu as pltpu
from jax.sharding import PartitionSpec as P

F32 = jnp.float32
BF16 = jnp.bfloat16
VMEM = pl.BlockSpec(memory_space=pltpu.VMEM)
SMEM = pl.BlockSpec(memory_space=pltpu.SMEM)
HBM = pl.BlockSpec(memory_space=pltpu.HBM)
PARAMS = pltpu.CompilerParams(vmem_limit_bytes=20 * 1024 * 1024)
GROUP = 4
LANES = 128
EXTRA = 16


LONG = pl.CostEstimate(flops=10**11, transcendentals=0, bytes_accessed=0)


def shape(dims, dtype):
    return jax.ShapeDtypeStruct(dims, dtype)


def mm(a, b):
    return jnp.dot(a, b, preferred_element_type=F32)


def cost(products, docs, tokens, width, labels):
    return pl.CostEstimate(
        flops=2 * products * docs * tokens * width * labels,
        transcendentals=docs * tokens * labels,
        bytes_accessed=4 * docs * tokens * width,
    )


def call(kernel, out_shape, ins, name, scratch=(), estimate=None, hbm=0):
    single = not isinstance(out_shape, (list, tuple))
    ins = [pltpu.with_memory_space_constraint(x, pltpu.HBM) for x in ins[:hbm]] + list(ins[hbm:])
    return pl.pallas_call(
        kernel,
        out_shape=out_shape,
        in_specs=[
            HBM if i < hbm else SMEM if x.ndim == 1 else VMEM for i, x in enumerate(ins)
        ],
        out_specs=VMEM if single else [VMEM] * len(out_shape),
        scratch_shapes=scratch,
        compiler_params=PARAMS,
        cost_estimate=estimate,
        name=name,
    )(*ins)


def lanes_of(k, labels):
    return pl.ds(pl.multiple_of((lax.axis_index("blk") ^ k) * labels, labels), labels)


def turn():
    rep = lax.axis_index("rep")
    return (rep & 1) * 2 + ((rep >> 1) & 1)


def label_chunk(docs, q, c, lanes, sums):
    qt = q.T
    ct = c.T.astype(F32)
    labels = q.shape[0]

    def products(doc):
        load, enc_ref, enct_ref, gate_ref = doc[:4]
        load()
        enc = enc_ref[...]
        g = gate_ref[:, lanes]
        both = mm(enc, jnp.concatenate([qt, (ct * g).astype(BF16)], axis=1))
        return g, both[:, :labels], both[:, labels:]

    query_grad, class_grad = sums
    ahead = products(docs[0])
    for i, (_, _, enct_ref, gate_ref, attn_ref, score_ref, logit_ref) in enumerate(docs):
        g, scores, attn_grad = ahead
        if i + 1 < len(docs):
            ahead = products(docs[i + 1])
        length = gate_ref[:, gate_ref.shape[1] - LANES :][:, :1]
        token = lax.broadcasted_iota(jnp.int32, scores.shape, 0).astype(F32)
        expo = jnp.where(token < length, jnp.exp(scores), 0.0)
        attn = expo * (1.0 / jnp.sum(expo, axis=0, keepdims=True))
        attn_b = attn.astype(BF16)
        attn_ref[...] = attn_b
        inner = jnp.sum(attn * attn_grad, axis=0, keepdims=True)
        score_grad = (attn * (attn_grad - inner)).astype(BF16)
        score_ref[...] = score_grad
        both = mm(enct_ref[...], jnp.concatenate([attn_b, score_grad], axis=1))
        context, part = both[:, :labels], both[:, labels:]
        query_grad = part if query_grad is None else query_grad + part
        logit_ref[...] = jnp.sum(context * ct, axis=0, keepdims=True)
        part = context * g
        class_grad = part if class_grad is None else class_grad + part
    return query_grad, class_grad


def doc_list(loads, enc_ref, enct_ref, gate_ref, attn_ref, score_ref, logit_ref):
    return [
        (loads[d], enc_ref.at[d], enct_ref.at[d], gate_ref.at[d : d + 1], attn_ref.at[d],
         score_ref.at[d], logit_ref.at[d : d + 1])
        for d in range(enc_ref.shape[0])
    ]


def turn_around(enc_ref, enct_ref, copies=None):
    def load(d):
        if copies is not None:
            copies[d].wait()
        enct_ref[d] = enc_ref[d].T

    return [functools.partial(load, d) for d in range(enc_ref.shape[0])]


def pack_kernel(q_in, c_in, qc_ref, sem):
    copies = [pltpu.make_async_copy(x, qc_ref.at[i], sem.at[i]) for i, x in enumerate((q_in, c_in))]
    for copy in copies:
        copy.start()
    for copy in copies:
        copy.wait()


def after_first(loads, then):
    load = loads[0]

    def both():
        load()
        then()

    loads[0] = both


def make_gates(gate_ref, grad_ref, beam_ref, lens_ref):
    docs, labels = beam_ref.shape
    gate_ref[:, :labels] = grad_ref[...] * beam_ref[...].astype(F32)
    for d in range(docs):
        gate_ref[d : d + 1, labels:] = jnp.full((1, LANES), lens_ref[d], jnp.int32).astype(F32)


def own_kernel(enc_in, beam_in, grad_in, lens_in, qc_ref, enc_ref, gate_ref, enct_ref, attn_ref,
               score_ref, logit_ref, qsum_ref, csum_ref, beam_ref, grad_ref, lens_ref, sem):
    docs = enc_ref.shape[0]
    small = [(beam_in, beam_ref), (grad_in, grad_ref), (lens_in, lens_ref)]
    small = [pltpu.make_async_copy(x, y, sem.at[docs + i]) for i, (x, y) in enumerate(small)]
    copies = [
        pltpu.make_async_copy(enc_in.at[d], enc_ref.at[d], sem.at[d]) for d in range(docs)
    ]
    for copy in copies[:1] + small + copies[1:]:
        copy.start()
    loads = turn_around(enc_ref, enct_ref, copies)

    def gates():
        for copy in small:
            copy.wait()
        make_gates(gate_ref, grad_ref, beam_ref, lens_ref)

    after_first(loads, gates)
    qsum_ref[...], csum_ref[...] = label_chunk(
        doc_list(loads, enc_ref, enct_ref, gate_ref, attn_ref, score_ref, logit_ref),
        qc_ref[0], qc_ref[1], lanes_of(0, qc_ref.shape[1]), (None, None),
    )


def to_blocks(sums, rows_ref, out_refs):
    query_grad, class_grad = sums
    width = query_grad.shape[0]
    rows_ref[:, :width] = query_grad.astype(BF16).T
    rows_ref[:, width:] = class_grad.astype(BF16).T
    size = rows_ref.shape[0] // GROUP
    count = GROUP // len(out_refs)
    for i in range(GROUP):
        ref = out_refs[i // count]
        block = rows_ref[pl.ds(pl.multiple_of((turn() ^ i) * size, size), size), :]
        ref[(i % count) * size : (i % count + 1) * size, :] = block.astype(ref.dtype)


def other_kernel(lens_in, beam_ref, grad_ref, enc_ref, qc_ref, qsum_ref, csum_ref, gate_ref,
                 enct_ref, attn_ref, score_ref, logit_ref, *refs):
    refs, (lens_ref, sem) = refs[:-2], refs[-2:]
    copy = pltpu.make_async_copy(lens_in, lens_ref, sem)
    copy.start()

    def gates():
        copy.wait()
        make_gates(gate_ref, grad_ref, beam_ref, lens_ref)

    loads = turn_around(enc_ref, enct_ref)
    after_first(loads, gates)
    sums = label_chunk(
        doc_list(loads, enc_ref, enct_ref, gate_ref, attn_ref, score_ref, logit_ref),
        qc_ref[0], qc_ref[1], lanes_of(0, qc_ref.shape[1]), (qsum_ref[...], csum_ref[...]),
    )
    to_blocks(sums, refs[-1], refs[:-1])


def far_kernel(gate_ref, gate2_ref, enc_ref, enc2_ref, enct_ref,
               enct2_ref, qc_ref, attn_ref, score_ref, logit_ref, attn2_ref, score2_ref,
               logit2_ref, *refs):
    loads = [lambda: None] * enc_ref.shape[0]
    sums = label_chunk(
        doc_list(loads, enc_ref, enct_ref, gate_ref, attn_ref, score_ref, logit_ref)
        + doc_list(loads, enc2_ref, enct2_ref, gate2_ref, attn2_ref, score2_ref,
                   logit2_ref),
        qc_ref[0], qc_ref[1], lanes_of(2, qc_ref.shape[1]), (None, None),
    )
    to_blocks(sums, refs[-1], refs[:-1])


def state_parts(ks, gate_ref, chunks):
    docs, labels = gate_ref.shape[0], chunks[2].shape[1]
    ctx_grads = []
    for n, k in enumerate(ks):
        gate = gate_ref[:, lanes_of(k, labels)]
        gate = jnp.concatenate([gate, jnp.zeros((128 - docs, labels), F32)], axis=0).T
        c = chunks[4 * n + 2][1].astype(F32)
        ctx_grads.append([(c * gate[:, d : d + 1]).astype(BF16) for d in range(docs)])
    for d in range(docs):
        total = None
        for n in range(len(ks)):
            attn_ref, score_ref, qc_ref = chunks[4 * n : 4 * n + 3]
            part = mm(attn_ref[d], ctx_grads[n][d]) + mm(score_ref[d], qc_ref[0])
            total = part if total is None else total + part
        yield d, total


def away_kernel(ks, gate_ref, *refs):
    chunks, out_ref = refs[:-1], refs[-1]
    tokens, labels = chunks[0].shape[1:]
    for d, total in state_parts(ks, gate_ref, chunks):
        out_ref[d, :tokens] = total.astype(BF16)
        for n in range(len(ks)):
            logit = chunks[4 * n + 3][d : d + 1, :]
            high = logit.astype(BF16).astype(F32)
            pad = jnp.zeros((EXTRA - 2, labels), F32)
            pair = jnp.concatenate([high, logit - high, pad], axis=0)
            out_ref[d, tokens:, n * labels : (n + 1) * labels] = pair.astype(BF16)


def home_kernel(ks, gate_ref, *refs):
    chunks, (in_ref, out_ref, logit_ref, done_ref, sem) = refs[:-5], refs[-5:]
    tokens, labels = chunks[0].shape[1:]
    copies = []
    for d, total in state_parts(ks, gate_ref, chunks):
        done_ref[d] = (total + in_ref[d, :tokens].astype(F32)).astype(BF16)
        copies.append(pltpu.make_async_copy(done_ref.at[d], out_ref.at[d], sem.at[d]))
        copies[-1].start()
        for n, k in enumerate(ks):
            pair = in_ref[d, tokens:, n * labels : (n + 1) * labels].astype(F32)
            logit_ref[d : d + 1, lanes_of(k, labels)] = chunks[4 * n + 3][d : d + 1, :]
            logit_ref[d : d + 1, lanes_of(k ^ 1, labels)] = pair[0:1] + pair[1:2]
    for copy in copies:
        copy.wait()


def state_grad(gate, parts, more):
    docs, tokens, labels = parts[0][0].shape
    width = parts[0][2].shape[2]
    ins = [gate, *parts[0], *parts[1], *more]
    estimate = cost(4, docs, tokens, width, labels)
    if not more:
        out = shape((docs, tokens + EXTRA, width), BF16)
        return call(functools.partial(away_kernel, (0, 2)), out, ins, "state_away", (), estimate)
    out = shape((docs, tokens, width), BF16)
    return pl.pallas_call(
        functools.partial(home_kernel, (0, 2)),
        out_shape=[out, shape((docs, gate.shape[1] - LANES), F32)],
        in_specs=[VMEM] * len(ins),
        out_specs=[pl.BlockSpec(memory_space=pl.ANY), VMEM],
        scratch_shapes=[pltpu.VMEM(out.shape, BF16), pltpu.SemaphoreType.DMA((docs,))],
        compiler_params=PARAMS,
        cost_estimate=estimate,
        name="state_home",
    )(*ins)


def add_kernel(count, *refs):
    total = refs[0][...].astype(F32)
    for ref in refs[1:count]:
        total = total + ref[...].astype(F32)
    size = refs[count].shape[0]
    for i, ref in enumerate(refs[count:]):
        ref[...] = total[i * size : (i + 1) * size].astype(ref.dtype)


def add(arrays, dtypes, estimate=None):
    rows, cols = arrays[0].shape
    out = [shape((rows // len(dtypes), cols), dtype) for dtype in dtypes]
    return call(
        functools.partial(add_kernel, len(arrays)), out, arrays, "add", estimate=estimate
    )


def rows_kernel(*refs):
    block_refs, (out_ref, rows_ref, sem) = refs[:-3], refs[-3:]
    size = block_refs[0].shape[0]
    core = lax.axis_index("blk") & 1
    copies = []
    for i, (ref, block) in enumerate(zip(block_refs, (0, 1 + core, 2 - core, 3))):
        rows_ref[i] = ref[...].astype(F32)
        to = pl.ds(pl.multiple_of((turn() ^ block) * size, size), size)
        copies.append(pltpu.make_async_copy(rows_ref.at[i], out_ref.at[to], sem.at[i]))
        copies[-1].start()
    for copy in copies:
        copy.wait()


def to_rows(blocks):
    count = len(blocks)
    rows, cols = blocks[0].shape
    return pl.pallas_call(
        rows_kernel,
        out_shape=shape((count * rows, cols), F32),
        in_specs=[VMEM] * count,
        out_specs=pl.BlockSpec(memory_space=pl.ANY),
        scratch_shapes=[pltpu.VMEM((count, rows, cols), F32), pltpu.SemaphoreType.DMA((count,))],
        compiler_params=PARAMS,
        name="to_rows",
    )(*blocks)


def per_device(reps, blks, encoded, queries, classifiers, lengths, beam, logit_grad):
    labels, width = queries.shape
    docs, tokens, _ = encoded.shape
    total = reps * blks

    def swap(x, mask, other=None):
        masks = (mask, mask if other is None else other)
        return lax.ppermute(x, ("rep", "blk"), [(i, i ^ masks[i & 1]) for i in range(total)])

    core, ax = 1, 2
    ay, az, azz = blks, 2 * blks, 4 * blks
    turns = [0, az, ay, ay | az]

    qc = call(
        pack_kernel, shape((2, labels, width), BF16), [queries, classifiers], "pack",
        [pltpu.SemaphoreType.DMA((2,))], hbm=2,
    )
    encoded2, qc = lax.optimization_barrier((encoded, qc))
    far_qc = swap(qc, ax)
    encoded2, beam2, grad2 = swap(encoded2, core), swap(beam, core), swap(logit_grad, core)
    lengths2 = swap(lengths, core)

    per_chunk = [
        shape((docs, tokens, labels), BF16),
        shape((docs, tokens, labels), BF16),
        shape((docs, labels), F32),
    ]
    gates = shape((docs, beam.shape[1] + LANES), F32)
    turned = shape((docs, width, tokens), BF16)
    block = shape((labels // GROUP, 2 * width), BF16)
    halves = [shape((labels // 2, 2 * width), BF16)] * 2
    rows = [pltpu.VMEM((labels, 2 * width), BF16)]
    sums = [shape((width, labels), F32)] * 2
    estimate = functools.partial(cost, tokens=tokens, width=width, labels=labels)

    enc, gate, enct, attn, score, logit, *acc = call(
        own_kernel,
        [shape(encoded.shape, BF16), gates, turned] + per_chunk + sums,
        [encoded, beam, logit_grad, lengths, qc], "own_labels",
        [pltpu.VMEM(beam.shape, jnp.int32), pltpu.VMEM(beam.shape, F32),
         pltpu.SMEM((docs,), jnp.int32), pltpu.SemaphoreType.DMA((docs + 3,))],
        estimate(4, docs), hbm=4,
    )
    gate2, enct2, attn2, score2, logit2, keep, send = call(
        other_kernel, [gates, turned] + per_chunk + halves,
        [lengths2, beam2, grad2, encoded2, qc, *acc], "own_labels_other_docs",
        rows + [pltpu.SMEM((docs,), jnp.int32), pltpu.SemaphoreType.DMA(())],
        estimate(4, docs), hbm=1,
    )
    received = swap(send, ay)
    far_attn, far_score, far_logit, far_attn2, far_score2, far_logit2, *far = call(
        far_kernel, per_chunk + per_chunk + [block] * GROUP,
        [gate, gate2, enc, encoded2, enct, enct2, far_qc],
        "far_labels", rows, estimate(4, 2 * docs),
    )

    far, keep, received = lax.optimization_barrier((far, keep, received))
    keep, send = add([keep, received], [F32, BF16])
    send, far = lax.optimization_barrier((send, far))
    relayed = swap(far[3], ay)
    received = [swap(far[0], ax), swap(far[2], ax | ay)]
    (first,) = add([far[1], relayed], [BF16])
    first, far_attn2 = lax.optimization_barrier((first, far_attn2))
    received.append(swap(first, ax | az))
    near = swap(send, az)
    state2 = state_grad(
        gate2,
        [(attn2, score2, qc, logit2), (far_attn2, far_score2, far_qc, far_logit2)], [],
    )
    received, near = lax.optimization_barrier((received, near))
    state_in = swap(state2, core)
    (own,) = add([keep, near, *received], [BF16], LONG)
    far_attn, far_score, own = lax.optimization_barrier((far_attn, far_score, own))
    state, logits = state_grad(
        gate, [(attn, score, qc, logit), (far_attn, far_score, far_qc, far_logit)],
        [state_in],
    )
    received, state = lax.optimization_barrier((swap(own, azz), state))
    (own,) = add([own, received], [BF16])
    if reps > 8:
        members = [[i * 8 + j for i in range(reps // 8)] for j in range(8)]
        own = lax.psum(own.astype(F32), "rep", axis_index_groups=members).astype(BF16)

    both, second, first = lax.optimization_barrier(
        [swap(own, ay | az), swap(own, ay, az), swap(own, az, ay)]
    )
    label_grad = to_rows([own, first, second, both])
    return logits, state, label_grad


def solution(mesh):
    reps, blks = mesh.shape["rep"], mesh.shape["blk"]
    assert blks == 4 and reps >= 8 and reps & (reps - 1) == 0
    in_specs = (
        P(("rep", "blk"), None, None),
        P("blk", None),
        P("blk", None),
        P(("rep", "blk")),
        P(("rep", "blk"), None),
        P(("rep", "blk"), None),
    )
    out_specs = (P(("rep", "blk"), None), P(("rep", "blk"), None, None), P("blk", None))
    return jax.shard_map(
        functools.partial(per_device, reps, blks),
        mesh=mesh, in_specs=in_specs, out_specs=out_specs, check_vma=False,
    )
```
